32 devices in a mesh: head: 4 (over y, core), seq: 8 (over z, x).
Axes of the slice: x: 2, y: 2, z: 4, core: 2. Of those that a mesh axis runs over, the one named last changes fastest.
Arguments:
- block_in: bfloat16 [4096, 2048], P(('seq', 'head')), may hold values from -6 to 6
- out_cot: bfloat16 [4096, 2048], P(('seq', 'head')), may hold values from -6 to 6
- gain_one: bfloat16 [2048], replicated, may hold values from 0.5 to 1.5
- qkv_weight: bfloat16 [2048, 16, 512], P(None, 'head'), may hold values from -0.125 to 0.125
- conv_weight: bfloat16 [4, 16, 512], P(None, 'head'), may hold values from -3 to 3
- gate_weight: bfloat16 [2048, 16, 256], P(None, 'head'), may hold values from -0.125 to 0.125
- gain_out: bfloat16 [256], replicated, may hold values from 0.5 to 1.5
- out_weight: bfloat16 [16, 256, 2048], P('head'), may hold values from -0.09375 to 0.09375
- gain_two: bfloat16 [2048], replicated, may hold values from 0.5 to 1.5
- mlp_gate: bfloat16 [2048, 5632], P(None, 'seq'), may hold values from -0.125 to 0.125
- mlp_up: bfloat16 [2048, 5632], P(None, 'seq'), may hold values from -0.125 to 0.125
- mlp_down: bfloat16 [5632, 2048], P('seq'), may hold values from -0.078125 to 0.078125
- decay_code: int32 [4096, 16], P('seq', 'head'), may hold values from 0 to 1024, as said below
- beta_code: int32 [4096, 16], P('seq', 'head'), may hold values from 0 to 256
Outputs:
- output: bfloat16 [4096, 2048], P(('seq', 'head'))
- d_input: bfloat16 [4096, 2048], P(('seq', 'head'))
- grad_gain_one: float32 [2048], P(('head', 'seq'))
- grad_qkv: float32 [2048, 16, 512], P('seq', 'head')
- grad_conv: float32 [4, 16, 512], P(None, 'head', 'seq')
- grad_gate: float32 [2048, 16, 256], P('seq', 'head')
- grad_gain_out: float32 [256], P(('head', 'seq'))
- grad_out: float32 [16, 256, 2048], P('head', None, 'seq')
- grad_gain_two: float32 [2048], P(('head', 'seq'))
- grad_mlp_gate: float32 [2048, 5632], P('head', 'seq')
- grad_mlp_up: float32 [2048, 5632], P('head', 'seq')
- grad_mlp_down: float32 [5632, 2048], P('seq', 'head')
The draws below stay inside these ranges and needn't reach their ends.
Inputs may be any that keep to these rules, and one draw needn't show every extreme that they name: `decay_code`: values to 1023 grade a head's forgetting at a token; 1024 marks a token at which the head's state loses a fixed share at once.
All inputs are finite; a program needn't handle non-finite values.
Results may differ from the reference program's by a relative error of at most 0.025.
Values may be sent and summed in bfloat16 or wider, within the bound.
A program may use at most 256 MiB of HBM per device.

```python
import math
import jax
import jax.numpy as jnp
from jax import lax

D = 2048
MIXER_HEADS = 16
DK = 128
DV = 256
FF = 5632
STRETCH = 64
CONV = 4
INNER = 512
SEQUENCE_TOKENS = 4096


def draw_decay_code(key, part):
    key = jax.random.fold_in(key, 17)
    quick_random_key, gradual_random_key, select_random_key, offset_random_key, spike_random_key, location_random_key = jax.random.split(key, 6)
    fast_base = jax.random.randint(quick_random_key, (1, MIXER_HEADS), 0, 400)
    slow_base = jax.random.randint(gradual_random_key, (1, MIXER_HEADS), 880, 901)
    slow_pick = jax.random.randint(select_random_key, (1, MIXER_HEADS), 0, 2)
    baseline_level = jnp.where(slow_pick == 1, slow_base, fast_base)
    random_offset = jax.random.randint(offset_random_key, (SEQUENCE_TOKENS, MIXER_HEADS), 0, 123)
    spike_events = jax.random.randint(spike_random_key, (SEQUENCE_TOKENS, MIXER_HEADS), 0, SEQUENCE_TOKENS) == 0
    located_items = jax.random.randint(location_random_key, (1, MIXER_HEADS), 0, SEQUENCE_TOKENS)
    token_locations = lax.broadcasted_iota(jnp.int32, (SEQUENCE_TOKENS, MIXER_HEADS), 0)
    spike_markers = jnp.logical_or(spike_events, token_locations == located_items)
    return jnp.where(spike_markers, 1024, baseline_level + random_offset).astype(jnp.int32)


def with_ends(drawn, own_key, least, top_value):
    place = [jax.random.randint(jax.random.fold_in(own_key, axis), (), 0, length) for axis, length in enumerate(drawn.shape)]
    longest = drawn.shape.index(max(drawn.shape))
    neighbour = place[:longest] + [(place[longest] + 1) % drawn.shape[longest]] + place[longest + 1:]
    return drawn.at[tuple(place)].set(least).at[tuple(neighbour)].set(top_value)


def block_scale(own_key, shape, pieces, smallest, largest):
    factor_of = 1.0
    for axis_at, shards_of in pieces:
        draws = jax.random.uniform(jax.random.fold_in(jax.random.fold_in(own_key, 6), axis_at), (shards_of,), jnp.float32, smallest / len(pieces), largest / len(pieces))
        factor_of = factor_of * jnp.repeat(jnp.exp(draws), shape[axis_at] // shards_of).reshape((-1,) + (1,) * (len(shape) - 1 - axis_at))
    return factor_of


def gaussian(stream_key, dims, scale, limit, cuts=(), held_as=jnp.bfloat16):
    level = block_scale(stream_key, dims, cuts, -0.22, 0.18) if cuts else 1.0
    drawn = jax.random.normal(stream_key, dims, jnp.float32) * scale * level
    return jnp.minimum(jnp.maximum(drawn, -limit), limit).astype(held_as)


def setup_inputs(seed: int = 0) -> dict:
    arg_keys = jax.random.split(jax.random.key(seed), 15)
    block_in = gaussian(arg_keys[0], (SEQUENCE_TOKENS, D), 1.0, 6.0, ((0, 32),))
    out_cot = gaussian(arg_keys[1], (SEQUENCE_TOKENS, D), 1.0, 6.0, ((0, 32),))
    gain_one = jnp.clip(1.0 + 0.1 * jax.random.normal(arg_keys[2], (D,), jnp.float32), 0.5, 1.5).astype(jnp.bfloat16)
    qkv_weight = gaussian(arg_keys[3], (D, MIXER_HEADS, INNER), D ** -0.5, 0.125, ((1, 4),))
    conv_weight = gaussian(arg_keys[4], (CONV, MIXER_HEADS, INNER), 0.5, 3.0, ((1, 4),))
    gate_weight = gaussian(arg_keys[5], (D, MIXER_HEADS, DV), D ** -0.5, 0.125, ((1, 4),))
    gain_out = jnp.clip(1.0 + 0.1 * jax.random.normal(arg_keys[6], (DV,), jnp.float32), 0.5, 1.5).astype(jnp.bfloat16)
    out_weight = gaussian(arg_keys[7], (MIXER_HEADS, DV, D), (MIXER_HEADS * DV) ** -0.5, 0.09375, ((0, 4),))
    gain_two = jnp.clip(1.0 + 0.1 * jax.random.normal(arg_keys[8], (D,), jnp.float32), 0.5, 1.5).astype(jnp.bfloat16)
    mlp_gate = gaussian(arg_keys[9], (D, FF), D ** -0.5, 0.125, ((1, 8),))
    mlp_up = gaussian(arg_keys[10], (D, FF), D ** -0.5, 0.125, ((1, 8),))
    mlp_down = gaussian(arg_keys[11], (FF, D), FF ** -0.5, 0.078125, ((0, 8),))
    decay_code = draw_decay_code(jax.random.fold_in(arg_keys[14], 71), 0)
    beta_code = with_ends(jax.random.randint(arg_keys[13], (SEQUENCE_TOKENS, MIXER_HEADS), 0, 257), jax.random.fold_in(arg_keys[13], 1), 0, 256).astype(jnp.int32)
    return dict(block_in=block_in, out_cot=out_cot, gain_one=gain_one, qkv_weight=qkv_weight, conv_weight=conv_weight, gate_weight=gate_weight, gain_out=gain_out, out_weight=out_weight, gain_two=gain_two, mlp_gate=mlp_gate, mlp_up=mlp_up, mlp_down=mlp_down, decay_code=decay_code, beta_code=beta_code)


@jax.custom_vjp
def low(v):
    return lax.optimization_barrier(v.astype(jnp.bfloat16)).astype(jnp.float32)

@jax.custom_vjp
def low_back(v):
    return v

def low_keep(v):
    return (low(v), None)

def low_pass(kept, grad):
    return (grad,)

def back_keep(v):
    return (v, None)

def back_low(kept, grad):
    return (low(grad),)
low.defvjp(low_keep, low_pass)
low_back.defvjp(back_keep, back_low)
epsilon = 1e-06
exact_mode = lax.Precision.HIGHEST

def exact_dot(form, left, right):
    return jnp.einsum(form, left, right, precision=exact_mode)

def rms_scale(tensor):
    return lax.rsqrt(lax.optimization_barrier(jnp.mean(tensor * tensor, axis=-1, keepdims=True)) + epsilon)

def unit_rows(tensor):
    return tensor * lax.rsqrt(lax.optimization_barrier(jnp.sum(tensor * tensor, axis=-1, keepdims=True)) + epsilon)

def log_rates(decay_code, total_len):
    code_level = decay_code.astype(jnp.float32) / 1023.0
    smooth = -jnp.exp(-code_level * math.log(total_len / 32.0)) / 32.0
    return jnp.where(decay_code == 1024, -0.25, smooth)

def conv_features(padded, conv_f):
    row_total = padded.shape[0] - conv_f.shape[0] + 1
    summed = conv_f[0] * padded[0:row_total]
    for tap_index in range(1, conv_f.shape[0]):
        summed = summed + conv_f[tap_index] * padded[tap_index:tap_index + row_total]
    activated = jax.nn.silu(summed)
    queries = unit_rows(activated[..., :DK]) * DK ** (-0.5)
    key_rows = unit_rows(activated[..., DK:2 * DK])
    return (queries, key_rows, activated[..., 2 * DK:])

def decay_masks(decay_log):
    block_size = decay_log.shape[-1]
    row_ids = lax.broadcasted_iota(jnp.int32, (block_size, block_size), 0)
    col_ids = lax.broadcasted_iota(jnp.int32, (block_size, block_size), 1)
    causal = (row_ids >= col_ids).astype(jnp.float32)
    strict = (row_ids > col_ids).astype(jnp.float32)
    log_gaps = decay_log[..., :, None] - decay_log[..., None, :]
    within = jnp.exp(log_gaps * causal) * causal
    return (within, strict)

def solve_parts(key_blk, value_blk, decay_log, beta_blk):
    within, strict = decay_masks(decay_log)
    key_dots = exact_dot('...ik,...jk->...ij', key_blk, key_blk)
    lower_part = within * strict * key_dots * beta_blk[..., :, None]
    block_size = decay_log.shape[-1]
    system = jnp.eye(block_size, dtype=jnp.float32) + lower_part
    decay_run = jnp.exp(decay_log)
    right_side = jnp.concatenate([beta_blk[..., None] * value_blk, (beta_blk * decay_run)[..., None] * key_blk], axis=-1)
    solved = jax.scipy.linalg.solve_triangular(system, right_side, lower=True, unit_diagonal=True)
    width_v = value_blk.shape[-1]
    return (solved[..., :width_v], solved[..., width_v:])

def stretch_out(query_blk, key_blk, decay_log, new_values, new_keys, states):
    within, strict = decay_masks(decay_log)
    decay_run = jnp.exp(decay_log)
    fresh_values = new_values - exact_dot('...ck,...vk->...cv', new_keys, states)
    scores = exact_dot('...ik,...jk->...ij', query_blk, key_blk) * within
    return decay_run[..., None] * exact_dot('...ck,...vk->...cv', query_blk, states) + exact_dot('...ij,...jv->...iv', scores, fresh_values)

def head_branch(core, gate_pre, gain_head):
    return core * rms_scale(core) * gain_head * jax.nn.silu(gate_pre)

def recurrence(queries, key_rows, values, rates, betas):
    block_count = queries.shape[0] // STRETCH

    def stretched(tensor):
        return tensor.reshape((block_count, STRETCH) + tensor.shape[1:]).swapaxes(1, 2)
    decay_blocks = jnp.cumsum(stretched(rates), axis=-1)

    @jax.checkpoint
    def advance(carried, block):
        query_blk, key_blk, value_blk, decay_log, beta_blk = block
        new_values, new_keys = solve_parts(key_blk, value_blk, decay_log, beta_blk)
        result = stretch_out(query_blk, key_blk, decay_log, new_values, new_keys, carried)
        fresh_values = new_values - exact_dot('hck,hvk->hcv', new_keys, carried)
        tail_decay = jnp.exp(decay_log[..., -1:] - decay_log)
        next_state = jnp.exp(decay_log[..., -1:])[..., None] * carried + exact_dot('hcv,hck->hvk', fresh_values * tail_decay[..., None], key_blk)
        return (next_state, result)
    start_state = jnp.zeros((queries.shape[1], values.shape[-1], queries.shape[-1]), jnp.float32)
    _, results = lax.scan(advance, start_state, (stretched(queries), stretched(key_rows), stretched(values), decay_blocks, stretched(betas)))
    return results.swapaxes(1, 2).reshape(queries.shape[:2] + (values.shape[-1],))

def reference(block_in, out_cot, gain_one, qkv_weight, conv_weight, gate_weight, gain_out, out_weight, gain_two, mlp_gate, mlp_up, mlp_down, decay_code, beta_code):
    rates = log_rates(decay_code, SEQUENCE_TOKENS)
    betas = 0.5 + beta_code.astype(jnp.float32) / 512.0

    def forward(input_f, gain_first, qkv_f, conv_f, gate_f, gain_head, out_f, gain_second, gate_mlp_f, up_mlp_f, down_mlp_f):
        hat_one = input_f * rms_scale(input_f)
        normed_one = low(hat_one * gain_first)
        mixed_in = low_back(low(exact_dot('td,dhc->thc', normed_one, qkv_f)))
        gate_pre = low_back(exact_dot('td,dhv->thv', normed_one, gate_f))
        padding = jnp.zeros((conv_f.shape[0] - 1,) + mixed_in.shape[1:], jnp.float32)
        queries, key_rows, values = conv_features(jnp.concatenate([padding, mixed_in], 0), conv_f)
        core = recurrence(queries, key_rows, values, rates, betas)
        branch = low(head_branch(core, gate_pre, gain_head))
        middle = input_f + low_back(exact_dot('thv,hvd->td', branch, out_f))
        hat_two = middle * rms_scale(middle)
        normed_two = low(hat_two * gain_second)
        gate_mlp = low_back(exact_dot('td,df->tf', normed_two, gate_mlp_f))
        up_mlp = low_back(exact_dot('td,df->tf', normed_two, up_mlp_f))
        hidden = low(jax.nn.silu(gate_mlp) * up_mlp)
        return middle + exact_dot('tf,fd->td', hidden, down_mlp_f)
    floats = tuple((tensor.astype(jnp.float32) for tensor in (block_in, gain_one, qkv_weight, conv_weight, gate_weight, gain_out, out_weight, gain_two, mlp_gate, mlp_up, mlp_down)))
    result, pullback = jax.vjp(forward, *floats)
    gradients = pullback(out_cot.astype(jnp.float32))
    return (result.astype(jnp.bfloat16), gradients[0].astype(jnp.bfloat16), gradients[1], gradients[2], gradients[3], gradients[4], gradients[5], gradients[6], gradients[7], gradients[8], gradients[9], gradients[10])
```

```python
import functools
import math

import jax
import jax.numpy as jnp
from jax import lax
from jax.experimental import pallas as pl
from jax.experimental.pallas import tpu as pltpu
from jax.sharding import PartitionSpec as P

DK = 128
DV = 256
STRETCH = 64
GROUP = 4 * STRETCH
INNER = 2 * DK + DV
BETA, GAMMA, BETA_GAMMA, TAIL, LAST, RUN = range(6)

epsilon = 1e-06
bf16 = jnp.bfloat16
f32 = jnp.float32
VMEM_BYTES = 48 * 2**20


def passed_along(value, axis, steps):
    count = lax.axis_size(axis)
    first, last = (max(0, -steps), min(count, count - steps))
    return lax.ppermute(value, axis, [(source, source + steps) for source in range(first, last)])


def rms_scale(tensor):
    return lax.rsqrt(jnp.mean(tensor * tensor, axis=-1, keepdims=True) + epsilon)


def log_rates(decay_code, total_len):
    code_level = decay_code.astype(f32) / 1023.0
    smooth = -jnp.exp(-code_level * math.log(total_len / 32.0)) / 32.0
    return jnp.where(decay_code == 1024, -0.25, smooth)


def token_columns(decay_code, beta_code, total_len):
    rows, heads = decay_code.shape
    rates = log_rates(decay_code, total_len)
    run = jnp.cumsum(rates.reshape(rows // STRETCH, STRETCH, heads), axis=1)
    last = jnp.broadcast_to(run[:, -1:], run.shape).reshape(rows, heads)
    run = run.reshape(rows, heads)
    beta = 0.5 + beta_code.astype(f32) / 512.0
    gamma = jnp.exp(run)
    columns = jnp.concatenate(
        [beta, gamma, beta * gamma, jnp.exp(last - run), jnp.exp(last), run], axis=1
    )
    columns = jnp.pad(columns, ((0, 0), (0, 128 - columns.shape[1])))
    run_rows = jnp.pad(run.T, ((0, 8 - heads % 8), (0, 0)))
    return columns, run_rows


def mm(left, right):
    return jnp.dot(left, right, preferred_element_type=f32)


def mm_nt(left, right):
    return lax.dot_general(left, right, (((1,), (1,)), ((), ())), preferred_element_type=f32)


def mm_tn(left, right):
    return lax.dot_general(left, right, (((0,), (0,)), ((), ())), preferred_element_type=f32)


def column(columns_ref, kind, head, heads):
    block = columns_ref[...]
    lanes = lax.broadcasted_iota(jnp.int32, block.shape, 1)
    return jnp.sum(jnp.where(lanes == kind * heads + head, block, 0.0), axis=1, keepdims=True)


def square_ids():
    return (
        lax.broadcasted_iota(jnp.int32, (GROUP, GROUP), 0),
        lax.broadcasted_iota(jnp.int32, (GROUP, GROUP), 1),
    )


def convolved(padded_ref, tail_ref, mixed_ref, taps_ref):
    rows = mixed_ref.shape[0]
    count = taps_ref.shape[0]
    padded_ref[0:8, :] = tail_ref[...]
    padded_ref[8 : 8 + rows, :] = mixed_ref[...].astype(f32)
    taps = taps_ref[...].astype(f32)
    start = 9 - count
    total = taps[0:1] * padded_ref[start : start + rows, :]
    for tap in range(1, count):
        total += taps[tap : tap + 1] * padded_ref[start + tap : start + tap + rows, :]
    return total


def chunk_masks_stack(transposed):
    lanes = lax.broadcasted_iota(jnp.int32, transposed.shape, 1) // STRETCH
    parts = [jnp.where(lanes == part, transposed, 0.0) for part in range(GROUP // STRETCH)]
    return jnp.concatenate(parts, axis=0).astype(bf16)


def local_forward(
    mixed_ref,
    tail_ref,
    taps_ref,
    columns_ref,
    run_rows_ref,
    solve_ref,
    score_ref,
    fresh_ref,
    reach_ref,
    inner_ref,
    turn_ref,
    local_ref,
    end_ref,
    padded,
    turn_t,
    offsets,
):
    head = pl.program_id(0)
    heads = pl.num_programs(0)
    rows = mixed_ref.shape[0]
    per_group = GROUP // STRETCH
    stretches = rows // STRETCH
    total = convolved(padded, tail_ref, mixed_ref, taps_ref)
    activated = total * jax.nn.sigmoid(total)
    raw_q, raw_k = activated[:, :DK], activated[:, DK : 2 * DK]
    queries = raw_q * (
        lax.rsqrt(jnp.sum(raw_q * raw_q, axis=1, keepdims=True) + epsilon) * DK ** (-0.5)
    )
    keys = raw_k * lax.rsqrt(jnp.sum(raw_k * raw_k, axis=1, keepdims=True) + epsilon)
    values = activated[:, 2 * DK :]
    beta = column(columns_ref, BETA, head, heads)
    gamma = column(columns_ref, GAMMA, head, heads)
    beta_gamma = column(columns_ref, BETA_GAMMA, head, heads)
    tail_decay = column(columns_ref, TAIL, head, heads)
    last = column(columns_ref, LAST, head, heads)
    run = column(columns_ref, RUN, head, heads)
    row_id, col_id = square_ids()
    same = row_id // STRETCH == col_id // STRETCH
    causal = same & (row_id >= col_id)
    diagonal = row_id == col_id
    eye = jnp.where(
        lax.broadcasted_iota(jnp.int32, (DK, DK), 0) == lax.broadcasted_iota(jnp.int32, (DK, DK), 1),
        1.0,
        0.0,
    )
    for group in range(rows // GROUP):
        span = slice(group * GROUP, (group + 1) * GROUP)
        key_b = keys[span].astype(bf16)
        query_b = queries[span].astype(bf16)
        gaps = run[span] - run_rows_ref[pl.ds(head, 1), span]
        within = jnp.exp(jnp.where(causal, gaps, -1e30))
        lower = jnp.where(diagonal, 0.0, beta[span] * within * mm_nt(key_b, key_b))
        solve = jnp.where(diagonal, 1.0, jnp.where(row_id // 2 == col_id // 2, -lower, 0.0))
        size = 2
        while size < STRETCH:
            crossing = (row_id // (2 * size) == col_id // (2 * size)) & (
                row_id // size != col_id // size
            )
            solve_b = solve.astype(bf16)
            half = mm(solve_b, jnp.where(crossing, lower, 0.0).astype(bf16))
            solve = solve - mm(half.astype(bf16), solve_b)
            size *= 2
        solve_b = solve.astype(bf16)
        right = jnp.concatenate([beta[span] * values[span], beta_gamma[span] * keys[span]], axis=1)
        fresh_b = mm(solve_b, right.astype(bf16)).astype(bf16)
        score_b = (within * mm_nt(query_b, key_b)).astype(bf16)
        scored = mm(score_b, fresh_b)
        solve_ref[group] = solve_b
        score_ref[group] = score_b
        fresh_ref[span, :] = fresh_b
        inner_ref[span, :] = scored[:, :DV]
        reach_ref[span, :] = (gamma[span] * queries[span] - scored[:, DV:]).astype(bf16)
        tail_keys = (tail_decay[span] * keys[span]).T
        moved = mm(chunk_masks_stack(tail_keys), fresh_b)
        for part in range(per_group):
            at = group * per_group + part
            block = moved[part * DK : (part + 1) * DK]
            stay = last[at * STRETCH : at * STRETCH + 1]
            turned = stay * eye - block[:, DV:]
            turn_t[head, at] = turned.astype(bf16)
            turn_ref[at] = turned.T.astype(bf16)
            offsets[head, at] = block[:, :DV]

    @pl.when(head == heads - 1)
    def _():
        states = [
            jnp.concatenate([jnp.zeros((DK, DV), f32), eye], axis=1)
            for _ in range(local_ref.shape[0])
        ]
        for at in range(stretches):
            for h in range(len(states)):
                state_b = states[h].astype(bf16)
                local_ref[h, at] = state_b
                moved = mm(turn_t[h, at], state_b)
                states[h] = jnp.concatenate(
                    [moved[:, :DV] + offsets[h, at], moved[:, DV:]], axis=1
                )
        for h in range(len(states)):
            end_ref[h] = states[h].astype(bf16)


def finish_forward(
    ends_ref, local_ref, reach_ref, inner_ref, gate_ref, gain_ref, state_ref, core_ref, branch_ref, start
):
    head = pl.program_id(0)
    heads, stretches = start.shape[0], local_ref.shape[0]

    @pl.when(head == 0)
    def _():
        start[...] = jnp.zeros_like(start)

        def one(source, carry):
            for h in range(heads):
                start[h] = (
                    mm(ends_ref[source, h, :, DV:], start[h].astype(bf16))
                    + ends_ref[source, h, :, :DV].astype(f32)
                )
            return carry

        lax.fori_loop(0, lax.axis_index("seq"), one, 0)

    start_b = start[head].astype(bf16)
    cores = []
    for at in range(stretches):
        state_b = (
            local_ref[at, :, :DV].astype(f32) + mm(local_ref[at, :, DV:], start_b)
        ).astype(bf16)
        state_ref[at] = state_b
        span = slice(at * STRETCH, (at + 1) * STRETCH)
        cores.append(inner_ref[span, :] + mm(reach_ref[span, :], state_b))
    core = jnp.concatenate(cores, axis=0)
    core_ref[...] = core
    gate = gate_ref[...]
    branch = core * rms_scale(core) * gain_ref[...].astype(f32) * (gate * jax.nn.sigmoid(gate))
    branch_ref[...] = branch.astype(bf16)


def local_backward(
    d_branch_ref,
    core_ref,
    gate_ref,
    gain_ref,
    reach_ref,
    turn_ref,
    d_core_ref,
    d_gate_ref,
    gain_part_ref,
    local_ref,
    end_ref,
    pulls,
):
    head = pl.program_id(0)
    heads = pl.num_programs(0)
    rows = core_ref.shape[0]
    per_group = GROUP // STRETCH
    stretches = rows // STRETCH
    core = core_ref[...]
    gate = gate_ref[...]
    gain = gain_ref[...].astype(f32)
    d_branch = d_branch_ref[...]
    scale = rms_scale(core)
    nhat = core * scale
    sig = jax.nn.sigmoid(gate)
    gated = d_branch * (gate * sig)

    @pl.when(head == 0)
    def _():
        gain_part_ref[...] = jnp.zeros_like(gain_part_ref)

    gain_part_ref[...] += jnp.sum(gated * nhat, axis=0, keepdims=True)
    f = gated * gain
    d_core = scale * (f - nhat * jnp.mean(f * nhat, axis=1, keepdims=True))
    d_gate_ref[...] = (d_branch * nhat * gain * sig * (1.0 + gate * (1.0 - sig))).astype(bf16)
    d_core_b = d_core.astype(bf16)
    d_core_ref[...] = d_core_b
    for group in range(rows // GROUP):
        span = slice(group * GROUP, (group + 1) * GROUP)
        pulled = mm(chunk_masks_stack(reach_ref[span, :].astype(f32).T), d_core_b[span])
        for part in range(per_group):
            pulls[head, group * per_group + part] = pulled[part * DK : (part + 1) * DK]

    @pl.when(head == heads - 1)
    def _():
        eye = jnp.where(
            lax.broadcasted_iota(jnp.int32, (DK, DK), 0)
            == lax.broadcasted_iota(jnp.int32, (DK, DK), 1),
            1.0,
            0.0,
        )
        grads = [
            jnp.concatenate([jnp.zeros((DK, DV), f32), eye], axis=1)
            for _ in range(local_ref.shape[0])
        ]
        for at in reversed(range(stretches)):
            for h in range(len(grads)):
                grad_b = grads[h].astype(bf16)
                local_ref[h, at] = grad_b
                moved = mm(turn_ref[h, at], grad_b)
                grads[h] = jnp.concatenate([moved[:, :DV] + pulls[h, at], moved[:, DV:]], axis=1)
        for h in range(len(grads)):
            end_ref[h] = grads[h][:, :DV].astype(bf16)


def finish_backward(
    ends_ref,
    grad_ends_ref,
    mixed_ref,
    tail_ref,
    taps_ref,
    columns_ref,
    run_rows_ref,
    solve_ref,
    score_ref,
    fresh_ref,
    state_ref,
    d_core_ref,
    local_ref,
    d_mixed_ref,
    tail_out_ref,
    lead_ref,
    grad_taps_ref,
    padded,
    spread,
    end,
):
    head = pl.program_id(0)
    heads = pl.num_programs(0)
    rows = mixed_ref.shape[0]
    per_group = GROUP // STRETCH

    @pl.when(head == 0)
    def _():
        end[...] = jnp.zeros_like(end)
        count = ends_ref.shape[0]

        def one(turn, carry):
            source = count - 1 - turn
            for h in range(end.shape[0]):
                end[h] = (
                    mm_tn(ends_ref[source, h, :, DV:], end[h].astype(bf16))
                    + grad_ends_ref[source, h].astype(f32)
                )
            return carry

        lax.fori_loop(0, count - 1 - lax.axis_index("seq"), one, 0)

    end_b = end[head].astype(bf16)
    total = convolved(padded, tail_ref, mixed_ref, taps_ref)
    sig = jax.nn.sigmoid(total)
    activated = total * sig
    raw_q, raw_k = activated[:, :DK], activated[:, DK : 2 * DK]
    scale_q = lax.rsqrt(jnp.sum(raw_q * raw_q, axis=1, keepdims=True) + epsilon)
    scale_k = lax.rsqrt(jnp.sum(raw_k * raw_k, axis=1, keepdims=True) + epsilon)
    unit_q = raw_q * scale_q
    keys = raw_k * scale_k
    beta = column(columns_ref, BETA, head, heads)
    gamma = column(columns_ref, GAMMA, head, heads)
    beta_gamma = column(columns_ref, BETA_GAMMA, head, heads)
    tail_decay = column(columns_ref, TAIL, head, heads)
    run = column(columns_ref, RUN, head, heads)
    row_id, col_id = square_ids()
    causal = (row_id // STRETCH == col_id // STRETCH) & (row_id >= col_id)
    diagonal = row_id == col_id
    d_queries, d_keys, d_values = [], [], []
    for group in range(rows // GROUP):
        span = slice(group * GROUP, (group + 1) * GROUP)
        key_b = keys[span].astype(bf16)
        query_b = (unit_q[span] * DK ** (-0.5)).astype(bf16)
        tail_keys = (tail_decay[span] * keys[span]).astype(bf16)
        d_core_b = d_core_ref[span, :]
        grad_bs, from_grad, fresh_parts, from_state = [], [], [], []
        for part in range(per_group):
            at = group * per_group + part
            own = slice(part * STRETCH, (part + 1) * STRETCH)
            rows_at = slice(at * STRETCH, (at + 1) * STRETCH)
            grad_b = (
                local_ref[at, :, :DV].astype(f32) + mm(local_ref[at, :, DV:], end_b)
            ).astype(bf16)
            grad_bs.append(grad_b)
            from_grad.append(mm(tail_keys[own], grad_b))
            fresh_parts.append(mm(fresh_ref[rows_at, DV:], state_ref[at]))
            from_state.append(mm_nt(d_core_b[own], state_ref[at]))
        d_fresh = mm_tn(score_ref[group], d_core_b) + jnp.concatenate(from_grad, axis=0)
        d_right = mm_tn(solve_ref[group], d_fresh.astype(bf16))
        d_right_b = d_right.astype(bf16)
        fresh = fresh_ref[span, :DV].astype(f32) - jnp.concatenate(fresh_parts, axis=0)
        fresh_b = fresh.astype(bf16)
        gaps = run[span] - run_rows_ref[pl.ds(head, 1), span]
        within = jnp.exp(jnp.where(causal, gaps, -1e30))
        d_score = (within * mm_nt(d_core_b, fresh_b)).astype(bf16)
        d_lower = jnp.where(
            diagonal, 0.0, -beta[span] * within * mm_nt(d_right_b, fresh_b)
        ).astype(bf16)
        state_keys, grad_keys = [], []
        for part in range(per_group):
            at = group * per_group + part
            own = slice(part * STRETCH, (part + 1) * STRETCH)
            state_keys.append(mm_nt(d_right_b[own], state_ref[at]))
            grad_keys.append(mm_nt(fresh_b[own], grad_bs[part]))
        d_queries.append(gamma[span] * jnp.concatenate(from_state, axis=0) + mm(d_score, key_b))
        d_keys.append(
            mm_tn(d_score, query_b)
            + mm_tn(d_lower, key_b)
            + mm(d_lower, key_b)
            + tail_decay[span] * jnp.concatenate(grad_keys, axis=0)
            - beta_gamma[span] * jnp.concatenate(state_keys, axis=0)
        )
        d_values.append(beta[span] * d_right)
    g_q = jnp.concatenate(d_queries, axis=0) * DK ** (-0.5)
    g_k = jnp.concatenate(d_keys, axis=0)
    d_act = jnp.concatenate(
        [
            scale_q * (g_q - unit_q * jnp.sum(unit_q * g_q, axis=1, keepdims=True)),
            scale_k * (g_k - keys * jnp.sum(keys * g_k, axis=1, keepdims=True)),
            jnp.concatenate(d_values, axis=0),
        ],
        axis=1,
    )
    d_conv = d_act * (sig * (1.0 + total * (1.0 - sig)))
    taps = taps_ref[...].astype(f32)
    count = taps_ref.shape[0]
    start = 9 - count
    grad_taps_ref[...] = jnp.concatenate(
        [
            jnp.sum(padded[start + tap : start + tap + rows, :] * d_conv, axis=0, keepdims=True)
            for tap in range(count)
        ],
        axis=0,
    )
    spread[0:8, :] = jnp.zeros((8, d_conv.shape[1]), f32)
    spread[8 : 8 + rows, :] = d_conv
    spread[8 + rows : 16 + rows, :] = jnp.zeros((8, d_conv.shape[1]), f32)
    lead = taps[0:1] * spread[8:16, :]
    d_mixed = taps[0:1] * spread[7 + count : 7 + count + rows, :]
    for tap in range(1, count):
        lead += taps[tap : tap + 1] * spread[8 - tap : 16 - tap, :]
        begin = 7 + count - tap
        d_mixed += taps[tap : tap + 1] * spread[begin : begin + rows, :]
    lead_ref[...] = lead
    d_mixed_ref[...] = d_mixed.astype(bf16)
    tail_out_ref[...] = d_mixed[rows - 8 :]


def whole(shape):
    return pl.BlockSpec(shape, lambda h: (0,) * len(shape))


def by_head(shape):
    return pl.BlockSpec((None,) + shape, lambda h: (h,) + (0,) * len(shape))


def by_columns(rows, width):
    return pl.BlockSpec((rows, width), lambda h: (0, h))


def kernel_call(body, heads, ins, outs, out_shapes, scratch, flops, moved):
    return pl.pallas_call(
        body,
        grid=(heads,),
        in_specs=ins,
        out_specs=outs,
        out_shape=out_shapes,
        scratch_shapes=scratch,
        compiler_params=pltpu.CompilerParams(
            dimension_semantics=("arbitrary",), vmem_limit_bytes=VMEM_BYTES
        ),
        cost_estimate=pl.CostEstimate(flops=flops, bytes_accessed=moved, transcendentals=0),
    )


def shaped(shape, kind):
    return jax.ShapeDtypeStruct(shape, kind)


def run_local_forward(mixed, tail, taps, columns, run_rows, heads):
    rows = mixed.shape[0]
    count = taps.shape[0]
    groups, stretches = rows // GROUP, rows // STRETCH
    return kernel_call(
        local_forward,
        heads,
        [
            by_columns(rows, INNER),
            by_columns(8, INNER),
            by_columns(count, INNER),
            whole(columns.shape),
            whole(run_rows.shape),
        ],
        [
            by_head((groups, GROUP, GROUP)),
            by_head((groups, GROUP, GROUP)),
            by_head((rows, DV + DK)),
            by_head((rows, DK)),
            by_columns(rows, DV),
            by_head((stretches, DK, DK)),
            whole((heads, stretches, DK, DV + DK)),
            whole((heads, DK, DV + DK)),
        ],
        [
            shaped((heads, groups, GROUP, GROUP), bf16),
            shaped((heads, groups, GROUP, GROUP), bf16),
            shaped((heads, rows, DV + DK), bf16),
            shaped((heads, rows, DK), bf16),
            shaped((rows, heads * DV), f32),
            shaped((heads, stretches, DK, DK), bf16),
            shaped((heads, stretches, DK, DV + DK), bf16),
            shaped((heads, DK, DV + DK), bf16),
        ],
        [
            pltpu.VMEM((rows + 8, INNER), f32),
            pltpu.VMEM((heads, stretches, DK, DK), bf16),
            pltpu.VMEM((heads, stretches, DK, DV), f32),
        ],
        12_000_000_000,
        20_000_000,
    )(mixed, tail, taps, columns, run_rows)


def run_finish_forward(ends, local, reach, inner, gate_pre, gain):
    heads, stretches = local.shape[:2]
    rows = inner.shape[0]
    return kernel_call(
        finish_forward,
        heads,
        [
            whole(ends.shape),
            by_head((stretches, DK, DV + DK)),
            by_head((rows, DK)),
            by_columns(rows, DV),
            by_columns(rows, DV),
            whole(gain.shape),
        ],
        [by_head((stretches, DK, DV)), by_columns(rows, DV), by_columns(rows, DV)],
        [
            shaped((heads, stretches, DK, DV), bf16),
            shaped((rows, heads * DV), f32),
            shaped((rows, heads * DV), bf16),
        ],
        [pltpu.VMEM((heads, DK, DV), f32)],
        3_000_000_000,
        20_000_000,
    )(ends, local, reach, inner, gate_pre, gain)


def run_local_backward(d_branch, core, gate_pre, gain, reach, turn):
    heads, stretches = turn.shape[:2]
    rows = core.shape[0]
    return kernel_call(
        local_backward,
        heads,
        [
            by_columns(rows, DV),
            by_columns(rows, DV),
            by_columns(rows, DV),
            whole(gain.shape),
            by_head((rows, DK)),
            whole(turn.shape),
        ],
        [
            by_columns(rows, DV),
            by_columns(rows, DV),
            whole((1, DV)),
            whole((heads, stretches, DK, DV + DK)),
            whole((heads, DK, DV)),
        ],
        [
            shaped((rows, heads * DV), bf16),
            shaped((rows, heads * DV), bf16),
            shaped((1, DV), f32),
            shaped((heads, stretches, DK, DV + DK), bf16),
            shaped((heads, DK, DV), bf16),
        ],
        [pltpu.VMEM((heads, stretches, DK, DV), f32)],
        4_000_000_000,
        20_000_000,
    )(d_branch, core, gate_pre, gain, reach, turn)


def run_finish_backward(
    ends, grad_ends, mixed, tail, taps, columns, run_rows, solve, score, fresh, states, d_core, local
):
    heads, stretches = local.shape[:2]
    rows = mixed.shape[0]
    groups = rows // GROUP
    count = taps.shape[0]
    return kernel_call(
        finish_backward,
        heads,
        [
            whole(ends.shape),
            whole(grad_ends.shape),
            by_columns(rows, INNER),
            by_columns(8, INNER),
            by_columns(count, INNER),
            whole(columns.shape),
            whole(run_rows.shape),
            by_head((groups, GROUP, GROUP)),
            by_head((groups, GROUP, GROUP)),
            by_head((rows, DV + DK)),
            by_head((stretches, DK, DV)),
            by_columns(rows, DV),
            by_head((stretches, DK, DV + DK)),
        ],
        [
            by_columns(rows, INNER),
            by_columns(8, INNER),
            by_columns(8, INNER),
            by_columns(count, INNER),
        ],
        [
            shaped((rows, heads * INNER), bf16),
            shaped((8, heads * INNER), f32),
            shaped((8, heads * INNER), f32),
            shaped((count, heads * INNER), f32),
        ],
        [
            pltpu.VMEM((rows + 8, INNER), f32),
            pltpu.VMEM((rows + 16, INNER), f32),
            pltpu.VMEM((heads, DK, DV), f32),
        ],
        12_000_000_000,
        20_000_000,
    )(ends, grad_ends, mixed, tail, taps, columns, run_rows, solve, score, fresh, states, d_core, local)


def silu_slope(tensor):
    sigmoid_part = jax.nn.sigmoid(tensor)
    return sigmoid_part * (1.0 + tensor * (1.0 - sigmoid_part))


def gathered(value, axis):
    return lax.all_gather(value, axis, axis=0, tiled=True)


def scattered(value, axis, dimension=0):
    return lax.psum_scatter(
        value.astype(bf16), axis, scatter_dimension=dimension, tiled=True
    ).astype(f32)


def on_device(
    block_in,
    out_cot,
    gain_one,
    qkv_weight,
    conv_weight,
    gate_weight,
    gain_out,
    out_weight,
    gain_two,
    mlp_gate,
    mlp_up,
    mlp_down,
    decay_code,
    beta_code,
):
    span_rows = decay_code.shape[0]
    width, heads, inner = qkv_weight.shape
    total_len = span_rows * lax.axis_size("seq")
    lead_rows = conv_weight.shape[0] - 1
    input_f = block_in.astype(f32)
    gain_first = gain_one.astype(f32)
    gain_second = gain_two.astype(f32)
    gain_head = gain_out.reshape(1, -1)
    taps = conv_weight.reshape(conv_weight.shape[0], heads * inner)
    qkv_flat = qkv_weight.reshape(width, heads * inner)
    gate_flat = gate_weight.reshape(width, heads * DV)
    out_flat = out_weight.reshape(heads * DV, width)
    columns, run_rows = token_columns(decay_code, beta_code, total_len)

    wide_in = gathered(block_in, "head").astype(f32)
    hat_first = wide_in * rms_scale(wide_in)
    normed_first = (hat_first * gain_first).astype(bf16)
    mixed_in = mm(normed_first, qkv_flat).astype(bf16)
    tail_in = passed_along(mixed_in[span_rows - 8 :], "seq", 1)
    tail_in = jnp.where(jnp.arange(8)[:, None] >= 8 - lead_rows, tail_in.astype(f32), 0.0)
    solve, score, fresh, reach, inner_part, turn, local_states, piece_end = run_local_forward(
        mixed_in, tail_in, taps, columns, run_rows, heads
    )
    ends = lax.all_gather(piece_end, "seq")
    gate_pre = mm(normed_first, gate_flat)
    states, core, branch = run_finish_forward(
        ends, local_states, reach, inner_part, gate_pre, gain_head
    )
    middle = input_f + scattered(mm(branch, out_flat), "head")
    scale_two = rms_scale(middle)
    hat_two = middle * scale_two
    normed_two = (hat_two * gain_second).astype(bf16)

    rows_out = gathered(normed_two, "seq")
    gate_part = mm(rows_out, mlp_gate)
    up_part = mm(rows_out, mlp_up)
    hidden = (jax.nn.silu(gate_part) * up_part).astype(bf16)
    mlp_out = scattered(mm(hidden, mlp_down), "seq")
    output = (middle + mlp_out).astype(bf16)
    cot_f = out_cot.astype(f32)
    cot_all = gathered(out_cot, "seq")
    d_hidden = mm_nt(cot_all, mlp_down)
    d_gate_mlp = (d_hidden * up_part * silu_slope(gate_part)).astype(bf16)
    d_up_mlp = (d_hidden * jax.nn.silu(gate_part)).astype(bf16)
    d_normed_two = scattered(mm_nt(d_gate_mlp, mlp_gate) + mm_nt(d_up_mlp, mlp_up), "seq")
    grad_down = mm_tn(hidden, cot_all)
    grad_mgate = mm_tn(rows_out, d_gate_mlp)
    grad_mup = mm_tn(rows_out, d_up_mlp)
    gain_two_part = jnp.sum(d_normed_two * hat_two, 0)
    e_two = d_normed_two * gain_second
    d_middle = cot_f + scale_two * (
        e_two - hat_two * jnp.mean(e_two * hat_two, axis=-1, keepdims=True)
    )
    d_mix_all = gathered(d_middle.astype(bf16), "head")
    d_branch = mm_nt(d_mix_all, out_flat)
    d_core, d_gate_low, gain_out_part, local_grads, grad_end = run_local_backward(
        d_branch, core, gate_pre, gain_head, reach, turn
    )
    grad_ends = lax.all_gather(grad_end, "seq")
    grad_out_w = mm_tn(branch, d_mix_all)
    d_mixed, d_tail, d_lead, grad_conv = run_finish_backward(
        ends,
        grad_ends,
        mixed_in,
        tail_in,
        taps,
        columns,
        run_rows,
        solve,
        score,
        fresh,
        states,
        d_core,
        local_grads,
    )
    from_next = passed_along(d_lead[:lead_rows], "seq", -1)
    d_tail = d_tail.at[8 - lead_rows :].add(from_next).astype(bf16)
    d_mixed = lax.dynamic_update_slice(d_mixed, d_tail, (span_rows - 8, 0))
    d_normed_part = mm_nt(d_mixed, qkv_flat) + mm_nt(d_gate_low, gate_flat)
    d_normed_one = scattered(d_normed_part, "head")
    grad_qkv = mm_tn(normed_first, d_mixed)
    grad_gate = mm_tn(normed_first, d_gate_low)
    gain_one_part = jnp.sum(d_normed_part * hat_first, 0)

    grad_mgate_h = scattered(grad_mgate, "head")
    grad_mup_h = scattered(grad_mup, "head")
    grad_down_h = scattered(grad_down, "head", 1)
    gain_parts = [
        scattered(scattered(part, "head"), "seq")
        for part in (gain_one_part, gain_two_part, gain_out_part.reshape(-1))
    ]
    scale_own = rms_scale(input_f)
    hat_own = input_f * scale_own
    e_one = d_normed_one * gain_first
    d_input = (
        d_middle + scale_own * (e_one - hat_own * jnp.mean(e_one * hat_own, axis=-1, keepdims=True))
    ).astype(bf16)
    grad_qkv_s = scattered(grad_qkv, "seq").reshape(-1, heads, inner)
    grad_gate_s = scattered(grad_gate, "seq").reshape(-1, heads, DV)
    grad_out_s = scattered(grad_out_w, "seq", 1).reshape(heads, DV, -1)
    grad_conv_s = scattered(grad_conv.reshape(-1, heads, inner), "seq", 2)
    return (
        output,
        d_input,
        gain_parts[0],
        grad_qkv_s,
        grad_conv_s,
        grad_gate_s,
        gain_parts[2],
        grad_out_s,
        gain_parts[1],
        grad_mgate_h,
        grad_mup_h,
        grad_down_h,
    )


def solution(mesh):
    in_specs = (
        P(("seq", "head"), None),
        P(("seq", "head"), None),
        P(),
        P(None, "head", None),
        P(None, "head", None),
        P(None, "head", None),
        P(),
        P("head", None, None),
        P(),
        P(None, "seq"),
        P(None, "seq"),
        P("seq", None),
        P("seq", "head"),
        P("seq", "head"),
    )
    out_specs = (
        P(("seq", "head"), None),
        P(("seq", "head"), None),
        P(("head", "seq")),
        P("seq", "head", None),
        P(None, "head", "seq"),
        P("seq", "head", None),
        P(("head", "seq")),
        P("head", None, "seq"),
        P(("head", "seq")),
        P("head", "seq"),
        P("head", "seq"),
        P("seq", "head"),
    )
    return jax.shard_map(
        on_device, mesh=mesh, in_specs=in_specs, out_specs=out_specs, check_vma=False
    )
```

```python
import functools
import math

import jax
import jax.numpy as jnp
from jax import lax
from jax.experimental import pallas as pl
from jax.experimental.pallas import tpu as pltpu
from jax.sharding import PartitionSpec as P

DK = 128
DV = 256
STRETCH = 64
GROUP = 4 * STRETCH
INNER = 2 * DK + DV
BETA, GAMMA, BETA_GAMMA, TAIL, LAST, RUN = range(6)

epsilon = 1e-06
bf16 = jnp.bfloat16
f32 = jnp.float32
VMEM_BYTES = 48 * 2**20


def passed_along(value, axis, steps):
    count = lax.axis_size(axis)
    first, last = (max(0, -steps), min(count, count - steps))
    return lax.ppermute(value, axis, [(source, source + steps) for source in range(first, last)])


def rms_scale(tensor):
    return lax.rsqrt(jnp.mean(tensor * tensor, axis=-1, keepdims=True) + epsilon)


def log_rates(decay_code, total_len):
    code_level = decay_code.astype(f32) / 1023.0
    smooth = -jnp.exp(-code_level * math.log(total_len / 32.0)) / 32.0
    return jnp.where(decay_code == 1024, -0.25, smooth)


def token_columns(decay_code, beta_code, total_len):
    rows, heads = decay_code.shape
    rates = log_rates(decay_code, total_len)
    run = jnp.cumsum(rates.reshape(rows // STRETCH, STRETCH, heads), axis=1)
    last = jnp.broadcast_to(run[:, -1:], run.shape).reshape(rows, heads)
    run = run.reshape(rows, heads)
    beta = 0.5 + beta_code.astype(f32) / 512.0
    gamma = jnp.exp(run)
    columns = jnp.concatenate(
        [beta, gamma, beta * gamma, jnp.exp(last - run), jnp.exp(last), run], axis=1
    )
    columns = jnp.pad(columns, ((0, 0), (0, 128 - columns.shape[1])))
    run_rows = jnp.pad(run.T, ((0, 8 - heads % 8), (0, 0)))
    return columns, run_rows


def mm(left, right):
    return jnp.dot(left, right, preferred_element_type=f32)


def mm_nt(left, right):
    return lax.dot_general(left, right, (((1,), (1,)), ((), ())), preferred_element_type=f32)


def mm_tn(left, right):
    return lax.dot_general(left, right, (((0,), (0,)), ((), ())), preferred_element_type=f32)


def column(columns_ref, kind, head, heads):
    block = columns_ref[...]
    lanes = lax.broadcasted_iota(jnp.int32, block.shape, 1)
    return jnp.sum(jnp.where(lanes == kind * heads + head, block, 0.0), axis=1, keepdims=True)


def square_ids():
    return (
        lax.broadcasted_iota(jnp.int32, (GROUP, GROUP), 0),
        lax.broadcasted_iota(jnp.int32, (GROUP, GROUP), 1),
    )


def convolved(padded_ref, tail_ref, mixed_ref, taps_ref):
    rows = mixed_ref.shape[0]
    count = taps_ref.shape[0]
    padded_ref[0:8, :] = tail_ref[...]
    padded_ref[8 : 8 + rows, :] = mixed_ref[...].astype(f32)
    taps = taps_ref[...].astype(f32)
    start = 9 - count
    total = taps[0:1] * padded_ref[start : start + rows, :]
    for tap in range(1, count):
        total += taps[tap : tap + 1] * padded_ref[start + tap : start + tap + rows, :]
    return total


def chunk_masks_stack(transposed):
    lanes = lax.broadcasted_iota(jnp.int32, transposed.shape, 1) // STRETCH
    parts = [jnp.where(lanes == part, transposed, 0.0) for part in range(GROUP // STRETCH)]
    return jnp.concatenate(parts, axis=0).astype(bf16)


def local_forward(
    mixed_ref,
    tail_ref,
    taps_ref,
    columns_ref,
    run_rows_ref,
    solve_ref,
    score_ref,
    fresh_ref,
    reach_ref,
    inner_ref,
    turn_ref,
    local_ref,
    end_ref,
    padded,
    turn_t,
    offsets,
):
    head = pl.program_id(0)
    heads = pl.num_programs(0)
    rows = mixed_ref.shape[0]
    per_group = GROUP // STRETCH
    stretches = rows // STRETCH
    total = convolved(padded, tail_ref, mixed_ref, taps_ref)
    activated = total * jax.nn.sigmoid(total)
    raw_q, raw_k = activated[:, :DK], activated[:, DK : 2 * DK]
    queries = raw_q * (
        lax.rsqrt(jnp.sum(raw_q * raw_q, axis=1, keepdims=True) + epsilon) * DK ** (-0.5)
    )
    keys = raw_k * lax.rsqrt(jnp.sum(raw_k * raw_k, axis=1, keepdims=True) + epsilon)
    values = activated[:, 2 * DK :]
    beta = column(columns_ref, BETA, head, heads)
    gamma = column(columns_ref, GAMMA, head, heads)
    beta_gamma = column(columns_ref, BETA_GAMMA, head, heads)
    tail_decay = column(columns_ref, TAIL, head, heads)
    last = column(columns_ref, LAST, head, heads)
    run = column(columns_ref, RUN, head, heads)
    row_id, col_id = square_ids()
    same = row_id // STRETCH == col_id // STRETCH
    causal = same & (row_id >= col_id)
    diagonal = row_id == col_id
    eye = jnp.where(
        lax.broadcasted_iota(jnp.int32, (DK, DK), 0) == lax.broadcasted_iota(jnp.int32, (DK, DK), 1),
        1.0,
        0.0,
    )
    for group in range(rows // GROUP):
        span = slice(group * GROUP, (group + 1) * GROUP)
        key_b = keys[span].astype(bf16)
        query_b = queries[span].astype(bf16)
        gaps = run[span] - run_rows_ref[pl.ds(head, 1), span]
        within = jnp.exp(jnp.where(causal, gaps, -1e30))
        lower = jnp.where(diagonal, 0.0, beta[span] * within * mm_nt(key_b, key_b))
        solve = jnp.where(diagonal, 1.0, jnp.where(row_id // 2 == col_id // 2, -lower, 0.0))
        size = 2
        while size < STRETCH:
            crossing = (row_id // (2 * size) == col_id // (2 * size)) & (
                row_id // size != col_id // size
            )
            solve_b = solve.astype(bf16)
            half = mm(solve_b, jnp.where(crossing, lower, 0.0).astype(bf16))
            solve = solve - mm(half.astype(bf16), solve_b)
            size *= 2
        solve_b = solve.astype(bf16)
        right = jnp.concatenate([beta[span] * values[span], beta_gamma[span] * keys[span]], axis=1)
        fresh_b = mm(solve_b, right.astype(bf16)).astype(bf16)
        score_b = (within * mm_nt(query_b, key_b)).astype(bf16)
        scored = mm(score_b, fresh_b)
        solve_ref[group] = solve_b
        score_ref[group] = score_b
        fresh_ref[span, :] = fresh_b
        inner_ref[span, :] = scored[:, :DV]
        reach_ref[span, :] = (gamma[span] * queries[span] - scored[:, DV:]).astype(bf16)
        tail_keys = (tail_decay[span] * keys[span]).T
        moved = mm(chunk_masks_stack(tail_keys), fresh_b)
        for part in range(per_group):
            at = group * per_group + part
            block = moved[part * DK : (part + 1) * DK]
            stay = last[at * STRETCH : at * STRETCH + 1]
            turned = stay * eye - block[:, DV:]
            turn_t[head, at] = turned.astype(bf16)
            turn_ref[at] = turned.T.astype(bf16)
            offsets[head, at] = block[:, :DV]

    @pl.when(head == heads - 1)
    def _():
        states = [
            jnp.concatenate([jnp.zeros((DK, DV), f32), eye], axis=1)
            for _ in range(local_ref.shape[0])
        ]
        for at in range(stretches):
            for h in range(len(states)):
                state_b = states[h].astype(bf16)
                local_ref[h, at] = state_b
                moved = mm(turn_t[h, at], state_b)
                states[h] = jnp.concatenate(
                    [moved[:, :DV] + offsets[h, at], moved[:, DV:]], axis=1
                )
        for h in range(len(states)):
            end_ref[h] = states[h].astype(bf16)


def finish_forward(
    ends_ref, local_ref, reach_ref, inner_ref, gate_ref, gain_ref, state_ref, core_ref, branch_ref, start
):
    head = pl.program_id(0)
    heads, stretches = start.shape[0], local_ref.shape[0]

    @pl.when(head == 0)
    def _():
        start[...] = jnp.zeros_like(start)

        def one(source, carry):
            for h in range(heads):
                start[h] = (
                    mm(ends_ref[source, h, :, DV:], start[h].astype(bf16))
                    + ends_ref[source, h, :, :DV].astype(f32)
                )
            return carry

        lax.fori_loop(0, lax.axis_index("seq"), one, 0)

    start_b = start[head].astype(bf16)
    cores = []
    for at in range(stretches):
        state_b = (
            local_ref[at, :, :DV].astype(f32) + mm(local_ref[at, :, DV:], start_b)
        ).astype(bf16)
        state_ref[at] = state_b
        span = slice(at * STRETCH, (at + 1) * STRETCH)
        cores.append(inner_ref[span, :] + mm(reach_ref[span, :], state_b))
    core = jnp.concatenate(cores, axis=0)
    core_ref[...] = core
    gate = gate_ref[...]
    branch = core * rms_scale(core) * gain_ref[...].astype(f32) * (gate * jax.nn.sigmoid(gate))
    branch_ref[...] = branch.astype(bf16)


def local_backward(
    d_branch_ref,
    core_ref,
    gate_ref,
    gain_ref,
    reach_ref,
    turn_ref,
    d_core_ref,
    d_gate_ref,
    gain_part_ref,
    local_ref,
    end_ref,
    pulls,
):
    head = pl.program_id(0)
    heads = pl.num_programs(0)
    rows = core_ref.shape[0]
    per_group = GROUP // STRETCH
    stretches = rows // STRETCH
    core = core_ref[...]
    gate = gate_ref[...]
    gain = gain_ref[...].astype(f32)
    d_branch = d_branch_ref[...]
    scale = rms_scale(core)
    nhat = core * scale
    sig = jax.nn.sigmoid(gate)
    gated = d_branch * (gate * sig)

    @pl.when(head == 0)
    def _():
        gain_part_ref[...] = jnp.zeros_like(gain_part_ref)

    gain_part_ref[...] += jnp.sum(gated * nhat, axis=0, keepdims=True)
    f = gated * gain
    d_core = scale * (f - nhat * jnp.mean(f * nhat, axis=1, keepdims=True))
    d_gate_ref[...] = (d_branch * nhat * gain * sig * (1.0 + gate * (1.0 - sig))).astype(bf16)
    d_core_b = d_core.astype(bf16)
    d_core_ref[...] = d_core_b
    for group in range(rows // GROUP):
        span = slice(group * GROUP, (group + 1) * GROUP)
        pulled = mm(chunk_masks_stack(reach_ref[span, :].astype(f32).T), d_core_b[span])
        for part in range(per_group):
            pulls[head, group * per_group + part] = pulled[part * DK : (part + 1) * DK]

    @pl.when(head == heads - 1)
    def _():
        eye = jnp.where(
            lax.broadcasted_iota(jnp.int32, (DK, DK), 0)
            == lax.broadcasted_iota(jnp.int32, (DK, DK), 1),
            1.0,
            0.0,
        )
        grads = [
            jnp.concatenate([jnp.zeros((DK, DV), f32), eye], axis=1)
            for _ in range(local_ref.shape[0])
        ]
        for at in reversed(range(stretches)):
            for h in range(len(grads)):
                grad_b = grads[h].astype(bf16)
                local_ref[h, at] = grad_b
                moved = mm(turn_ref[h, at], grad_b)
                grads[h] = jnp.concatenate([moved[:, :DV] + pulls[h, at], moved[:, DV:]], axis=1)
        for h in range(len(grads)):
            end_ref[h] = grads[h][:, :DV].astype(bf16)


def finish_backward(
    ends_ref,
    grad_ends_ref,
    mixed_ref,
    tail_ref,
    taps_ref,
    columns_ref,
    run_rows_ref,
    solve_ref,
    score_ref,
    fresh_ref,
    state_ref,
    d_core_ref,
    local_ref,
    d_mixed_ref,
    tail_out_ref,
    lead_ref,
    grad_taps_ref,
    padded,
    spread,
    end,
):
    head = pl.program_id(0)
    heads = pl.num_programs(0)
    rows = mixed_ref.shape[0]
    per_group = GROUP // STRETCH

    @pl.when(head == 0)
    def _():
        end[...] = jnp.zeros_like(end)
        count = ends_ref.shape[0]

        def one(turn, carry):
            source = count - 1 - turn
            for h in range(end.shape[0]):
                end[h] = (
                    mm_tn(ends_ref[source, h, :, DV:], end[h].astype(bf16))
                    + grad_ends_ref[source, h].astype(f32)
                )
            return carry

        lax.fori_loop(0, count - 1 - lax.axis_index("seq"), one, 0)

    end_b = end[head].astype(bf16)
    total = convolved(padded, tail_ref, mixed_ref, taps_ref)
    sig = jax.nn.sigmoid(total)
    activated = total * sig
    raw_q, raw_k = activated[:, :DK], activated[:, DK : 2 * DK]
    scale_q = lax.rsqrt(jnp.sum(raw_q * raw_q, axis=1, keepdims=True) + epsilon)
    scale_k = lax.rsqrt(jnp.sum(raw_k * raw_k, axis=1, keepdims=True) + epsilon)
    unit_q = raw_q * scale_q
    keys = raw_k * scale_k
    beta = column(columns_ref, BETA, head, heads)
    gamma = column(columns_ref, GAMMA, head, heads)
    beta_gamma = column(columns_ref, BETA_GAMMA, head, heads)
    tail_decay = column(columns_ref, TAIL, head, heads)
    run = column(columns_ref, RUN, head, heads)
    row_id, col_id = square_ids()
    causal = (row_id // STRETCH == col_id // STRETCH) & (row_id >= col_id)
    diagonal = row_id == col_id
    d_queries, d_keys, d_values = [], [], []
    for group in range(rows // GROUP):
        span = slice(group * GROUP, (group + 1) * GROUP)
        key_b = keys[span].astype(bf16)
        query_b = (unit_q[span] * DK ** (-0.5)).astype(bf16)
        tail_keys = (tail_decay[span] * keys[span]).astype(bf16)
        d_core_b = d_core_ref[span, :]
        grad_bs, from_grad, fresh_parts, from_state = [], [], [], []
        for part in range(per_group):
            at = group * per_group + part
            own = slice(part * STRETCH, (part + 1) * STRETCH)
            rows_at = slice(at * STRETCH, (at + 1) * STRETCH)
            grad_b = (
                local_ref[at, :, :DV].astype(f32) + mm(local_ref[at, :, DV:], end_b)
            ).astype(bf16)
            grad_bs.append(grad_b)
            from_grad.append(mm(tail_keys[own], grad_b))
            fresh_parts.append(mm(fresh_ref[rows_at, DV:], state_ref[at]))
            from_state.append(mm_nt(d_core_b[own], state_ref[at]))
        d_fresh = mm_tn(score_ref[group], d_core_b) + jnp.concatenate(from_grad, axis=0)
        d_right = mm_tn(solve_ref[group], d_fresh.astype(bf16))
        d_right_b = d_right.astype(bf16)
        fresh = fresh_ref[span, :DV].astype(f32) - jnp.concatenate(fresh_parts, axis=0)
        fresh_b = fresh.astype(bf16)
        gaps = run[span] - run_rows_ref[pl.ds(head, 1), span]
        within = jnp.exp(jnp.where(causal, gaps, -1e30))
        d_score = (within * mm_nt(d_core_b, fresh_b)).astype(bf16)
        d_lower = jnp.where(
            diagonal, 0.0, -beta[span] * within * mm_nt(d_right_b, fresh_b)
        ).astype(bf16)
        state_keys, grad_keys = [], []
        for part in range(per_group):
            at = group * per_group + part
            own = slice(part * STRETCH, (part + 1) * STRETCH)
            state_keys.append(mm_nt(d_right_b[own], state_ref[at]))
            grad_keys.append(mm_nt(fresh_b[own], grad_bs[part]))
        d_queries.append(gamma[span] * jnp.concatenate(from_state, axis=0) + mm(d_score, key_b))
        d_keys.append(
            mm_tn(d_score, query_b)
            + mm_tn(d_lower, key_b)
            + mm(d_lower, key_b)
            + tail_decay[span] * jnp.concatenate(grad_keys, axis=0)
            - beta_gamma[span] * jnp.concatenate(state_keys, axis=0)
        )
        d_values.append(beta[span] * d_right)
    g_q = jnp.concatenate(d_queries, axis=0) * DK ** (-0.5)
    g_k = jnp.concatenate(d_keys, axis=0)
    d_act = jnp.concatenate(
        [
            scale_q * (g_q - unit_q * jnp.sum(unit_q * g_q, axis=1, keepdims=True)),
            scale_k * (g_k - keys * jnp.sum(keys * g_k, axis=1, keepdims=True)),
            jnp.concatenate(d_values, axis=0),
        ],
        axis=1,
    )
    d_conv = d_act * (sig * (1.0 + total * (1.0 - sig)))
    taps = taps_ref[...].astype(f32)
    count = taps_ref.shape[0]
    start = 9 - count
    grad_taps_ref[...] = jnp.concatenate(
        [
            jnp.sum(padded[start + tap : start + tap + rows, :] * d_conv, axis=0, keepdims=True)
            for tap in range(count)
        ],
        axis=0,
    )
    spread[0:8, :] = jnp.zeros((8, d_conv.shape[1]), f32)
    spread[8 : 8 + rows, :] = d_conv
    spread[8 + rows : 16 + rows, :] = jnp.zeros((8, d_conv.shape[1]), f32)
    lead = taps[0:1] * spread[8:16, :]
    d_mixed = taps[0:1] * spread[7 + count : 7 + count + rows, :]
    for tap in range(1, count):
        lead += taps[tap : tap + 1] * spread[8 - tap : 16 - tap, :]
        begin = 7 + count - tap
        d_mixed += taps[tap : tap + 1] * spread[begin : begin + rows, :]
    lead_ref[...] = lead
    d_mixed_ref[...] = d_mixed.astype(bf16)
    tail_out_ref[...] = d_mixed[rows - 8 :]


def whole(shape):
    return pl.BlockSpec(shape, lambda h: (0,) * len(shape))


def by_head(shape):
    return pl.BlockSpec((None,) + shape, lambda h: (h,) + (0,) * len(shape))


def by_columns(rows, width):
    return pl.BlockSpec((rows, width), lambda h: (0, h))


def kernel_call(body, heads, ins, outs, out_shapes, scratch, flops, moved):
    return pl.pallas_call(
        body,
        grid=(heads,),
        in_specs=ins,
        out_specs=outs,
        out_shape=out_shapes,
        scratch_shapes=scratch,
        compiler_params=pltpu.CompilerParams(
            dimension_semantics=("arbitrary",), vmem_limit_bytes=VMEM_BYTES
        ),
        cost_estimate=pl.CostEstimate(flops=flops, bytes_accessed=moved, transcendentals=0),
    )


def shaped(shape, kind):
    return jax.ShapeDtypeStruct(shape, kind)


def run_local_forward(mixed, tail, taps, columns, run_rows, heads):
    rows = mixed.shape[0]
    count = taps.shape[0]
    groups, stretches = rows // GROUP, rows // STRETCH
    return kernel_call(
        local_forward,
        heads,
        [
            by_columns(rows, INNER),
            by_columns(8, INNER),
            by_columns(count, INNER),
            whole(columns.shape),
            whole(run_rows.shape),
        ],
        [
            by_head((groups, GROUP, GROUP)),
            by_head((groups, GROUP, GROUP)),
            by_head((rows, DV + DK)),
            by_head((rows, DK)),
            by_columns(rows, DV),
            by_head((stretches, DK, DK)),
            whole((heads, stretches, DK, DV + DK)),
            whole((heads, DK, DV + DK)),
        ],
        [
            shaped((heads, groups, GROUP, GROUP), bf16),
            shaped((heads, groups, GROUP, GROUP), bf16),
            shaped((heads, rows, DV + DK), bf16),
            shaped((heads, rows, DK), bf16),
            shaped((rows, heads * DV), f32),
            shaped((heads, stretches, DK, DK), bf16),
            shaped((heads, stretches, DK, DV + DK), bf16),
            shaped((heads, DK, DV + DK), bf16),
        ],
        [
            pltpu.VMEM((rows + 8, INNER), f32),
            pltpu.VMEM((heads, stretches, DK, DK), bf16),
            pltpu.VMEM((heads, stretches, DK, DV), f32),
        ],
        12_000_000_000,
        20_000_000,
    )(mixed, tail, taps, columns, run_rows)


def run_finish_forward(ends, local, reach, inner, gate_pre, gain):
    heads, stretches = local.shape[:2]
    rows = inner.shape[0]
    return kernel_call(
        finish_forward,
        heads,
        [
            whole(ends.shape),
            by_head((stretches, DK, DV + DK)),
            by_head((rows, DK)),
            by_columns(rows, DV),
            by_columns(rows, DV),
            whole(gain.shape),
        ],
        [by_head((stretches, DK, DV)), by_columns(rows, DV), by_columns(rows, DV)],
        [
            shaped((heads, stretches, DK, DV), bf16),
            shaped((rows, heads * DV), f32),
            shaped((rows, heads * DV), bf16),
        ],
        [pltpu.VMEM((heads, DK, DV), f32)],
        3_000_000_000,
        20_000_000,
    )(ends, local, reach, inner, gate_pre, gain)


def run_local_backward(d_branch, core, gate_pre, gain, reach, turn):
    heads, stretches = turn.shape[:2]
    rows = core.shape[0]
    return kernel_call(
        local_backward,
        heads,
        [
            by_columns(rows, DV),
            by_columns(rows, DV),
            by_columns(rows, DV),
            whole(gain.shape),
            by_head((rows, DK)),
            whole(turn.shape),
        ],
        [
            by_columns(rows, DV),
            by_columns(rows, DV),
            whole((1, DV)),
            whole((heads, stretches, DK, DV + DK)),
            whole((heads, DK, DV)),
        ],
        [
            shaped((rows, heads * DV), bf16),
            shaped((rows, heads * DV), bf16),
            shaped((1, DV), f32),
            shaped((heads, stretches, DK, DV + DK), bf16),
            shaped((heads, DK, DV), bf16),
        ],
        [pltpu.VMEM((heads, stretches, DK, DV), f32)],
        4_000_000_000,
        20_000_000,
    )(d_branch, core, gate_pre, gain, reach, turn)


def run_finish_backward(
    ends, grad_ends, mixed, tail, taps, columns, run_rows, solve, score, fresh, states, d_core, local
):
    heads, stretches = local.shape[:2]
    rows = mixed.shape[0]
    groups = rows // GROUP
    count = taps.shape[0]
    return kernel_call(
        finish_backward,
        heads,
        [
            whole(ends.shape),
            whole(grad_ends.shape),
            by_columns(rows, INNER),
            by_columns(8, INNER),
            by_columns(count, INNER),
            whole(columns.shape),
            whole(run_rows.shape),
            by_head((groups, GROUP, GROUP)),
            by_head((groups, GROUP, GROUP)),
            by_head((rows, DV + DK)),
            by_head((stretches, DK, DV)),
            by_columns(rows, DV),
            by_head((stretches, DK, DV + DK)),
        ],
        [
            by_columns(rows, INNER),
            by_columns(8, INNER),
            by_columns(8, INNER),
            by_columns(count, INNER),
        ],
        [
            shaped((rows, heads * INNER), bf16),
            shaped((8, heads * INNER), f32),
            shaped((8, heads * INNER), f32),
            shaped((count, heads * INNER), f32),
        ],
        [
            pltpu.VMEM((rows + 8, INNER), f32),
            pltpu.VMEM((rows + 16, INNER), f32),
            pltpu.VMEM((heads, DK, DV), f32),
        ],
        12_000_000_000,
        20_000_000,
    )(ends, grad_ends, mixed, tail, taps, columns, run_rows, solve, score, fresh, states, d_core, local)


MESH = pl.DeviceIdType.MESH
SIDE = 2


def remote(source, target, send, arrive, device):
    return pltpu.make_async_remote_copy(
        src_ref=source,
        dst_ref=target,
        send_sem=send,
        recv_sem=arrive,
        device_id=device,
        device_id_type=MESH,
    )


def greet(partners):
    barrier = pltpu.get_barrier_semaphore()
    expected = 0
    for device, there in partners:
        if there is None:
            pl.semaphore_signal(barrier, inc=1, device_id=device, device_id_type=MESH)
            expected = expected + 1
        else:

            @pl.when(there)
            def _(device=device):
                pl.semaphore_signal(barrier, inc=1, device_id=device, device_id_type=MESH)

            expected = expected + there.astype(jnp.int32)
    pl.semaphore_wait(barrier, expected)


def head_places():
    head, seq = lax.axis_index("head"), lax.axis_index("seq")
    core = lax.rem(head, 2)
    sibling = head + 1 - 2 * core
    across = lax.rem(head + 2, 4)
    return head, seq, sibling, across


def head_partners():
    head, seq, sibling, across = head_places()
    return [((sibling, seq), None), ((across, seq), None)]


def seq_places():
    head, seq = lax.axis_index("head"), lax.axis_index("seq")
    return head, seq // SIDE, lax.rem(seq, SIDE)


def seq_partners(count):
    head, line, side = seq_places()
    return [
        ((head, line * SIDE + 1 - side), None),
        ((head, (line + 1) * SIDE + side), line < count - 1),
        ((head, (line - 1) * SIDE + side), line > 0),
    ]


def run_together(steps):
    steps = list(steps)
    while steps:
        alive = []
        for step in steps:
            try:
                next(step)
                alive.append(step)
            except StopIteration:
                pass
        steps = alive


def gather_head(own_ref, out_ref, local, send, arrive, pieces):
    head, seq, sibling, across = head_places()
    far = lax.rem(sibling + 2, 4)
    rows = own_ref.shape[0] // pieces
    keep = pltpu.make_async_copy(own_ref, out_ref.at[head], local.at[0])
    keep.start()

    def part(ref, piece):
        return ref.at[pl.ds(piece * rows, rows)]

    outgoing = []
    for piece in range(pieces):
        outgoing.append(
            remote(
                part(own_ref, piece),
                part(out_ref.at[head], piece),
                send.at[0, piece],
                arrive.at[0, piece],
                (across, seq),
            )
        )
    for piece in range(pieces):
        outgoing.append(
            remote(
                part(own_ref, piece),
                part(out_ref.at[head], piece),
                send.at[1, piece],
                arrive.at[1, piece],
                (sibling, seq),
            )
        )
    for copy in outgoing:
        copy.start()
    yield
    forwards = []
    for piece in range(pieces):
        outgoing[piece].wait_recv()
        forward = remote(
            part(out_ref.at[across], piece),
            part(out_ref.at[across], piece),
            send.at[2, piece],
            arrive.at[2, piece],
            (sibling, seq),
        )
        forward.start()
        forwards.append(forward)
        yield
    for copy in outgoing[pieces:] + forwards:
        copy.wait_recv()
    for copy in outgoing + forwards:
        copy.wait_send()
    keep.wait()


def scatter_head(source_at, out_ref, own, crossed, passed, local, send, arrive):
    head, seq, sibling, across = head_places()
    far = lax.rem(sibling + 2, 4)
    loads = [
        pltpu.make_async_copy(source_at(target), own.at[slot], local.at[slot])
        for slot, target in enumerate((across, head))
    ]
    copies = [
        remote(source_at(target), crossed.at[slot], send.at[slot], arrive.at[slot], (sibling, seq))
        for slot, target in enumerate((far, sibling))
    ]
    for slot in range(2):
        copies[slot].start()
        loads[slot].start()
    yield
    loads[0].wait()
    copies[0].wait_recv()
    own[0] = (own[0].astype(f32) + crossed[0].astype(f32)).astype(own.dtype)
    onward = remote(own.at[0], passed, send.at[2], arrive.at[2], (across, seq))
    onward.start()
    yield
    loads[1].wait()
    copies[1].wait_recv()
    out_ref[...] = own[1].astype(f32) + crossed[1].astype(f32)
    yield
    onward.wait_recv()
    out_ref[...] += passed[...].astype(f32)
    onward.wait_send()
    for copy in copies:
        copy.wait_send()


def gather_seq(own_ref, out_ref, local, side_send, side_arrive, line_send, line_arrive, count):
    head, line, side = seq_places()
    me = line * SIDE + side
    beside = (head, line * SIDE + 1 - side)
    ways = ((1, line < count - 1), (-1, line > 0))
    keep = pltpu.make_async_copy(own_ref, out_ref.at[me], local.at[0])
    keep.start()

    def along(source, block, way, step):
        slot = step if way > 0 else count + step
        return remote(
            source,
            out_ref.at[block],
            line_send.at[slot],
            line_arrive.at[slot],
            (head, (line + way) * SIDE + side),
        )

    def over(source, block, slot):
        return remote(source, out_ref.at[block], side_send.at[slot], side_arrive.at[slot], beside)

    for way, onward in ways:

        @pl.when(onward)
        def _(way=way):
            along(own_ref, me, way, 0).start()

    over(own_ref, me, 0).start()
    yield
    for step in range(1, count):
        for way, onward in ways:
            block = me - way * step * SIDE
            arrives = line >= step if way > 0 else line + step < count

            @pl.when(arrives)
            def _(way=way, onward=onward, block=block, step=step):
                landed = out_ref.at[block]
                slot = step if way > 0 else count + step
                remote(
                    landed, landed, line_send.at[slot - 1], line_arrive.at[slot - 1], beside
                ).wait_recv()

                @pl.when(onward)
                def _():
                    along(landed, block, way, step).start()

                over(landed, block, slot).start()

        yield
    over(own_ref, me, 0).wait()
    for way, onward in ways:

        @pl.when(onward)
        def _(way=way):
            along(own_ref, me, way, 0).wait_send()

    for step in range(1, count):
        for way, onward in ways:
            block = me - way * step * SIDE
            arrives = line >= step if way > 0 else line + step < count

            @pl.when(arrives)
            def _(way=way, onward=onward, block=block, step=step):
                landed = out_ref.at[block]
                slot = step if way > 0 else count + step
                over(landed, block, slot).wait()

                @pl.when(onward)
                def _():
                    along(landed, block, way, step).wait_send()

    keep.wait()


def scatter_seq(source_at, out_at, own, crossed, risen, fallen, local, sends, arrivals, count):
    head, line, side = seq_places()
    beside = (head, line * SIDE + 1 - side)
    pieces = own.shape[0]

    def targets(distance):
        if distance == 0:
            return [(line, None, 0)]
        return [
            (line - distance, line >= distance, -1),
            (line + distance, line + distance < count, 1),
        ]

    def load(piece, target):
        return pltpu.make_async_copy(
            source_at(target * SIDE + side, piece), own.at[piece, target], local.at[piece, target]
        )

    def cross(piece, target):
        return remote(
            source_at(target * SIDE + 1 - side, piece),
            crossed.at[piece, target],
            sends.at[0, piece, target],
            arrivals.at[0, piece, target],
            beside,
        )

    def onward(piece, target, way, arriving=False):
        landing = risen if way > 0 else fallen
        return remote(
            own.at[piece, target],
            landing.at[piece, target],
            sends.at[1, piece, target],
            arrivals.at[1 if way > 0 else 2, piece, target],
            beside if arriving else (head, (line + way) * SIDE + side),
        )

    def guarded(there, body):
        if there is None:
            body()
        else:
            pl.when(there)(body)

    for piece in range(pieces):
        for distance in range(count - 1, -1, -1):
            for target, there, _ in targets(distance):

                def begin(piece=piece, target=target):
                    cross(piece, target).start()
                    load(piece, target).start()

                guarded(there, begin)
    yield
    for piece in range(pieces):
        for distance in range(count - 1, 0, -1):
            for way in (-1, 1):
                target = line + way * distance
                there = line >= distance if way < 0 else line + distance < count
                first = line == count - 1 if way < 0 else line == 0
                landing = risen if way > 0 else fallen

                @pl.when(there)
                def _(piece=piece, target=target, way=way, first=first, landing=landing):
                    load(piece, target).wait()
                    cross(piece, target).wait_recv()
                    total = own[piece, target].astype(f32) + crossed[piece, target].astype(f32)

                    @pl.when(first)
                    def _():
                        own[piece, target] = total.astype(own.dtype)

                    @pl.when(jnp.logical_not(first))
                    def _():
                        onward(piece, target, way, True).wait_recv()
                        own[piece, target] = (
                            total + landing[piece, target].astype(f32)
                        ).astype(own.dtype)

                    onward(piece, target, way).start()

            yield
        load(piece, line).wait()
        cross(piece, line).wait_recv()
        out = out_at(piece)
        out[...] = own[piece, line].astype(f32) + crossed[piece, line].astype(f32)
        yield
        for way, arrives in ((-1, line < count - 1), (1, line > 0)):
            landing = risen if way > 0 else fallen

            @pl.when(arrives)
            def _(way=way, landing=landing, piece=piece, out=out):
                onward(piece, line, way, True).wait_recv()
                out[...] += landing[piece, line].astype(f32)

        yield
    for piece in range(pieces):
        for distance in range(count - 1, -1, -1):
            for target, there, way in targets(distance):

                def finish(piece=piece, target=target, way=way):
                    cross(piece, target).wait_send()
                    if way:
                        onward(piece, target, way).wait_send()

                guarded(there, finish)


ANY = pl.BlockSpec(memory_space=pl.ANY)
IN_VMEM = pl.BlockSpec(memory_space=pltpu.VMEM)
DMA = pltpu.SemaphoreType.DMA


def link_call(body, number, ins, outs, shapes, scratch, moved):
    return pl.pallas_call(
        body,
        in_specs=ins,
        out_specs=outs,
        out_shape=shapes,
        scratch_shapes=scratch,
        compiler_params=pltpu.CompilerParams(
            collective_id=number, has_side_effects=True, vmem_limit_bytes=VMEM_BYTES
        ),
        cost_estimate=pl.CostEstimate(flops=0, bytes_accessed=moved, transcendentals=0),
    )


def gathered_head(value, number, pieces=4):
    count = lax.axis_size("head")
    if count != 4:
        return lax.all_gather(value, "head", axis=0, tiled=True)
    rows, width = value.shape

    def body(own_ref, out_ref, local, send, arrive):
        greet(head_partners())
        run_together([gather_head(own_ref, out_ref, local, send, arrive, pieces)])

    out = link_call(
        body,
        number,
        [ANY],
        ANY,
        shaped((count, rows, width), value.dtype),
        [DMA((1,)), DMA((3, pieces)), DMA((3, pieces))],
        60_000_000,
    )(value)
    return out.reshape(count * rows, width)


def gathered_seq(value, number):
    total = lax.axis_size("seq")
    count = total // SIDE
    rows, width = value.shape
    if total % SIDE or count < 2:
        return lax.all_gather(value, "seq")

    def body(own_ref, out_ref, *sems):
        greet(seq_partners(count))
        run_together([gather_seq(own_ref, out_ref, *sems, count)])

    return link_call(
        body,
        number,
        [ANY],
        ANY,
        shaped((total, rows, width), value.dtype),
        [DMA((1,))] + [DMA((2 * count,)) for _ in range(4)],
        120_000_000,
    )(value)


def head_scratch(rows, width):
    return [
        pltpu.VMEM((2, rows, width), bf16),
        pltpu.VMEM((2, rows, width), bf16),
        pltpu.VMEM((rows, width), bf16),
        DMA((2,)),
        DMA((3,)),
        DMA((3,)),
    ]


def seq_scratch(pieces, count, rows, width):
    return [pltpu.VMEM((pieces, count, rows, width), bf16) for _ in range(4)] + [
        DMA((pieces, count)),
        DMA((2, pieces, count)),
        DMA((3, pieces, count)),
    ]


def scattered_head(value, number, pieces=2):
    count = lax.axis_size("head")
    if count != 4:
        return scattered(value, "head")
    rows, width = value.shape[0] // count, value.shape[1] // pieces

    def body(source, out, *rest):
        greet(head_partners())
        steps = []
        for piece in range(pieces):
            span = pl.ds(piece * width, width)

            def source_at(target, span=span):
                return source.at[pl.ds(pl.multiple_of(target * rows, rows), rows), span]

            steps.append(
                scatter_head(source_at, out.at[:, span], *rest[6 * piece : 6 * piece + 6])
            )
        run_together(steps)

    return link_call(
        body,
        number,
        [ANY],
        IN_VMEM,
        shaped((rows, value.shape[1]), f32),
        head_scratch(rows, width) * pieces,
        60_000_000,
    )(value)


def scattered_seq(value, number, pieces=2):
    total = lax.axis_size("seq")
    count = total // SIDE
    if total % SIDE or count < 2:
        return scattered(value, "seq")
    rows, width = value.shape[0] // total, value.shape[1] // pieces

    def body(source, out, *rest):
        greet(seq_partners(count))

        def source_at(target, piece):
            return source.at[
                pl.ds(pl.multiple_of(target * rows, rows), rows), pl.ds(piece * width, width)
            ]

        def out_at(piece):
            return out.at[:, pl.ds(piece * width, width)]

        run_together([scatter_seq(source_at, out_at, *rest, count)])

    return link_call(
        body,
        number,
        [ANY],
        IN_VMEM,
        shaped((rows, value.shape[1]), f32),
        seq_scratch(pieces, count, rows, width),
        120_000_000,
    )(value)


def scattered_last(qkv, normed, mlp, number, pieces=4):
    total, heads = lax.axis_size("seq"), lax.axis_size("head")
    count = total // SIDE
    if total % SIDE or count < 2 or heads != 4:
        return (
            scattered(qkv, "seq"),
            scattered(normed, "head"),
            [scattered(part, "head", 1) for part in mlp],
        )
    rows, width = qkv.shape[0] // total, qkv.shape[1] // pieces
    own_rows = normed.shape[0] // heads
    units, slices = mlp[0].shape[0], mlp[0].shape[1] // heads

    def body(qkv_ref, normed_ref, *rest):
        mlp_refs, rest = rest[: len(mlp)], rest[len(mlp) :]
        qkv_out, normed_out, rest = rest[0], rest[1], rest[2:]
        mlp_outs, rest = rest[: len(mlp)], rest[len(mlp) :]
        greet(head_partners() + seq_partners(count))

        def qkv_at(target, piece):
            return qkv_ref.at[
                pl.ds(pl.multiple_of(target * rows, rows), rows), pl.ds(piece * width, width)
            ]

        def qkv_out_at(piece):
            return qkv_out.at[:, pl.ds(piece * width, width)]

        def normed_at(target):
            return normed_ref.at[pl.ds(pl.multiple_of(target * own_rows, own_rows), own_rows)]

        steps = [scatter_seq(qkv_at, qkv_out_at, *rest[:7], count)]
        steps.append(scatter_head(normed_at, normed_out, *rest[7:13]))
        for index, (ref, out) in enumerate(zip(mlp_refs, mlp_outs)):

            def mlp_at(target, ref=ref):
                return ref.at[:, pl.ds(pl.multiple_of(target * slices, slices), slices)]

            begin = 13 + 6 * index
            steps.append(scatter_head(mlp_at, out, *rest[begin : begin + 6]))
        run_together(steps)

    outs = link_call(
        body,
        number,
        [ANY] * (2 + len(mlp)),
        [IN_VMEM] * (2 + len(mlp)),
        [shaped((rows, qkv.shape[1]), f32), shaped((own_rows, normed.shape[1]), f32)]
        + [shaped((units, slices), f32) for _ in mlp],
        seq_scratch(pieces, count, rows, width)
        + head_scratch(own_rows, normed.shape[1])
        + head_scratch(units, slices) * len(mlp),
        250_000_000,
    )(qkv, normed, *mlp)
    return outs[0], outs[1], list(outs[2:])


def silu_slope(tensor):
    sigmoid_part = jax.nn.sigmoid(tensor)
    return sigmoid_part * (1.0 + tensor * (1.0 - sigmoid_part))


def gathered(value, axis):
    return lax.all_gather(value, axis, axis=0, tiled=True)


def scattered(value, axis, dimension=0):
    return lax.psum_scatter(
        value.astype(bf16), axis, scatter_dimension=dimension, tiled=True
    ).astype(f32)


def on_device(
    block_in,
    out_cot,
    gain_one,
    qkv_weight,
    conv_weight,
    gate_weight,
    gain_out,
    out_weight,
    gain_two,
    mlp_gate,
    mlp_up,
    mlp_down,
    decay_code,
    beta_code,
):
    span_rows = decay_code.shape[0]
    width, heads, inner = qkv_weight.shape
    total_len = span_rows * lax.axis_size("seq")
    lead_rows = conv_weight.shape[0] - 1
    input_f = block_in.astype(f32)
    gain_first = gain_one.astype(f32)
    gain_second = gain_two.astype(f32)
    gain_head = gain_out.reshape(1, -1)
    taps = conv_weight.reshape(conv_weight.shape[0], heads * inner)
    qkv_flat = qkv_weight.reshape(width, heads * inner)
    gate_flat = gate_weight.reshape(width, heads * DV)
    out_flat = out_weight.reshape(heads * DV, width)
    columns, run_rows = token_columns(decay_code, beta_code, total_len)

    wide_in = gathered_head(block_in, 1).astype(f32)
    hat_first = wide_in * rms_scale(wide_in)
    normed_first = (hat_first * gain_first).astype(bf16)
    mixed_in = mm(normed_first, qkv_flat).astype(bf16)
    tail_in = passed_along(mixed_in[span_rows - 8 :], "seq", 1)
    tail_in = jnp.where(jnp.arange(8)[:, None] >= 8 - lead_rows, tail_in.astype(f32), 0.0)
    cot_all = gathered(out_cot, "seq")
    solve, score, fresh, reach, inner_part, turn, local_states, piece_end = run_local_forward(
        mixed_in, tail_in, taps, columns, run_rows, heads
    )
    ends = gathered_seq(piece_end.reshape(-1, DV + DK), 2).reshape(-1, heads, DK, DV + DK)
    gate_pre = mm(normed_first, gate_flat)
    states, core, branch = run_finish_forward(
        ends, local_states, reach, inner_part, gate_pre, gain_head
    )
    middle = input_f + scattered_head(mm(branch, out_flat).astype(bf16), 3)
    scale_two = rms_scale(middle)
    hat_two = middle * scale_two
    normed_two = (hat_two * gain_second).astype(bf16)
    normed_two, cot_all = lax.optimization_barrier((normed_two, cot_all))

    rows_out = gathered_seq(normed_two, 4).reshape(-1, width)
    gate_part = mm(rows_out, mlp_gate)
    up_part = mm(rows_out, mlp_up)
    hidden = (jax.nn.silu(gate_part) * up_part).astype(bf16)
    cot_f = out_cot.astype(f32)
    d_hidden = mm_nt(cot_all, mlp_down)
    d_gate_mlp = (d_hidden * up_part * silu_slope(gate_part)).astype(bf16)
    d_up_mlp = (d_hidden * jax.nn.silu(gate_part)).astype(bf16)
    d_rows = (mm_nt(d_gate_mlp, mlp_gate) + mm_nt(d_up_mlp, mlp_up)).astype(bf16)
    d_normed_two = scattered_seq(d_rows, 5)
    hidden, d_normed_two = lax.optimization_barrier((hidden, d_normed_two))
    mlp_out = scattered(mm(hidden, mlp_down), "seq")
    output = (middle + mlp_out).astype(bf16)
    gain_two_part = jnp.sum(d_normed_two * hat_two, 0)
    e_two = d_normed_two * gain_second
    d_middle = cot_f + scale_two * (
        e_two - hat_two * jnp.mean(e_two * hat_two, axis=-1, keepdims=True)
    )
    d_mix_all = gathered_head(d_middle.astype(bf16), 6)
    d_branch = mm_nt(d_mix_all, out_flat)
    d_core, d_gate_low, gain_out_part, local_grads, grad_end = run_local_backward(
        d_branch, core, gate_pre, gain_head, reach, turn
    )
    grad_ends = gathered_seq(grad_end.reshape(-1, DV), 7).reshape(-1, heads, DK, DV)
    grad_out_w = mm_tn(branch, d_mix_all)
    grad_out_s = scattered(grad_out_w, "seq", 1).reshape(heads, DV, -1)
    grad_gate = mm_tn(normed_first, d_gate_low)
    grad_gate_s = scattered(grad_gate, "seq").reshape(-1, heads, DV)
    d_mixed, d_tail, d_lead, grad_conv = run_finish_backward(
        ends,
        grad_ends,
        mixed_in,
        tail_in,
        taps,
        columns,
        run_rows,
        solve,
        score,
        fresh,
        states,
        d_core,
        local_grads,
    )
    from_next = passed_along(d_lead[:lead_rows], "seq", -1)
    d_tail = d_tail.at[8 - lead_rows :].add(from_next).astype(bf16)
    d_mixed = lax.dynamic_update_slice(d_mixed, d_tail, (span_rows - 8, 0))
    d_normed_part = mm_nt(d_mixed, qkv_flat) + mm_nt(d_gate_low, gate_flat)
    gain_one_part = jnp.sum(d_normed_part * hat_first, 0)
    grad_qkv = mm_tn(normed_first, d_mixed).astype(bf16)
    grad_mgate = mm_tn(d_gate_mlp, rows_out).astype(bf16)
    grad_mup = mm_tn(d_up_mlp, rows_out).astype(bf16)
    grad_down = mm_tn(hidden, cot_all).astype(bf16)

    small = jnp.concatenate(
        [gain_one_part, gain_two_part, gain_out_part.reshape(-1), grad_conv.reshape(-1)]
    ).astype(bf16)
    small_all = lax.all_gather(small, ("seq", "head"))
    grad_qkv_s, d_normed_one, (grad_mgate_t, grad_mup_t, grad_down_h) = scattered_last(
        grad_qkv, d_normed_part.astype(bf16), [grad_mgate, grad_mup, grad_down], 8
    )
    scale_own = rms_scale(input_f)
    hat_own = input_f * scale_own
    e_one = d_normed_one * gain_first
    d_input = (
        d_middle + scale_own * (e_one - hat_own * jnp.mean(e_one * hat_own, axis=-1, keepdims=True))
    ).astype(bf16)

    seq_count, head_count = lax.axis_size("seq"), lax.axis_size("head")
    seq_at, head_at = lax.axis_index("seq"), lax.axis_index("head")
    gains = jnp.sum(small_all[:, : 2 * width + DV].astype(f32), axis=0)

    def own_slice(vector):
        length = vector.shape[0] // (seq_count * head_count)
        return lax.dynamic_slice(vector, ((head_at * seq_count + seq_at) * length,), (length,))

    gain_one_g = own_slice(gains[:width])
    gain_two_g = own_slice(gains[width : 2 * width])
    gain_out_g = own_slice(gains[2 * width :])
    conv_all = lax.dynamic_index_in_dim(
        small_all[:, 2 * width + DV :].reshape(seq_count, head_count, -1), head_at, 1, False
    )
    conv_sum = jnp.sum(conv_all.astype(f32), axis=0).reshape(-1, heads, inner)
    grad_conv_s = lax.dynamic_slice_in_dim(
        conv_sum, seq_at * (inner // seq_count), inner // seq_count, 2
    )
    return (
        output,
        d_input,
        gain_one_g,
        grad_qkv_s.reshape(-1, heads, inner),
        grad_conv_s,
        grad_gate_s,
        gain_out_g,
        grad_out_s,
        gain_two_g,
        grad_mgate_t.T,
        grad_mup_t.T,
        grad_down_h,
    )


def solution(mesh):
    in_specs = (
        P(("seq", "head"), None),
        P(("seq", "head"), None),
        P(),
        P(None, "head", None),
        P(None, "head", None),
        P(None, "head", None),
        P(),
        P("head", None, None),
        P(),
        P(None, "seq"),
        P(None, "seq"),
        P("seq", None),
        P("seq", "head"),
        P("seq", "head"),
    )
    out_specs = (
        P(("seq", "head"), None),
        P(("seq", "head"), None),
        P(("head", "seq")),
        P("seq", "head", None),
        P(None, "head", "seq"),
        P("seq", "head", None),
        P(("head", "seq")),
        P("head", None, "seq"),
        P(("head", "seq")),
        P("head", "seq"),
        P("head", "seq"),
        P("seq", "head"),
    )
    return jax.shard_map(
        on_device, mesh=mesh, in_specs=in_specs, out_specs=out_specs, check_vma=False
    )
```

```python
import functools
import math

import jax
import jax.numpy as jnp
from jax import lax
from jax.experimental import pallas as pl
from jax.experimental.pallas import tpu as pltpu
from jax.sharding import PartitionSpec as P

DK = 128
DV = 256
STRETCH = 64
GROUP = 4 * STRETCH
INNER = 2 * DK + DV
BETA, GAMMA, BETA_GAMMA, TAIL, LAST, RUN = range(6)

epsilon = 1e-06
bf16 = jnp.bfloat16
f32 = jnp.float32
VMEM_BYTES = 56 * 2**20


def passed_along(value, axis, steps):
    count = lax.axis_size(axis)
    first, last = (max(0, -steps), min(count, count - steps))
    return lax.ppermute(value, axis, [(source, source + steps) for source in range(first, last)])


def rms_scale(tensor):
    return lax.rsqrt(jnp.mean(tensor * tensor, axis=-1, keepdims=True) + epsilon)


def log_rates(decay_code, total_len):
    code_level = decay_code.astype(f32) / 1023.0
    smooth = -jnp.exp(-code_level * math.log(total_len / 32.0)) / 32.0
    return jnp.where(decay_code == 1024, -0.25, smooth)


def token_columns(decay_code, beta_code, total_len):
    rows, heads = decay_code.shape
    rates = log_rates(decay_code, total_len)
    run = jnp.einsum(
        "ij,bjh->bih",
        jnp.tril(jnp.ones((STRETCH, STRETCH), f32)),
        rates.reshape(rows // STRETCH, STRETCH, heads),
        precision=lax.Precision.HIGHEST,
    )
    last = jnp.broadcast_to(run[:, -1:], run.shape).reshape(rows, heads)
    run = run.reshape(rows, heads)
    beta = 0.5 + beta_code.astype(f32) / 512.0
    gamma = jnp.exp(run)
    columns = jnp.concatenate(
        [beta, gamma, beta * gamma, jnp.exp(last - run), jnp.exp(last), run], axis=1
    )
    columns = jnp.pad(columns, ((0, 0), (0, 128 - columns.shape[1])))
    run_rows = jnp.pad(run.T, ((0, 8 - heads % 8), (0, 0)))
    return columns, run_rows


def mm(left, right):
    return jnp.dot(left, right, preferred_element_type=f32)


def mm_nt(left, right):
    return lax.dot_general(left, right, (((1,), (1,)), ((), ())), preferred_element_type=f32)


def mm_tn(left, right):
    return lax.dot_general(left, right, (((0,), (0,)), ((), ())), preferred_element_type=f32)


def column(columns_ref, kind, head, heads):
    block = columns_ref[...]
    lanes = lax.broadcasted_iota(jnp.int32, block.shape, 1)
    return jnp.sum(jnp.where(lanes == kind * heads + head, block, 0.0), axis=1, keepdims=True)


def square_ids():
    return (
        lax.broadcasted_iota(jnp.int32, (GROUP, GROUP), 0),
        lax.broadcasted_iota(jnp.int32, (GROUP, GROUP), 1),
    )


def convolved(padded_ref, tail_ref, mixed_ref, taps_ref):
    rows = mixed_ref.shape[0]
    count = taps_ref.shape[0]
    padded_ref[0:8, :] = tail_ref[...]
    padded_ref[8 : 8 + rows, :] = mixed_ref[...].astype(f32)
    taps = taps_ref[...].astype(f32)
    start = 9 - count
    total = taps[0:1] * padded_ref[start : start + rows, :]
    for tap in range(1, count):
        total += taps[tap : tap + 1] * padded_ref[start + tap : start + tap + rows, :]
    return total


def chunk_masks_stack(transposed):
    lanes = lax.broadcasted_iota(jnp.int32, transposed.shape, 1) // STRETCH
    parts = [jnp.where(lanes == part, transposed, 0.0) for part in range(GROUP // STRETCH)]
    return jnp.concatenate(parts, axis=0).astype(bf16)


def local_forward(
    mixed_ref,
    tail_ref,
    taps_ref,
    columns_ref,
    run_rows_ref,
    solve_ref,
    score_ref,
    fresh_ref,
    reach_ref,
    inner_ref,
    turn_ref,
    local_ref,
    end_ref,
    padded,
    turn_t,
    offsets,
):
    head = pl.program_id(0)
    heads = pl.num_programs(0)
    rows = mixed_ref.shape[0]
    per_group = GROUP // STRETCH
    stretches = rows // STRETCH
    total = convolved(padded, tail_ref, mixed_ref, taps_ref)
    activated = total * jax.nn.sigmoid(total)
    raw_q, raw_k = activated[:, :DK], activated[:, DK : 2 * DK]
    queries = raw_q * (
        lax.rsqrt(jnp.sum(raw_q * raw_q, axis=1, keepdims=True) + epsilon) * DK ** (-0.5)
    )
    keys = raw_k * lax.rsqrt(jnp.sum(raw_k * raw_k, axis=1, keepdims=True) + epsilon)
    values = activated[:, 2 * DK :]
    beta = column(columns_ref, BETA, head, heads)
    gamma = column(columns_ref, GAMMA, head, heads)
    beta_gamma = column(columns_ref, BETA_GAMMA, head, heads)
    tail_decay = column(columns_ref, TAIL, head, heads)
    last = column(columns_ref, LAST, head, heads)
    run = column(columns_ref, RUN, head, heads)
    row_id, col_id = square_ids()
    same = row_id // STRETCH == col_id // STRETCH
    causal = same & (row_id >= col_id)
    diagonal = row_id == col_id
    eye = jnp.where(
        lax.broadcasted_iota(jnp.int32, (DK, DK), 0) == lax.broadcasted_iota(jnp.int32, (DK, DK), 1),
        1.0,
        0.0,
    )
    for group in range(rows // GROUP):
        span = slice(group * GROUP, (group + 1) * GROUP)
        key_b = keys[span].astype(bf16)
        query_b = queries[span].astype(bf16)
        gaps = run[span] - run_rows_ref[pl.ds(head, 1), span]
        within = jnp.exp(jnp.where(causal, gaps, -1e30))
        lower = jnp.where(diagonal, 0.0, beta[span] * within * mm_nt(key_b, key_b))
        solve = jnp.where(diagonal, 1.0, jnp.where(row_id // 2 == col_id // 2, -lower, 0.0))
        size = 2
        while size < STRETCH:
            crossing = (row_id // (2 * size) == col_id // (2 * size)) & (
                row_id // size != col_id // size
            )
            solve_b = solve.astype(bf16)
            half = mm(solve_b, jnp.where(crossing, lower, 0.0).astype(bf16))
            solve = solve - mm(half.astype(bf16), solve_b)
            size *= 2
        solve_b = solve.astype(bf16)
        right = jnp.concatenate([beta[span] * values[span], beta_gamma[span] * keys[span]], axis=1)
        fresh_b = mm(solve_b, right.astype(bf16)).astype(bf16)
        score_b = (within * mm_nt(query_b, key_b)).astype(bf16)
        scored = mm(score_b, fresh_b)
        solve_ref[group] = solve_b
        score_ref[group] = score_b
        fresh_ref[span, :] = fresh_b
        inner_ref[span, :] = scored[:, :DV]
        reach_ref[span, :] = (gamma[span] * queries[span] - scored[:, DV:]).astype(bf16)
        tail_keys = (tail_decay[span] * keys[span]).T
        moved = mm(chunk_masks_stack(tail_keys), fresh_b)
        for part in range(per_group):
            at = group * per_group + part
            block = moved[part * DK : (part + 1) * DK]
            stay = last[at * STRETCH : at * STRETCH + 1]
            turned = stay * eye - block[:, DV:]
            turn_t[head, at] = turned.astype(bf16)
            turn_ref[at] = turned.T.astype(bf16)
            offsets[head, at] = block[:, :DV]

    @pl.when(head == heads - 1)
    def _():
        states = [
            jnp.concatenate([jnp.zeros((DK, DV), f32), eye], axis=1)
            for _ in range(local_ref.shape[0])
        ]
        for at in range(stretches):
            for h in range(len(states)):
                state_b = states[h].astype(bf16)
                local_ref[h, at] = state_b
                moved = mm(turn_t[h, at], state_b)
                states[h] = jnp.concatenate(
                    [moved[:, :DV] + offsets[h, at], moved[:, DV:]], axis=1
                )
        for h in range(len(states)):
            end_ref[h] = states[h].astype(bf16)


def finish_forward(
    ends_ref, local_ref, reach_ref, inner_ref, gate_ref, gain_ref, state_ref, core_ref, branch_ref, start
):
    head = pl.program_id(0)
    heads, stretches = start.shape[0], local_ref.shape[0]

    @pl.when(head == 0)
    def _():
        start[...] = jnp.zeros_like(start)

        def one(source, carry):
            for h in range(heads):
                start[h] = (
                    mm(ends_ref[source, h, :, DV:], start[h].astype(bf16))
                    + ends_ref[source, h, :, :DV].astype(f32)
                )
            return carry

        lax.fori_loop(0, lax.axis_index("seq"), one, 0)

    start_b = start[head].astype(bf16)
    cores = []
    for at in range(stretches):
        state_b = (
            local_ref[at, :, :DV].astype(f32) + mm(local_ref[at, :, DV:], start_b)
        ).astype(bf16)
        state_ref[at] = state_b
        span = slice(at * STRETCH, (at + 1) * STRETCH)
        cores.append(inner_ref[span, :] + mm(reach_ref[span, :], state_b))
    core = jnp.concatenate(cores, axis=0)
    core_ref[...] = core
    gate = gate_ref[...]
    branch = core * rms_scale(core) * gain_ref[...].astype(f32) * (gate * jax.nn.sigmoid(gate))
    branch_ref[...] = branch.astype(bf16)


def local_backward(
    d_branch_ref,
    core_ref,
    gate_ref,
    gain_ref,
    reach_ref,
    turn_ref,
    d_core_ref,
    d_gate_ref,
    gain_part_ref,
    local_ref,
    end_ref,
    pulls,
):
    head = pl.program_id(0)
    heads = pl.num_programs(0)
    rows = core_ref.shape[0]
    per_group = GROUP // STRETCH
    stretches = rows // STRETCH
    core = core_ref[...]
    gate = gate_ref[...]
    gain = gain_ref[...].astype(f32)
    d_branch = d_branch_ref[...]
    scale = rms_scale(core)
    nhat = core * scale
    sig = jax.nn.sigmoid(gate)
    gated = d_branch * (gate * sig)

    @pl.when(head == 0)
    def _():
        gain_part_ref[...] = jnp.zeros_like(gain_part_ref)

    gain_part_ref[...] += jnp.sum(gated * nhat, axis=0, keepdims=True)
    f = gated * gain
    d_core = scale * (f - nhat * jnp.mean(f * nhat, axis=1, keepdims=True))
    d_gate_ref[...] = (d_branch * nhat * gain * sig * (1.0 + gate * (1.0 - sig))).astype(bf16)
    d_core_b = d_core.astype(bf16)
    d_core_ref[...] = d_core_b
    for group in range(rows // GROUP):
        span = slice(group * GROUP, (group + 1) * GROUP)
        pulled = mm(chunk_masks_stack(reach_ref[span, :].astype(f32).T), d_core_b[span])
        for part in range(per_group):
            pulls[head, group * per_group + part] = pulled[part * DK : (part + 1) * DK]

    @pl.when(head == heads - 1)
    def _():
        eye = jnp.where(
            lax.broadcasted_iota(jnp.int32, (DK, DK), 0)
            == lax.broadcasted_iota(jnp.int32, (DK, DK), 1),
            1.0,
            0.0,
        )
        grads = [
            jnp.concatenate([jnp.zeros((DK, DV), f32), eye], axis=1)
            for _ in range(local_ref.shape[0])
        ]
        for at in reversed(range(stretches)):
            for h in range(len(grads)):
                grad_b = grads[h].astype(bf16)
                local_ref[h, at] = grad_b
                moved = mm(turn_ref[h, at], grad_b)
                grads[h] = jnp.concatenate([moved[:, :DV] + pulls[h, at], moved[:, DV:]], axis=1)
        for h in range(len(grads)):
            end_ref[h] = grads[h][:, :DV].astype(bf16)


def finish_backward(
    ends_ref,
    grad_ends_ref,
    mixed_ref,
    tail_ref,
    taps_ref,
    columns_ref,
    run_rows_ref,
    solve_ref,
    score_ref,
    fresh_ref,
    state_ref,
    d_core_ref,
    local_ref,
    d_mixed_ref,
    tail_out_ref,
    lead_ref,
    grad_taps_ref,
    padded,
    spread,
    end,
):
    head = pl.program_id(0)
    heads = pl.num_programs(0)
    rows = mixed_ref.shape[0]
    per_group = GROUP // STRETCH

    @pl.when(head == 0)
    def _():
        end[...] = jnp.zeros_like(end)
        count = ends_ref.shape[0]

        def one(turn, carry):
            source = count - 1 - turn
            for h in range(end.shape[0]):
                end[h] = (
                    mm_tn(ends_ref[source, h, :, DV:], end[h].astype(bf16))
                    + grad_ends_ref[source, h].astype(f32)
                )
            return carry

        lax.fori_loop(0, count - 1 - lax.axis_index("seq"), one, 0)

    end_b = end[head].astype(bf16)
    total = convolved(padded, tail_ref, mixed_ref, taps_ref)
    sig = jax.nn.sigmoid(total)
    activated = total * sig
    raw_q, raw_k = activated[:, :DK], activated[:, DK : 2 * DK]
    scale_q = lax.rsqrt(jnp.sum(raw_q * raw_q, axis=1, keepdims=True) + epsilon)
    scale_k = lax.rsqrt(jnp.sum(raw_k * raw_k, axis=1, keepdims=True) + epsilon)
    unit_q = raw_q * scale_q
    keys = raw_k * scale_k
    beta = column(columns_ref, BETA, head, heads)
    gamma = column(columns_ref, GAMMA, head, heads)
    beta_gamma = column(columns_ref, BETA_GAMMA, head, heads)
    tail_decay = column(columns_ref, TAIL, head, heads)
    run = column(columns_ref, RUN, head, heads)
    row_id, col_id = square_ids()
    causal = (row_id // STRETCH == col_id // STRETCH) & (row_id >= col_id)
    diagonal = row_id == col_id
    d_queries, d_keys, d_values = [], [], []
    for group in range(rows // GROUP):
        span = slice(group * GROUP, (group + 1) * GROUP)
        key_b = keys[span].astype(bf16)
        query_b = (unit_q[span] * DK ** (-0.5)).astype(bf16)
        tail_keys = (tail_decay[span] * keys[span]).astype(bf16)
        d_core_b = d_core_ref[span, :]
        grad_bs, from_grad, fresh_parts, from_state = [], [], [], []
        for part in range(per_group):
            at = group * per_group + part
            own = slice(part * STRETCH, (part + 1) * STRETCH)
            rows_at = slice(at * STRETCH, (at + 1) * STRETCH)
            grad_b = (
                local_ref[at, :, :DV].astype(f32) + mm(local_ref[at, :, DV:], end_b)
            ).astype(bf16)
            grad_bs.append(grad_b)
            from_grad.append(mm(tail_keys[own], grad_b))
            fresh_parts.append(mm(fresh_ref[rows_at, DV:], state_ref[at]))
            from_state.append(mm_nt(d_core_b[own], state_ref[at]))
        d_fresh = mm_tn(score_ref[group], d_core_b) + jnp.concatenate(from_grad, axis=0)
        d_right = mm_tn(solve_ref[group], d_fresh.astype(bf16))
        d_right_b = d_right.astype(bf16)
        fresh = fresh_ref[span, :DV].astype(f32) - jnp.concatenate(fresh_parts, axis=0)
        fresh_b = fresh.astype(bf16)
        gaps = run[span] - run_rows_ref[pl.ds(head, 1), span]
        within = jnp.exp(jnp.where(causal, gaps, -1e30))
        d_score = (within * mm_nt(d_core_b, fresh_b)).astype(bf16)
        d_lower = jnp.where(
            diagonal, 0.0, -beta[span] * within * mm_nt(d_right_b, fresh_b)
        ).astype(bf16)
        state_keys, grad_keys = [], []
        for part in range(per_group):
            at = group * per_group + part
            own = slice(part * STRETCH, (part + 1) * STRETCH)
            state_keys.append(mm_nt(d_right_b[own], state_ref[at]))
            grad_keys.append(mm_nt(fresh_b[own], grad_bs[part]))
        d_queries.append(gamma[span] * jnp.concatenate(from_state, axis=0) + mm(d_score, key_b))
        d_keys.append(
            mm_tn(d_score, query_b)
            + mm_tn(d_lower, key_b)
            + mm(d_lower, key_b)
            + tail_decay[span] * jnp.concatenate(grad_keys, axis=0)
            - beta_gamma[span] * jnp.concatenate(state_keys, axis=0)
        )
        d_values.append(beta[span] * d_right)
    g_q = jnp.concatenate(d_queries, axis=0) * DK ** (-0.5)
    g_k = jnp.concatenate(d_keys, axis=0)
    d_act = jnp.concatenate(
        [
            scale_q * (g_q - unit_q * jnp.sum(unit_q * g_q, axis=1, keepdims=True)),
            scale_k * (g_k - keys * jnp.sum(keys * g_k, axis=1, keepdims=True)),
            jnp.concatenate(d_values, axis=0),
        ],
        axis=1,
    )
    d_conv = d_act * (sig * (1.0 + total * (1.0 - sig)))
    taps = taps_ref[...].astype(f32)
    count = taps_ref.shape[0]
    start = 9 - count
    grad_taps_ref[...] = jnp.concatenate(
        [
            jnp.sum(padded[start + tap : start + tap + rows, :] * d_conv, axis=0, keepdims=True)
            for tap in range(count)
        ],
        axis=0,
    )
    spread[0:8, :] = jnp.zeros((8, d_conv.shape[1]), f32)
    spread[8 : 8 + rows, :] = d_conv
    spread[8 + rows : 16 + rows, :] = jnp.zeros((8, d_conv.shape[1]), f32)
    lead = taps[0:1] * spread[8:16, :]
    d_mixed = taps[0:1] * spread[7 + count : 7 + count + rows, :]
    for tap in range(1, count):
        lead += taps[tap : tap + 1] * spread[8 - tap : 16 - tap, :]
        begin = 7 + count - tap
        d_mixed += taps[tap : tap + 1] * spread[begin : begin + rows, :]
    lead_ref[...] = lead
    d_mixed_ref[...] = d_mixed.astype(bf16)
    tail_out_ref[...] = d_mixed[rows - 8 :]


def whole(shape):
    return pl.BlockSpec(shape, lambda h: (0,) * len(shape))


def by_head(shape):
    return pl.BlockSpec((None,) + shape, lambda h: (h,) + (0,) * len(shape))


def by_columns(rows, width):
    return pl.BlockSpec((rows, width), lambda h: (0, h))


def kernel_call(body, heads, ins, outs, out_shapes, scratch, flops, moved):
    return pl.pallas_call(
        body,
        grid=(heads,),
        in_specs=ins,
        out_specs=outs,
        out_shape=out_shapes,
        scratch_shapes=scratch,
        compiler_params=pltpu.CompilerParams(
            dimension_semantics=("arbitrary",), vmem_limit_bytes=VMEM_BYTES
        ),
        cost_estimate=pl.CostEstimate(flops=flops, bytes_accessed=moved, transcendentals=0),
    )


def shaped(shape, kind):
    return jax.ShapeDtypeStruct(shape, kind)


def run_local_forward(mixed, tail, taps, columns, run_rows, heads):
    rows = mixed.shape[0]
    count = taps.shape[0]
    groups, stretches = rows // GROUP, rows // STRETCH
    return kernel_call(
        local_forward,
        heads,
        [
            by_columns(rows, INNER),
            by_columns(8, INNER),
            by_columns(count, INNER),
            whole(columns.shape),
            whole(run_rows.shape),
        ],
        [
            by_head((groups, GROUP, GROUP)),
            by_head((groups, GROUP, GROUP)),
            by_head((rows, DV + DK)),
            by_head((rows, DK)),
            by_columns(rows, DV),
            by_head((stretches, DK, DK)),
            whole((heads, stretches, DK, DV + DK)),
            whole((heads, DK, DV + DK)),
        ],
        [
            shaped((heads, groups, GROUP, GROUP), bf16),
            shaped((heads, groups, GROUP, GROUP), bf16),
            shaped((heads, rows, DV + DK), bf16),
            shaped((heads, rows, DK), bf16),
            shaped((rows, heads * DV), f32),
            shaped((heads, stretches, DK, DK), bf16),
            shaped((heads, stretches, DK, DV + DK), bf16),
            shaped((heads, DK, DV + DK), bf16),
        ],
        [
            pltpu.VMEM((rows + 8, INNER), f32),
            pltpu.VMEM((heads, stretches, DK, DK), bf16),
            pltpu.VMEM((heads, stretches, DK, DV), f32),
        ],
        12_000_000_000,
        20_000_000,
    )(mixed, tail, taps, columns, run_rows)


def run_finish_forward(ends, local, reach, inner, gate_pre, gain):
    heads, stretches = local.shape[:2]
    rows = inner.shape[0]
    return kernel_call(
        finish_forward,
        heads,
        [
            whole(ends.shape),
            by_head((stretches, DK, DV + DK)),
            by_head((rows, DK)),
            by_columns(rows, DV),
            by_columns(rows, DV),
            whole(gain.shape),
        ],
        [by_head((stretches, DK, DV)), by_columns(rows, DV), by_columns(rows, DV)],
        [
            shaped((heads, stretches, DK, DV), bf16),
            shaped((rows, heads * DV), f32),
            shaped((rows, heads * DV), bf16),
        ],
        [pltpu.VMEM((heads, DK, DV), f32)],
        3_000_000_000,
        20_000_000,
    )(ends, local, reach, inner, gate_pre, gain)


def run_local_backward(d_branch, core, gate_pre, gain, reach, turn):
    heads, stretches = turn.shape[:2]
    rows = core.shape[0]
    return kernel_call(
        local_backward,
        heads,
        [
            by_columns(rows, DV),
            by_columns(rows, DV),
            by_columns(rows, DV),
            whole(gain.shape),
            by_head((rows, DK)),
            whole(turn.shape),
        ],
        [
            by_columns(rows, DV),
            by_columns(rows, DV),
            whole((1, DV)),
            whole((heads, stretches, DK, DV + DK)),
            whole((heads, DK, DV)),
        ],
        [
            shaped((rows, heads * DV), bf16),
            shaped((rows, heads * DV), bf16),
            shaped((1, DV), f32),
            shaped((heads, stretches, DK, DV + DK), bf16),
            shaped((heads, DK, DV), bf16),
        ],
        [pltpu.VMEM((heads, stretches, DK, DV), f32)],
        4_000_000_000,
        20_000_000,
    )(d_branch, core, gate_pre, gain, reach, turn)


def run_finish_backward(
    ends, grad_ends, mixed, tail, taps, columns, run_rows, solve, score, fresh, states, d_core, local
):
    heads, stretches = local.shape[:2]
    rows = mixed.shape[0]
    groups = rows // GROUP
    count = taps.shape[0]
    return kernel_call(
        finish_backward,
        heads,
        [
            whole(ends.shape),
            whole(grad_ends.shape),
            by_columns(rows, INNER),
            by_columns(8, INNER),
            by_columns(count, INNER),
            whole(columns.shape),
            whole(run_rows.shape),
            by_head((groups, GROUP, GROUP)),
            by_head((groups, GROUP, GROUP)),
            by_head((rows, DV + DK)),
            by_head((stretches, DK, DV)),
            by_columns(rows, DV),
            by_head((stretches, DK, DV + DK)),
        ],
        [
            by_columns(rows, INNER),
            by_columns(8, INNER),
            by_columns(8, INNER),
            by_columns(count, INNER),
        ],
        [
            shaped((rows, heads * INNER), bf16),
            shaped((8, heads * INNER), f32),
            shaped((8, heads * INNER), f32),
            shaped((count, heads * INNER), f32),
        ],
        [
            pltpu.VMEM((rows + 8, INNER), f32),
            pltpu.VMEM((rows + 16, INNER), f32),
            pltpu.VMEM((heads, DK, DV), f32),
        ],
        12_000_000_000,
        20_000_000,
    )(ends, grad_ends, mixed, tail, taps, columns, run_rows, solve, score, fresh, states, d_core, local)


MESH = pl.DeviceIdType.MESH
SIDE = 2


def remote(source, target, send, arrive, device):
    return pltpu.make_async_remote_copy(
        src_ref=source,
        dst_ref=target,
        send_sem=send,
        recv_sem=arrive,
        device_id=device,
        device_id_type=MESH,
    )


def greet(partners):
    barrier = pltpu.get_barrier_semaphore()
    expected = 0
    for device, there in partners:
        if there is None:
            pl.semaphore_signal(barrier, inc=1, device_id=device, device_id_type=MESH)
            expected = expected + 1
        else:

            @pl.when(there)
            def _(device=device):
                pl.semaphore_signal(barrier, inc=1, device_id=device, device_id_type=MESH)

            expected = expected + there.astype(jnp.int32)
    pl.semaphore_wait(barrier, expected)


def head_places():
    head, seq = lax.axis_index("head"), lax.axis_index("seq")
    core = lax.rem(head, 2)
    sibling = head + 1 - 2 * core
    across = lax.rem(head + 2, 4)
    return head, seq, sibling, across


def head_partners():
    head, seq, sibling, across = head_places()
    return [((sibling, seq), None), ((across, seq), None)]


def seq_places():
    head, seq = lax.axis_index("head"), lax.axis_index("seq")
    return head, seq // SIDE, lax.rem(seq, SIDE)


def seq_partners(count):
    head, line, side = seq_places()
    return [
        ((head, line * SIDE + 1 - side), None),
        ((head, (line + 1) * SIDE + side), line < count - 1),
        ((head, (line - 1) * SIDE + side), line > 0),
    ]


def run_together(steps):
    steps = list(steps)
    while steps:
        alive = []
        for step in steps:
            try:
                next(step)
                alive.append(step)
            except StopIteration:
                pass
        steps = alive


def gather_head(own_ref, out_ref, local, send, arrive, pieces):
    head, seq, sibling, across = head_places()
    far = lax.rem(sibling + 2, 4)
    rows = own_ref.shape[0] // pieces
    keep = pltpu.make_async_copy(own_ref, out_ref.at[head], local.at[0])
    keep.start()

    def part(ref, piece):
        return ref.at[pl.ds(piece * rows, rows)]

    outgoing = []
    for piece in range(pieces):
        outgoing.append(
            remote(
                part(own_ref, piece),
                part(out_ref.at[head], piece),
                send.at[0, piece],
                arrive.at[0, piece],
                (across, seq),
            )
        )
    for piece in range(pieces):
        outgoing.append(
            remote(
                part(own_ref, piece),
                part(out_ref.at[head], piece),
                send.at[1, piece],
                arrive.at[1, piece],
                (sibling, seq),
            )
        )
    for copy in outgoing:
        copy.start()
    yield
    forwards = []
    for piece in range(pieces):
        outgoing[piece].wait_recv()
        forward = remote(
            part(out_ref.at[across], piece),
            part(out_ref.at[across], piece),
            send.at[2, piece],
            arrive.at[2, piece],
            (sibling, seq),
        )
        forward.start()
        forwards.append(forward)
        yield
    for copy in outgoing[pieces:] + forwards:
        copy.wait_recv()
    for copy in outgoing + forwards:
        copy.wait_send()
    keep.wait()


def scatter_head(source_at, out_ref, own, crossed, passed, local, send, arrive):
    head, seq, sibling, across = head_places()
    far = lax.rem(sibling + 2, 4)
    loads = [
        pltpu.make_async_copy(source_at(target), own.at[slot], local.at[slot])
        for slot, target in enumerate((across, head))
    ]
    copies = [
        remote(source_at(target), crossed.at[slot], send.at[slot], arrive.at[slot], (sibling, seq))
        for slot, target in enumerate((far, sibling))
    ]
    for slot in range(2):
        copies[slot].start()
        loads[slot].start()
    yield
    loads[0].wait()
    copies[0].wait_recv()
    own[0] = (own[0].astype(f32) + crossed[0].astype(f32)).astype(own.dtype)
    onward = remote(own.at[0], passed, send.at[2], arrive.at[2], (across, seq))
    onward.start()
    yield
    loads[1].wait()
    copies[1].wait_recv()
    onward.wait_recv()
    total = own[1].astype(f32) + crossed[1].astype(f32) + passed[...].astype(f32)
    out_ref[...] = total.astype(out_ref.dtype)
    onward.wait_send()
    for copy in copies:
        copy.wait_send()


def gather_seq(own_ref, out_ref, local, side_send, side_arrive, line_send, line_arrive, count):
    head, line, side = seq_places()
    me = line * SIDE + side
    beside = (head, line * SIDE + 1 - side)
    ways = ((1, line < count - 1), (-1, line > 0))
    keep = pltpu.make_async_copy(own_ref, out_ref.at[me], local.at[0])
    keep.start()

    def along(source, block, way, step):
        slot = step if way > 0 else count + step
        return remote(
            source,
            out_ref.at[block],
            line_send.at[slot],
            line_arrive.at[slot],
            (head, (line + way) * SIDE + side),
        )

    def over(source, block, slot):
        return remote(source, out_ref.at[block], side_send.at[slot], side_arrive.at[slot], beside)

    for way, onward in ways:

        @pl.when(onward)
        def _(way=way):
            along(own_ref, me, way, 0).start()

    over(own_ref, me, 0).start()
    yield
    for step in range(1, count):
        for way, onward in ways:
            block = me - way * step * SIDE
            arrives = line >= step if way > 0 else line + step < count

            @pl.when(arrives)
            def _(way=way, onward=onward, block=block, step=step):
                landed = out_ref.at[block]
                slot = step if way > 0 else count + step
                remote(
                    landed, landed, line_send.at[slot - 1], line_arrive.at[slot - 1], beside
                ).wait_recv()

                @pl.when(onward)
                def _():
                    along(landed, block, way, step).start()

                over(landed, block, slot).start()

        yield
    over(own_ref, me, 0).wait()
    for way, onward in ways:

        @pl.when(onward)
        def _(way=way):
            along(own_ref, me, way, 0).wait_send()

    for step in range(1, count):
        for way, onward in ways:
            block = me - way * step * SIDE
            arrives = line >= step if way > 0 else line + step < count

            @pl.when(arrives)
            def _(way=way, onward=onward, block=block, step=step):
                landed = out_ref.at[block]
                slot = step if way > 0 else count + step
                over(landed, block, slot).wait()

                @pl.when(onward)
                def _():
                    along(landed, block, way, step).wait_send()

    keep.wait()


def scatter_seq(source_at, out_at, own, crossed, risen, fallen, local, sends, arrivals, count):
    head, line, side = seq_places()
    beside = (head, line * SIDE + 1 - side)
    pieces = own.shape[0]

    def targets(distance):
        if distance == 0:
            return [(line, None, 0)]
        return [
            (line - distance, line >= distance, -1),
            (line + distance, line + distance < count, 1),
        ]

    def load(piece, target):
        return pltpu.make_async_copy(
            source_at(target, side, piece), own.at[piece, target], local.at[piece, target]
        )

    def cross(piece, target):
        return remote(
            source_at(target, 1 - side, piece),
            crossed.at[piece, target],
            sends.at[0, piece, target],
            arrivals.at[0, piece, target],
            beside,
        )

    def onward(piece, target, way, arriving=False):
        landing = risen if way > 0 else fallen
        return remote(
            own.at[piece, target],
            landing.at[piece, target],
            sends.at[1, piece, target],
            arrivals.at[1 if way > 0 else 2, piece, target],
            beside if arriving else (head, (line + way) * SIDE + side),
        )

    def guarded(there, body):
        if there is None:
            body()
        else:
            pl.when(there)(body)

    def here(piece, target):
        load(piece, target).wait()
        total = own[piece, target].astype(f32)
        if crossed is not None:
            cross(piece, target).wait_recv()
            total += crossed[piece, target].astype(f32)
        return total

    def arrived(piece, target, way):
        landing = risen if way > 0 else fallen
        onward(piece, target, way, True).wait_recv()
        return landing[piece, target].astype(f32)

    for piece in range(pieces):
        for distance in range(count - 1, -1, -1):
            for target, there, _ in targets(distance):

                def begin(piece=piece, target=target):
                    if crossed is not None:
                        cross(piece, target).start()
                    load(piece, target).start()

                guarded(there, begin)
    yield
    for piece in range(pieces):
        for distance in range(count - 1, 0, -1):
            for target, there, way in targets(distance):
                first = line == count - 1 if way < 0 else line == 0

                @pl.when(jnp.logical_and(there, first))
                def _(piece=piece, target=target, way=way):
                    own[piece, target] = here(piece, target).astype(own.dtype)
                    onward(piece, target, way).start()

                @pl.when(jnp.logical_and(there, jnp.logical_not(first)))
                def _(piece=piece, target=target, way=way):
                    total = here(piece, target) + arrived(piece, target, way)
                    own[piece, target] = total.astype(own.dtype)
                    onward(piece, target, way).start()

            yield
        out = out_at(piece)

        @pl.when(line == 0)
        def _(piece=piece, out=out):
            out[...] = (here(piece, line) + arrived(piece, line, -1)).astype(out.dtype)

        @pl.when(line == count - 1)
        def _(piece=piece, out=out):
            out[...] = (here(piece, line) + arrived(piece, line, 1)).astype(out.dtype)

        @pl.when(jnp.logical_and(line > 0, line < count - 1))
        def _(piece=piece, out=out):
            total = here(piece, line) + arrived(piece, line, -1) + arrived(piece, line, 1)
            out[...] = total.astype(out.dtype)

        yield
    for piece in range(pieces):
        for distance in range(count - 1, -1, -1):
            for target, there, way in targets(distance):

                def finish(piece=piece, target=target, way=way):
                    if crossed is not None:
                        cross(piece, target).wait_send()
                    if way:
                        onward(piece, target, way).wait_send()

                guarded(there, finish)


ANY = pl.BlockSpec(memory_space=pl.ANY)
IN_VMEM = pl.BlockSpec(memory_space=pltpu.VMEM)
DMA = pltpu.SemaphoreType.DMA


def link_call(body, number, ins, outs, shapes, scratch, moved):
    return pl.pallas_call(
        body,
        in_specs=ins,
        out_specs=outs,
        out_shape=shapes,
        scratch_shapes=scratch,
        compiler_params=pltpu.CompilerParams(
            collective_id=number, has_side_effects=True, vmem_limit_bytes=VMEM_BYTES
        ),
        cost_estimate=pl.CostEstimate(flops=0, bytes_accessed=moved, transcendentals=0),
    )


def gathered_head(value, number, pieces=4):
    count = lax.axis_size("head")
    if count != 4:
        return lax.all_gather(value, "head", axis=0, tiled=True)
    rows, width = value.shape

    def body(own_ref, out_ref, local, send, arrive):
        greet(head_partners())
        run_together([gather_head(own_ref, out_ref, local, send, arrive, pieces)])

    out = link_call(
        body,
        number,
        [ANY],
        ANY,
        shaped((count, rows, width), value.dtype),
        [DMA((1,)), DMA((3, pieces)), DMA((3, pieces))],
        60_000_000,
    )(value)
    return out.reshape(count * rows, width)


def gathered_seq(value, number):
    total = lax.axis_size("seq")
    count = total // SIDE
    rows, width = value.shape
    if total % SIDE or count < 2:
        return lax.all_gather(value, "seq")

    def body(own_ref, out_ref, *sems):
        greet(seq_partners(count))
        run_together([gather_seq(own_ref, out_ref, *sems, count)])

    return link_call(
        body,
        number,
        [ANY],
        ANY,
        shaped((total, rows, width), value.dtype),
        [DMA((1,))] + [DMA((2 * count,)) for _ in range(4)],
        120_000_000,
    )(value)


def head_scratch(rows, width):
    return [
        pltpu.VMEM((2, rows, width), bf16),
        pltpu.VMEM((2, rows, width), bf16),
        pltpu.VMEM((rows, width), bf16),
        DMA((2,)),
        DMA((3,)),
        DMA((3,)),
    ]


def seq_scratch(pieces, count, rows, width):
    return [pltpu.VMEM((pieces, count, rows, width), bf16) for _ in range(4)] + [
        DMA((pieces, count)),
        DMA((2, pieces, count)),
        DMA((3, pieces, count)),
    ]


def scattered_head(value, number, pieces=2):
    count = lax.axis_size("head")
    if count != 4:
        return scattered(value, "head")
    rows, width = value.shape[0] // count, value.shape[1] // pieces

    def body(source, out, *rest):
        greet(head_partners())
        steps = []
        for piece in range(pieces):
            span = pl.ds(piece * width, width)

            def source_at(target, span=span):
                return source.at[pl.ds(pl.multiple_of(target * rows, rows), rows), span]

            steps.append(
                scatter_head(source_at, out.at[:, span], *rest[6 * piece : 6 * piece + 6])
            )
        run_together(steps)

    return link_call(
        body,
        number,
        [ANY],
        IN_VMEM,
        shaped((rows, value.shape[1]), f32),
        head_scratch(rows, width) * pieces,
        60_000_000,
    )(value)


def scattered_seq(value, number, pieces=2):
    total = lax.axis_size("seq")
    count = total // SIDE
    if total % SIDE or count < 2:
        return scattered(value, "seq")
    rows, width = value.shape[0] // total, value.shape[1] // pieces

    def body(source, out, *rest):
        greet(seq_partners(count))

        def source_at(target, side, piece):
            begin = pl.multiple_of((target * SIDE + side) * rows, rows)
            return source.at[pl.ds(begin, rows), pl.ds(piece * width, width)]

        def out_at(piece):
            return out.at[:, pl.ds(piece * width, width)]

        run_together([scatter_seq(source_at, out_at, *rest, count)])

    return link_call(
        body,
        number,
        [ANY],
        IN_VMEM,
        shaped((rows, value.shape[1]), f32),
        seq_scratch(pieces, count, rows, width),
        120_000_000,
    )(value)


def scattered_last(qkv, gate, normed, mlp, small, gain_rows, number, pieces=4, gate_pieces=2):
    total, heads = lax.axis_size("seq"), lax.axis_size("head")
    count = total // SIDE
    rows, width = qkv.shape[0] // total, qkv.shape[1] // pieces
    gate_width = gate.shape[1] // gate_pieces
    own_rows = normed.shape[0] // heads
    units, slices = mlp[0].shape[0], mlp[0].shape[1] // heads
    small_rows = small.shape[0]

    def body(qkv_ref, gate_ref, normed_ref, small_ref, *rest):
        mlp_refs, rest = rest[: len(mlp)], rest[len(mlp) :]
        qkv_out, gate_out, normed_out, small_out, rest = rest[0], rest[1], rest[2], rest[3], rest[4:]
        mlp_outs, rest = rest[: len(mlp)], rest[len(mlp) :]
        greet(head_partners() + seq_partners(count))

        def qkv_at(target, side, piece):
            begin = pl.multiple_of((target * SIDE + side) * rows, rows)
            return qkv_ref.at[pl.ds(begin, rows), pl.ds(piece * width, width)]

        def gate_at(target, side, piece):
            begin = pl.multiple_of(target * rows, rows)
            return gate_ref.at[pl.ds(begin, rows), pl.ds(piece * gate_width, gate_width)]

        def normed_at(target):
            return normed_ref.at[pl.ds(pl.multiple_of(target * own_rows, own_rows), own_rows)]

        def small_steps(four, own, local, *sems):
            yield from gather_head(small_ref, four, sems[0], sems[1], sems[2], 1)
            own[...] = four[lax.axis_index("head")]
            own[:gain_rows] = jnp.sum(four[:, :gain_rows], axis=0)
            yield from gather_seq(own, small_out, local, *sems[3:7], count)

        steps = [
            scatter_seq(qkv_at, lambda piece: qkv_out.at[:, pl.ds(piece * width, width)], *rest[:7], count),
            scatter_seq(
                gate_at,
                lambda piece: gate_out.at[:, pl.ds(piece * gate_width, gate_width)],
                rest[7],
                None,
                *rest[8:13],
                count,
            ),
            scatter_head(normed_at, normed_out, *rest[13:19]),
            small_steps(*rest[19:29]),
        ]
        for index, (ref, out) in enumerate(zip(mlp_refs, mlp_outs)):

            def mlp_at(target, ref=ref):
                return ref.at[:, pl.ds(pl.multiple_of(target * slices, slices), slices)]

            begin = 29 + 6 * index
            steps.append(scatter_head(mlp_at, out, *rest[begin : begin + 6]))
        run_together(steps)

    line_scratch = seq_scratch(gate_pieces, count, rows, gate_width)
    outs = link_call(
        body,
        number,
        [ANY] * (4 + len(mlp)),
        [IN_VMEM] * (4 + len(mlp)),
        [
            shaped((rows, qkv.shape[1]), bf16),
            shaped((rows, gate.shape[1]), bf16),
            shaped((own_rows, normed.shape[1]), f32),
            shaped((total, small_rows, small.shape[1]), f32),
        ]
        + [shaped((units, slices), bf16) for _ in mlp],
        seq_scratch(pieces, count, rows, width)
        + line_scratch[1:]
        + head_scratch(own_rows, normed.shape[1])
        + [
            pltpu.VMEM((heads, small_rows, small.shape[1]), f32),
            pltpu.VMEM((small_rows, small.shape[1]), f32),
            DMA((1,)),
            DMA((1,)),
            DMA((3, 1)),
            DMA((3, 1)),
        ]
        + [DMA((2 * count,)) for _ in range(4)]
        + head_scratch(units, slices) * len(mlp),
        250_000_000,
    )(qkv, gate, normed, small, *mlp)
    return outs[0], outs[1], outs[2], outs[3], list(outs[4:])


def side_columns(value, side, rows):
    count = value.shape[1] // (rows * SIDE)
    return jnp.concatenate(
        [
            lax.dynamic_slice_in_dim(value, (place * SIDE + side) * rows, rows, 1)
            for place in range(count)
        ],
        axis=1,
    )


def swapped(value):
    count = lax.axis_size("seq")
    return lax.ppermute(value, "seq", [(place, place ^ 1) for place in range(count)])


def silu_slope(tensor):
    sigmoid_part = jax.nn.sigmoid(tensor)
    return sigmoid_part * (1.0 + tensor * (1.0 - sigmoid_part))


def gathered(value, axis):
    return lax.all_gather(value, axis, axis=0, tiled=True)


def scattered(value, axis, dimension=0):
    return lax.psum_scatter(
        value.astype(bf16), axis, scatter_dimension=dimension, tiled=True
    ).astype(f32)


def on_device(
    block_in,
    out_cot,
    gain_one,
    qkv_weight,
    conv_weight,
    gate_weight,
    gain_out,
    out_weight,
    gain_two,
    mlp_gate,
    mlp_up,
    mlp_down,
    decay_code,
    beta_code,
):
    span_rows = decay_code.shape[0]
    width, heads, inner = qkv_weight.shape
    total_len = span_rows * lax.axis_size("seq")
    lead_rows = conv_weight.shape[0] - 1
    input_f = block_in.astype(f32)
    gain_first = gain_one.astype(f32)
    gain_second = gain_two.astype(f32)
    gain_head = gain_out.reshape(1, -1)
    taps = conv_weight.reshape(conv_weight.shape[0], heads * inner)
    qkv_flat = qkv_weight.reshape(width, heads * inner)
    gate_flat = gate_weight.reshape(width, heads * DV)
    out_flat = out_weight.reshape(heads * DV, width)
    columns, run_rows = token_columns(decay_code, beta_code, total_len)

    seq_count, head_count = lax.axis_size("seq"), lax.axis_size("head")
    seq_at, head_at = lax.axis_index("seq"), lax.axis_index("head")
    side = lax.rem(seq_at, SIDE)
    slice_rows = width // seq_count
    scale_own = rms_scale(input_f)
    hat_own = input_f * scale_own
    normed_own = (hat_own * gain_first).astype(bf16)
    normed_first = gathered(normed_own, "head")
    normed_side = gathered(swapped(side_columns(normed_own, 1 - side, slice_rows)), "head")
    mixed_in = mm(normed_first, qkv_flat).astype(bf16)
    tail_in = passed_along(mixed_in[span_rows - 8 :], "seq", 1)
    tail_in = jnp.where(jnp.arange(8)[:, None] >= 8 - lead_rows, tail_in.astype(f32), 0.0)
    cot_all = gathered(out_cot, "seq")
    solve, score, fresh, reach, inner_part, turn, local_states, piece_end = run_local_forward(
        mixed_in, tail_in, taps, columns, run_rows, heads
    )
    ends = gathered_seq(piece_end.reshape(-1, DV + DK), 2).reshape(-1, heads, DK, DV + DK)
    gate_pre = mm(normed_first, gate_flat)
    states, core, branch = run_finish_forward(
        ends, local_states, reach, inner_part, gate_pre, gain_head
    )
    middle = input_f + scattered_head(mm(branch, out_flat).astype(bf16), 3)
    scale_two = rms_scale(middle)
    hat_two = middle * scale_two
    normed_two = (hat_two * gain_second).astype(bf16)
    normed_two, cot_all = lax.optimization_barrier((normed_two, cot_all))

    rows_out = gathered_seq(normed_two, 4).reshape(-1, width)
    gate_part = mm(rows_out, mlp_gate)
    up_part = mm(rows_out, mlp_up)
    hidden = (jax.nn.silu(gate_part) * up_part).astype(bf16)
    cot_f = out_cot.astype(f32)
    d_hidden = mm_nt(cot_all, mlp_down)
    d_gate_mlp = (d_hidden * up_part * silu_slope(gate_part)).astype(bf16)
    d_up_mlp = (d_hidden * jax.nn.silu(gate_part)).astype(bf16)
    d_rows = (mm_nt(d_gate_mlp, mlp_gate) + mm_nt(d_up_mlp, mlp_up)).astype(bf16)
    d_normed_two = scattered_seq(d_rows, 5)
    hidden, d_normed_two = lax.optimization_barrier((hidden, d_normed_two))
    mlp_out = scattered(mm(hidden, mlp_down), "seq")
    output = (middle + mlp_out).astype(bf16)
    gain_two_part = jnp.sum(d_normed_two * hat_two, 0)
    e_two = d_normed_two * gain_second
    d_middle = cot_f + scale_two * (
        e_two - hat_two * jnp.mean(e_two * hat_two, axis=-1, keepdims=True)
    )
    d_mix_all = gathered_head(d_middle.astype(bf16), 6)
    d_branch = mm_nt(d_mix_all, out_flat)
    d_core, d_gate_low, gain_out_part, local_grads, grad_end = run_local_backward(
        d_branch, core, gate_pre, gain_head, reach, turn
    )
    grad_ends = gathered_seq(grad_end.reshape(-1, DV), 7).reshape(-1, heads, DK, DV)
    grad_out_w = mm_tn(branch, d_mix_all)
    grad_out_s = scattered(grad_out_w, "seq", 1).reshape(heads, DV, -1)
    d_gate_side = swapped(d_gate_low)
    d_mixed, d_tail, d_lead, grad_conv = run_finish_backward(
        ends,
        grad_ends,
        mixed_in,
        tail_in,
        taps,
        columns,
        run_rows,
        solve,
        score,
        fresh,
        states,
        d_core,
        local_grads,
    )
    from_next = passed_along(d_lead[:lead_rows], "seq", -1)
    d_tail = d_tail.at[8 - lead_rows :].add(from_next).astype(bf16)
    d_mixed = lax.dynamic_update_slice(d_mixed, d_tail, (span_rows - 8, 0))
    d_normed_part = mm_nt(d_mixed, qkv_flat) + mm_nt(d_gate_low, gate_flat)
    gain_one_part = jnp.sum(d_normed_part * normed_first.astype(f32), 0) / gain_first
    grad_qkv = mm_tn(normed_first, d_mixed).astype(bf16)
    grad_gate = (
        mm_tn(side_columns(normed_first, side, slice_rows), d_gate_low)
        + mm_tn(normed_side, d_gate_side)
    ).astype(bf16)
    grad_mgate = mm_tn(d_gate_mlp, rows_out).astype(bf16)
    grad_mup = mm_tn(d_up_mlp, rows_out).astype(bf16)
    grad_down = mm_tn(hidden, cot_all).astype(bf16)

    gains = jnp.concatenate([gain_one_part, gain_two_part, gain_out_part.reshape(-1)])
    gain_rows = -(-gains.shape[0] // 1024) * 8
    gains = jnp.pad(gains, (0, gain_rows * 128 - gains.shape[0])).reshape(gain_rows, 128)
    small = jnp.concatenate([gains, grad_conv.reshape(-1, 128)])
    grad_qkv_s, grad_gate_s, d_normed_one, small_all, (grad_mgate_t, grad_mup_t, grad_down_h) = (
        scattered_last(
            grad_qkv,
            grad_gate,
            d_normed_part.astype(bf16),
            [grad_mgate, grad_mup, grad_down],
            small,
            gain_rows,
            8,
        )
    )
    e_one = d_normed_one * gain_first
    d_input = (
        d_middle + scale_own * (e_one - hat_own * jnp.mean(e_one * hat_own, axis=-1, keepdims=True))
    ).astype(bf16)

    small_sum = jnp.sum(small_all, axis=0)
    gains = small_sum[:gain_rows].reshape(-1)

    def own_slice(begin, length):
        length = length // (seq_count * head_count)
        return lax.dynamic_slice(
            gains, (begin + (head_at * seq_count + seq_at) * length,), (length,)
        )

    grad_conv_s = lax.dynamic_slice_in_dim(
        small_sum[gain_rows:].reshape(-1, heads, inner),
        seq_at * (inner // seq_count),
        inner // seq_count,
        2,
    )
    return (
        output,
        d_input,
        own_slice(0, width),
        grad_qkv_s.astype(f32).reshape(-1, heads, inner),
        grad_conv_s,
        grad_gate_s.astype(f32).reshape(-1, heads, DV),
        own_slice(2 * width, DV),
        grad_out_s,
        own_slice(width, width),
        grad_mgate_t.astype(f32).T,
        grad_mup_t.astype(f32).T,
        grad_down_h.astype(f32),
    )


def solution(mesh):
    in_specs = (
        P(("seq", "head"), None),
        P(("seq", "head"), None),
        P(),
        P(None, "head", None),
        P(None, "head", None),
        P(None, "head", None),
        P(),
        P("head", None, None),
        P(),
        P(None, "seq"),
        P(None, "seq"),
        P("seq", None),
        P("seq", "head"),
        P("seq", "head"),
    )
    out_specs = (
        P(("seq", "head"), None),
        P(("seq", "head"), None),
        P(("head", "seq")),
        P("seq", "head", None),
        P(None, "head", "seq"),
        P("seq", "head", None),
        P(("head", "seq")),
        P("head", None, "seq"),
        P(("head", "seq")),
        P("head", "seq"),
        P("head", "seq"),
        P("seq", "head"),
    )
    return jax.shard_map(
        on_device, mesh=mesh, in_specs=in_specs, out_specs=out_specs, check_vma=False
    )
```

```python
import functools
import math

import jax
import jax.numpy as jnp
from jax import lax
from jax.experimental import pallas as pl
from jax.experimental.pallas import tpu as pltpu
from jax.sharding import PartitionSpec as P

DK = 128
DV = 256
STRETCH = 64
GROUP = 4 * STRETCH
INNER = 2 * DK + DV
BETA, GAMMA, BETA_GAMMA, TAIL, LAST, RUN = range(6)

epsilon = 1e-06
bf16 = jnp.bfloat16
f32 = jnp.float32
VMEM_BYTES = 56 * 2**20


def passed_along(value, axis, steps):
    count = lax.axis_size(axis)
    first, last = (max(0, -steps), min(count, count - steps))
    return lax.ppermute(value, axis, [(source, source + steps) for source in range(first, last)])


def rms_scale(tensor):
    return lax.rsqrt(jnp.mean(tensor * tensor, axis=-1, keepdims=True) + epsilon)


def log_rates(decay_code, total_len):
    code_level = decay_code.astype(f32) / 1023.0
    smooth = -jnp.exp(-code_level * math.log(total_len / 32.0)) / 32.0
    return jnp.where(decay_code == 1024, -0.25, smooth)


def token_columns(decay_code, beta_code, total_len):
    rows, heads = decay_code.shape
    rates = log_rates(decay_code, total_len)
    run = jnp.einsum(
        "ij,bjh->bih",
        jnp.tril(jnp.ones((STRETCH, STRETCH), f32)),
        rates.reshape(rows // STRETCH, STRETCH, heads),
        precision=lax.Precision.HIGHEST,
    )
    last = jnp.broadcast_to(run[:, -1:], run.shape).reshape(rows, heads)
    run = run.reshape(rows, heads)
    beta = 0.5 + beta_code.astype(f32) / 512.0
    gamma = jnp.exp(run)
    columns = jnp.concatenate(
        [beta, gamma, beta * gamma, jnp.exp(last - run), jnp.exp(last), run], axis=1
    )
    columns = jnp.pad(columns, ((0, 0), (0, 128 - columns.shape[1])))
    run_rows = jnp.pad(run.T, ((0, 8 - heads % 8), (0, 0)))
    return columns, run_rows


def mm(left, right):
    return jnp.dot(left, right, preferred_element_type=f32)


def mm_nt(left, right):
    return lax.dot_general(left, right, (((1,), (1,)), ((), ())), preferred_element_type=f32)


def mm_tn(left, right):
    return lax.dot_general(left, right, (((0,), (0,)), ((), ())), preferred_element_type=f32)


def column(columns_ref, kind, head, heads):
    block = columns_ref[...]
    lanes = lax.broadcasted_iota(jnp.int32, block.shape, 1)
    return jnp.sum(jnp.where(lanes == kind * heads + head, block, 0.0), axis=1, keepdims=True)


def square_ids():
    return (
        lax.broadcasted_iota(jnp.int32, (GROUP, GROUP), 0),
        lax.broadcasted_iota(jnp.int32, (GROUP, GROUP), 1),
    )


def convolved(padded_ref, tail_ref, mixed_ref, taps_ref):
    rows = mixed_ref.shape[0]
    count = taps_ref.shape[0]
    padded_ref[0:8, :] = tail_ref[...]
    padded_ref[8 : 8 + rows, :] = mixed_ref[...].astype(f32)
    taps = taps_ref[...].astype(f32)
    start = 9 - count
    total = taps[0:1] * padded_ref[start : start + rows, :]
    for tap in range(1, count):
        total += taps[tap : tap + 1] * padded_ref[start + tap : start + tap + rows, :]
    return total


def chunk_masks_stack(transposed):
    lanes = lax.broadcasted_iota(jnp.int32, transposed.shape, 1) // STRETCH
    parts = [jnp.where(lanes == part, transposed, 0.0) for part in range(GROUP // STRETCH)]
    return jnp.concatenate(parts, axis=0).astype(bf16)


def local_forward(
    mixed_ref,
    tail_ref,
    taps_ref,
    columns_ref,
    run_rows_ref,
    solve_ref,
    score_ref,
    fresh_ref,
    reach_ref,
    inner_ref,
    turn_ref,
    local_ref,
    end_ref,
    padded,
    turn_t,
    offsets,
):
    head = pl.program_id(0)
    heads = pl.num_programs(0)
    rows = mixed_ref.shape[0]
    per_group = GROUP // STRETCH
    stretches = rows // STRETCH
    total = convolved(padded, tail_ref, mixed_ref, taps_ref)
    activated = total * jax.nn.sigmoid(total)
    raw_q, raw_k = activated[:, :DK], activated[:, DK : 2 * DK]
    queries = raw_q * (
        lax.rsqrt(jnp.sum(raw_q * raw_q, axis=1, keepdims=True) + epsilon) * DK ** (-0.5)
    )
    keys = raw_k * lax.rsqrt(jnp.sum(raw_k * raw_k, axis=1, keepdims=True) + epsilon)
    values = activated[:, 2 * DK :]
    beta = column(columns_ref, BETA, head, heads)
    gamma = column(columns_ref, GAMMA, head, heads)
    beta_gamma = column(columns_ref, BETA_GAMMA, head, heads)
    tail_decay = column(columns_ref, TAIL, head, heads)
    last = column(columns_ref, LAST, head, heads)
    run = column(columns_ref, RUN, head, heads)
    row_id, col_id = square_ids()
    same = row_id // STRETCH == col_id // STRETCH
    causal = same & (row_id >= col_id)
    diagonal = row_id == col_id
    eye = jnp.where(
        lax.broadcasted_iota(jnp.int32, (DK, DK), 0) == lax.broadcasted_iota(jnp.int32, (DK, DK), 1),
        1.0,
        0.0,
    )
    for group in range(rows // GROUP):
        span = slice(group * GROUP, (group + 1) * GROUP)
        key_b = keys[span].astype(bf16)
        query_b = queries[span].astype(bf16)
        gaps = run[span] - run_rows_ref[pl.ds(head, 1), span]
        within = jnp.exp(jnp.where(causal, gaps, -1e30))
        lower = jnp.where(diagonal, 0.0, beta[span] * within * mm_nt(key_b, key_b))
        solve = jnp.where(diagonal, 1.0, jnp.where(row_id // 2 == col_id // 2, -lower, 0.0))
        size = 2
        while size < STRETCH:
            crossing = (row_id // (2 * size) == col_id // (2 * size)) & (
                row_id // size != col_id // size
            )
            solve_b = solve.astype(bf16)
            half = mm(solve_b, jnp.where(crossing, lower, 0.0).astype(bf16))
            solve = solve - mm(half.astype(bf16), solve_b)
            size *= 2
        solve_b = solve.astype(bf16)
        right = jnp.concatenate([beta[span] * values[span], beta_gamma[span] * keys[span]], axis=1)
        fresh_b = mm(solve_b, right.astype(bf16)).astype(bf16)
        score_b = (within * mm_nt(query_b, key_b)).astype(bf16)
        scored = mm(score_b, fresh_b)
        solve_ref[group] = solve_b
        score_ref[group] = score_b
        fresh_ref[span, :] = fresh_b
        inner_ref[span, :] = scored[:, :DV]
        reach_ref[span, :] = (gamma[span] * queries[span] - scored[:, DV:]).astype(bf16)
        tail_keys = (tail_decay[span] * keys[span]).T
        moved = mm(chunk_masks_stack(tail_keys), fresh_b)
        for part in range(per_group):
            at = group * per_group + part
            block = moved[part * DK : (part + 1) * DK]
            stay = last[at * STRETCH : at * STRETCH + 1]
            turned = stay * eye - block[:, DV:]
            turn_t[head, at] = turned.astype(bf16)
            turn_ref[at] = turned.T.astype(bf16)
            offsets[head, at] = block[:, :DV]

    @pl.when(head == heads - 1)
    def _():
        states = [
            jnp.concatenate([jnp.zeros((DK, DV), f32), eye], axis=1)
            for _ in range(local_ref.shape[0])
        ]
        for at in range(stretches):
            for h in range(len(states)):
                state_b = states[h].astype(bf16)
                local_ref[h, at] = state_b
                moved = mm(turn_t[h, at], state_b)
                states[h] = jnp.concatenate(
                    [moved[:, :DV] + offsets[h, at], moved[:, DV:]], axis=1
                )
        for h in range(len(states)):
            end_ref[h] = states[h].astype(bf16)


def finish_forward(
    ends_ref, local_ref, reach_ref, inner_ref, gate_ref, gain_ref, state_ref, core_ref, branch_ref, start
):
    head = pl.program_id(0)
    heads, stretches = start.shape[0], local_ref.shape[0]

    @pl.when(head == 0)
    def _():
        start[...] = jnp.zeros_like(start)

        def one(source, carry):
            for h in range(heads):
                start[h] = (
                    mm(ends_ref[source, h, :, DV:], start[h].astype(bf16))
                    + ends_ref[source, h, :, :DV].astype(f32)
                )
            return carry

        lax.fori_loop(0, lax.axis_index("seq"), one, 0)

    start_b = start[head].astype(bf16)
    cores = []
    for at in range(stretches):
        state_b = (
            local_ref[at, :, :DV].astype(f32) + mm(local_ref[at, :, DV:], start_b)
        ).astype(bf16)
        state_ref[at] = state_b
        span = slice(at * STRETCH, (at + 1) * STRETCH)
        cores.append(inner_ref[span, :] + mm(reach_ref[span, :], state_b))
    core = jnp.concatenate(cores, axis=0)
    core_ref[...] = core
    gate = gate_ref[...]
    branch = core * rms_scale(core) * gain_ref[...].astype(f32) * (gate * jax.nn.sigmoid(gate))
    branch_ref[...] = branch.astype(bf16)


def local_backward(
    d_branch_ref,
    core_ref,
    gate_ref,
    gain_ref,
    reach_ref,
    turn_ref,
    d_core_ref,
    d_gate_ref,
    gain_part_ref,
    local_ref,
    end_ref,
    pulls,
):
    head = pl.program_id(0)
    heads = pl.num_programs(0)
    rows = core_ref.shape[0]
    per_group = GROUP // STRETCH
    stretches = rows // STRETCH
    core = core_ref[...]
    gate = gate_ref[...]
    gain = gain_ref[...].astype(f32)
    d_branch = d_branch_ref[...]
    scale = rms_scale(core)
    nhat = core * scale
    sig = jax.nn.sigmoid(gate)
    gated = d_branch * (gate * sig)

    @pl.when(head == 0)
    def _():
        gain_part_ref[...] = jnp.zeros_like(gain_part_ref)

    gain_part_ref[...] += jnp.sum(gated * nhat, axis=0, keepdims=True)
    f = gated * gain
    d_core = scale * (f - nhat * jnp.mean(f * nhat, axis=1, keepdims=True))
    d_gate_ref[...] = (d_branch * nhat * gain * sig * (1.0 + gate * (1.0 - sig))).astype(bf16)
    d_core_b = d_core.astype(bf16)
    d_core_ref[...] = d_core_b
    for group in range(rows // GROUP):
        span = slice(group * GROUP, (group + 1) * GROUP)
        pulled = mm(chunk_masks_stack(reach_ref[span, :].astype(f32).T), d_core_b[span])
        for part in range(per_group):
            pulls[head, group * per_group + part] = pulled[part * DK : (part + 1) * DK]

    @pl.when(head == heads - 1)
    def _():
        eye = jnp.where(
            lax.broadcasted_iota(jnp.int32, (DK, DK), 0)
            == lax.broadcasted_iota(jnp.int32, (DK, DK), 1),
            1.0,
            0.0,
        )
        grads = [
            jnp.concatenate([jnp.zeros((DK, DV), f32), eye], axis=1)
            for _ in range(local_ref.shape[0])
        ]
        for at in reversed(range(stretches)):
            for h in range(len(grads)):
                grad_b = grads[h].astype(bf16)
                local_ref[h, at] = grad_b
                moved = mm(turn_ref[h, at], grad_b)
                grads[h] = jnp.concatenate([moved[:, :DV] + pulls[h, at], moved[:, DV:]], axis=1)
        for h in range(len(grads)):
            end_ref[h] = grads[h][:, :DV].astype(bf16)


def finish_backward(
    ends_ref,
    grad_ends_ref,
    mixed_ref,
    tail_ref,
    taps_ref,
    columns_ref,
    run_rows_ref,
    solve_ref,
    score_ref,
    fresh_ref,
    state_ref,
    d_core_ref,
    local_ref,
    d_mixed_ref,
    tail_out_ref,
    lead_ref,
    grad_taps_ref,
    padded,
    spread,
    end,
):
    head = pl.program_id(0)
    heads = pl.num_programs(0)
    rows = mixed_ref.shape[0]
    per_group = GROUP // STRETCH

    @pl.when(head == 0)
    def _():
        end[...] = jnp.zeros_like(end)
        count = ends_ref.shape[0]

        def one(turn, carry):
            source = count - 1 - turn
            for h in range(end.shape[0]):
                end[h] = (
                    mm_tn(ends_ref[source, h, :, DV:], end[h].astype(bf16))
                    + grad_ends_ref[source, h].astype(f32)
                )
            return carry

        lax.fori_loop(0, count - 1 - lax.axis_index("seq"), one, 0)

    end_b = end[head].astype(bf16)
    total = convolved(padded, tail_ref, mixed_ref, taps_ref)
    sig = jax.nn.sigmoid(total)
    activated = total * sig
    raw_q, raw_k = activated[:, :DK], activated[:, DK : 2 * DK]
    scale_q = lax.rsqrt(jnp.sum(raw_q * raw_q, axis=1, keepdims=True) + epsilon)
    scale_k = lax.rsqrt(jnp.sum(raw_k * raw_k, axis=1, keepdims=True) + epsilon)
    unit_q = raw_q * scale_q
    keys = raw_k * scale_k
    beta = column(columns_ref, BETA, head, heads)
    gamma = column(columns_ref, GAMMA, head, heads)
    beta_gamma = column(columns_ref, BETA_GAMMA, head, heads)
    tail_decay = column(columns_ref, TAIL, head, heads)
    run = column(columns_ref, RUN, head, heads)
    row_id, col_id = square_ids()
    causal = (row_id // STRETCH == col_id // STRETCH) & (row_id >= col_id)
    diagonal = row_id == col_id
    d_queries, d_keys, d_values = [], [], []
    for group in range(rows // GROUP):
        span = slice(group * GROUP, (group + 1) * GROUP)
        key_b = keys[span].astype(bf16)
        query_b = (unit_q[span] * DK ** (-0.5)).astype(bf16)
        tail_keys = (tail_decay[span] * keys[span]).astype(bf16)
        d_core_b = d_core_ref[span, :]
        grad_bs, from_grad, fresh_parts, from_state = [], [], [], []
        for part in range(per_group):
            at = group * per_group + part
            own = slice(part * STRETCH, (part + 1) * STRETCH)
            rows_at = slice(at * STRETCH, (at + 1) * STRETCH)
            grad_b = (
                local_ref[at, :, :DV].astype(f32) + mm(local_ref[at, :, DV:], end_b)
            ).astype(bf16)
            grad_bs.append(grad_b)
            from_grad.append(mm(tail_keys[own], grad_b))
            fresh_parts.append(mm(fresh_ref[rows_at, DV:], state_ref[at]))
            from_state.append(mm_nt(d_core_b[own], state_ref[at]))
        d_fresh = mm_tn(score_ref[group], d_core_b) + jnp.concatenate(from_grad, axis=0)
        d_right = mm_tn(solve_ref[group], d_fresh.astype(bf16))
        d_right_b = d_right.astype(bf16)
        fresh = fresh_ref[span, :DV].astype(f32) - jnp.concatenate(fresh_parts, axis=0)
        fresh_b = fresh.astype(bf16)
        gaps = run[span] - run_rows_ref[pl.ds(head, 1), span]
        within = jnp.exp(jnp.where(causal, gaps, -1e30))
        d_score = (within * mm_nt(d_core_b, fresh_b)).astype(bf16)
        d_lower = jnp.where(
            diagonal, 0.0, -beta[span] * within * mm_nt(d_right_b, fresh_b)
        ).astype(bf16)
        state_keys, grad_keys = [], []
        for part in range(per_group):
            at = group * per_group + part
            own = slice(part * STRETCH, (part + 1) * STRETCH)
            state_keys.append(mm_nt(d_right_b[own], state_ref[at]))
            grad_keys.append(mm_nt(fresh_b[own], grad_bs[part]))
        d_queries.append(gamma[span] * jnp.concatenate(from_state, axis=0) + mm(d_score, key_b))
        d_keys.append(
            mm_tn(d_score, query_b)
            + mm_tn(d_lower, key_b)
            + mm(d_lower, key_b)
            + tail_decay[span] * jnp.concatenate(grad_keys, axis=0)
            - beta_gamma[span] * jnp.concatenate(state_keys, axis=0)
        )
        d_values.append(beta[span] * d_right)
    g_q = jnp.concatenate(d_queries, axis=0) * DK ** (-0.5)
    g_k = jnp.concatenate(d_keys, axis=0)
    d_act = jnp.concatenate(
        [
            scale_q * (g_q - unit_q * jnp.sum(unit_q * g_q, axis=1, keepdims=True)),
            scale_k * (g_k - keys * jnp.sum(keys * g_k, axis=1, keepdims=True)),
            jnp.concatenate(d_values, axis=0),
        ],
        axis=1,
    )
    d_conv = d_act * (sig * (1.0 + total * (1.0 - sig)))
    taps = taps_ref[...].astype(f32)
    count = taps_ref.shape[0]
    start = 9 - count
    grad_taps_ref[...] = jnp.concatenate(
        [
            jnp.sum(padded[start + tap : start + tap + rows, :] * d_conv, axis=0, keepdims=True)
            for tap in range(count)
        ],
        axis=0,
    )
    spread[0:8, :] = jnp.zeros((8, d_conv.shape[1]), f32)
    spread[8 : 8 + rows, :] = d_conv
    spread[8 + rows : 16 + rows, :] = jnp.zeros((8, d_conv.shape[1]), f32)
    lead = taps[0:1] * spread[8:16, :]
    d_mixed = taps[0:1] * spread[7 + count : 7 + count + rows, :]
    for tap in range(1, count):
        lead += taps[tap : tap + 1] * spread[8 - tap : 16 - tap, :]
        begin = 7 + count - tap
        d_mixed += taps[tap : tap + 1] * spread[begin : begin + rows, :]
    lead_ref[...] = lead
    d_mixed_ref[...] = d_mixed.astype(bf16)
    tail_out_ref[...] = d_mixed[rows - 8 :]


def whole(shape):
    return pl.BlockSpec(shape, lambda h: (0,) * len(shape))


def by_head(shape):
    return pl.BlockSpec((None,) + shape, lambda h: (h,) + (0,) * len(shape))


def by_columns(rows, width):
    return pl.BlockSpec((rows, width), lambda h: (0, h))


def kernel_call(body, heads, ins, outs, out_shapes, scratch, flops, moved):
    return pl.pallas_call(
        body,
        grid=(heads,),
        in_specs=ins,
        out_specs=outs,
        out_shape=out_shapes,
        scratch_shapes=scratch,
        compiler_params=pltpu.CompilerParams(
            dimension_semantics=("arbitrary",), vmem_limit_bytes=VMEM_BYTES
        ),
        cost_estimate=pl.CostEstimate(flops=flops, bytes_accessed=moved, transcendentals=0),
    )


def shaped(shape, kind):
    return jax.ShapeDtypeStruct(shape, kind)


def run_local_forward(mixed, tail, taps, columns, run_rows, heads):
    rows = mixed.shape[0]
    count = taps.shape[0]
    groups, stretches = rows // GROUP, rows // STRETCH
    return kernel_call(
        local_forward,
        heads,
        [
            by_columns(rows, INNER),
            by_columns(8, INNER),
            by_columns(count, INNER),
            whole(columns.shape),
            whole(run_rows.shape),
        ],
        [
            by_head((groups, GROUP, GROUP)),
            by_head((groups, GROUP, GROUP)),
            by_head((rows, DV + DK)),
            by_head((rows, DK)),
            by_columns(rows, DV),
            by_head((stretches, DK, DK)),
            whole((heads, stretches, DK, DV + DK)),
            whole((heads, DK, DV + DK)),
        ],
        [
            shaped((heads, groups, GROUP, GROUP), bf16),
            shaped((heads, groups, GROUP, GROUP), bf16),
            shaped((heads, rows, DV + DK), bf16),
            shaped((heads, rows, DK), bf16),
            shaped((rows, heads * DV), f32),
            shaped((heads, stretches, DK, DK), bf16),
            shaped((heads, stretches, DK, DV + DK), bf16),
            shaped((heads, DK, DV + DK), bf16),
        ],
        [
            pltpu.VMEM((rows + 8, INNER), f32),
            pltpu.VMEM((heads, stretches, DK, DK), bf16),
            pltpu.VMEM((heads, stretches, DK, DV), f32),
        ],
        12_000_000_000,
        20_000_000,
    )(mixed, tail, taps, columns, run_rows)


def run_finish_forward(ends, local, reach, inner, gate_pre, gain):
    heads, stretches = local.shape[:2]
    rows = inner.shape[0]
    return kernel_call(
        finish_forward,
        heads,
        [
            whole(ends.shape),
            by_head((stretches, DK, DV + DK)),
            by_head((rows, DK)),
            by_columns(rows, DV),
            by_columns(rows, DV),
            whole(gain.shape),
        ],
        [by_head((stretches, DK, DV)), by_columns(rows, DV), by_columns(rows, DV)],
        [
            shaped((heads, stretches, DK, DV), bf16),
            shaped((rows, heads * DV), f32),
            shaped((rows, heads * DV), bf16),
        ],
        [pltpu.VMEM((heads, DK, DV), f32)],
        3_000_000_000,
        20_000_000,
    )(ends, local, reach, inner, gate_pre, gain)


def run_local_backward(d_branch, core, gate_pre, gain, reach, turn):
    heads, stretches = turn.shape[:2]
    rows = core.shape[0]
    return kernel_call(
        local_backward,
        heads,
        [
            by_columns(rows, DV),
            by_columns(rows, DV),
            by_columns(rows, DV),
            whole(gain.shape),
            by_head((rows, DK)),
            whole(turn.shape),
        ],
        [
            by_columns(rows, DV),
            by_columns(rows, DV),
            whole((1, DV)),
            whole((heads, stretches, DK, DV + DK)),
            whole((heads, DK, DV)),
        ],
        [
            shaped((rows, heads * DV), bf16),
            shaped((rows, heads * DV), bf16),
            shaped((1, DV), f32),
            shaped((heads, stretches, DK, DV + DK), bf16),
            shaped((heads, DK, DV), bf16),
        ],
        [pltpu.VMEM((heads, stretches, DK, DV), f32)],
        4_000_000_000,
        20_000_000,
    )(d_branch, core, gate_pre, gain, reach, turn)


def run_finish_backward(
    ends, grad_ends, mixed, tail, taps, columns, run_rows, solve, score, fresh, states, d_core, local
):
    heads, stretches = local.shape[:2]
    rows = mixed.shape[0]
    groups = rows // GROUP
    count = taps.shape[0]
    return kernel_call(
        finish_backward,
        heads,
        [
            whole(ends.shape),
            whole(grad_ends.shape),
            by_columns(rows, INNER),
            by_columns(8, INNER),
            by_columns(count, INNER),
            whole(columns.shape),
            whole(run_rows.shape),
            by_head((groups, GROUP, GROUP)),
            by_head((groups, GROUP, GROUP)),
            by_head((rows, DV + DK)),
            by_head((stretches, DK, DV)),
            by_columns(rows, DV),
            by_head((stretches, DK, DV + DK)),
        ],
        [
            by_columns(rows, INNER),
            by_columns(8, INNER),
            by_columns(8, INNER),
            by_columns(count, INNER),
        ],
        [
            shaped((rows, heads * INNER), bf16),
            shaped((8, heads * INNER), f32),
            shaped((8, heads * INNER), f32),
            shaped((count, heads * INNER), f32),
        ],
        [
            pltpu.VMEM((rows + 8, INNER), f32),
            pltpu.VMEM((rows + 16, INNER), f32),
            pltpu.VMEM((heads, DK, DV), f32),
        ],
        12_000_000_000,
        20_000_000,
    )(ends, grad_ends, mixed, tail, taps, columns, run_rows, solve, score, fresh, states, d_core, local)


MESH = pl.DeviceIdType.MESH
SIDE = 2


def remote(source, target, send, arrive, device):
    return pltpu.make_async_remote_copy(
        src_ref=source,
        dst_ref=target,
        send_sem=send,
        recv_sem=arrive,
        device_id=device,
        device_id_type=MESH,
    )


def greet(partners):
    barrier = pltpu.get_barrier_semaphore()
    expected = 0
    for device, there in partners:
        if there is None:
            pl.semaphore_signal(barrier, inc=1, device_id=device, device_id_type=MESH)
            expected = expected + 1
        else:

            @pl.when(there)
            def _(device=device):
                pl.semaphore_signal(barrier, inc=1, device_id=device, device_id_type=MESH)

            expected = expected + there.astype(jnp.int32)
    pl.semaphore_wait(barrier, expected)


def head_places():
    head, seq = lax.axis_index("head"), lax.axis_index("seq")
    core = lax.rem(head, 2)
    sibling = head + 1 - 2 * core
    across = lax.rem(head + 2, 4)
    return head, seq, sibling, across


def head_partners():
    head, seq, sibling, across = head_places()
    return [((sibling, seq), None), ((across, seq), None)]


def seq_places():
    head, seq = lax.axis_index("head"), lax.axis_index("seq")
    return head, seq // SIDE, lax.rem(seq, SIDE)


def seq_partners(count):
    head, line, side = seq_places()
    return [
        ((head, line * SIDE + 1 - side), None),
        ((head, (line + 1) * SIDE + side), line < count - 1),
        ((head, (line - 1) * SIDE + side), line > 0),
    ]


def run_together(steps):
    steps = list(steps)
    while steps:
        alive = []
        for step in steps:
            try:
                next(step)
                alive.append(step)
            except StopIteration:
                pass
        steps = alive


def gather_head(own_ref, out_ref, local, send, arrive, pieces):
    head, seq, sibling, across = head_places()
    far = lax.rem(sibling + 2, 4)
    rows = own_ref.shape[0] // pieces
    keep = pltpu.make_async_copy(own_ref, out_ref.at[head], local.at[0])
    keep.start()

    def part(ref, piece):
        return ref.at[pl.ds(piece * rows, rows)]

    outgoing = []
    for piece in range(pieces):
        outgoing.append(
            remote(
                part(own_ref, piece),
                part(out_ref.at[head], piece),
                send.at[0, piece],
                arrive.at[0, piece],
                (across, seq),
            )
        )
    for piece in range(pieces):
        outgoing.append(
            remote(
                part(own_ref, piece),
                part(out_ref.at[head], piece),
                send.at[1, piece],
                arrive.at[1, piece],
                (sibling, seq),
            )
        )
    for copy in outgoing:
        copy.start()
    yield
    forwards = []
    for piece in range(pieces):
        outgoing[piece].wait_recv()
        forward = remote(
            part(out_ref.at[across], piece),
            part(out_ref.at[across], piece),
            send.at[2, piece],
            arrive.at[2, piece],
            (sibling, seq),
        )
        forward.start()
        forwards.append(forward)
        yield
    for copy in outgoing[pieces:] + forwards:
        copy.wait_recv()
    for copy in outgoing + forwards:
        copy.wait_send()
    keep.wait()


def scatter_head(source_at, out_ref, own, crossed, passed, local, send, arrive, pause=0):
    head, seq, sibling, across = head_places()
    far = lax.rem(sibling + 2, 4)
    loads = [
        pltpu.make_async_copy(source_at(target), own.at[slot], local.at[slot])
        for slot, target in enumerate((across, head))
    ]
    copies = [
        remote(source_at(target), crossed.at[slot], send.at[slot], arrive.at[slot], (sibling, seq))
        for slot, target in enumerate((far, sibling))
    ]
    for slot in range(2):
        copies[slot].start()
        loads[slot].start()
    yield
    loads[0].wait()
    copies[0].wait_recv()
    own[0] = (own[0].astype(f32) + crossed[0].astype(f32)).astype(own.dtype)
    onward = remote(own.at[0], passed, send.at[2], arrive.at[2], (across, seq))
    onward.start()
    for _ in range(1 + pause):
        yield
    loads[1].wait()
    copies[1].wait_recv()
    onward.wait_recv()
    total = own[1].astype(f32) + crossed[1].astype(f32) + passed[...].astype(f32)
    out_ref[...] = total.astype(out_ref.dtype)
    onward.wait_send()
    for copy in copies:
        copy.wait_send()


def gather_seq(own_ref, out_ref, local, side_send, side_arrive, line_send, line_arrive, count):
    head, line, side = seq_places()
    me = line * SIDE + side
    beside = (head, line * SIDE + 1 - side)
    ways = ((1, line < count - 1), (-1, line > 0))
    keep = pltpu.make_async_copy(own_ref, out_ref.at[me], local.at[0])
    keep.start()

    def along(source, block, way, step):
        slot = step if way > 0 else count + step
        return remote(
            source,
            out_ref.at[block],
            line_send.at[slot],
            line_arrive.at[slot],
            (head, (line + way) * SIDE + side),
        )

    def over(source, block, slot):
        return remote(source, out_ref.at[block], side_send.at[slot], side_arrive.at[slot], beside)

    for way, onward in ways:

        @pl.when(onward)
        def _(way=way):
            along(own_ref, me, way, 0).start()

    over(own_ref, me, 0).start()
    yield
    for step in range(1, count):
        for way, onward in ways:
            block = me - way * step * SIDE
            arrives = line >= step if way > 0 else line + step < count

            @pl.when(arrives)
            def _(way=way, onward=onward, block=block, step=step):
                landed = out_ref.at[block]
                slot = step if way > 0 else count + step
                remote(
                    landed, landed, line_send.at[slot - 1], line_arrive.at[slot - 1], beside
                ).wait_recv()

                @pl.when(onward)
                def _():
                    along(landed, block, way, step).start()

                over(landed, block, slot).start()

        yield
    over(own_ref, me, 0).wait()
    for way, onward in ways:

        @pl.when(onward)
        def _(way=way):
            along(own_ref, me, way, 0).wait_send()

    for step in range(1, count):
        for way, onward in ways:
            block = me - way * step * SIDE
            arrives = line >= step if way > 0 else line + step < count

            @pl.when(arrives)
            def _(way=way, onward=onward, block=block, step=step):
                landed = out_ref.at[block]
                slot = step if way > 0 else count + step
                over(landed, block, slot).wait()

                @pl.when(onward)
                def _():
                    along(landed, block, way, step).wait_send()

    keep.wait()


def scatter_seq(source_at, out_at, own, crossed, risen, fallen, local, sends, arrivals, count):
    head, line, side = seq_places()
    beside = (head, line * SIDE + 1 - side)
    pieces = own.shape[0]

    def targets(distance):
        if distance == 0:
            return [(line, None, 0)]
        return [
            (line - distance, line >= distance, -1),
            (line + distance, line + distance < count, 1),
        ]

    def load(piece, target):
        return pltpu.make_async_copy(
            source_at(target, side, piece), own.at[piece, target], local.at[piece, target]
        )

    def cross(piece, target):
        return remote(
            source_at(target, 1 - side, piece),
            crossed.at[piece, target],
            sends.at[0, piece, target],
            arrivals.at[0, piece, target],
            beside,
        )

    def onward(piece, target, way, arriving=False):
        landing = risen if way > 0 else fallen
        return remote(
            own.at[piece, target],
            landing.at[piece, target],
            sends.at[1, piece, target],
            arrivals.at[1 if way > 0 else 2, piece, target],
            beside if arriving else (head, (line + way) * SIDE + side),
        )

    def guarded(there, body):
        if there is None:
            body()
        else:
            pl.when(there)(body)

    def here(piece, target):
        load(piece, target).wait()
        total = own[piece, target].astype(f32)
        if crossed is not None:
            cross(piece, target).wait_recv()
            total += crossed[piece, target].astype(f32)
        return total

    def arrived(piece, target, way):
        landing = risen if way > 0 else fallen
        onward(piece, target, way, True).wait_recv()
        return landing[piece, target].astype(f32)

    for piece in range(pieces):
        for distance in range(count - 1, -1, -1):
            for target, there, _ in targets(distance):

                def begin(piece=piece, target=target):
                    if crossed is not None:
                        cross(piece, target).start()
                    load(piece, target).start()

                guarded(there, begin)
    yield
    for piece in range(pieces):
        for distance in range(count - 1, 0, -1):
            for target, there, way in targets(distance):
                first = line == count - 1 if way < 0 else line == 0

                @pl.when(jnp.logical_and(there, first))
                def _(piece=piece, target=target, way=way):
                    own[piece, target] = here(piece, target).astype(own.dtype)
                    onward(piece, target, way).start()

                @pl.when(jnp.logical_and(there, jnp.logical_not(first)))
                def _(piece=piece, target=target, way=way):
                    total = here(piece, target) + arrived(piece, target, way)
                    own[piece, target] = total.astype(own.dtype)
                    onward(piece, target, way).start()

            yield
        out = out_at(piece)

        @pl.when(line == 0)
        def _(piece=piece, out=out):
            out[...] = (here(piece, line) + arrived(piece, line, -1)).astype(out.dtype)

        @pl.when(line == count - 1)
        def _(piece=piece, out=out):
            out[...] = (here(piece, line) + arrived(piece, line, 1)).astype(out.dtype)

        @pl.when(jnp.logical_and(line > 0, line < count - 1))
        def _(piece=piece, out=out):
            total = here(piece, line) + arrived(piece, line, -1) + arrived(piece, line, 1)
            out[...] = total.astype(out.dtype)

        yield
    for piece in range(pieces):
        for distance in range(count - 1, -1, -1):
            for target, there, way in targets(distance):

                def finish(piece=piece, target=target, way=way):
                    if crossed is not None:
                        cross(piece, target).wait_send()
                    if way:
                        onward(piece, target, way).wait_send()

                guarded(there, finish)


ANY = pl.BlockSpec(memory_space=pl.ANY)
IN_VMEM = pl.BlockSpec(memory_space=pltpu.VMEM)
DMA = pltpu.SemaphoreType.DMA


def link_call(body, number, ins, outs, shapes, scratch, moved):
    return pl.pallas_call(
        body,
        in_specs=ins,
        out_specs=outs,
        out_shape=shapes,
        scratch_shapes=scratch,
        compiler_params=pltpu.CompilerParams(
            collective_id=number, has_side_effects=True, vmem_limit_bytes=VMEM_BYTES
        ),
        cost_estimate=pl.CostEstimate(flops=0, bytes_accessed=moved // 8, transcendentals=0),
    )


def gathered_head(value, number, pieces=4):
    count = lax.axis_size("head")
    if count != 4:
        return lax.all_gather(value, "head", axis=0, tiled=True)
    rows, width = value.shape

    def body(own_ref, out_ref, local, send, arrive):
        greet(head_partners())
        run_together([gather_head(own_ref, out_ref, local, send, arrive, pieces)])

    out = link_call(
        body,
        number,
        [ANY],
        ANY,
        shaped((count, rows, width), value.dtype),
        [DMA((1,)), DMA((3, pieces)), DMA((3, pieces))],
        60_000_000,
    )(value)
    return out.reshape(count * rows, width)


def gathered_sided(value, half, number, pieces=4, half_pieces=2):
    count = lax.axis_size("head")
    rows, width = value.shape

    def body(own_ref, half_ref, out_ref, beside_ref, landing, *sems):
        head, line, side = seq_places()
        beside = (head, line * SIDE + 1 - side)
        greet(head_partners() + [(beside, None)])

        def half_steps():
            copy = remote(half_ref, landing, sems[6].at[0], sems[6].at[1], beside)
            copy.start()
            yield
            yield
            copy.wait()
            yield from gather_head(landing, beside_ref, *sems[3:6], half_pieces)

        run_together([half_steps(), gather_head(own_ref, out_ref, *sems[:3], pieces)])

    out, beside = link_call(
        body,
        number,
        [ANY, ANY],
        [ANY, ANY],
        [
            shaped((count, rows, width), value.dtype),
            shaped((count, rows, half.shape[1]), value.dtype),
        ],
        [pltpu.VMEM(half.shape, half.dtype)]
        + [DMA((1,)), DMA((3, pieces)), DMA((3, pieces))]
        + [DMA((1,)), DMA((3, half_pieces)), DMA((3, half_pieces))]
        + [DMA((2,))],
        60_000_000,
    )(value, half)
    return out.reshape(count * rows, width), beside.reshape(count * rows, half.shape[1])


def gathered_seq(value, number):
    total = lax.axis_size("seq")
    count = total // SIDE
    rows, width = value.shape
    if total % SIDE or count < 2:
        return lax.all_gather(value, "seq")

    def body(own_ref, out_ref, *sems):
        greet(seq_partners(count))
        run_together([gather_seq(own_ref, out_ref, *sems, count)])

    return link_call(
        body,
        number,
        [ANY],
        ANY,
        shaped((total, rows, width), value.dtype),
        [DMA((1,))] + [DMA((2 * count,)) for _ in range(4)],
        120_000_000,
    )(value)


def head_scratch(rows, width):
    return [
        pltpu.VMEM((2, rows, width), bf16),
        pltpu.VMEM((2, rows, width), bf16),
        pltpu.VMEM((rows, width), bf16),
        DMA((2,)),
        DMA((3,)),
        DMA((3,)),
    ]


def seq_scratch(pieces, count, rows, width):
    return [pltpu.VMEM((pieces, count, rows, width), bf16) for _ in range(4)] + [
        DMA((pieces, count)),
        DMA((2, pieces, count)),
        DMA((3, pieces, count)),
    ]


def scattered_head(value, number, pieces=2):
    count = lax.axis_size("head")
    if count != 4:
        return scattered(value, "head")
    rows, width = value.shape[0] // count, value.shape[1] // pieces

    def body(source, out, *rest):
        greet(head_partners())
        steps = []
        for piece in range(pieces):
            span = pl.ds(piece * width, width)

            def source_at(target, span=span):
                return source.at[pl.ds(pl.multiple_of(target * rows, rows), rows), span]

            steps.append(
                scatter_head(source_at, out.at[:, span], *rest[6 * piece : 6 * piece + 6])
            )
        run_together(steps)

    return link_call(
        body,
        number,
        [ANY],
        IN_VMEM,
        shaped((rows, value.shape[1]), f32),
        head_scratch(rows, width) * pieces,
        60_000_000,
    )(value)


def scattered_seq(value, number, pieces=2):
    total = lax.axis_size("seq")
    count = total // SIDE
    if total % SIDE or count < 2:
        return scattered(value, "seq")
    rows, width = value.shape[0] // total, value.shape[1] // pieces

    def body(source, out, *rest):
        greet(seq_partners(count))

        def source_at(target, side, piece):
            begin = pl.multiple_of((target * SIDE + side) * rows, rows)
            return source.at[pl.ds(begin, rows), pl.ds(piece * width, width)]

        def out_at(piece):
            return out.at[:, pl.ds(piece * width, width)]

        run_together([scatter_seq(source_at, out_at, *rest, count)])

    return link_call(
        body,
        number,
        [ANY],
        IN_VMEM,
        shaped((rows, value.shape[1]), f32),
        seq_scratch(pieces, count, rows, width),
        120_000_000,
    )(value)


def scattered_last(qkv, gate, normed, mlp, small, gain_rows, number, pieces=4, gate_pieces=2):
    total, heads = lax.axis_size("seq"), lax.axis_size("head")
    count = total // SIDE
    rows, width = qkv.shape[0] // total, qkv.shape[1] // pieces
    gate_width = gate.shape[1] // gate_pieces
    own_rows = normed.shape[0] // heads
    units, slices = mlp[0].shape[0], mlp[0].shape[1] // heads
    small_rows = small.shape[0]

    def body(qkv_ref, gate_ref, normed_ref, small_ref, *rest):
        mlp_refs, rest = rest[: len(mlp)], rest[len(mlp) :]
        qkv_out, gate_out, normed_out, small_out, rest = rest[0], rest[1], rest[2], rest[3], rest[4:]
        mlp_outs, rest = rest[: len(mlp)], rest[len(mlp) :]
        greet(head_partners() + seq_partners(count))

        def qkv_at(target, side, piece):
            begin = pl.multiple_of((target * SIDE + side) * rows, rows)
            return qkv_ref.at[pl.ds(begin, rows), pl.ds(piece * width, width)]

        def gate_at(target, side, piece):
            begin = pl.multiple_of(target * rows, rows)
            return gate_ref.at[pl.ds(begin, rows), pl.ds(piece * gate_width, gate_width)]

        def normed_at(target):
            return normed_ref.at[pl.ds(pl.multiple_of(target * own_rows, own_rows), own_rows)]

        def small_steps(four, own, local, *sems):
            yield from gather_head(small_ref, four, sems[0], sems[1], sems[2], 1)
            own[...] = four[lax.axis_index("head")]
            own[:gain_rows] = jnp.sum(four[:, :gain_rows], axis=0)
            for step in gather_seq(own, small_out, local, *sems[3:7], count):
                for _ in range(3):
                    yield

        steps = [
            small_steps(*rest[19:29]),
            scatter_seq(
                gate_at,
                lambda piece: gate_out.at[:, pl.ds(piece * gate_width, gate_width)],
                rest[7],
                None,
                *rest[8:13],
                count,
            ),
            scatter_seq(
                qkv_at,
                lambda piece: qkv_out.at[:, pl.ds(piece * width, width)],
                *rest[:7],
                count,
            ),
            scatter_head(normed_at, normed_out, *rest[13:19], 2),
        ]
        for index, (ref, out) in enumerate(zip(mlp_refs, mlp_outs)):

            def mlp_at(target, ref=ref):
                return ref.at[:, pl.ds(pl.multiple_of(target * slices, slices), slices)]

            begin = 29 + 6 * index
            steps.append(
                scatter_head(mlp_at, out, *rest[begin : begin + 6], 5 + 3 * index)
            )
        run_together(steps)

    line_scratch = seq_scratch(gate_pieces, count, rows, gate_width)
    outs = link_call(
        body,
        number,
        [ANY] * (4 + len(mlp)),
        [IN_VMEM] * (4 + len(mlp)),
        [
            shaped((rows, qkv.shape[1]), bf16),
            shaped((rows, gate.shape[1]), bf16),
            shaped((own_rows, normed.shape[1]), f32),
            shaped((total, small_rows, small.shape[1]), f32),
        ]
        + [shaped((units, slices), bf16) for _ in mlp],
        seq_scratch(pieces, count, rows, width)
        + line_scratch[1:]
        + head_scratch(own_rows, normed.shape[1])
        + [
            pltpu.VMEM((heads, small_rows, small.shape[1]), f32),
            pltpu.VMEM((small_rows, small.shape[1]), f32),
            DMA((1,)),
            DMA((1,)),
            DMA((3, 1)),
            DMA((3, 1)),
        ]
        + [DMA((2 * count,)) for _ in range(4)]
        + head_scratch(units, slices) * len(mlp),
        250_000_000,
    )(qkv, gate, normed, small, *mlp)
    return outs[0], outs[1], outs[2], outs[3], list(outs[4:])


def side_columns(value, side, rows):
    count = value.shape[1] // (rows * SIDE)
    return jnp.concatenate(
        [
            lax.dynamic_slice_in_dim(value, (place * SIDE + side) * rows, rows, 1)
            for place in range(count)
        ],
        axis=1,
    )


def swapped(value):
    count = lax.axis_size("seq")
    return lax.ppermute(value, "seq", [(place, place ^ 1) for place in range(count)])


def silu_slope(tensor):
    sigmoid_part = jax.nn.sigmoid(tensor)
    return sigmoid_part * (1.0 + tensor * (1.0 - sigmoid_part))


def gathered(value, axis):
    return lax.all_gather(value, axis, axis=0, tiled=True)


def scattered(value, axis, dimension=0):
    return lax.psum_scatter(
        value.astype(bf16), axis, scatter_dimension=dimension, tiled=True
    ).astype(f32)


def on_device(
    block_in,
    out_cot,
    gain_one,
    qkv_weight,
    conv_weight,
    gate_weight,
    gain_out,
    out_weight,
    gain_two,
    mlp_gate,
    mlp_up,
    mlp_down,
    decay_code,
    beta_code,
):
    span_rows = decay_code.shape[0]
    width, heads, inner = qkv_weight.shape
    total_len = span_rows * lax.axis_size("seq")
    lead_rows = conv_weight.shape[0] - 1
    input_f = block_in.astype(f32)
    gain_first = gain_one.astype(f32)
    gain_second = gain_two.astype(f32)
    gain_head = gain_out.reshape(1, -1)
    taps = conv_weight.reshape(conv_weight.shape[0], heads * inner)
    qkv_flat = qkv_weight.reshape(width, heads * inner)
    gate_flat = gate_weight.reshape(width, heads * DV)
    out_flat = out_weight.reshape(heads * DV, width)
    columns, run_rows = token_columns(decay_code, beta_code, total_len)

    cot_all = gathered(out_cot, "seq")
    seq_count, head_count = lax.axis_size("seq"), lax.axis_size("head")
    seq_at, head_at = lax.axis_index("seq"), lax.axis_index("head")
    side = lax.rem(seq_at, SIDE)
    slice_rows = width // seq_count
    scale_own = rms_scale(input_f)
    hat_own = input_f * scale_own
    normed_own = (hat_own * gain_first).astype(bf16)
    normed_first, normed_side = gathered_sided(
        normed_own, side_columns(normed_own, 1 - side, slice_rows), 1
    )
    mixed_in = mm(normed_first, qkv_flat).astype(bf16)
    tail_in = passed_along(mixed_in[span_rows - 8 :], "seq", 1)
    tail_in = jnp.where(jnp.arange(8)[:, None] >= 8 - lead_rows, tail_in.astype(f32), 0.0)
    solve, score, fresh, reach, inner_part, turn, local_states, piece_end = run_local_forward(
        mixed_in, tail_in, taps, columns, run_rows, heads
    )
    ends = gathered_seq(piece_end.reshape(-1, DV + DK), 2).reshape(-1, heads, DK, DV + DK)
    gate_pre = mm(normed_first, gate_flat)
    states, core, branch = run_finish_forward(
        ends, local_states, reach, inner_part, gate_pre, gain_head
    )
    branch, cot_all = lax.optimization_barrier((branch, cot_all))
    middle = input_f + scattered_head(mm(branch, out_flat).astype(bf16), 3)
    scale_two = rms_scale(middle)
    hat_two = middle * scale_two
    normed_two = (hat_two * gain_second).astype(bf16)

    rows_out = gathered_seq(normed_two, 4).reshape(-1, width)
    gate_part = mm(rows_out, mlp_gate)
    up_part = mm(rows_out, mlp_up)
    hidden = (jax.nn.silu(gate_part) * up_part).astype(bf16)
    cot_f = out_cot.astype(f32)
    d_hidden = mm_nt(cot_all, mlp_down)
    d_gate_mlp = (d_hidden * up_part * silu_slope(gate_part)).astype(bf16)
    d_up_mlp = (d_hidden * jax.nn.silu(gate_part)).astype(bf16)
    d_rows = (mm_nt(d_gate_mlp, mlp_gate) + mm_nt(d_up_mlp, mlp_up)).astype(bf16)
    d_normed_two = scattered_seq(d_rows, 5)
    hidden, d_normed_two = lax.optimization_barrier((hidden, d_normed_two))
    mlp_out = scattered(mm(hidden, mlp_down), "seq")
    output = (middle + mlp_out).astype(bf16)
    gain_two_part = jnp.sum(d_normed_two * hat_two, 0)
    e_two = d_normed_two * gain_second
    d_middle = cot_f + scale_two * (
        e_two - hat_two * jnp.mean(e_two * hat_two, axis=-1, keepdims=True)
    )
    d_mix_all = gathered_head(d_middle.astype(bf16), 6)
    d_branch = mm_nt(d_mix_all, out_flat)
    d_core, d_gate_low, gain_out_part, local_grads, grad_end = run_local_backward(
        d_branch, core, gate_pre, gain_head, reach, turn
    )
    grad_ends = gathered_seq(grad_end.reshape(-1, DV), 7).reshape(-1, heads, DK, DV)
    grad_out_w = mm_tn(branch, d_mix_all)
    grad_out_s = scattered(grad_out_w, "seq", 1).reshape(heads, DV, -1)
    d_gate_side = swapped(d_gate_low)
    d_mixed, d_tail, d_lead, grad_conv = run_finish_backward(
        ends,
        grad_ends,
        mixed_in,
        tail_in,
        taps,
        columns,
        run_rows,
        solve,
        score,
        fresh,
        states,
        d_core,
        local_grads,
    )
    from_next = passed_along(d_lead[:lead_rows], "seq", -1)
    d_tail = d_tail.at[8 - lead_rows :].add(from_next).astype(bf16)
    d_mixed = lax.dynamic_update_slice(d_mixed, d_tail, (span_rows - 8, 0))
    d_normed_part = mm_nt(d_mixed, qkv_flat) + mm_nt(d_gate_low, gate_flat)
    gain_one_part = jnp.sum(d_normed_part * normed_first.astype(f32), 0) / gain_first
    grad_qkv = mm_tn(normed_first, d_mixed).astype(bf16)
    grad_gate = (
        mm_tn(side_columns(normed_first, side, slice_rows), d_gate_low)
        + mm_tn(normed_side, d_gate_side)
    ).astype(bf16)
    grad_mgate = mm_tn(d_gate_mlp, rows_out).astype(bf16)
    grad_mup = mm_tn(d_up_mlp, rows_out).astype(bf16)
    grad_down = mm_tn(hidden, cot_all).astype(bf16)

    gains = jnp.concatenate([gain_one_part, gain_two_part, gain_out_part.reshape(-1)])
    gain_rows = -(-gains.shape[0] // 1024) * 8
    gains = jnp.pad(gains, (0, gain_rows * 128 - gains.shape[0])).reshape(gain_rows, 128)
    small = jnp.concatenate([gains, grad_conv.reshape(-1, 128)])
    grad_qkv_s, grad_gate_s, d_normed_one, small_all, (grad_mgate_t, grad_mup_t, grad_down_h) = (
        scattered_last(
            grad_qkv,
            grad_gate,
            d_normed_part.astype(bf16),
            [grad_mgate, grad_mup, grad_down],
            small,
            gain_rows,
            8,
        )
    )
    e_one = d_normed_one * gain_first
    d_input = (
        d_middle + scale_own * (e_one - hat_own * jnp.mean(e_one * hat_own, axis=-1, keepdims=True))
    ).astype(bf16)

    small_sum = jnp.sum(small_all, axis=0)
    gains = small_sum[:gain_rows].reshape(-1)

    def own_slice(begin, length):
        length = length // (seq_count * head_count)
        return lax.dynamic_slice(
            gains, (begin + (head_at * seq_count + seq_at) * length,), (length,)
        )

    grad_conv_s = lax.dynamic_slice_in_dim(
        small_sum[gain_rows:].reshape(-1, heads, inner),
        seq_at * (inner // seq_count),
        inner // seq_count,
        2,
    )
    return (
        output,
        d_input,
        own_slice(0, width),
        grad_qkv_s.astype(f32).reshape(-1, heads, inner),
        grad_conv_s,
        grad_gate_s.astype(f32).reshape(-1, heads, DV),
        own_slice(2 * width, DV),
        grad_out_s,
        own_slice(width, width),
        grad_mgate_t.astype(f32).T,
        grad_mup_t.astype(f32).T,
        grad_down_h.astype(f32),
    )


def solution(mesh):
    in_specs = (
        P(("seq", "head"), None),
        P(("seq", "head"), None),
        P(),
        P(None, "head", None),
        P(None, "head", None),
        P(None, "head", None),
        P(),
        P("head", None, None),
        P(),
        P(None, "seq"),
        P(None, "seq"),
        P("seq", None),
        P("seq", "head"),
        P("seq", "head"),
    )
    out_specs = (
        P(("seq", "head"), None),
        P(("seq", "head"), None),
        P(("head", "seq")),
        P("seq", "head", None),
        P(None, "head", "seq"),
        P("seq", "head", None),
        P(("head", "seq")),
        P("head", None, "seq"),
        P(("head", "seq")),
        P("head", "seq"),
        P("head", "seq"),
        P("seq", "head"),
    )
    return jax.shard_map(
        on_device, mesh=mesh, in_specs=in_specs, out_specs=out_specs, check_vma=False
    )
```

```python
import functools
import math

import jax
import jax.numpy as jnp
from jax import lax
from jax.experimental import pallas as pl
from jax.experimental.pallas import tpu as pltpu
from jax.sharding import PartitionSpec as P

DK = 128
DV = 256
STRETCH = 64
GROUP = 4 * STRETCH
INNER = 2 * DK + DV
BETA, GAMMA, BETA_GAMMA, TAIL, LAST, RUN = range(6)

epsilon = 1e-06
bf16 = jnp.bfloat16
f32 = jnp.float32
VMEM_BYTES = 56 * 2**20


def passed_along(value, axis, steps):
    count = lax.axis_size(axis)
    first, last = (max(0, -steps), min(count, count - steps))
    return lax.ppermute(value, axis, [(source, source + steps) for source in range(first, last)])


def rms_scale(tensor):
    return lax.rsqrt(jnp.mean(tensor * tensor, axis=-1, keepdims=True) + epsilon)


def log_rates(decay_code, total_len):
    code_level = decay_code.astype(f32) / 1023.0
    smooth = -jnp.exp(-code_level * math.log(total_len / 32.0)) / 32.0
    return jnp.where(decay_code == 1024, -0.25, smooth)


def token_columns(decay_code, beta_code, total_len):
    rows, heads = decay_code.shape
    rates = log_rates(decay_code, total_len)
    run = jnp.einsum(
        "ij,bjh->bih",
        jnp.tril(jnp.ones((STRETCH, STRETCH), f32)),
        rates.reshape(rows // STRETCH, STRETCH, heads),
        precision=lax.Precision.HIGHEST,
    )
    last = jnp.broadcast_to(run[:, -1:], run.shape).reshape(rows, heads)
    run = run.reshape(rows, heads)
    beta = 0.5 + beta_code.astype(f32) / 512.0
    gamma = jnp.exp(run)
    columns = jnp.concatenate(
        [beta, gamma, beta * gamma, jnp.exp(last - run), jnp.exp(last), run], axis=1
    )
    columns = jnp.pad(columns, ((0, 0), (0, 128 - columns.shape[1])))
    run_rows = jnp.pad(run.T, ((0, 8 - heads % 8), (0, 0)))
    return columns, run_rows


def mm(left, right):
    return jnp.dot(left, right, preferred_element_type=f32)


def mm_nt(left, right):
    return lax.dot_general(left, right, (((1,), (1,)), ((), ())), preferred_element_type=f32)


def mm_tn(left, right):
    return lax.dot_general(left, right, (((0,), (0,)), ((), ())), preferred_element_type=f32)


def column(columns_ref, kind, head, heads):
    block = columns_ref[...]
    lanes = lax.broadcasted_iota(jnp.int32, block.shape, 1)
    return jnp.sum(jnp.where(lanes == kind * heads + head, block, 0.0), axis=1, keepdims=True)


def square_ids():
    return (
        lax.broadcasted_iota(jnp.int32, (GROUP, GROUP), 0),
        lax.broadcasted_iota(jnp.int32, (GROUP, GROUP), 1),
    )


def convolved(padded_ref, tail_ref, mixed_ref, taps_ref):
    rows = mixed_ref.shape[0]
    count = taps_ref.shape[0]
    padded_ref[0:8, :] = tail_ref[...]
    padded_ref[8 : 8 + rows, :] = mixed_ref[...].astype(f32)
    taps = taps_ref[...].astype(f32)
    start = 9 - count
    total = taps[0:1] * padded_ref[start : start + rows, :]
    for tap in range(1, count):
        total += taps[tap : tap + 1] * padded_ref[start + tap : start + tap + rows, :]
    return total


def chunk_masks_stack(transposed):
    lanes = lax.broadcasted_iota(jnp.int32, transposed.shape, 1) // STRETCH
    parts = [jnp.where(lanes == part, transposed, 0.0) for part in range(GROUP // STRETCH)]
    return jnp.concatenate(parts, axis=0).astype(bf16)


def local_forward(
    mixed_ref,
    tail_ref,
    taps_ref,
    columns_ref,
    run_rows_ref,
    solve_ref,
    score_ref,
    fresh_ref,
    reach_ref,
    inner_ref,
    turn_ref,
    local_ref,
    end_ref,
    padded,
    turn_t,
    offsets,
):
    head = pl.program_id(0)
    heads = pl.num_programs(0)
    rows = mixed_ref.shape[0]
    per_group = GROUP // STRETCH
    stretches = rows // STRETCH
    total = convolved(padded, tail_ref, mixed_ref, taps_ref)
    activated = total * jax.nn.sigmoid(total)
    raw_q, raw_k = activated[:, :DK], activated[:, DK : 2 * DK]
    queries = raw_q * (
        lax.rsqrt(jnp.sum(raw_q * raw_q, axis=1, keepdims=True) + epsilon) * DK ** (-0.5)
    )
    keys = raw_k * lax.rsqrt(jnp.sum(raw_k * raw_k, axis=1, keepdims=True) + epsilon)
    values = activated[:, 2 * DK :]
    beta = column(columns_ref, BETA, head, heads)
    gamma = column(columns_ref, GAMMA, head, heads)
    beta_gamma = column(columns_ref, BETA_GAMMA, head, heads)
    tail_decay = column(columns_ref, TAIL, head, heads)
    last = column(columns_ref, LAST, head, heads)
    run = column(columns_ref, RUN, head, heads)
    row_id, col_id = square_ids()
    same = row_id // STRETCH == col_id // STRETCH
    causal = same & (row_id >= col_id)
    diagonal = row_id == col_id
    eye = jnp.where(
        lax.broadcasted_iota(jnp.int32, (DK, DK), 0) == lax.broadcasted_iota(jnp.int32, (DK, DK), 1),
        1.0,
        0.0,
    )
    for group in range(rows // GROUP):
        span = slice(group * GROUP, (group + 1) * GROUP)
        key_b = keys[span].astype(bf16)
        query_b = queries[span].astype(bf16)
        gaps = run[span] - run_rows_ref[pl.ds(head, 1), span]
        within = jnp.exp(jnp.where(causal, gaps, -1e30))
        lower = jnp.where(diagonal, 0.0, beta[span] * within * mm_nt(key_b, key_b))
        solve = jnp.where(diagonal, 1.0, jnp.where(row_id // 2 == col_id // 2, -lower, 0.0))
        size = 2
        while size < STRETCH:
            crossing = (row_id // (2 * size) == col_id // (2 * size)) & (
                row_id // size != col_id // size
            )
            solve_b = solve.astype(bf16)
            half = mm(solve_b, jnp.where(crossing, lower, 0.0).astype(bf16))
            solve = solve - mm(half.astype(bf16), solve_b)
            size *= 2
        solve_b = solve.astype(bf16)
        right = jnp.concatenate([beta[span] * values[span], beta_gamma[span] * keys[span]], axis=1)
        fresh_b = mm(solve_b, right.astype(bf16)).astype(bf16)
        score_b = (within * mm_nt(query_b, key_b)).astype(bf16)
        scored = mm(score_b, fresh_b)
        solve_ref[group] = solve_b
        score_ref[group] = score_b
        fresh_ref[span, :] = fresh_b
        inner_ref[span, :] = scored[:, :DV]
        reach_ref[span, :] = (gamma[span] * queries[span] - scored[:, DV:]).astype(bf16)
        tail_keys = (tail_decay[span] * keys[span]).T
        moved = mm(chunk_masks_stack(tail_keys), fresh_b)
        for part in range(per_group):
            at = group * per_group + part
            block = moved[part * DK : (part + 1) * DK]
            stay = last[at * STRETCH : at * STRETCH + 1]
            turned = stay * eye - block[:, DV:]
            turn_t[head, at] = turned.astype(bf16)
            turn_ref[at] = turned.T.astype(bf16)
            offsets[head, at] = block[:, :DV]

    @pl.when(head == heads - 1)
    def _():
        states = [
            jnp.concatenate([jnp.zeros((DK, DV), f32), eye], axis=1)
            for _ in range(local_ref.shape[0])
        ]
        for at in range(stretches):
            for h in range(len(states)):
                state_b = states[h].astype(bf16)
                local_ref[h, at] = state_b
                moved = mm(turn_t[h, at], state_b)
                states[h] = jnp.concatenate(
                    [moved[:, :DV] + offsets[h, at], moved[:, DV:]], axis=1
                )
        for h in range(len(states)):
            end_ref[h] = states[h].astype(bf16)


def finish_forward(
    ends_ref, local_ref, reach_ref, inner_ref, gate_ref, gain_ref, state_ref, core_ref, branch_ref, start
):
    head = pl.program_id(0)
    heads, stretches = start.shape[0], local_ref.shape[0]

    @pl.when(head == 0)
    def _():
        start[...] = jnp.zeros_like(start)

        def one(source, carry):
            for h in range(heads):
                start[h] = (
                    mm(ends_ref[source, h, :, DV:], start[h].astype(bf16))
                    + ends_ref[source, h, :, :DV].astype(f32)
                )
            return carry

        lax.fori_loop(0, lax.axis_index("seq"), one, 0)

    start_b = start[head].astype(bf16)
    cores = []
    for at in range(stretches):
        state_b = (
            local_ref[at, :, :DV].astype(f32) + mm(local_ref[at, :, DV:], start_b)
        ).astype(bf16)
        state_ref[at] = state_b
        span = slice(at * STRETCH, (at + 1) * STRETCH)
        cores.append(inner_ref[span, :] + mm(reach_ref[span, :], state_b))
    core = jnp.concatenate(cores, axis=0)
    core_ref[...] = core
    gate = gate_ref[...]
    branch = core * rms_scale(core) * gain_ref[...].astype(f32) * (gate * jax.nn.sigmoid(gate))
    branch_ref[...] = branch.astype(bf16)


def local_backward(
    d_branch_ref,
    core_ref,
    gate_ref,
    gain_ref,
    reach_ref,
    turn_ref,
    d_core_ref,
    d_gate_ref,
    gain_part_ref,
    local_ref,
    end_ref,
    pulls,
):
    head = pl.program_id(0)
    heads = pl.num_programs(0)
    rows = core_ref.shape[0]
    per_group = GROUP // STRETCH
    stretches = rows // STRETCH
    core = core_ref[...]
    gate = gate_ref[...]
    gain = gain_ref[...].astype(f32)
    d_branch = d_branch_ref[...]
    scale = rms_scale(core)
    nhat = core * scale
    sig = jax.nn.sigmoid(gate)
    gated = d_branch * (gate * sig)

    @pl.when(head == 0)
    def _():
        gain_part_ref[...] = jnp.zeros_like(gain_part_ref)

    gain_part_ref[...] += jnp.sum(gated * nhat, axis=0, keepdims=True)
    f = gated * gain
    d_core = scale * (f - nhat * jnp.mean(f * nhat, axis=1, keepdims=True))
    d_gate_ref[...] = (d_branch * nhat * gain * sig * (1.0 + gate * (1.0 - sig))).astype(bf16)
    d_core_b = d_core.astype(bf16)
    d_core_ref[...] = d_core_b
    for group in range(rows // GROUP):
        span = slice(group * GROUP, (group + 1) * GROUP)
        pulled = mm(chunk_masks_stack(reach_ref[span, :].astype(f32).T), d_core_b[span])
        for part in range(per_group):
            pulls[head, group * per_group + part] = pulled[part * DK : (part + 1) * DK]

    @pl.when(head == heads - 1)
    def _():
        eye = jnp.where(
            lax.broadcasted_iota(jnp.int32, (DK, DK), 0)
            == lax.broadcasted_iota(jnp.int32, (DK, DK), 1),
            1.0,
            0.0,
        )
        grads = [
            jnp.concatenate([jnp.zeros((DK, DV), f32), eye], axis=1)
            for _ in range(local_ref.shape[0])
        ]
        for at in reversed(range(stretches)):
            for h in range(len(grads)):
                grad_b = grads[h].astype(bf16)
                local_ref[h, at] = grad_b
                moved = mm(turn_ref[h, at], grad_b)
                grads[h] = jnp.concatenate([moved[:, :DV] + pulls[h, at], moved[:, DV:]], axis=1)
        for h in range(len(grads)):
            end_ref[h] = grads[h][:, :DV].astype(bf16)


def finish_backward(
    ends_ref,
    grad_ends_ref,
    mixed_ref,
    tail_ref,
    taps_ref,
    columns_ref,
    run_rows_ref,
    solve_ref,
    score_ref,
    fresh_ref,
    state_ref,
    d_core_ref,
    local_ref,
    d_mixed_ref,
    tail_out_ref,
    lead_ref,
    grad_taps_ref,
    padded,
    spread,
    end,
):
    head = pl.program_id(0)
    heads = pl.num_programs(0)
    rows = mixed_ref.shape[0]
    per_group = GROUP // STRETCH

    @pl.when(head == 0)
    def _():
        end[...] = jnp.zeros_like(end)
        count = ends_ref.shape[0]

        def one(turn, carry):
            source = count - 1 - turn
            for h in range(end.shape[0]):
                end[h] = (
                    mm_tn(ends_ref[source, h, :, DV:], end[h].astype(bf16))
                    + grad_ends_ref[source, h].astype(f32)
                )
            return carry

        lax.fori_loop(0, count - 1 - lax.axis_index("seq"), one, 0)

    end_b = end[head].astype(bf16)
    total = convolved(padded, tail_ref, mixed_ref, taps_ref)
    sig = jax.nn.sigmoid(total)
    activated = total * sig
    raw_q, raw_k = activated[:, :DK], activated[:, DK : 2 * DK]
    scale_q = lax.rsqrt(jnp.sum(raw_q * raw_q, axis=1, keepdims=True) + epsilon)
    scale_k = lax.rsqrt(jnp.sum(raw_k * raw_k, axis=1, keepdims=True) + epsilon)
    unit_q = raw_q * scale_q
    keys = raw_k * scale_k
    beta = column(columns_ref, BETA, head, heads)
    gamma = column(columns_ref, GAMMA, head, heads)
    beta_gamma = column(columns_ref, BETA_GAMMA, head, heads)
    tail_decay = column(columns_ref, TAIL, head, heads)
    run = column(columns_ref, RUN, head, heads)
    row_id, col_id = square_ids()
    causal = (row_id // STRETCH == col_id // STRETCH) & (row_id >= col_id)
    diagonal = row_id == col_id
    d_queries, d_keys, d_values = [], [], []
    for group in range(rows // GROUP):
        span = slice(group * GROUP, (group + 1) * GROUP)
        key_b = keys[span].astype(bf16)
        query_b = (unit_q[span] * DK ** (-0.5)).astype(bf16)
        tail_keys = (tail_decay[span] * keys[span]).astype(bf16)
        d_core_b = d_core_ref[span, :]
        grad_bs, from_grad, fresh_parts, from_state = [], [], [], []
        for part in range(per_group):
            at = group * per_group + part
            own = slice(part * STRETCH, (part + 1) * STRETCH)
            rows_at = slice(at * STRETCH, (at + 1) * STRETCH)
            grad_b = (
                local_ref[at, :, :DV].astype(f32) + mm(local_ref[at, :, DV:], end_b)
            ).astype(bf16)
            grad_bs.append(grad_b)
            from_grad.append(mm(tail_keys[own], grad_b))
            fresh_parts.append(mm(fresh_ref[rows_at, DV:], state_ref[at]))
            from_state.append(mm_nt(d_core_b[own], state_ref[at]))
        d_fresh = mm_tn(score_ref[group], d_core_b) + jnp.concatenate(from_grad, axis=0)
        d_right = mm_tn(solve_ref[group], d_fresh.astype(bf16))
        d_right_b = d_right.astype(bf16)
        fresh = fresh_ref[span, :DV].astype(f32) - jnp.concatenate(fresh_parts, axis=0)
        fresh_b = fresh.astype(bf16)
        gaps = run[span] - run_rows_ref[pl.ds(head, 1), span]
        within = jnp.exp(jnp.where(causal, gaps, -1e30))
        d_score = (within * mm_nt(d_core_b, fresh_b)).astype(bf16)
        d_lower = jnp.where(
            diagonal, 0.0, -beta[span] * within * mm_nt(d_right_b, fresh_b)
        ).astype(bf16)
        state_keys, grad_keys = [], []
        for part in range(per_group):
            at = group * per_group + part
            own = slice(part * STRETCH, (part + 1) * STRETCH)
            state_keys.append(mm_nt(d_right_b[own], state_ref[at]))
            grad_keys.append(mm_nt(fresh_b[own], grad_bs[part]))
        d_queries.append(gamma[span] * jnp.concatenate(from_state, axis=0) + mm(d_score, key_b))
        d_keys.append(
            mm_tn(d_score, query_b)
            + mm_tn(d_lower, key_b)
            + mm(d_lower, key_b)
            + tail_decay[span] * jnp.concatenate(grad_keys, axis=0)
            - beta_gamma[span] * jnp.concatenate(state_keys, axis=0)
        )
        d_values.append(beta[span] * d_right)
    g_q = jnp.concatenate(d_queries, axis=0) * DK ** (-0.5)
    g_k = jnp.concatenate(d_keys, axis=0)
    d_act = jnp.concatenate(
        [
            scale_q * (g_q - unit_q * jnp.sum(unit_q * g_q, axis=1, keepdims=True)),
            scale_k * (g_k - keys * jnp.sum(keys * g_k, axis=1, keepdims=True)),
            jnp.concatenate(d_values, axis=0),
        ],
        axis=1,
    )
    d_conv = d_act * (sig * (1.0 + total * (1.0 - sig)))
    taps = taps_ref[...].astype(f32)
    count = taps_ref.shape[0]
    start = 9 - count
    grad_taps_ref[...] = jnp.concatenate(
        [
            jnp.sum(padded[start + tap : start + tap + rows, :] * d_conv, axis=0, keepdims=True)
            for tap in range(count)
        ],
        axis=0,
    )
    spread[0:8, :] = jnp.zeros((8, d_conv.shape[1]), f32)
    spread[8 : 8 + rows, :] = d_conv
    spread[8 + rows : 16 + rows, :] = jnp.zeros((8, d_conv.shape[1]), f32)
    lead = taps[0:1] * spread[8:16, :]
    d_mixed = taps[0:1] * spread[7 + count : 7 + count + rows, :]
    for tap in range(1, count):
        lead += taps[tap : tap + 1] * spread[8 - tap : 16 - tap, :]
        begin = 7 + count - tap
        d_mixed += taps[tap : tap + 1] * spread[begin : begin + rows, :]
    lead_ref[...] = lead
    d_mixed_ref[...] = d_mixed.astype(bf16)
    tail_out_ref[...] = d_mixed[rows - 8 :]


def whole(shape):
    return pl.BlockSpec(shape, lambda h: (0,) * len(shape))


def by_head(shape):
    return pl.BlockSpec((None,) + shape, lambda h: (h,) + (0,) * len(shape))


def by_columns(rows, width):
    return pl.BlockSpec((rows, width), lambda h: (0, h))


def kernel_call(body, heads, ins, outs, out_shapes, scratch, flops, moved):
    return pl.pallas_call(
        body,
        grid=(heads,),
        in_specs=ins,
        out_specs=outs,
        out_shape=out_shapes,
        scratch_shapes=scratch,
        compiler_params=pltpu.CompilerParams(
            dimension_semantics=("arbitrary",), vmem_limit_bytes=VMEM_BYTES
        ),
        cost_estimate=pl.CostEstimate(flops=flops, bytes_accessed=moved, transcendentals=0),
    )


def shaped(shape, kind):
    return jax.ShapeDtypeStruct(shape, kind)


def run_local_forward(mixed, tail, taps, columns, run_rows, heads):
    rows = mixed.shape[1]
    count = taps.shape[0]
    groups, stretches = rows // GROUP, rows // STRETCH
    return kernel_call(
        local_forward,
        heads,
        [
            by_head((rows, INNER)),
            by_head((8, INNER)),
            by_columns(count, INNER),
            whole(columns.shape),
            whole(run_rows.shape),
        ],
        [
            by_head((groups, GROUP, GROUP)),
            by_head((groups, GROUP, GROUP)),
            by_head((rows, DV + DK)),
            by_head((rows, DK)),
            by_columns(rows, DV),
            by_head((stretches, DK, DK)),
            whole((heads, stretches, DK, DV + DK)),
            whole((heads, DK, DV + DK)),
        ],
        [
            shaped((heads, groups, GROUP, GROUP), bf16),
            shaped((heads, groups, GROUP, GROUP), bf16),
            shaped((heads, rows, DV + DK), bf16),
            shaped((heads, rows, DK), bf16),
            shaped((rows, heads * DV), f32),
            shaped((heads, stretches, DK, DK), bf16),
            shaped((heads, stretches, DK, DV + DK), bf16),
            shaped((heads, DK, DV + DK), bf16),
        ],
        [
            pltpu.VMEM((rows + 8, INNER), f32),
            pltpu.VMEM((heads, stretches, DK, DK), bf16),
            pltpu.VMEM((heads, stretches, DK, DV), f32),
        ],
        12_000_000_000,
        20_000_000,
    )(mixed, tail, taps, columns, run_rows)


def run_finish_forward(ends, local, reach, inner, gate_pre, gain):
    heads, stretches = local.shape[:2]
    rows = inner.shape[0]
    return kernel_call(
        finish_forward,
        heads,
        [
            whole(ends.shape),
            by_head((stretches, DK, DV + DK)),
            by_head((rows, DK)),
            by_columns(rows, DV),
            by_head((rows, DV)),
            whole(gain.shape),
        ],
        [by_head((stretches, DK, DV)), by_columns(rows, DV), by_columns(rows, DV)],
        [
            shaped((heads, stretches, DK, DV), bf16),
            shaped((rows, heads * DV), f32),
            shaped((rows, heads * DV), bf16),
        ],
        [pltpu.VMEM((heads, DK, DV), f32)],
        3_000_000_000,
        20_000_000,
    )(ends, local, reach, inner, gate_pre, gain)


def run_local_backward(d_branch, core, gate_pre, gain, reach, turn):
    heads, stretches = turn.shape[:2]
    rows = core.shape[0]
    return kernel_call(
        local_backward,
        heads,
        [
            by_columns(rows, DV),
            by_columns(rows, DV),
            by_head((rows, DV)),
            whole(gain.shape),
            by_head((rows, DK)),
            whole(turn.shape),
        ],
        [
            by_columns(rows, DV),
            by_columns(rows, DV),
            whole((1, DV)),
            whole((heads, stretches, DK, DV + DK)),
            whole((heads, DK, DV)),
        ],
        [
            shaped((rows, heads * DV), bf16),
            shaped((rows, heads * DV), bf16),
            shaped((1, DV), f32),
            shaped((heads, stretches, DK, DV + DK), bf16),
            shaped((heads, DK, DV), bf16),
        ],
        [pltpu.VMEM((heads, stretches, DK, DV), f32)],
        4_000_000_000,
        20_000_000,
    )(d_branch, core, gate_pre, gain, reach, turn)


def run_finish_backward(
    ends, grad_ends, mixed, tail, taps, columns, run_rows, solve, score, fresh, states, d_core, local
):
    heads, stretches = local.shape[:2]
    rows = mixed.shape[1]
    groups = rows // GROUP
    count = taps.shape[0]
    return kernel_call(
        finish_backward,
        heads,
        [
            whole(ends.shape),
            whole(grad_ends.shape),
            by_head((rows, INNER)),
            by_head((8, INNER)),
            by_columns(count, INNER),
            whole(columns.shape),
            whole(run_rows.shape),
            by_head((groups, GROUP, GROUP)),
            by_head((groups, GROUP, GROUP)),
            by_head((rows, DV + DK)),
            by_head((stretches, DK, DV)),
            by_columns(rows, DV),
            by_head((stretches, DK, DV + DK)),
        ],
        [
            by_columns(rows, INNER),
            by_columns(8, INNER),
            by_columns(8, INNER),
            by_columns(count, INNER),
        ],
        [
            shaped((rows, heads * INNER), bf16),
            shaped((8, heads * INNER), f32),
            shaped((8, heads * INNER), f32),
            shaped((count, heads * INNER), f32),
        ],
        [
            pltpu.VMEM((rows + 8, INNER), f32),
            pltpu.VMEM((rows + 16, INNER), f32),
            pltpu.VMEM((heads, DK, DV), f32),
        ],
        12_000_000_000,
        20_000_000,
    )(ends, grad_ends, mixed, tail, taps, columns, run_rows, solve, score, fresh, states, d_core, local)


MESH = pl.DeviceIdType.MESH
SIDE = 2


def remote(source, target, send, arrive, device):
    return pltpu.make_async_remote_copy(
        src_ref=source,
        dst_ref=target,
        send_sem=send,
        recv_sem=arrive,
        device_id=device,
        device_id_type=MESH,
    )


def greet(partners):
    barrier = pltpu.get_barrier_semaphore()
    expected = 0
    for device, there in partners:
        if there is None:
            pl.semaphore_signal(barrier, inc=1, device_id=device, device_id_type=MESH)
            expected = expected + 1
        else:

            @pl.when(there)
            def _(device=device):
                pl.semaphore_signal(barrier, inc=1, device_id=device, device_id_type=MESH)

            expected = expected + there.astype(jnp.int32)
    pl.semaphore_wait(barrier, expected)


def head_places():
    head, seq = lax.axis_index("head"), lax.axis_index("seq")
    core = lax.rem(head, 2)
    sibling = head + 1 - 2 * core
    across = lax.rem(head + 2, 4)
    return head, seq, sibling, across


def head_partners():
    head, seq, sibling, across = head_places()
    return [((sibling, seq), None), ((across, seq), None)]


def seq_places():
    head, seq = lax.axis_index("head"), lax.axis_index("seq")
    return head, seq // SIDE, lax.rem(seq, SIDE)


def seq_partners(count):
    head, line, side = seq_places()
    return [
        ((head, line * SIDE + 1 - side), None),
        ((head, (line + 1) * SIDE + side), line < count - 1),
        ((head, (line - 1) * SIDE + side), line > 0),
    ]


def run_together(steps):
    steps = list(steps)
    while steps:
        alive = []
        for step in steps:
            try:
                next(step)
                alive.append(step)
            except StopIteration:
                pass
        steps = alive


def gather_head(own_ref, out_ref, local, send, arrive, pieces):
    head, seq, sibling, across = head_places()
    far = lax.rem(sibling + 2, 4)
    rows = own_ref.shape[0] // pieces
    keep = pltpu.make_async_copy(own_ref, out_ref.at[head], local.at[0])
    keep.start()

    def part(ref, piece):
        return ref.at[pl.ds(piece * rows, rows)]

    outgoing = []
    for piece in range(pieces):
        outgoing.append(
            remote(
                part(own_ref, piece),
                part(out_ref.at[head], piece),
                send.at[0, piece],
                arrive.at[0, piece],
                (across, seq),
            )
        )
    for piece in range(pieces):
        outgoing.append(
            remote(
                part(own_ref, piece),
                part(out_ref.at[head], piece),
                send.at[1, piece],
                arrive.at[1, piece],
                (sibling, seq),
            )
        )
    for copy in outgoing:
        copy.start()
    yield
    forwards = []
    for piece in range(pieces):
        outgoing[piece].wait_recv()
        forward = remote(
            part(out_ref.at[across], piece),
            part(out_ref.at[across], piece),
            send.at[2, piece],
            arrive.at[2, piece],
            (sibling, seq),
        )
        forward.start()
        forwards.append(forward)
        yield
    for copy in outgoing[pieces:] + forwards:
        copy.wait_recv()
    for copy in outgoing + forwards:
        copy.wait_send()
    keep.wait()


def scatter_head(source_at, out_ref, own, crossed, passed, local, send, arrive, pause=0):
    head, seq, sibling, across = head_places()
    far = lax.rem(sibling + 2, 4)
    loads = [
        pltpu.make_async_copy(source_at(target), own.at[slot], local.at[slot])
        for slot, target in enumerate((across, head))
    ]
    copies = [
        remote(source_at(target), crossed.at[slot], send.at[slot], arrive.at[slot], (sibling, seq))
        for slot, target in enumerate((far, sibling))
    ]
    for slot in range(2):
        copies[slot].start()
        loads[slot].start()
    yield
    loads[0].wait()
    copies[0].wait_recv()
    own[0] = (own[0].astype(f32) + crossed[0].astype(f32)).astype(own.dtype)
    onward = remote(own.at[0], passed, send.at[2], arrive.at[2], (across, seq))
    onward.start()
    for _ in range(1 + pause):
        yield
    loads[1].wait()
    copies[1].wait_recv()
    onward.wait_recv()
    total = own[1].astype(f32) + crossed[1].astype(f32) + passed[...].astype(f32)
    out_ref[...] = total.astype(out_ref.dtype)
    onward.wait_send()
    for copy in copies:
        copy.wait_send()


def gather_seq(own_ref, out_ref, local, side_send, side_arrive, line_send, line_arrive, count):
    head, line, side = seq_places()
    me = line * SIDE + side
    beside = (head, line * SIDE + 1 - side)
    ways = ((1, line < count - 1), (-1, line > 0))
    keep = pltpu.make_async_copy(own_ref, out_ref.at[me], local.at[0])
    keep.start()

    def along(source, block, way, step):
        slot = step if way > 0 else count + step
        return remote(
            source,
            out_ref.at[block],
            line_send.at[slot],
            line_arrive.at[slot],
            (head, (line + way) * SIDE + side),
        )

    def over(source, block, slot):
        return remote(source, out_ref.at[block], side_send.at[slot], side_arrive.at[slot], beside)

    for way, onward in ways:

        @pl.when(onward)
        def _(way=way):
            along(own_ref, me, way, 0).start()

    over(own_ref, me, 0).start()
    yield
    for step in range(1, count):
        for way, onward in ways:
            block = me - way * step * SIDE
            arrives = line >= step if way > 0 else line + step < count

            @pl.when(arrives)
            def _(way=way, onward=onward, block=block, step=step):
                landed = out_ref.at[block]
                slot = step if way > 0 else count + step
                remote(
                    landed, landed, line_send.at[slot - 1], line_arrive.at[slot - 1], beside
                ).wait_recv()

                @pl.when(onward)
                def _():
                    along(landed, block, way, step).start()

                over(landed, block, slot).start()

        yield
    over(own_ref, me, 0).wait()
    for way, onward in ways:

        @pl.when(onward)
        def _(way=way):
            along(own_ref, me, way, 0).wait_send()

    for step in range(1, count):
        for way, onward in ways:
            block = me - way * step * SIDE
            arrives = line >= step if way > 0 else line + step < count

            @pl.when(arrives)
            def _(way=way, onward=onward, block=block, step=step):
                landed = out_ref.at[block]
                slot = step if way > 0 else count + step
                over(landed, block, slot).wait()

                @pl.when(onward)
                def _():
                    along(landed, block, way, step).wait_send()

    keep.wait()


def scatter_seq(source_at, out_at, own, crossed, risen, fallen, local, sends, arrivals, count):
    head, line, side = seq_places()
    beside = (head, line * SIDE + 1 - side)
    pieces = own.shape[0]

    def targets(distance):
        if distance == 0:
            return [(line, None, 0)]
        return [
            (line - distance, line >= distance, -1),
            (line + distance, line + distance < count, 1),
        ]

    def load(piece, target):
        return pltpu.make_async_copy(
            source_at(target, side, piece), own.at[piece, target], local.at[piece, target]
        )

    def cross(piece, target):
        return remote(
            source_at(target, 1 - side, piece),
            crossed.at[piece, target],
            sends.at[0, piece, target],
            arrivals.at[0, piece, target],
            beside,
        )

    def onward(piece, target, way, arriving=False):
        landing = risen if way > 0 else fallen
        return remote(
            own.at[piece, target],
            landing.at[piece, target],
            sends.at[1, piece, target],
            arrivals.at[1 if way > 0 else 2, piece, target],
            beside if arriving else (head, (line + way) * SIDE + side),
        )

    def guarded(there, body):
        if there is None:
            body()
        else:
            pl.when(there)(body)

    def here(piece, target):
        load(piece, target).wait()
        total = own[piece, target].astype(f32)
        if crossed is not None:
            cross(piece, target).wait_recv()
            total += crossed[piece, target].astype(f32)
        return total

    def arrived(piece, target, way):
        landing = risen if way > 0 else fallen
        onward(piece, target, way, True).wait_recv()
        return landing[piece, target].astype(f32)

    for piece in range(pieces):
        for distance in range(count - 1, -1, -1):
            for target, there, _ in targets(distance):

                def begin(piece=piece, target=target):
                    if crossed is not None:
                        cross(piece, target).start()
                    load(piece, target).start()

                guarded(there, begin)
    yield
    for piece in range(pieces):
        for distance in range(count - 1, 0, -1):
            for target, there, way in targets(distance):
                first = line == count - 1 if way < 0 else line == 0

                @pl.when(jnp.logical_and(there, first))
                def _(piece=piece, target=target, way=way):
                    own[piece, target] = here(piece, target).astype(own.dtype)
                    onward(piece, target, way).start()

                @pl.when(jnp.logical_and(there, jnp.logical_not(first)))
                def _(piece=piece, target=target, way=way):
                    total = here(piece, target) + arrived(piece, target, way)
                    own[piece, target] = total.astype(own.dtype)
                    onward(piece, target, way).start()

            yield
        out = out_at(piece)

        @pl.when(line == 0)
        def _(piece=piece, out=out):
            out[...] = (here(piece, line) + arrived(piece, line, -1)).astype(out.dtype)

        @pl.when(line == count - 1)
        def _(piece=piece, out=out):
            out[...] = (here(piece, line) + arrived(piece, line, 1)).astype(out.dtype)

        @pl.when(jnp.logical_and(line > 0, line < count - 1))
        def _(piece=piece, out=out):
            total = here(piece, line) + arrived(piece, line, -1) + arrived(piece, line, 1)
            out[...] = total.astype(out.dtype)

        yield
    for piece in range(pieces):
        for distance in range(count - 1, -1, -1):
            for target, there, way in targets(distance):

                def finish(piece=piece, target=target, way=way):
                    if crossed is not None:
                        cross(piece, target).wait_send()
                    if way:
                        onward(piece, target, way).wait_send()

                guarded(there, finish)


ANY = pl.BlockSpec(memory_space=pl.ANY)
IN_VMEM = pl.BlockSpec(memory_space=pltpu.VMEM)
DMA = pltpu.SemaphoreType.DMA


def link_call(body, number, ins, outs, shapes, scratch, moved):
    return pl.pallas_call(
        body,
        in_specs=ins,
        out_specs=outs,
        out_shape=shapes,
        scratch_shapes=scratch,
        compiler_params=pltpu.CompilerParams(
            collective_id=number, has_side_effects=True, vmem_limit_bytes=VMEM_BYTES
        ),
        cost_estimate=pl.CostEstimate(flops=0, bytes_accessed=moved // 8, transcendentals=0),
    )


def gathered_head(value, number, pieces=4):
    count = lax.axis_size("head")
    if count != 4:
        return lax.all_gather(value, "head", axis=0, tiled=True)
    rows, width = value.shape

    def body(own_ref, out_ref, local, send, arrive):
        greet(head_partners())
        run_together([gather_head(own_ref, out_ref, local, send, arrive, pieces)])

    out = link_call(
        body,
        number,
        [ANY],
        ANY,
        shaped((count, rows, width), value.dtype),
        [DMA((1,)), DMA((3, pieces)), DMA((3, pieces))],
        60_000_000,
    )(value)
    return out.reshape(count * rows, width)


def gathered_sided(value, half, number, pieces=4, half_pieces=2):
    count = lax.axis_size("head")
    rows, width = value.shape

    def body(own_ref, half_ref, out_ref, beside_ref, landing, *sems):
        head, line, side = seq_places()
        beside = (head, line * SIDE + 1 - side)
        greet(head_partners() + [(beside, None)])

        def half_steps():
            copy = remote(half_ref, landing, sems[6].at[0], sems[6].at[1], beside)
            copy.start()
            yield
            yield
            copy.wait()
            yield from gather_head(landing, beside_ref, *sems[3:6], half_pieces)

        run_together([half_steps(), gather_head(own_ref, out_ref, *sems[:3], pieces)])

    out, beside = link_call(
        body,
        number,
        [ANY, ANY],
        [ANY, ANY],
        [
            shaped((count, rows, width), value.dtype),
            shaped((count, rows, half.shape[1]), value.dtype),
        ],
        [pltpu.VMEM(half.shape, half.dtype)]
        + [DMA((1,)), DMA((3, pieces)), DMA((3, pieces))]
        + [DMA((1,)), DMA((3, half_pieces)), DMA((3, half_pieces))]
        + [DMA((2,))],
        60_000_000,
    )(value, half)
    return out.reshape(count * rows, width), beside.reshape(count * rows, half.shape[1])


def gathered_seq(value, number):
    total = lax.axis_size("seq")
    count = total // SIDE
    rows, width = value.shape
    if total % SIDE or count < 2:
        return lax.all_gather(value, "seq")

    def body(own_ref, out_ref, *sems):
        greet(seq_partners(count))
        run_together([gather_seq(own_ref, out_ref, *sems, count)])

    return link_call(
        body,
        number,
        [ANY],
        ANY,
        shaped((total, rows, width), value.dtype),
        [DMA((1,))] + [DMA((2 * count,)) for _ in range(4)],
        120_000_000,
    )(value)


def head_scratch(rows, width):
    return [
        pltpu.VMEM((2, rows, width), bf16),
        pltpu.VMEM((2, rows, width), bf16),
        pltpu.VMEM((rows, width), bf16),
        DMA((2,)),
        DMA((3,)),
        DMA((3,)),
    ]


def seq_scratch(pieces, count, rows, width):
    return [pltpu.VMEM((pieces, count, rows, width), bf16) for _ in range(4)] + [
        DMA((pieces, count)),
        DMA((2, pieces, count)),
        DMA((3, pieces, count)),
    ]


def scattered_head(value, number, pieces=2):
    count = lax.axis_size("head")
    if count != 4:
        return scattered(value, "head")
    rows, width = value.shape[0] // count, value.shape[1] // pieces

    def body(source, out, *rest):
        greet(head_partners())
        steps = []
        for piece in range(pieces):
            span = pl.ds(piece * width, width)

            def source_at(target, span=span):
                return source.at[pl.ds(pl.multiple_of(target * rows, rows), rows), span]

            steps.append(
                scatter_head(source_at, out.at[:, span], *rest[6 * piece : 6 * piece + 6])
            )
        run_together(steps)

    return link_call(
        body,
        number,
        [ANY],
        IN_VMEM,
        shaped((rows, value.shape[1]), f32),
        head_scratch(rows, width) * pieces,
        60_000_000,
    )(value)


def scattered_seq(value, number, pieces=2):
    total = lax.axis_size("seq")
    count = total // SIDE
    if total % SIDE or count < 2:
        return scattered(value, "seq")
    rows, width = value.shape[0] // total, value.shape[1] // pieces

    def body(source, out, *rest):
        greet(seq_partners(count))

        def source_at(target, side, piece):
            begin = pl.multiple_of((target * SIDE + side) * rows, rows)
            return source.at[pl.ds(begin, rows), pl.ds(piece * width, width)]

        def out_at(piece):
            return out.at[:, pl.ds(piece * width, width)]

        run_together([scatter_seq(source_at, out_at, *rest, count)])

    return link_call(
        body,
        number,
        [ANY],
        IN_VMEM,
        shaped((rows, value.shape[1]), f32),
        seq_scratch(pieces, count, rows, width),
        120_000_000,
    )(value)


def product_steps(left_hbm, right_hbm, out_refs, picks, lefts, rights, tiles, load, store, per_round):
    loads = [
        pltpu.make_async_copy(ref, held, load.at[index])
        for index, (ref, held) in enumerate(zip(left_hbm + right_hbm, lefts + rights))
    ]
    for copy in loads:
        copy.start()
    yield
    for copy in loads:
        copy.wait()
    units, width = tiles.shape[1:]
    block = units // 4 if units % 64 == 0 else units
    span = 512
    stores = []
    done = 0
    for index, pick in enumerate(picks):
        for begin in range(0, width, span):
            columns = pl.ds(begin, span)

            def one(part, carry, index=index, pick=pick, columns=columns):
                rows = pl.ds(pl.multiple_of(part * block, block), block)
                tiles[index, rows, columns] = mm(
                    lefts[index][rows, :], rights[pick][:, columns]
                ).astype(tiles.dtype)
                return carry

            lax.fori_loop(0, units // block, one, 0)
            done += 1
            if done % per_round == 0:
                yield
        copy = pltpu.make_async_copy(tiles.at[index], out_refs[index], store.at[index])
        copy.start()
        stores.append(copy)
    for copy in stores:
        copy.wait()


def scattered_seq_products(value, lefts, rights, picks, number, pieces=2):
    total = lax.axis_size("seq")
    count = total // SIDE
    rows, width = value.shape[0] // total, value.shape[1] // pieces
    units, depth = lefts[0].shape
    breadth = rights[0].shape[1]
    n_left, n_right = len(lefts), len(rights)
    held = 4 * value.size // SIDE + n_left * units * (depth + breadth) + n_right * rights[0].size
    if 2 * held > VMEM_BYTES:
        products = [mm(left, rights[pick]).astype(bf16) for left, pick in zip(lefts, picks)]
        return scattered_seq(value, number, pieces), products

    def body(source, *rest):
        left_hbm, rest = rest[:n_left], rest[n_left:]
        right_hbm, rest = rest[:n_right], rest[n_right:]
        out, out_refs, rest = rest[0], rest[1 : 1 + n_left], rest[1 + n_left :]
        link, rest = rest[:7], rest[7:]
        left_held, rest = rest[:n_left], rest[n_left:]
        right_held, rest = rest[:n_right], rest[n_right:]
        greet(seq_partners(count))

        def source_at(target, side, piece):
            begin = pl.multiple_of((target * SIDE + side) * rows, rows)
            return source.at[pl.ds(begin, rows), pl.ds(piece * width, width)]

        def out_at(piece):
            return out.at[:, pl.ds(piece * width, width)]

        run_together(
            [
                scatter_seq(source_at, out_at, *link, count),
                product_steps(
                    left_hbm, right_hbm, out_refs, picks, left_held, right_held, *rest, 2
                ),
            ]
        )

    outs = link_call(
        body,
        number,
        [ANY] * (1 + n_left + n_right),
        [IN_VMEM] + [ANY] * n_left,
        [shaped((rows, value.shape[1]), f32)]
        + [shaped((units, breadth), bf16) for _ in lefts],
        seq_scratch(pieces, count, rows, width)
        + [pltpu.VMEM((units, depth), bf16) for _ in lefts]
        + [pltpu.VMEM((depth, breadth), bf16) for _ in rights]
        + [
            pltpu.VMEM((n_left, units, breadth), bf16),
            DMA((n_left + n_right,)),
            DMA((n_left,)),
        ],
        120_000_000,
    )(value, *lefts, *rights)
    return outs[0], list(outs[1:])


def gathered_swapped(ends, d_gate, number):
    total = lax.axis_size("seq")
    count = total // SIDE

    def body(ends_ref, gate_ref, ends_out, gate_out, *rest):
        head, line, side = seq_places()
        beside = (head, line * SIDE + 1 - side)
        greet(seq_partners(count))

        def swap_steps():
            yield
            yield
            copy = remote(gate_ref, gate_out, rest[5].at[0], rest[5].at[1], beside)
            copy.start()
            for _ in range(count):
                yield
            copy.wait()

        run_together([gather_seq(ends_ref, ends_out, *rest[:5], count), swap_steps()])

    return link_call(
        body,
        number,
        [ANY] * 2,
        [ANY] * 2,
        [
            shaped((total,) + ends.shape, ends.dtype),
            shaped(d_gate.shape, d_gate.dtype),
        ],
        [DMA((1,))] + [DMA((2 * count,)) for _ in range(4)] + [DMA((2,))],
        150_000_000,
    )(ends, d_gate)


def scattered_last(qkv, gate, normed, hat, mlp, small, gain_rows, number, pieces=4, gate_pieces=2):
    total, heads = lax.axis_size("seq"), lax.axis_size("head")
    count = total // SIDE
    rows, width = qkv.shape[0] // total, qkv.shape[1] // pieces
    gate_width = gate.shape[1] // gate_pieces
    own_rows = normed.shape[0] // heads
    units, slices = mlp[0].shape[0], mlp[0].shape[1] // heads
    small_rows = small.shape[0]

    def body(qkv_ref, gate_ref, normed_ref, hat_ref, small_ref, *rest):
        mlp_refs, rest = rest[: len(mlp)], rest[len(mlp) :]
        qkv_out, gate_out, normed_out, small_out, rest = rest[0], rest[1], rest[2], rest[3], rest[4:]
        mlp_outs, rest = rest[: len(mlp)], rest[len(mlp) :]
        greet(head_partners() + seq_partners(count))

        def qkv_at(target, side, piece):
            begin = pl.multiple_of((target * SIDE + side) * rows, rows)
            return qkv_ref.at[pl.ds(begin, rows), pl.ds(piece * width, width)]

        def gate_at(target, side, piece):
            begin = pl.multiple_of(target * rows, rows)
            return gate_ref.at[pl.ds(begin, rows), pl.ds(piece * gate_width, gate_width)]

        def normed_at(target):
            return normed_ref.at[pl.ds(pl.multiple_of(target * own_rows, own_rows), own_rows)]

        def normed_steps(four, own, local, *sems):
            yield from scatter_head(normed_at, normed_out, *rest[13:19], 1)
            own[...] = small_ref[...]
            product = jnp.sum(normed_out[...] * hat_ref[...], axis=0, keepdims=True)
            for row in range(product.shape[1] // 128):
                own[row : row + 1] = product[:, row * 128 : (row + 1) * 128]
            yield
            yield from gather_head(own, four, sems[0], sems[1], sems[2], 1)
            own[:gain_rows] = jnp.sum(four[:, :gain_rows], axis=0)
            for step in gather_seq(own, small_out, local, *sems[3:7], count):
                for _ in range(3):
                    yield

        steps = [
            normed_steps(*rest[19:29]),
            scatter_seq(
                gate_at,
                lambda piece: gate_out.at[:, pl.ds(piece * gate_width, gate_width)],
                rest[7],
                None,
                *rest[8:13],
                count,
            ),
            scatter_seq(
                qkv_at,
                lambda piece: qkv_out.at[:, pl.ds(piece * width, width)],
                *rest[:7],
                count,
            ),
        ]
        for index, (ref, out) in enumerate(zip(mlp_refs, mlp_outs)):

            def mlp_at(target, ref=ref):
                return ref.at[:, pl.ds(pl.multiple_of(target * slices, slices), slices)]

            begin = 29 + 6 * index
            steps.append(
                scatter_head(mlp_at, out, *rest[begin : begin + 6], 5 + 3 * index)
            )
        run_together(steps)

    line_scratch = seq_scratch(gate_pieces, count, rows, gate_width)
    outs = link_call(
        body,
        number,
        [ANY] * 3 + [IN_VMEM] * 2 + [ANY] * len(mlp),
        [IN_VMEM] * (4 + len(mlp)),
        [
            shaped((rows, qkv.shape[1]), bf16),
            shaped((rows, gate.shape[1]), bf16),
            shaped((own_rows, normed.shape[1]), f32),
            shaped((total, small_rows, small.shape[1]), f32),
        ]
        + [shaped((units, slices), bf16) for _ in mlp],
        seq_scratch(pieces, count, rows, width)
        + line_scratch[1:]
        + head_scratch(own_rows, normed.shape[1])
        + [
            pltpu.VMEM((heads, small_rows, small.shape[1]), f32),
            pltpu.VMEM((small_rows, small.shape[1]), f32),
            DMA((1,)),
            DMA((1,)),
            DMA((3, 1)),
            DMA((3, 1)),
        ]
        + [DMA((2 * count,)) for _ in range(4)]
        + head_scratch(units, slices) * len(mlp),
        250_000_000,
    )(qkv, gate, normed, hat, small, *mlp)
    return outs[0], outs[1], outs[2], outs[3], list(outs[4:])


def side_columns(value, side, rows):
    count = value.shape[1] // (rows * SIDE)
    return jnp.concatenate(
        [
            lax.dynamic_slice_in_dim(value, (place * SIDE + side) * rows, rows, 1)
            for place in range(count)
        ],
        axis=1,
    )


def swapped(value):
    count = lax.axis_size("seq")
    return lax.ppermute(value, "seq", [(place, place ^ 1) for place in range(count)])


def silu_slope(tensor):
    sigmoid_part = jax.nn.sigmoid(tensor)
    return sigmoid_part * (1.0 + tensor * (1.0 - sigmoid_part))


def gathered(value, axis):
    return lax.all_gather(value, axis, axis=0, tiled=True)


def scattered(value, axis, dimension=0):
    return lax.psum_scatter(
        value.astype(bf16), axis, scatter_dimension=dimension, tiled=True
    ).astype(f32)


def on_device(
    block_in,
    out_cot,
    gain_one,
    qkv_weight,
    conv_weight,
    gate_weight,
    gain_out,
    out_weight,
    gain_two,
    mlp_gate,
    mlp_up,
    mlp_down,
    decay_code,
    beta_code,
):
    span_rows = decay_code.shape[0]
    width, heads, inner = qkv_weight.shape
    total_len = span_rows * lax.axis_size("seq")
    lead_rows = conv_weight.shape[0] - 1
    input_f = block_in.astype(f32)
    gain_first = gain_one.astype(f32)
    gain_second = gain_two.astype(f32)
    gain_head = gain_out.reshape(1, -1)
    taps = conv_weight.reshape(conv_weight.shape[0], heads * inner)
    out_flat = out_weight.reshape(heads * DV, width)
    columns, run_rows = token_columns(decay_code, beta_code, total_len)

    cot_all = gathered(out_cot, "seq")
    seq_count, head_count = lax.axis_size("seq"), lax.axis_size("head")
    seq_at, head_at = lax.axis_index("seq"), lax.axis_index("head")
    side = lax.rem(seq_at, SIDE)
    slice_rows = width // seq_count
    scale_own = rms_scale(input_f)
    hat_own = input_f * scale_own
    normed_own = (hat_own * gain_first).astype(bf16)
    normed_first, normed_side = gathered_sided(
        normed_own, side_columns(normed_own, 1 - side, slice_rows), 1
    )
    mixed_in = jnp.einsum(
        "td,dhc->htc", normed_first, qkv_weight, preferred_element_type=f32
    ).astype(bf16)
    tail_in = passed_along(mixed_in[:, span_rows - 8 :], "seq", 1)
    tail_in = jnp.where(jnp.arange(8)[:, None] >= 8 - lead_rows, tail_in.astype(f32), 0.0)
    solve, score, fresh, reach, inner_part, turn, local_states, piece_end = run_local_forward(
        mixed_in, tail_in, taps, columns, run_rows, heads
    )
    ends = gathered_seq(piece_end.reshape(-1, DV + DK), 2).reshape(-1, heads, DK, DV + DK)
    gate_pre = jnp.einsum("td,dhv->htv", normed_first, gate_weight, preferred_element_type=f32)
    states, core, branch = run_finish_forward(
        ends, local_states, reach, inner_part, gate_pre, gain_head
    )
    branch, cot_all = lax.optimization_barrier((branch, cot_all))
    branch_side = swapped(branch)
    middle = input_f + scattered_head(mm(branch, out_flat).astype(bf16), 3)
    scale_two = rms_scale(middle)
    hat_two = middle * scale_two
    normed_two = (hat_two * gain_second).astype(bf16)

    rows_out = gathered_seq(normed_two, 4).reshape(-1, width)
    cot_f = out_cot.astype(f32)
    gate_units, up_units = mlp_gate.T, mlp_up.T
    gate_part = mm_nt(gate_units, rows_out)
    up_part = mm_nt(up_units, rows_out)
    d_hidden = mm_nt(mlp_down, cot_all)
    hidden = (jax.nn.silu(gate_part) * up_part).astype(bf16)
    d_gate_mlp = (d_hidden * up_part * silu_slope(gate_part)).astype(bf16)
    d_up_mlp = (d_hidden * jax.nn.silu(gate_part)).astype(bf16)
    d_rows = (mm_tn(d_gate_mlp, gate_units) + mm_tn(d_up_mlp, up_units)).astype(bf16)
    d_normed_two, (grad_mgate, grad_mup, grad_down) = scattered_seq_products(
        d_rows, [d_gate_mlp, d_up_mlp, hidden], [rows_out, cot_all], [0, 0, 1], 5
    )
    gain_two_part = jnp.sum(d_normed_two * hat_two, 0)
    e_two = d_normed_two * gain_second
    d_middle = cot_f + scale_two * (
        e_two - hat_two * jnp.mean(e_two * hat_two, axis=-1, keepdims=True)
    )
    hidden, d_middle = lax.optimization_barrier((hidden, d_middle))
    mlp_part, d_middle = lax.optimization_barrier(
        (mm_tn(hidden, mlp_down).astype(bf16), d_middle)
    )
    mlp_out = scattered(mlp_part, "seq")
    d_mix = d_middle.astype(bf16)
    d_mix_all, d_mix_side = gathered_sided(d_mix, side_columns(d_mix, 1 - side, slice_rows), 6)
    d_branch = mm_nt(d_mix_all, out_flat)
    out_half = (
        mm_tn(side_columns(d_mix_all, side, slice_rows), branch) + mm_tn(d_mix_side, branch_side)
    ).astype(bf16)
    d_core, d_gate_low, gain_out_part, local_grads, grad_end = run_local_backward(
        d_branch, core, gate_pre, gain_head, reach, turn
    )
    out_half, grad_end = lax.optimization_barrier((out_half, grad_end))
    grad_out_s = lax.psum_scatter(
        out_half,
        "seq",
        scatter_dimension=0,
        axis_index_groups=[
            [place * SIDE + across for place in range(seq_count // SIDE)] for across in range(SIDE)
        ],
        tiled=True,
    )
    grad_ends, d_gate_side = gathered_swapped(grad_end.reshape(-1, DV), d_gate_low, 7)
    grad_ends = grad_ends.reshape(-1, heads, DK, DV)
    mlp_out, grad_ends = lax.optimization_barrier((mlp_out, grad_ends))
    output = (middle + mlp_out).astype(bf16)
    d_mixed, d_tail, d_lead, grad_conv = run_finish_backward(
        ends,
        grad_ends,
        mixed_in,
        tail_in,
        taps,
        columns,
        run_rows,
        solve,
        score,
        fresh,
        states,
        d_core,
        local_grads,
    )
    from_next = passed_along(d_lead[:lead_rows], "seq", -1)
    d_tail = d_tail.at[8 - lead_rows :].add(from_next).astype(bf16)
    d_mixed = lax.dynamic_update_slice(d_mixed, d_tail, (span_rows - 8, 0))
    d_normed_part = jnp.einsum(
        "thc,dhc->td",
        d_mixed.reshape(span_rows, heads, inner),
        qkv_weight,
        preferred_element_type=f32,
    ) + jnp.einsum(
        "thv,dhv->td",
        d_gate_low.reshape(span_rows, heads, DV),
        gate_weight,
        preferred_element_type=f32,
    )
    grad_qkv = mm_tn(normed_first, d_mixed).astype(bf16)
    grad_gate = (
        mm_tn(side_columns(normed_first, side, slice_rows), d_gate_low)
        + mm_tn(normed_side, d_gate_side)
    ).astype(bf16)

    gains = jnp.concatenate([jnp.zeros_like(gain_two_part), gain_two_part, gain_out_part.reshape(-1)])
    gain_rows = -(-gains.shape[0] // 1024) * 8
    gains = jnp.pad(gains, (0, gain_rows * 128 - gains.shape[0])).reshape(gain_rows, 128)
    small = jnp.concatenate([gains, grad_conv.reshape(-1, 128)])
    grad_qkv_s, grad_gate_s, d_normed_one, small_all, (grad_mgate_t, grad_mup_t, grad_down_h) = (
        scattered_last(
            grad_qkv,
            grad_gate,
            d_normed_part.astype(bf16),
            hat_own,
            [grad_mgate, grad_mup, grad_down],
            small,
            gain_rows,
            8,
        )
    )
    e_one = d_normed_one * gain_first
    d_input = (
        d_middle + scale_own * (e_one - hat_own * jnp.mean(e_one * hat_own, axis=-1, keepdims=True))
    ).astype(bf16)

    small_sum = jnp.sum(small_all, axis=0)
    gains = small_sum[:gain_rows].reshape(-1)

    def own_slice(begin, length):
        length = length // (seq_count * head_count)
        return lax.dynamic_slice(
            gains, (begin + (head_at * seq_count + seq_at) * length,), (length,)
        )

    grad_conv_s = lax.dynamic_slice_in_dim(
        small_sum[gain_rows:].reshape(-1, heads, inner),
        seq_at * (inner // seq_count),
        inner // seq_count,
        2,
    )
    return (
        output,
        d_input,
        own_slice(0, width),
        grad_qkv_s.astype(f32).reshape(-1, heads, inner),
        grad_conv_s,
        grad_gate_s.astype(f32).reshape(-1, heads, DV),
        own_slice(2 * width, DV),
        grad_out_s.astype(f32).T.reshape(heads, DV, -1),
        own_slice(width, width),
        grad_mgate_t.astype(f32).T,
        grad_mup_t.astype(f32).T,
        grad_down_h.astype(f32),
    )


def solution(mesh):
    in_specs = (
        P(("seq", "head"), None),
        P(("seq", "head"), None),
        P(),
        P(None, "head", None),
        P(None, "head", None),
        P(None, "head", None),
        P(),
        P("head", None, None),
        P(),
        P(None, "seq"),
        P(None, "seq"),
        P("seq", None),
        P("seq", "head"),
        P("seq", "head"),
    )
    out_specs = (
        P(("seq", "head"), None),
        P(("seq", "head"), None),
        P(("head", "seq")),
        P("seq", "head", None),
        P(None, "head", "seq"),
        P("seq", "head", None),
        P(("head", "seq")),
        P("head", None, "seq"),
        P(("head", "seq")),
        P("head", "seq"),
        P("head", "seq"),
        P("seq", "head"),
    )
    return jax.shard_map(
        on_device, mesh=mesh, in_specs=in_specs, out_specs=out_specs, check_vma=False
    )
```

```python
import functools
import math

import jax
import jax.numpy as jnp
from jax import lax
from jax.experimental import pallas as pl
from jax.experimental.pallas import tpu as pltpu
from jax.sharding import PartitionSpec as P

DK = 128
DV = 256
STRETCH = 64
GROUP = 4 * STRETCH
INNER = 2 * DK + DV
BETA, GAMMA, BETA_GAMMA, TAIL, LAST, RUN = range(6)

epsilon = 1e-06
bf16 = jnp.bfloat16
f32 = jnp.float32
VMEM_BYTES = 56 * 2**20
HOLD = 4


def passed_along(value, axis, steps):
    count = lax.axis_size(axis)
    first, last = (max(0, -steps), min(count, count - steps))
    return lax.ppermute(value, axis, [(source, source + steps) for source in range(first, last)])


def rms_scale(tensor):
    return lax.rsqrt(jnp.mean(tensor * tensor, axis=-1, keepdims=True) + epsilon)


def log_rates(decay_code, total_len):
    code_level = decay_code.astype(f32) / 1023.0
    smooth = -jnp.exp(-code_level * math.log(total_len / 32.0)) / 32.0
    return jnp.where(decay_code == 1024, -0.25, smooth)


def token_columns(decay_code, beta_code, total_len):
    rows, heads = decay_code.shape
    rates = log_rates(decay_code, total_len)
    run = jnp.einsum(
        "ij,bjh->bih",
        jnp.tril(jnp.ones((STRETCH, STRETCH), f32)),
        rates.reshape(rows // STRETCH, STRETCH, heads),
        precision=lax.Precision.HIGHEST,
    )
    last = jnp.broadcast_to(run[:, -1:], run.shape).reshape(rows, heads)
    run = run.reshape(rows, heads)
    beta = 0.5 + beta_code.astype(f32) / 512.0
    gamma = jnp.exp(run)
    columns = jnp.concatenate(
        [beta, gamma, beta * gamma, jnp.exp(last - run), jnp.exp(last), run], axis=1
    )
    columns = jnp.pad(columns, ((0, 0), (0, 128 - columns.shape[1])))
    run_rows = jnp.pad(run.T, ((0, 8 - heads % 8), (0, 0)))
    return columns, run_rows


def mm(left, right):
    return jnp.dot(left, right, preferred_element_type=f32)


def mm_nt(left, right):
    return lax.dot_general(left, right, (((1,), (1,)), ((), ())), preferred_element_type=f32)


def mm_tn(left, right):
    return lax.dot_general(left, right, (((0,), (0,)), ((), ())), preferred_element_type=f32)


def column(columns_ref, kind, head, heads):
    block = columns_ref[...]
    lanes = lax.broadcasted_iota(jnp.int32, block.shape, 1)
    return jnp.sum(jnp.where(lanes == kind * heads + head, block, 0.0), axis=1, keepdims=True)


def square_ids():
    return (
        lax.broadcasted_iota(jnp.int32, (GROUP, GROUP), 0),
        lax.broadcasted_iota(jnp.int32, (GROUP, GROUP), 1),
    )


def convolved(padded_ref, tail_ref, mixed_ref, taps_ref):
    rows = mixed_ref.shape[0]
    count = taps_ref.shape[0]
    padded_ref[0:8, :] = tail_ref[...]
    padded_ref[8 : 8 + rows, :] = mixed_ref[...].astype(f32)
    taps = taps_ref[...].astype(f32)
    start = 9 - count
    total = taps[0:1] * padded_ref[start : start + rows, :]
    for tap in range(1, count):
        total += taps[tap : tap + 1] * padded_ref[start + tap : start + tap + rows, :]
    return total


def chunk_masks_stack(transposed):
    lanes = lax.broadcasted_iota(jnp.int32, transposed.shape, 1) // STRETCH
    parts = [jnp.where(lanes == part, transposed, 0.0) for part in range(GROUP // STRETCH)]
    return jnp.concatenate(parts, axis=0).astype(bf16)


def local_forward(
    mixed_ref,
    tail_ref,
    taps_ref,
    columns_ref,
    run_rows_ref,
    solve_ref,
    score_ref,
    fresh_ref,
    reach_ref,
    inner_ref,
    turn_ref,
    local_ref,
    end_ref,
    padded,
    turn_t,
    offsets,
):
    head = pl.program_id(0)
    heads = pl.num_programs(0)
    rows = mixed_ref.shape[0]
    per_group = GROUP // STRETCH
    stretches = rows // STRETCH
    total = convolved(padded, tail_ref, mixed_ref, taps_ref)
    activated = total * jax.nn.sigmoid(total)
    raw_q, raw_k = activated[:, :DK], activated[:, DK : 2 * DK]
    queries = raw_q * (
        lax.rsqrt(jnp.sum(raw_q * raw_q, axis=1, keepdims=True) + epsilon) * DK ** (-0.5)
    )
    keys = raw_k * lax.rsqrt(jnp.sum(raw_k * raw_k, axis=1, keepdims=True) + epsilon)
    values = activated[:, 2 * DK :]
    beta = column(columns_ref, BETA, head, heads)
    gamma = column(columns_ref, GAMMA, head, heads)
    beta_gamma = column(columns_ref, BETA_GAMMA, head, heads)
    tail_decay = column(columns_ref, TAIL, head, heads)
    last = column(columns_ref, LAST, head, heads)
    run = column(columns_ref, RUN, head, heads)
    row_id, col_id = square_ids()
    same = row_id // STRETCH == col_id // STRETCH
    causal = same & (row_id >= col_id)
    diagonal = row_id == col_id
    eye = jnp.where(
        lax.broadcasted_iota(jnp.int32, (DK, DK), 0) == lax.broadcasted_iota(jnp.int32, (DK, DK), 1),
        1.0,
        0.0,
    )
    for group in range(rows // GROUP):
        span = slice(group * GROUP, (group + 1) * GROUP)
        key_b = keys[span].astype(bf16)
        query_b = queries[span].astype(bf16)
        gaps = run[span] - run_rows_ref[pl.ds(head, 1), span]
        within = jnp.exp(jnp.where(causal, gaps, -1e30))
        lower = jnp.where(diagonal, 0.0, beta[span] * within * mm_nt(key_b, key_b))
        solve = jnp.where(diagonal, 1.0, jnp.where(row_id // 2 == col_id // 2, -lower, 0.0))
        size = 2
        while size < STRETCH:
            crossing = (row_id // (2 * size) == col_id // (2 * size)) & (
                row_id // size != col_id // size
            )
            solve_b = solve.astype(bf16)
            half = mm(solve_b, jnp.where(crossing, lower, 0.0).astype(bf16))
            solve = solve - mm(half.astype(bf16), solve_b)
            size *= 2
        solve_b = solve.astype(bf16)
        right = jnp.concatenate([beta[span] * values[span], beta_gamma[span] * keys[span]], axis=1)
        fresh_b = mm(solve_b, right.astype(bf16)).astype(bf16)
        score_b = (within * mm_nt(query_b, key_b)).astype(bf16)
        scored = mm(score_b, fresh_b)
        solve_ref[group] = solve_b
        score_ref[group] = score_b
        fresh_ref[span, :] = fresh_b
        inner_ref[span, :] = scored[:, :DV]
        reach_ref[span, :] = (gamma[span] * queries[span] - scored[:, DV:]).astype(bf16)
        tail_keys = (tail_decay[span] * keys[span]).T
        moved = mm(chunk_masks_stack(tail_keys), fresh_b)
        for part in range(per_group):
            at = group * per_group + part
            block = moved[part * DK : (part + 1) * DK]
            stay = last[at * STRETCH : at * STRETCH + 1]
            turned = stay * eye - block[:, DV:]
            turn_t[head, at] = turned.astype(bf16)
            turn_ref[at] = turned.T.astype(bf16)
            offsets[head, at] = block[:, :DV]

    @pl.when(head == heads - 1)
    def _():
        states = [
            jnp.concatenate([jnp.zeros((DK, DV), f32), eye], axis=1)
            for _ in range(local_ref.shape[0])
        ]
        for at in range(stretches):
            for h in range(len(states)):
                state_b = states[h].astype(bf16)
                local_ref[h, at] = state_b
                moved = mm(turn_t[h, at], state_b)
                states[h] = jnp.concatenate(
                    [moved[:, :DV] + offsets[h, at], moved[:, DV:]], axis=1
                )
        for h in range(len(states)):
            end_ref[h] = states[h].astype(bf16)


def finish_forward(
    ends_ref, local_ref, reach_ref, inner_ref, gate_ref, gain_ref, state_ref, core_ref, branch_ref, start
):
    head = pl.program_id(0)
    heads, stretches = start.shape[0], local_ref.shape[0]

    @pl.when(head == 0)
    def _():
        start[...] = jnp.zeros_like(start)

        def one(source, carry):
            for h in range(heads):
                start[h] = (
                    mm(ends_ref[source, h, :, DV:], start[h].astype(bf16))
                    + ends_ref[source, h, :, :DV].astype(f32)
                )
            return carry

        lax.fori_loop(0, lax.axis_index("seq"), one, 0)

    start_b = start[head].astype(bf16)
    cores = []
    for at in range(stretches):
        state_b = (
            local_ref[at, :, :DV].astype(f32) + mm(local_ref[at, :, DV:], start_b)
        ).astype(bf16)
        state_ref[at] = state_b
        span = slice(at * STRETCH, (at + 1) * STRETCH)
        cores.append(inner_ref[span, :] + mm(reach_ref[span, :], state_b))
    core = jnp.concatenate(cores, axis=0)
    core_ref[...] = core
    gate = gate_ref[...]
    branch = core * rms_scale(core) * gain_ref[...].astype(f32) * (gate * jax.nn.sigmoid(gate))
    branch_ref[...] = branch.astype(bf16)


def local_backward(
    d_branch_ref,
    core_ref,
    gate_ref,
    gain_ref,
    reach_ref,
    turn_ref,
    d_core_ref,
    d_gate_ref,
    gain_part_ref,
    local_ref,
    end_ref,
    pulls,
):
    head = pl.program_id(0)
    heads = pl.num_programs(0)
    rows = core_ref.shape[0]
    per_group = GROUP // STRETCH
    stretches = rows // STRETCH
    core = core_ref[...]
    gate = gate_ref[...]
    gain = gain_ref[...].astype(f32)
    d_branch = d_branch_ref[...]
    scale = rms_scale(core)
    nhat = core * scale
    sig = jax.nn.sigmoid(gate)
    gated = d_branch * (gate * sig)

    @pl.when(head == 0)
    def _():
        gain_part_ref[...] = jnp.zeros_like(gain_part_ref)

    gain_part_ref[...] += jnp.sum(gated * nhat, axis=0, keepdims=True)
    f = gated * gain
    d_core = scale * (f - nhat * jnp.mean(f * nhat, axis=1, keepdims=True))
    d_gate_ref[...] = (d_branch * nhat * gain * sig * (1.0 + gate * (1.0 - sig))).astype(bf16)
    d_core_b = d_core.astype(bf16)
    d_core_ref[...] = d_core_b
    for group in range(rows // GROUP):
        span = slice(group * GROUP, (group + 1) * GROUP)
        pulled = mm(chunk_masks_stack(reach_ref[span, :].astype(f32).T), d_core_b[span])
        for part in range(per_group):
            pulls[head, group * per_group + part] = pulled[part * DK : (part + 1) * DK]

    @pl.when(head == heads - 1)
    def _():
        eye = jnp.where(
            lax.broadcasted_iota(jnp.int32, (DK, DK), 0)
            == lax.broadcasted_iota(jnp.int32, (DK, DK), 1),
            1.0,
            0.0,
        )
        grads = [
            jnp.concatenate([jnp.zeros((DK, DV), f32), eye], axis=1)
            for _ in range(local_ref.shape[0])
        ]
        for at in reversed(range(stretches)):
            for h in range(len(grads)):
                grad_b = grads[h].astype(bf16)
                local_ref[h, at] = grad_b
                moved = mm(turn_ref[h, at], grad_b)
                grads[h] = jnp.concatenate([moved[:, :DV] + pulls[h, at], moved[:, DV:]], axis=1)
        for h in range(len(grads)):
            end_ref[h] = grads[h][:, :DV].astype(bf16)


def finish_backward(
    ends_ref,
    grad_ends_ref,
    mixed_ref,
    tail_ref,
    taps_ref,
    columns_ref,
    run_rows_ref,
    solve_ref,
    score_ref,
    fresh_ref,
    state_ref,
    d_core_ref,
    local_ref,
    d_mixed_ref,
    tail_out_ref,
    lead_ref,
    grad_taps_ref,
    padded,
    spread,
    end,
):
    head = pl.program_id(0)
    heads = pl.num_programs(0)
    rows = mixed_ref.shape[0]
    per_group = GROUP // STRETCH

    @pl.when(head == 0)
    def _():
        end[...] = jnp.zeros_like(end)
        count = ends_ref.shape[0]

        def one(turn, carry):
            source = count - 1 - turn
            for h in range(end.shape[0]):
                end[h] = (
                    mm_tn(ends_ref[source, h, :, DV:], end[h].astype(bf16))
                    + grad_ends_ref[source, h].astype(f32)
                )
            return carry

        lax.fori_loop(0, count - 1 - lax.axis_index("seq"), one, 0)

    end_b = end[head].astype(bf16)
    total = convolved(padded, tail_ref, mixed_ref, taps_ref)
    sig = jax.nn.sigmoid(total)
    activated = total * sig
    raw_q, raw_k = activated[:, :DK], activated[:, DK : 2 * DK]
    scale_q = lax.rsqrt(jnp.sum(raw_q * raw_q, axis=1, keepdims=True) + epsilon)
    scale_k = lax.rsqrt(jnp.sum(raw_k * raw_k, axis=1, keepdims=True) + epsilon)
    unit_q = raw_q * scale_q
    keys = raw_k * scale_k
    beta = column(columns_ref, BETA, head, heads)
    gamma = column(columns_ref, GAMMA, head, heads)
    beta_gamma = column(columns_ref, BETA_GAMMA, head, heads)
    tail_decay = column(columns_ref, TAIL, head, heads)
    run = column(columns_ref, RUN, head, heads)
    row_id, col_id = square_ids()
    causal = (row_id // STRETCH == col_id // STRETCH) & (row_id >= col_id)
    diagonal = row_id == col_id
    d_queries, d_keys, d_values = [], [], []
    for group in range(rows // GROUP):
        span = slice(group * GROUP, (group + 1) * GROUP)
        key_b = keys[span].astype(bf16)
        query_b = (unit_q[span] * DK ** (-0.5)).astype(bf16)
        tail_keys = (tail_decay[span] * keys[span]).astype(bf16)
        d_core_b = d_core_ref[span, :]
        grad_bs, from_grad, fresh_parts, from_state = [], [], [], []
        for part in range(per_group):
            at = group * per_group + part
            own = slice(part * STRETCH, (part + 1) * STRETCH)
            rows_at = slice(at * STRETCH, (at + 1) * STRETCH)
            grad_b = (
                local_ref[at, :, :DV].astype(f32) + mm(local_ref[at, :, DV:], end_b)
            ).astype(bf16)
            grad_bs.append(grad_b)
            from_grad.append(mm(tail_keys[own], grad_b))
            fresh_parts.append(mm(fresh_ref[rows_at, DV:], state_ref[at]))
            from_state.append(mm_nt(d_core_b[own], state_ref[at]))
        d_fresh = mm_tn(score_ref[group], d_core_b) + jnp.concatenate(from_grad, axis=0)
        d_right = mm_tn(solve_ref[group], d_fresh.astype(bf16))
        d_right_b = d_right.astype(bf16)
        fresh = fresh_ref[span, :DV].astype(f32) - jnp.concatenate(fresh_parts, axis=0)
        fresh_b = fresh.astype(bf16)
        gaps = run[span] - run_rows_ref[pl.ds(head, 1), span]
        within = jnp.exp(jnp.where(causal, gaps, -1e30))
        d_score = (within * mm_nt(d_core_b, fresh_b)).astype(bf16)
        d_lower = jnp.where(
            diagonal, 0.0, -beta[span] * within * mm_nt(d_right_b, fresh_b)
        ).astype(bf16)
        state_keys, grad_keys = [], []
        for part in range(per_group):
            at = group * per_group + part
            own = slice(part * STRETCH, (part + 1) * STRETCH)
            state_keys.append(mm_nt(d_right_b[own], state_ref[at]))
            grad_keys.append(mm_nt(fresh_b[own], grad_bs[part]))
        d_queries.append(gamma[span] * jnp.concatenate(from_state, axis=0) + mm(d_score, key_b))
        d_keys.append(
            mm_tn(d_score, query_b)
            + mm_tn(d_lower, key_b)
            + mm(d_lower, key_b)
            + tail_decay[span] * jnp.concatenate(grad_keys, axis=0)
            - beta_gamma[span] * jnp.concatenate(state_keys, axis=0)
        )
        d_values.append(beta[span] * d_right)
    g_q = jnp.concatenate(d_queries, axis=0) * DK ** (-0.5)
    g_k = jnp.concatenate(d_keys, axis=0)
    d_act = jnp.concatenate(
        [
            scale_q * (g_q - unit_q * jnp.sum(unit_q * g_q, axis=1, keepdims=True)),
            scale_k * (g_k - keys * jnp.sum(keys * g_k, axis=1, keepdims=True)),
            jnp.concatenate(d_values, axis=0),
        ],
        axis=1,
    )
    d_conv = d_act * (sig * (1.0 + total * (1.0 - sig)))
    taps = taps_ref[...].astype(f32)
    count = taps_ref.shape[0]
    start = 9 - count
    grad_taps_ref[...] = jnp.concatenate(
        [
            jnp.sum(padded[start + tap : start + tap + rows, :] * d_conv, axis=0, keepdims=True)
            for tap in range(count)
        ],
        axis=0,
    )
    spread[0:8, :] = jnp.zeros((8, d_conv.shape[1]), f32)
    spread[8 : 8 + rows, :] = d_conv
    spread[8 + rows : 16 + rows, :] = jnp.zeros((8, d_conv.shape[1]), f32)
    lead = taps[0:1] * spread[8:16, :]
    d_mixed = taps[0:1] * spread[7 + count : 7 + count + rows, :]
    for tap in range(1, count):
        lead += taps[tap : tap + 1] * spread[8 - tap : 16 - tap, :]
        begin = 7 + count - tap
        d_mixed += taps[tap : tap + 1] * spread[begin : begin + rows, :]
    lead_ref[...] = lead
    d_mixed_ref[...] = d_mixed.astype(bf16)
    tail_out_ref[...] = d_mixed[rows - 8 :]


def whole(shape):
    return pl.BlockSpec(shape, lambda h: (0,) * len(shape))


def by_head(shape):
    return pl.BlockSpec((None,) + shape, lambda h: (h,) + (0,) * len(shape))


def by_columns(rows, width):
    return pl.BlockSpec((rows, width), lambda h: (0, h))


def kernel_call(body, heads, ins, outs, out_shapes, scratch, flops, moved):
    return pl.pallas_call(
        body,
        grid=(heads,),
        in_specs=ins,
        out_specs=outs,
        out_shape=out_shapes,
        scratch_shapes=scratch,
        compiler_params=pltpu.CompilerParams(
            dimension_semantics=("arbitrary",), vmem_limit_bytes=VMEM_BYTES
        ),
        cost_estimate=pl.CostEstimate(flops=flops, bytes_accessed=moved, transcendentals=0),
    )


def shaped(shape, kind):
    return jax.ShapeDtypeStruct(shape, kind)


def run_local_forward(mixed, tail, taps, columns, run_rows, heads):
    rows = mixed.shape[1]
    count = taps.shape[0]
    groups, stretches = rows // GROUP, rows // STRETCH
    return kernel_call(
        local_forward,
        heads,
        [
            by_head((rows, INNER)),
            by_head((8, INNER)),
            by_columns(count, INNER),
            whole(columns.shape),
            whole(run_rows.shape),
        ],
        [
            by_head((groups, GROUP, GROUP)),
            by_head((groups, GROUP, GROUP)),
            by_head((rows, DV + DK)),
            by_head((rows, DK)),
            by_columns(rows, DV),
            by_head((stretches, DK, DK)),
            whole((heads, stretches, DK, DV + DK)),
            whole((heads, DK, DV + DK)),
        ],
        [
            shaped((heads, groups, GROUP, GROUP), bf16),
            shaped((heads, groups, GROUP, GROUP), bf16),
            shaped((heads, rows, DV + DK), bf16),
            shaped((heads, rows, DK), bf16),
            shaped((rows, heads * DV), f32),
            shaped((heads, stretches, DK, DK), bf16),
            shaped((heads, stretches, DK, DV + DK), bf16),
            shaped((heads, DK, DV + DK), bf16),
        ],
        [
            pltpu.VMEM((rows + 8, INNER), f32),
            pltpu.VMEM((heads, stretches, DK, DK), bf16),
            pltpu.VMEM((heads, stretches, DK, DV), f32),
        ],
        12_000_000_000,
        20_000_000,
    )(mixed, tail, taps, columns, run_rows)


def run_finish_forward(ends, local, reach, inner, gate_pre, gain):
    heads, stretches = local.shape[:2]
    rows = inner.shape[0]
    return kernel_call(
        finish_forward,
        heads,
        [
            whole(ends.shape),
            by_head((stretches, DK, DV + DK)),
            by_head((rows, DK)),
            by_columns(rows, DV),
            by_head((rows, DV)),
            whole(gain.shape),
        ],
        [by_head((stretches, DK, DV)), by_columns(rows, DV), by_columns(rows, DV)],
        [
            shaped((heads, stretches, DK, DV), bf16),
            shaped((rows, heads * DV), f32),
            shaped((rows, heads * DV), bf16),
        ],
        [pltpu.VMEM((heads, DK, DV), f32)],
        3_000_000_000,
        20_000_000,
    )(ends, local, reach, inner, gate_pre, gain)


def run_local_backward(d_branch, core, gate_pre, gain, reach, turn):
    heads, stretches = turn.shape[:2]
    rows = core.shape[0]
    return kernel_call(
        local_backward,
        heads,
        [
            by_columns(rows, DV),
            by_columns(rows, DV),
            by_head((rows, DV)),
            whole(gain.shape),
            by_head((rows, DK)),
            whole(turn.shape),
        ],
        [
            by_columns(rows, DV),
            by_columns(rows, DV),
            whole((1, DV)),
            whole((heads, stretches, DK, DV + DK)),
            whole((heads, DK, DV)),
        ],
        [
            shaped((rows, heads * DV), bf16),
            shaped((rows, heads * DV), bf16),
            shaped((1, DV), f32),
            shaped((heads, stretches, DK, DV + DK), bf16),
            shaped((heads, DK, DV), bf16),
        ],
        [pltpu.VMEM((heads, stretches, DK, DV), f32)],
        4_000_000_000,
        20_000_000,
    )(d_branch, core, gate_pre, gain, reach, turn)


def run_finish_backward(
    ends, grad_ends, mixed, tail, taps, columns, run_rows, solve, score, fresh, states, d_core, local
):
    heads, stretches = local.shape[:2]
    rows = mixed.shape[1]
    groups = rows // GROUP
    count = taps.shape[0]
    return kernel_call(
        finish_backward,
        heads,
        [
            whole(ends.shape),
            whole(grad_ends.shape),
            by_head((rows, INNER)),
            by_head((8, INNER)),
            by_columns(count, INNER),
            whole(columns.shape),
            whole(run_rows.shape),
            by_head((groups, GROUP, GROUP)),
            by_head((groups, GROUP, GROUP)),
            by_head((rows, DV + DK)),
            by_head((stretches, DK, DV)),
            by_columns(rows, DV),
            by_head((stretches, DK, DV + DK)),
        ],
        [
            by_columns(rows, INNER),
            by_columns(8, INNER),
            by_columns(8, INNER),
            by_columns(count, INNER),
        ],
        [
            shaped((rows, heads * INNER), bf16),
            shaped((8, heads * INNER), f32),
            shaped((8, heads * INNER), f32),
            shaped((count, heads * INNER), f32),
        ],
        [
            pltpu.VMEM((rows + 8, INNER), f32),
            pltpu.VMEM((rows + 16, INNER), f32),
            pltpu.VMEM((heads, DK, DV), f32),
        ],
        12_000_000_000,
        20_000_000,
    )(ends, grad_ends, mixed, tail, taps, columns, run_rows, solve, score, fresh, states, d_core, local)


MESH = pl.DeviceIdType.MESH
SIDE = 2


def remote(source, target, send, arrive, device):
    return pltpu.make_async_remote_copy(
        src_ref=source,
        dst_ref=target,
        send_sem=send,
        recv_sem=arrive,
        device_id=device,
        device_id_type=MESH,
    )


def greet(partners):
    barrier = pltpu.get_barrier_semaphore()
    expected = 0
    for device, there in partners:
        if there is None:
            pl.semaphore_signal(barrier, inc=1, device_id=device, device_id_type=MESH)
            expected = expected + 1
        else:

            @pl.when(there)
            def _(device=device):
                pl.semaphore_signal(barrier, inc=1, device_id=device, device_id_type=MESH)

            expected = expected + there.astype(jnp.int32)
    pl.semaphore_wait(barrier, expected)


def head_places():
    head, seq = lax.axis_index("head"), lax.axis_index("seq")
    core = lax.rem(head, 2)
    sibling = head + 1 - 2 * core
    across = lax.rem(head + 2, 4)
    return head, seq, sibling, across


def head_partners():
    head, seq, sibling, across = head_places()
    return [((sibling, seq), None), ((across, seq), None)]


def seq_places():
    head, seq = lax.axis_index("head"), lax.axis_index("seq")
    return head, seq // SIDE, lax.rem(seq, SIDE)


def seq_partners(count):
    head, line, side = seq_places()
    return [
        ((head, line * SIDE + 1 - side), None),
        ((head, (line + 1) * SIDE + side), line < count - 1),
        ((head, (line - 1) * SIDE + side), line > 0),
    ]


def run_together(steps):
    steps = list(steps)
    while steps:
        alive = []
        for step in steps:
            try:
                next(step)
                alive.append(step)
            except StopIteration:
                pass
        steps = alive


def gather_head(own_ref, out_ref, local, send, arrive, pieces):
    head, seq, sibling, across = head_places()
    far = lax.rem(sibling + 2, 4)
    rows = own_ref.shape[0] // pieces
    keep = pltpu.make_async_copy(own_ref, out_ref.at[head], local.at[0])
    keep.start()

    def part(ref, piece):
        return ref.at[pl.ds(piece * rows, rows)]

    outgoing = []
    for piece in range(pieces):
        outgoing.append(
            remote(
                part(own_ref, piece),
                part(out_ref.at[head], piece),
                send.at[0, piece],
                arrive.at[0, piece],
                (across, seq),
            )
        )
    for piece in range(pieces):
        outgoing.append(
            remote(
                part(own_ref, piece),
                part(out_ref.at[head], piece),
                send.at[1, piece],
                arrive.at[1, piece],
                (sibling, seq),
            )
        )
    for copy in outgoing:
        copy.start()
    yield
    forwards = []
    for piece in range(pieces):
        outgoing[piece].wait_recv()
        forward = remote(
            part(out_ref.at[across], piece),
            part(out_ref.at[across], piece),
            send.at[2, piece],
            arrive.at[2, piece],
            (sibling, seq),
        )
        forward.start()
        forwards.append(forward)
        yield
    for copy in outgoing[pieces:] + forwards:
        copy.wait_recv()
    for copy in outgoing + forwards:
        copy.wait_send()
    keep.wait()


def scatter_head(source_at, out_ref, own, crossed, passed, local, send, arrive, hold=0, pause=0):
    head, seq, sibling, across = head_places()
    far = lax.rem(sibling + 2, 4)
    loads = [
        pltpu.make_async_copy(source_at(target), own.at[slot], local.at[slot])
        for slot, target in enumerate((across, head))
    ]
    copies = [
        remote(source_at(target), crossed.at[slot], send.at[slot], arrive.at[slot], (sibling, seq))
        for slot, target in enumerate((far, sibling))
    ]
    for slot in range(2):
        copies[slot].start()
        loads[slot].start()
    for _ in range(1 + hold):
        yield
    loads[0].wait()
    copies[0].wait_recv()
    own[0] = (own[0].astype(f32) + crossed[0].astype(f32)).astype(own.dtype)
    onward = remote(own.at[0], passed, send.at[2], arrive.at[2], (across, seq))
    onward.start()
    for _ in range(1 + pause):
        yield
    loads[1].wait()
    copies[1].wait_recv()
    onward.wait_recv()
    total = own[1].astype(f32) + crossed[1].astype(f32) + passed[...].astype(f32)
    out_ref[...] = total.astype(out_ref.dtype)
    onward.wait_send()
    for copy in copies:
        copy.wait_send()


def gather_seq(own_ref, out_ref, local, side_send, side_arrive, line_send, line_arrive, count):
    head, line, side = seq_places()
    me = line * SIDE + side
    beside = (head, line * SIDE + 1 - side)
    ways = ((1, line < count - 1), (-1, line > 0))
    keep = pltpu.make_async_copy(own_ref, out_ref.at[me], local.at[0])
    keep.start()

    def along(source, block, way, step):
        slot = step if way > 0 else count + step
        return remote(
            source,
            out_ref.at[block],
            line_send.at[slot],
            line_arrive.at[slot],
            (head, (line + way) * SIDE + side),
        )

    def over(source, block, slot):
        return remote(source, out_ref.at[block], side_send.at[slot], side_arrive.at[slot], beside)

    for way, onward in ways:

        @pl.when(onward)
        def _(way=way):
            along(own_ref, me, way, 0).start()

    over(own_ref, me, 0).start()
    yield
    for step in range(1, count):
        for way, onward in ways:
            block = me - way * step * SIDE
            arrives = line >= step if way > 0 else line + step < count

            @pl.when(arrives)
            def _(way=way, onward=onward, block=block, step=step):
                landed = out_ref.at[block]
                slot = step if way > 0 else count + step
                remote(
                    landed, landed, line_send.at[slot - 1], line_arrive.at[slot - 1], beside
                ).wait_recv()

                @pl.when(onward)
                def _():
                    along(landed, block, way, step).start()

                over(landed, block, slot).start()

        yield
    over(own_ref, me, 0).wait()
    for way, onward in ways:

        @pl.when(onward)
        def _(way=way):
            along(own_ref, me, way, 0).wait_send()

    for step in range(1, count):
        for way, onward in ways:
            block = me - way * step * SIDE
            arrives = line >= step if way > 0 else line + step < count

            @pl.when(arrives)
            def _(way=way, onward=onward, block=block, step=step):
                landed = out_ref.at[block]
                slot = step if way > 0 else count + step
                over(landed, block, slot).wait()

                @pl.when(onward)
                def _():
                    along(landed, block, way, step).wait_send()

    keep.wait()


def scatter_seq(source_at, out_at, own, crossed, risen, fallen, local, sends, arrivals, count):
    head, line, side = seq_places()
    beside = (head, line * SIDE + 1 - side)
    pieces = own.shape[0]

    def targets(distance):
        if distance == 0:
            return [(line, None, 0)]
        return [
            (line - distance, line >= distance, -1),
            (line + distance, line + distance < count, 1),
        ]

    def load(piece, target):
        return pltpu.make_async_copy(
            source_at(target, side, piece), own.at[piece, target], local.at[piece, target]
        )

    def cross(piece, target):
        return remote(
            source_at(target, 1 - side, piece),
            crossed.at[piece, target],
            sends.at[0, piece, target],
            arrivals.at[0, piece, target],
            beside,
        )

    def onward(piece, target, way, arriving=False):
        landing = risen if way > 0 else fallen
        return remote(
            own.at[piece, target],
            landing.at[piece, target],
            sends.at[1, piece, target],
            arrivals.at[1 if way > 0 else 2, piece, target],
            beside if arriving else (head, (line + way) * SIDE + side),
        )

    def guarded(there, body):
        if there is None:
            body()
        else:
            pl.when(there)(body)

    def here(piece, target):
        load(piece, target).wait()
        total = own[piece, target].astype(f32)
        if crossed is not None:
            cross(piece, target).wait_recv()
            total += crossed[piece, target].astype(f32)
        return total

    def arrived(piece, target, way):
        landing = risen if way > 0 else fallen
        onward(piece, target, way, True).wait_recv()
        return landing[piece, target].astype(f32)

    for piece in range(pieces):
        for distance in range(count - 1, -1, -1):
            for target, there, _ in targets(distance):

                def begin(piece=piece, target=target):
                    if crossed is not None:
                        cross(piece, target).start()
                    load(piece, target).start()

                guarded(there, begin)
    yield
    for piece in range(pieces):
        for distance in range(count - 1, 0, -1):
            for target, there, way in targets(distance):
                first = line == count - 1 if way < 0 else line == 0

                @pl.when(jnp.logical_and(there, first))
                def _(piece=piece, target=target, way=way):
                    own[piece, target] = here(piece, target).astype(own.dtype)
                    onward(piece, target, way).start()

                @pl.when(jnp.logical_and(there, jnp.logical_not(first)))
                def _(piece=piece, target=target, way=way):
                    total = here(piece, target) + arrived(piece, target, way)
                    own[piece, target] = total.astype(own.dtype)
                    onward(piece, target, way).start()

            yield
        out = out_at(piece)

        @pl.when(line == 0)
        def _(piece=piece, out=out):
            out[...] = (here(piece, line) + arrived(piece, line, -1)).astype(out.dtype)

        @pl.when(line == count - 1)
        def _(piece=piece, out=out):
            out[...] = (here(piece, line) + arrived(piece, line, 1)).astype(out.dtype)

        @pl.when(jnp.logical_and(line > 0, line < count - 1))
        def _(piece=piece, out=out):
            total = here(piece, line) + arrived(piece, line, -1) + arrived(piece, line, 1)
            out[...] = total.astype(out.dtype)

        yield
    for piece in range(pieces):
        for distance in range(count - 1, -1, -1):
            for target, there, way in targets(distance):

                def finish(piece=piece, target=target, way=way):
                    if crossed is not None:
                        cross(piece, target).wait_send()
                    if way:
                        onward(piece, target, way).wait_send()

                guarded(there, finish)


ANY = pl.BlockSpec(memory_space=pl.ANY)
IN_VMEM = pl.BlockSpec(memory_space=pltpu.VMEM)
DMA = pltpu.SemaphoreType.DMA


def link_call(body, number, ins, outs, shapes, scratch, moved):
    return pl.pallas_call(
        body,
        in_specs=ins,
        out_specs=outs,
        out_shape=shapes,
        scratch_shapes=scratch,
        compiler_params=pltpu.CompilerParams(
            collective_id=number, has_side_effects=True, vmem_limit_bytes=VMEM_BYTES
        ),
        cost_estimate=pl.CostEstimate(flops=0, bytes_accessed=moved // 8, transcendentals=0),
    )


def gathered_head(value, number, pieces=4):
    count = lax.axis_size("head")
    if count != 4:
        return lax.all_gather(value, "head", axis=0, tiled=True)
    rows, width = value.shape

    def body(own_ref, out_ref, local, send, arrive):
        greet(head_partners())
        run_together([gather_head(own_ref, out_ref, local, send, arrive, pieces)])

    out = link_call(
        body,
        number,
        [ANY],
        ANY,
        shaped((count, rows, width), value.dtype),
        [DMA((1,)), DMA((3, pieces)), DMA((3, pieces))],
        60_000_000,
    )(value)
    return out.reshape(count * rows, width)


def gathered_sided(value, half, number, pieces=4, half_pieces=2):
    count = lax.axis_size("head")
    rows, width = value.shape

    def body(own_ref, half_ref, out_ref, beside_ref, landing, *sems):
        head, line, side = seq_places()
        beside = (head, line * SIDE + 1 - side)
        greet(head_partners() + [(beside, None)])

        def half_steps():
            copy = remote(half_ref, landing, sems[6].at[0], sems[6].at[1], beside)
            copy.start()
            yield
            yield
            copy.wait()
            yield from gather_head(landing, beside_ref, *sems[3:6], half_pieces)

        run_together([half_steps(), gather_head(own_ref, out_ref, *sems[:3], pieces)])

    out, beside = link_call(
        body,
        number,
        [ANY, ANY],
        [ANY, ANY],
        [
            shaped((count, rows, width), value.dtype),
            shaped((count, rows, half.shape[1]), value.dtype),
        ],
        [pltpu.VMEM(half.shape, half.dtype)]
        + [DMA((1,)), DMA((3, pieces)), DMA((3, pieces))]
        + [DMA((1,)), DMA((3, half_pieces)), DMA((3, half_pieces))]
        + [DMA((2,))],
        60_000_000,
    )(value, half)
    return out.reshape(count * rows, width), beside.reshape(count * rows, half.shape[1])


def gathered_seq(value, number):
    total = lax.axis_size("seq")
    count = total // SIDE
    rows, width = value.shape
    if total % SIDE or count < 2:
        return lax.all_gather(value, "seq")

    def body(own_ref, out_ref, *sems):
        greet(seq_partners(count))
        run_together([gather_seq(own_ref, out_ref, *sems, count)])

    return link_call(
        body,
        number,
        [ANY],
        ANY,
        shaped((total, rows, width), value.dtype),
        [DMA((1,))] + [DMA((2 * count,)) for _ in range(4)],
        120_000_000,
    )(value)


def head_scratch(rows, width):
    return [
        pltpu.VMEM((2, rows, width), bf16),
        pltpu.VMEM((2, rows, width), bf16),
        pltpu.VMEM((rows, width), bf16),
        DMA((2,)),
        DMA((3,)),
        DMA((3,)),
    ]


def seq_scratch(pieces, count, rows, width):
    return [pltpu.VMEM((pieces, count, rows, width), bf16) for _ in range(4)] + [
        DMA((pieces, count)),
        DMA((2, pieces, count)),
        DMA((3, pieces, count)),
    ]


def scattered_head(value, number, pieces=2):
    count = lax.axis_size("head")
    if count != 4:
        return scattered(value, "head")
    rows, width = value.shape[0] // count, value.shape[1] // pieces

    def body(source, out, *rest):
        greet(head_partners())
        steps = []
        for piece in range(pieces):
            span = pl.ds(piece * width, width)

            def source_at(target, span=span):
                return source.at[pl.ds(pl.multiple_of(target * rows, rows), rows), span]

            steps.append(
                scatter_head(source_at, out.at[:, span], *rest[6 * piece : 6 * piece + 6])
            )
        run_together(steps)

    return link_call(
        body,
        number,
        [ANY],
        IN_VMEM,
        shaped((rows, value.shape[1]), f32),
        head_scratch(rows, width) * pieces,
        60_000_000,
    )(value)


def scattered_seq(value, number, pieces=2):
    total = lax.axis_size("seq")
    count = total // SIDE
    if total % SIDE or count < 2:
        return scattered(value, "seq")
    rows, width = value.shape[0] // total, value.shape[1] // pieces

    def body(source, out, *rest):
        greet(seq_partners(count))

        def source_at(target, side, piece):
            begin = pl.multiple_of((target * SIDE + side) * rows, rows)
            return source.at[pl.ds(begin, rows), pl.ds(piece * width, width)]

        def out_at(piece):
            return out.at[:, pl.ds(piece * width, width)]

        run_together([scatter_seq(source_at, out_at, *rest, count)])

    return link_call(
        body,
        number,
        [ANY],
        IN_VMEM,
        shaped((rows, value.shape[1]), f32),
        seq_scratch(pieces, count, rows, width),
        120_000_000,
    )(value)


def product_steps(left_hbm, right_hbm, out_refs, picks, lefts, rights, tiles, load, store, per_round):
    loads = [
        pltpu.make_async_copy(ref, held, load.at[index])
        for index, (ref, held) in enumerate(zip(left_hbm + right_hbm, lefts + rights))
    ]
    for copy in loads:
        copy.start()
    yield
    for copy in loads:
        copy.wait()
    units, width = tiles.shape[1:]
    block = units // 4 if units % 64 == 0 else units
    span = 512
    stores = []
    done = 0
    for index, pick in enumerate(picks):
        for begin in range(0, width, span):
            columns = pl.ds(begin, span)

            def one(part, carry, index=index, pick=pick, columns=columns):
                rows = pl.ds(pl.multiple_of(part * block, block), block)
                tiles[index, rows, columns] = mm(
                    lefts[index][rows, :], rights[pick][:, columns]
                ).astype(tiles.dtype)
                return carry

            lax.fori_loop(0, units // block, one, 0)
            done += 1
            if done % per_round == 0:
                yield
        copy = pltpu.make_async_copy(tiles.at[index], out_refs[index], store.at[index])
        copy.start()
        stores.append(copy)
    for copy in stores:
        copy.wait()


def scattered_seq_products(value, lefts, rights, picks, number, pieces=2):
    total = lax.axis_size("seq")
    count = total // SIDE
    rows, width = value.shape[0] // total, value.shape[1] // pieces
    units, depth = lefts[0].shape
    breadth = rights[0].shape[1]
    n_left, n_right = len(lefts), len(rights)
    held = 4 * value.size // SIDE + n_left * units * (depth + breadth) + n_right * rights[0].size
    if 2 * held > VMEM_BYTES:
        products = [mm(left, rights[pick]).astype(bf16) for left, pick in zip(lefts, picks)]
        return scattered_seq(value, number, pieces), products

    def body(source, *rest):
        left_hbm, rest = rest[:n_left], rest[n_left:]
        right_hbm, rest = rest[:n_right], rest[n_right:]
        out, out_refs, rest = rest[0], rest[1 : 1 + n_left], rest[1 + n_left :]
        link, rest = rest[:7], rest[7:]
        left_held, rest = rest[:n_left], rest[n_left:]
        right_held, rest = rest[:n_right], rest[n_right:]
        greet(seq_partners(count))

        def source_at(target, side, piece):
            begin = pl.multiple_of((target * SIDE + side) * rows, rows)
            return source.at[pl.ds(begin, rows), pl.ds(piece * width, width)]

        def out_at(piece):
            return out.at[:, pl.ds(piece * width, width)]

        run_together(
            [
                scatter_seq(source_at, out_at, *link, count),
                product_steps(
                    left_hbm, right_hbm, out_refs, picks, left_held, right_held, *rest, 2
                ),
            ]
        )

    outs = link_call(
        body,
        number,
        [ANY] * (1 + n_left + n_right),
        [IN_VMEM] + [ANY] * n_left,
        [shaped((rows, value.shape[1]), f32)]
        + [shaped((units, breadth), bf16) for _ in lefts],
        seq_scratch(pieces, count, rows, width)
        + [pltpu.VMEM((units, depth), bf16) for _ in lefts]
        + [pltpu.VMEM((depth, breadth), bf16) for _ in rights]
        + [
            pltpu.VMEM((n_left, units, breadth), bf16),
            DMA((n_left + n_right,)),
            DMA((n_left,)),
        ],
        120_000_000,
    )(value, *lefts, *rights)
    return outs[0], list(outs[1:])


def gathered_swapped(ends, d_gate, number):
    total = lax.axis_size("seq")
    count = total // SIDE

    def body(ends_ref, gate_ref, ends_out, gate_out, *rest):
        head, line, side = seq_places()
        beside = (head, line * SIDE + 1 - side)
        greet(seq_partners(count))

        def swap_steps():
            yield
            yield
            copy = remote(gate_ref, gate_out, rest[5].at[0], rest[5].at[1], beside)
            copy.start()
            for _ in range(count):
                yield
            copy.wait()

        run_together([gather_seq(ends_ref, ends_out, *rest[:5], count), swap_steps()])

    return link_call(
        body,
        number,
        [ANY] * 2,
        [ANY] * 2,
        [
            shaped((total,) + ends.shape, ends.dtype),
            shaped(d_gate.shape, d_gate.dtype),
        ],
        [DMA((1,))] + [DMA((2 * count,)) for _ in range(4)] + [DMA((2,))],
        150_000_000,
    )(ends, d_gate)


def scattered_last(qkv, gate, normed, hat, mlp, small, gain_rows, number, pieces=4, gate_pieces=2):
    total, heads = lax.axis_size("seq"), lax.axis_size("head")
    count = total // SIDE
    rows, width = qkv.shape[0] // total, qkv.shape[1] // pieces
    gate_width = gate.shape[1] // gate_pieces
    own_rows = normed.shape[0] // heads
    units, slices = mlp[0].shape[0], mlp[0].shape[1] // heads
    small_rows = small.shape[0]

    def body(qkv_ref, gate_ref, normed_ref, hat_ref, small_ref, *rest):
        mlp_refs, rest = rest[: len(mlp)], rest[len(mlp) :]
        qkv_out, gate_out, normed_out, small_out, rest = rest[0], rest[1], rest[2], rest[3], rest[4:]
        mlp_outs, rest = rest[: len(mlp)], rest[len(mlp) :]
        greet(head_partners() + seq_partners(count))

        def qkv_at(target, side, piece):
            begin = pl.multiple_of((target * SIDE + side) * rows, rows)
            return qkv_ref.at[pl.ds(begin, rows), pl.ds(piece * width, width)]

        def gate_at(target, side, piece):
            begin = pl.multiple_of(target * rows, rows)
            return gate_ref.at[pl.ds(begin, rows), pl.ds(piece * gate_width, gate_width)]

        def normed_at(target):
            return normed_ref.at[pl.ds(pl.multiple_of(target * own_rows, own_rows), own_rows)]

        def normed_steps(four, own, local, *sems):
            yield from scatter_head(normed_at, normed_out, *rest[13:19], 0, 1)
            own[...] = small_ref[...]
            product = jnp.sum(normed_out[...] * hat_ref[...], axis=0, keepdims=True)
            for row in range(product.shape[1] // 128):
                own[row : row + 1] = product[:, row * 128 : (row + 1) * 128]
            yield
            yield from gather_head(own, four, sems[0], sems[1], sems[2], 1)
            own[:gain_rows] = jnp.sum(four[:, :gain_rows], axis=0)
            for step in gather_seq(own, small_out, local, *sems[3:7], count):
                for _ in range(3):
                    yield

        steps = [
            normed_steps(*rest[19:29]),
            scatter_seq(
                gate_at,
                lambda piece: gate_out.at[:, pl.ds(piece * gate_width, gate_width)],
                rest[7],
                None,
                *rest[8:13],
                count,
            ),
            scatter_seq(
                qkv_at,
                lambda piece: qkv_out.at[:, pl.ds(piece * width, width)],
                *rest[:7],
                count,
            ),
        ]
        for index, (ref, out) in enumerate(zip(mlp_refs, mlp_outs)):

            def mlp_at(target, ref=ref):
                return ref.at[:, pl.ds(pl.multiple_of(target * slices, slices), slices)]

            begin = 29 + 6 * index
            steps.append(
                scatter_head(mlp_at, out, *rest[begin : begin + 6], HOLD, 2 + 3 * index)
            )
        run_together(steps)

    line_scratch = seq_scratch(gate_pieces, count, rows, gate_width)
    outs = link_call(
        body,
        number,
        [ANY] * 3 + [IN_VMEM] * 2 + [ANY] * len(mlp),
        [IN_VMEM] * (4 + len(mlp)),
        [
            shaped((rows, qkv.shape[1]), bf16),
            shaped((rows, gate.shape[1]), bf16),
            shaped((own_rows, normed.shape[1]), f32),
            shaped((total, small_rows, small.shape[1]), f32),
        ]
        + [shaped((units, slices), bf16) for _ in mlp],
        seq_scratch(pieces, count, rows, width)
        + line_scratch[1:]
        + head_scratch(own_rows, normed.shape[1])
        + [
            pltpu.VMEM((heads, small_rows, small.shape[1]), f32),
            pltpu.VMEM((small_rows, small.shape[1]), f32),
            DMA((1,)),
            DMA((1,)),
            DMA((3, 1)),
            DMA((3, 1)),
        ]
        + [DMA((2 * count,)) for _ in range(4)]
        + head_scratch(units, slices) * len(mlp),
        250_000_000,
    )(qkv, gate, normed, hat, small, *mlp)
    return outs[0], outs[1], outs[2], outs[3], list(outs[4:])


def side_columns(value, side, rows):
    count = value.shape[1] // (rows * SIDE)
    return jnp.concatenate(
        [
            lax.dynamic_slice_in_dim(value, (place * SIDE + side) * rows, rows, 1)
            for place in range(count)
        ],
        axis=1,
    )


def swapped(value):
    count = lax.axis_size("seq")
    return lax.ppermute(value, "seq", [(place, place ^ 1) for place in range(count)])


def silu_slope(tensor):
    sigmoid_part = jax.nn.sigmoid(tensor)
    return sigmoid_part * (1.0 + tensor * (1.0 - sigmoid_part))


def gathered(value, axis):
    return lax.all_gather(value, axis, axis=0, tiled=True)


def scattered(value, axis, dimension=0):
    return lax.psum_scatter(
        value.astype(bf16), axis, scatter_dimension=dimension, tiled=True
    ).astype(f32)


def on_device(
    block_in,
    out_cot,
    gain_one,
    qkv_weight,
    conv_weight,
    gate_weight,
    gain_out,
    out_weight,
    gain_two,
    mlp_gate,
    mlp_up,
    mlp_down,
    decay_code,
    beta_code,
):
    span_rows = decay_code.shape[0]
    width, heads, inner = qkv_weight.shape
    total_len = span_rows * lax.axis_size("seq")
    lead_rows = conv_weight.shape[0] - 1
    input_f = block_in.astype(f32)
    gain_first = gain_one.astype(f32)
    gain_second = gain_two.astype(f32)
    gain_head = gain_out.reshape(1, -1)
    taps = conv_weight.reshape(conv_weight.shape[0], heads * inner)
    out_flat = out_weight.reshape(heads * DV, width)
    columns, run_rows = token_columns(decay_code, beta_code, total_len)

    cot_all = gathered(out_cot, "seq")
    seq_count, head_count = lax.axis_size("seq"), lax.axis_size("head")
    seq_at, head_at = lax.axis_index("seq"), lax.axis_index("head")
    side = lax.rem(seq_at, SIDE)
    slice_rows = width // seq_count
    scale_own = rms_scale(input_f)
    hat_own = input_f * scale_own
    normed_own = (hat_own * gain_first).astype(bf16)
    normed_first, normed_side = gathered_sided(
        normed_own, side_columns(normed_own, 1 - side, slice_rows), 1
    )
    mixed_in = jnp.einsum(
        "td,dhc->htc", normed_first, qkv_weight, preferred_element_type=f32
    ).astype(bf16)
    tail_in = passed_along(mixed_in[:, span_rows - 8 :], "seq", 1)
    tail_in = jnp.where(jnp.arange(8)[:, None] >= 8 - lead_rows, tail_in.astype(f32), 0.0)
    solve, score, fresh, reach, inner_part, turn, local_states, piece_end = run_local_forward(
        mixed_in, tail_in, taps, columns, run_rows, heads
    )
    ends = gathered_seq(piece_end.reshape(-1, DV + DK), 2).reshape(-1, heads, DK, DV + DK)
    gate_pre = jnp.einsum("td,dhv->htv", normed_first, gate_weight, preferred_element_type=f32)
    states, core, branch = run_finish_forward(
        ends, local_states, reach, inner_part, gate_pre, gain_head
    )
    branch, cot_all = lax.optimization_barrier((branch, cot_all))
    branch_side = swapped(branch)
    middle = input_f + scattered_head(mm(branch, out_flat).astype(bf16), 3)
    scale_two = rms_scale(middle)
    hat_two = middle * scale_two
    normed_two = (hat_two * gain_second).astype(bf16)

    rows_out = gathered_seq(normed_two, 4).reshape(-1, width)
    cot_f = out_cot.astype(f32)
    gate_units, up_units = mlp_gate.T, mlp_up.T
    gate_part = mm_nt(gate_units, rows_out)
    up_part = mm_nt(up_units, rows_out)
    d_hidden = mm_nt(mlp_down, cot_all)
    hidden = (jax.nn.silu(gate_part) * up_part).astype(bf16)
    d_gate_mlp = (d_hidden * up_part * silu_slope(gate_part)).astype(bf16)
    d_up_mlp = (d_hidden * jax.nn.silu(gate_part)).astype(bf16)
    d_rows = (mm_tn(d_gate_mlp, gate_units) + mm_tn(d_up_mlp, up_units)).astype(bf16)
    d_normed_two, (grad_mgate, grad_mup, grad_down) = scattered_seq_products(
        d_rows, [d_gate_mlp, d_up_mlp, hidden], [rows_out, cot_all], [0, 0, 1], 5
    )
    gain_two_part = jnp.sum(d_normed_two * hat_two, 0)
    e_two = d_normed_two * gain_second
    d_middle = cot_f + scale_two * (
        e_two - hat_two * jnp.mean(e_two * hat_two, axis=-1, keepdims=True)
    )
    hidden, d_middle = lax.optimization_barrier((hidden, d_middle))
    mlp_part, d_middle = lax.optimization_barrier(
        (mm_tn(hidden, mlp_down).astype(bf16), d_middle)
    )
    mlp_out = scattered(mlp_part, "seq")
    d_mix = d_middle.astype(bf16)
    d_mix_all, d_mix_side = gathered_sided(d_mix, side_columns(d_mix, 1 - side, slice_rows), 6)
    d_branch = mm_nt(d_mix_all, out_flat)
    out_half = (
        mm_tn(side_columns(d_mix_all, side, slice_rows), branch) + mm_tn(d_mix_side, branch_side)
    ).astype(bf16)
    d_core, d_gate_low, gain_out_part, local_grads, grad_end = run_local_backward(
        d_branch, core, gate_pre, gain_head, reach, turn
    )
    grad_ends, d_gate_side = gathered_swapped(grad_end.reshape(-1, DV), d_gate_low, 7)
    out_half, grad_ends, mlp_out = lax.optimization_barrier((out_half, grad_ends, mlp_out))
    output = (middle + mlp_out).astype(bf16)
    grad_out_s = lax.psum_scatter(
        out_half,
        "seq",
        scatter_dimension=0,
        axis_index_groups=[
            [place * SIDE + across for place in range(seq_count // SIDE)] for across in range(SIDE)
        ],
        tiled=True,
    )
    grad_ends = grad_ends.reshape(-1, heads, DK, DV)
    d_mixed, d_tail, d_lead, grad_conv = run_finish_backward(
        ends,
        grad_ends,
        mixed_in,
        tail_in,
        taps,
        columns,
        run_rows,
        solve,
        score,
        fresh,
        states,
        d_core,
        local_grads,
    )
    d_lead, grad_out_s = lax.optimization_barrier((d_lead, grad_out_s))
    from_next = passed_along(d_lead[:lead_rows], "seq", -1)
    d_tail = d_tail.at[8 - lead_rows :].add(from_next).astype(bf16)
    d_mixed = lax.dynamic_update_slice(d_mixed, d_tail, (span_rows - 8, 0))
    d_normed_part = jnp.einsum(
        "thc,dhc->td",
        d_mixed.reshape(span_rows, heads, inner),
        qkv_weight,
        preferred_element_type=f32,
    ) + jnp.einsum(
        "thv,dhv->td",
        d_gate_low.reshape(span_rows, heads, DV),
        gate_weight,
        preferred_element_type=f32,
    )
    grad_qkv = mm_tn(normed_first, d_mixed).astype(bf16)
    grad_gate = (
        mm_tn(side_columns(normed_first, side, slice_rows), d_gate_low)
        + mm_tn(normed_side, d_gate_side)
    ).astype(bf16)

    gains = jnp.concatenate([jnp.zeros_like(gain_two_part), gain_two_part, gain_out_part.reshape(-1)])
    gain_rows = -(-gains.shape[0] // 1024) * 8
    gains = jnp.pad(gains, (0, gain_rows * 128 - gains.shape[0])).reshape(gain_rows, 128)
    small = jnp.concatenate([gains, grad_conv.reshape(-1, 128)])
    grad_qkv_s, grad_gate_s, d_normed_one, small_all, (grad_mgate_t, grad_mup_t, grad_down_h) = (
        scattered_last(
            grad_qkv,
            grad_gate,
            d_normed_part.astype(bf16),
            hat_own,
            [grad_mgate, grad_mup, grad_down],
            small,
            gain_rows,
            8,
        )
    )
    e_one = d_normed_one * gain_first
    d_input = (
        d_middle + scale_own * (e_one - hat_own * jnp.mean(e_one * hat_own, axis=-1, keepdims=True))
    ).astype(bf16)

    small_sum = jnp.sum(small_all, axis=0)
    gains = small_sum[:gain_rows].reshape(-1)

    def own_slice(begin, length):
        length = length // (seq_count * head_count)
        return lax.dynamic_slice(
            gains, (begin + (head_at * seq_count + seq_at) * length,), (length,)
        )

    grad_conv_s = lax.dynamic_slice_in_dim(
        small_sum[gain_rows:].reshape(-1, heads, inner),
        seq_at * (inner // seq_count),
        inner // seq_count,
        2,
    )
    return (
        output,
        d_input,
        own_slice(0, width),
        grad_qkv_s.astype(f32).reshape(-1, heads, inner),
        grad_conv_s,
        grad_gate_s.astype(f32).reshape(-1, heads, DV),
        own_slice(2 * width, DV),
        grad_out_s.astype(f32).T.reshape(heads, DV, -1),
        own_slice(width, width),
        grad_mgate_t.astype(f32).T,
        grad_mup_t.astype(f32).T,
        grad_down_h.astype(f32),
    )


def solution(mesh):
    in_specs = (
        P(("seq", "head"), None),
        P(("seq", "head"), None),
        P(),
        P(None, "head", None),
        P(None, "head", None),
        P(None, "head", None),
        P(),
        P("head", None, None),
        P(),
        P(None, "seq"),
        P(None, "seq"),
        P("seq", None),
        P("seq", "head"),
        P("seq", "head"),
    )
    out_specs = (
        P(("seq", "head"), None),
        P(("seq", "head"), None),
        P(("head", "seq")),
        P("seq", "head", None),
        P(None, "head", "seq"),
        P("seq", "head", None),
        P(("head", "seq")),
        P("head", None, "seq"),
        P(("head", "seq")),
        P("head", "seq"),
        P("head", "seq"),
        P("seq", "head"),
    )
    return jax.shard_map(
        on_device, mesh=mesh, in_specs=in_specs, out_specs=out_specs, check_vma=False
    )
```

```python
import functools
import math

import jax
import jax.numpy as jnp
from jax import lax
from jax.experimental import pallas as pl
from jax.experimental.pallas import tpu as pltpu
from jax.sharding import PartitionSpec as P

DK = 128
DV = 256
STRETCH = 64
GROUP = 4 * STRETCH
INNER = 2 * DK + DV
BETA, GAMMA, BETA_GAMMA, TAIL, LAST, RUN = range(6)

epsilon = 1e-06
bf16 = jnp.bfloat16
f32 = jnp.float32
VMEM_BYTES = 56 * 2**20
HOLD = 4


def passed_along(value, axis, steps):
    count = lax.axis_size(axis)
    first, last = (max(0, -steps), min(count, count - steps))
    return lax.ppermute(value, axis, [(source, source + steps) for source in range(first, last)])


def rms_scale(tensor):
    return lax.rsqrt(jnp.mean(tensor * tensor, axis=-1, keepdims=True) + epsilon)


def log_rates(decay_code, total_len):
    code_level = decay_code.astype(f32) / 1023.0
    smooth = -jnp.exp(-code_level * math.log(total_len / 32.0)) / 32.0
    return jnp.where(decay_code == 1024, -0.25, smooth)


def token_columns(decay_code, beta_code, total_len):
    rows, heads = decay_code.shape
    rates = log_rates(decay_code, total_len)
    run = jnp.einsum(
        "ij,bjh->bih",
        jnp.tril(jnp.ones((STRETCH, STRETCH), f32)),
        rates.reshape(rows // STRETCH, STRETCH, heads),
        precision=lax.Precision.HIGHEST,
    )
    last = jnp.broadcast_to(run[:, -1:], run.shape).reshape(rows, heads)
    run = run.reshape(rows, heads)
    beta = 0.5 + beta_code.astype(f32) / 512.0
    gamma = jnp.exp(run)
    columns = jnp.concatenate(
        [beta, gamma, beta * gamma, jnp.exp(last - run), jnp.exp(last), run], axis=1
    )
    columns = jnp.pad(columns, ((0, 0), (0, 128 - columns.shape[1])))
    run_rows = jnp.pad(run.T, ((0, 8 - heads % 8), (0, 0)))
    return columns, run_rows


def mm(left, right):
    return jnp.dot(left, right, preferred_element_type=f32)


def mm_nt(left, right):
    return lax.dot_general(left, right, (((1,), (1,)), ((), ())), preferred_element_type=f32)


def mm_tn(left, right):
    return lax.dot_general(left, right, (((0,), (0,)), ((), ())), preferred_element_type=f32)


def column(columns_ref, kind, head, heads):
    block = columns_ref[...]
    lanes = lax.broadcasted_iota(jnp.int32, block.shape, 1)
    return jnp.sum(jnp.where(lanes == kind * heads + head, block, 0.0), axis=1, keepdims=True)


def square_ids():
    return (
        lax.broadcasted_iota(jnp.int32, (GROUP, GROUP), 0),
        lax.broadcasted_iota(jnp.int32, (GROUP, GROUP), 1),
    )


def convolved(padded_ref, tail_ref, mixed_ref, taps_ref):
    rows = mixed_ref.shape[0]
    count = taps_ref.shape[0]
    padded_ref[0:8, :] = tail_ref[...]
    padded_ref[8 : 8 + rows, :] = mixed_ref[...].astype(f32)
    taps = taps_ref[...].astype(f32)
    start = 9 - count
    total = taps[0:1] * padded_ref[start : start + rows, :]
    for tap in range(1, count):
        total += taps[tap : tap + 1] * padded_ref[start + tap : start + tap + rows, :]
    return total


def chunk_masks_stack(transposed):
    lanes = lax.broadcasted_iota(jnp.int32, transposed.shape, 1) // STRETCH
    parts = [jnp.where(lanes == part, transposed, 0.0) for part in range(GROUP // STRETCH)]
    return jnp.concatenate(parts, axis=0).astype(bf16)


def local_forward(
    mixed_ref,
    tail_ref,
    taps_ref,
    columns_ref,
    run_rows_ref,
    solve_ref,
    score_ref,
    fresh_ref,
    reach_ref,
    inner_ref,
    turn_ref,
    local_ref,
    end_ref,
    padded,
    turn_t,
    offsets,
):
    head = pl.program_id(0)
    heads = pl.num_programs(0)
    rows = mixed_ref.shape[0]
    per_group = GROUP // STRETCH
    stretches = rows // STRETCH
    total = convolved(padded, tail_ref, mixed_ref, taps_ref)
    activated = total * jax.nn.sigmoid(total)
    raw_q, raw_k = activated[:, :DK], activated[:, DK : 2 * DK]
    queries = raw_q * (
        lax.rsqrt(jnp.sum(raw_q * raw_q, axis=1, keepdims=True) + epsilon) * DK ** (-0.5)
    )
    keys = raw_k * lax.rsqrt(jnp.sum(raw_k * raw_k, axis=1, keepdims=True) + epsilon)
    values = activated[:, 2 * DK :]
    beta = column(columns_ref, BETA, head, heads)
    gamma = column(columns_ref, GAMMA, head, heads)
    beta_gamma = column(columns_ref, BETA_GAMMA, head, heads)
    tail_decay = column(columns_ref, TAIL, head, heads)
    last = column(columns_ref, LAST, head, heads)
    run = column(columns_ref, RUN, head, heads)
    row_id, col_id = square_ids()
    same = row_id // STRETCH == col_id // STRETCH
    causal = same & (row_id >= col_id)
    diagonal = row_id == col_id
    eye = jnp.where(
        lax.broadcasted_iota(jnp.int32, (DK, DK), 0) == lax.broadcasted_iota(jnp.int32, (DK, DK), 1),
        1.0,
        0.0,
    )
    for group in range(rows // GROUP):
        span = slice(group * GROUP, (group + 1) * GROUP)
        key_b = keys[span].astype(bf16)
        query_b = queries[span].astype(bf16)
        gaps = run[span] - run_rows_ref[pl.ds(head, 1), span]
        within = jnp.exp(jnp.where(causal, gaps, -1e30))
        lower = jnp.where(diagonal, 0.0, beta[span] * within * mm_nt(key_b, key_b))
        solve = jnp.where(diagonal, 1.0, jnp.where(row_id // 2 == col_id // 2, -lower, 0.0))
        size = 2
        while size < STRETCH:
            crossing = (row_id // (2 * size) == col_id // (2 * size)) & (
                row_id // size != col_id // size
            )
            solve_b = solve.astype(bf16)
            half = mm(solve_b, jnp.where(crossing, lower, 0.0).astype(bf16))
            solve = solve - mm(half.astype(bf16), solve_b)
            size *= 2
        solve_b = solve.astype(bf16)
        right = jnp.concatenate([beta[span] * values[span], beta_gamma[span] * keys[span]], axis=1)
        fresh_b = mm(solve_b, right.astype(bf16)).astype(bf16)
        score_b = (within * mm_nt(query_b, key_b)).astype(bf16)
        scored = mm(score_b, fresh_b)
        solve_ref[group] = solve_b
        score_ref[group] = score_b
        fresh_ref[span, :] = fresh_b
        inner_ref[span, :] = scored[:, :DV]
        reach_ref[span, :] = (gamma[span] * queries[span] - scored[:, DV:]).astype(bf16)
        tail_keys = (tail_decay[span] * keys[span]).T
        moved = mm(chunk_masks_stack(tail_keys), fresh_b)
        for part in range(per_group):
            at = group * per_group + part
            block = moved[part * DK : (part + 1) * DK]
            stay = last[at * STRETCH : at * STRETCH + 1]
            turned = stay * eye - block[:, DV:]
            turn_t[head, at] = turned.astype(bf16)
            turn_ref[at] = turned.T.astype(bf16)
            offsets[head, at] = block[:, :DV]

    @pl.when(head == heads - 1)
    def _():
        states = [
            jnp.concatenate([jnp.zeros((DK, DV), f32), eye], axis=1)
            for _ in range(local_ref.shape[0])
        ]
        for at in range(stretches):
            for h in range(len(states)):
                state_b = states[h].astype(bf16)
                local_ref[h, at] = state_b
                moved = mm(turn_t[h, at], state_b)
                states[h] = jnp.concatenate(
                    [moved[:, :DV] + offsets[h, at], moved[:, DV:]], axis=1
                )
        for h in range(len(states)):
            end_ref[h] = states[h].astype(bf16)


def finish_forward(
    ends_ref, local_ref, reach_ref, inner_ref, gate_ref, gain_ref, state_ref, core_ref, branch_ref, start
):
    head = pl.program_id(0)
    heads, stretches = start.shape[0], local_ref.shape[0]

    @pl.when(head == 0)
    def _():
        start[...] = jnp.zeros_like(start)

        def one(source, carry):
            for h in range(heads):
                start[h] = (
                    mm(ends_ref[source, h, :, DV:], start[h].astype(bf16))
                    + ends_ref[source, h, :, :DV].astype(f32)
                )
            return carry

        lax.fori_loop(0, lax.axis_index("seq"), one, 0)

    start_b = start[head].astype(bf16)
    cores = []
    for at in range(stretches):
        state_b = (
            local_ref[at, :, :DV].astype(f32) + mm(local_ref[at, :, DV:], start_b)
        ).astype(bf16)
        state_ref[at] = state_b
        span = slice(at * STRETCH, (at + 1) * STRETCH)
        cores.append(inner_ref[span, :] + mm(reach_ref[span, :], state_b))
    core = jnp.concatenate(cores, axis=0)
    core_ref[...] = core
    gate = gate_ref[...]
    branch = core * rms_scale(core) * gain_ref[...].astype(f32) * (gate * jax.nn.sigmoid(gate))
    branch_ref[...] = branch.astype(bf16)


def local_backward(
    d_branch_ref,
    core_ref,
    gate_ref,
    gain_ref,
    reach_ref,
    turn_ref,
    d_core_ref,
    d_gate_ref,
    gain_part_ref,
    local_ref,
    end_ref,
    pulls,
):
    head = pl.program_id(0)
    heads = pl.num_programs(0)
    rows = core_ref.shape[0]
    per_group = GROUP // STRETCH
    stretches = rows // STRETCH
    core = core_ref[...]
    gate = gate_ref[...]
    gain = gain_ref[...].astype(f32)
    d_branch = d_branch_ref[...]
    scale = rms_scale(core)
    nhat = core * scale
    sig = jax.nn.sigmoid(gate)
    gated = d_branch * (gate * sig)

    @pl.when(head == 0)
    def _():
        gain_part_ref[...] = jnp.zeros_like(gain_part_ref)

    gain_part_ref[...] += jnp.sum(gated * nhat, axis=0, keepdims=True)
    f = gated * gain
    d_core = scale * (f - nhat * jnp.mean(f * nhat, axis=1, keepdims=True))
    d_gate_ref[...] = (d_branch * nhat * gain * sig * (1.0 + gate * (1.0 - sig))).astype(bf16)
    d_core_b = d_core.astype(bf16)
    d_core_ref[...] = d_core_b
    for group in range(rows // GROUP):
        span = slice(group * GROUP, (group + 1) * GROUP)
        pulled = mm(chunk_masks_stack(reach_ref[span, :].astype(f32).T), d_core_b[span])
        for part in range(per_group):
            pulls[head, group * per_group + part] = pulled[part * DK : (part + 1) * DK]

    @pl.when(head == heads - 1)
    def _():
        eye = jnp.where(
            lax.broadcasted_iota(jnp.int32, (DK, DK), 0)
            == lax.broadcasted_iota(jnp.int32, (DK, DK), 1),
            1.0,
            0.0,
        )
        grads = [
            jnp.concatenate([jnp.zeros((DK, DV), f32), eye], axis=1)
            for _ in range(local_ref.shape[0])
        ]
        for at in reversed(range(stretches)):
            for h in range(len(grads)):
                grad_b = grads[h].astype(bf16)
                local_ref[h, at] = grad_b
                moved = mm(turn_ref[h, at], grad_b)
                grads[h] = jnp.concatenate([moved[:, :DV] + pulls[h, at], moved[:, DV:]], axis=1)
        for h in range(len(grads)):
            end_ref[h] = grads[h][:, :DV].astype(bf16)


def finish_backward(
    ends_ref,
    grad_ends_ref,
    mixed_ref,
    tail_ref,
    taps_ref,
    columns_ref,
    run_rows_ref,
    solve_ref,
    score_ref,
    fresh_ref,
    state_ref,
    d_core_ref,
    local_ref,
    d_mixed_ref,
    tail_out_ref,
    lead_ref,
    grad_taps_ref,
    padded,
    spread,
    end,
):
    head = pl.program_id(0)
    heads = pl.num_programs(0)
    rows = mixed_ref.shape[0]
    per_group = GROUP // STRETCH

    @pl.when(head == 0)
    def _():
        end[...] = jnp.zeros_like(end)
        count = ends_ref.shape[0]

        def one(turn, carry):
            source = count - 1 - turn
            for h in range(end.shape[0]):
                end[h] = (
                    mm_tn(ends_ref[source, h, :, DV:], end[h].astype(bf16))
                    + grad_ends_ref[source, h].astype(f32)
                )
            return carry

        lax.fori_loop(0, count - 1 - lax.axis_index("seq"), one, 0)

    end_b = end[head].astype(bf16)
    total = convolved(padded, tail_ref, mixed_ref, taps_ref)
    sig = jax.nn.sigmoid(total)
    activated = total * sig
    raw_q, raw_k = activated[:, :DK], activated[:, DK : 2 * DK]
    scale_q = lax.rsqrt(jnp.sum(raw_q * raw_q, axis=1, keepdims=True) + epsilon)
    scale_k = lax.rsqrt(jnp.sum(raw_k * raw_k, axis=1, keepdims=True) + epsilon)
    unit_q = raw_q * scale_q
    keys = raw_k * scale_k
    beta = column(columns_ref, BETA, head, heads)
    gamma = column(columns_ref, GAMMA, head, heads)
    beta_gamma = column(columns_ref, BETA_GAMMA, head, heads)
    tail_decay = column(columns_ref, TAIL, head, heads)
    run = column(columns_ref, RUN, head, heads)
    row_id, col_id = square_ids()
    causal = (row_id // STRETCH == col_id // STRETCH) & (row_id >= col_id)
    diagonal = row_id == col_id
    d_queries, d_keys, d_values = [], [], []
    for group in range(rows // GROUP):
        span = slice(group * GROUP, (group + 1) * GROUP)
        key_b = keys[span].astype(bf16)
        query_b = (unit_q[span] * DK ** (-0.5)).astype(bf16)
        tail_keys = (tail_decay[span] * keys[span]).astype(bf16)
        d_core_b = d_core_ref[span, :]
        grad_bs, from_grad, fresh_parts, from_state = [], [], [], []
        for part in range(per_group):
            at = group * per_group + part
            own = slice(part * STRETCH, (part + 1) * STRETCH)
            rows_at = slice(at * STRETCH, (at + 1) * STRETCH)
            grad_b = (
                local_ref[at, :, :DV].astype(f32) + mm(local_ref[at, :, DV:], end_b)
            ).astype(bf16)
            grad_bs.append(grad_b)
            from_grad.append(mm(tail_keys[own], grad_b))
            fresh_parts.append(mm(fresh_ref[rows_at, DV:], state_ref[at]))
            from_state.append(mm_nt(d_core_b[own], state_ref[at]))
        d_fresh = mm_tn(score_ref[group], d_core_b) + jnp.concatenate(from_grad, axis=0)
        d_right = mm_tn(solve_ref[group], d_fresh.astype(bf16))
        d_right_b = d_right.astype(bf16)
        fresh = fresh_ref[span, :DV].astype(f32) - jnp.concatenate(fresh_parts, axis=0)
        fresh_b = fresh.astype(bf16)
        gaps = run[span] - run_rows_ref[pl.ds(head, 1), span]
        within = jnp.exp(jnp.where(causal, gaps, -1e30))
        d_score = (within * mm_nt(d_core_b, fresh_b)).astype(bf16)
        d_lower = jnp.where(
            diagonal, 0.0, -beta[span] * within * mm_nt(d_right_b, fresh_b)
        ).astype(bf16)
        state_keys, grad_keys = [], []
        for part in range(per_group):
            at = group * per_group + part
            own = slice(part * STRETCH, (part + 1) * STRETCH)
            state_keys.append(mm_nt(d_right_b[own], state_ref[at]))
            grad_keys.append(mm_nt(fresh_b[own], grad_bs[part]))
        d_queries.append(gamma[span] * jnp.concatenate(from_state, axis=0) + mm(d_score, key_b))
        d_keys.append(
            mm_tn(d_score, query_b)
            + mm_tn(d_lower, key_b)
            + mm(d_lower, key_b)
            + tail_decay[span] * jnp.concatenate(grad_keys, axis=0)
            - beta_gamma[span] * jnp.concatenate(state_keys, axis=0)
        )
        d_values.append(beta[span] * d_right)
    g_q = jnp.concatenate(d_queries, axis=0) * DK ** (-0.5)
    g_k = jnp.concatenate(d_keys, axis=0)
    d_act = jnp.concatenate(
        [
            scale_q * (g_q - unit_q * jnp.sum(unit_q * g_q, axis=1, keepdims=True)),
            scale_k * (g_k - keys * jnp.sum(keys * g_k, axis=1, keepdims=True)),
            jnp.concatenate(d_values, axis=0),
        ],
        axis=1,
    )
    d_conv = d_act * (sig * (1.0 + total * (1.0 - sig)))
    taps = taps_ref[...].astype(f32)
    count = taps_ref.shape[0]
    start = 9 - count
    grad_taps_ref[...] = jnp.concatenate(
        [
            jnp.sum(padded[start + tap : start + tap + rows, :] * d_conv, axis=0, keepdims=True)
            for tap in range(count)
        ],
        axis=0,
    )
    spread[0:8, :] = jnp.zeros((8, d_conv.shape[1]), f32)
    spread[8 : 8 + rows, :] = d_conv
    spread[8 + rows : 16 + rows, :] = jnp.zeros((8, d_conv.shape[1]), f32)
    lead = taps[0:1] * spread[8:16, :]
    d_mixed = taps[0:1] * spread[7 + count : 7 + count + rows, :]
    for tap in range(1, count):
        lead += taps[tap : tap + 1] * spread[8 - tap : 16 - tap, :]
        begin = 7 + count - tap
        d_mixed += taps[tap : tap + 1] * spread[begin : begin + rows, :]
    lead_ref[...] = lead
    d_mixed_ref[...] = d_mixed.astype(bf16)
    tail_out_ref[...] = d_mixed[rows - 8 :]


def whole(shape):
    return pl.BlockSpec(shape, lambda h: (0,) * len(shape))


def by_head(shape):
    return pl.BlockSpec((None,) + shape, lambda h: (h,) + (0,) * len(shape))


def by_columns(rows, width):
    return pl.BlockSpec((rows, width), lambda h: (0, h))


def kernel_call(body, heads, ins, outs, out_shapes, scratch, flops, moved):
    return pl.pallas_call(
        body,
        grid=(heads,),
        in_specs=ins,
        out_specs=outs,
        out_shape=out_shapes,
        scratch_shapes=scratch,
        compiler_params=pltpu.CompilerParams(
            dimension_semantics=("arbitrary",), vmem_limit_bytes=VMEM_BYTES
        ),
        cost_estimate=pl.CostEstimate(flops=flops, bytes_accessed=moved, transcendentals=0),
    )


def shaped(shape, kind):
    return jax.ShapeDtypeStruct(shape, kind)


def run_local_forward(mixed, tail, taps, columns, run_rows, heads):
    rows = mixed.shape[1]
    count = taps.shape[0]
    groups, stretches = rows // GROUP, rows // STRETCH
    return kernel_call(
        local_forward,
        heads,
        [
            by_head((rows, INNER)),
            by_head((8, INNER)),
            by_columns(count, INNER),
            whole(columns.shape),
            whole(run_rows.shape),
        ],
        [
            by_head((groups, GROUP, GROUP)),
            by_head((groups, GROUP, GROUP)),
            by_head((rows, DV + DK)),
            by_head((rows, DK)),
            by_columns(rows, DV),
            by_head((stretches, DK, DK)),
            whole((heads, stretches, DK, DV + DK)),
            whole((heads, DK, DV + DK)),
        ],
        [
            shaped((heads, groups, GROUP, GROUP), bf16),
            shaped((heads, groups, GROUP, GROUP), bf16),
            shaped((heads, rows, DV + DK), bf16),
            shaped((heads, rows, DK), bf16),
            shaped((rows, heads * DV), f32),
            shaped((heads, stretches, DK, DK), bf16),
            shaped((heads, stretches, DK, DV + DK), bf16),
            shaped((heads, DK, DV + DK), bf16),
        ],
        [
            pltpu.VMEM((rows + 8, INNER), f32),
            pltpu.VMEM((heads, stretches, DK, DK), bf16),
            pltpu.VMEM((heads, stretches, DK, DV), f32),
        ],
        12_000_000_000,
        20_000_000,
    )(mixed, tail, taps, columns, run_rows)


def run_finish_forward(ends, local, reach, inner, gate_pre, gain):
    heads, stretches = local.shape[:2]
    rows = inner.shape[0]
    return kernel_call(
        finish_forward,
        heads,
        [
            whole(ends.shape),
            by_head((stretches, DK, DV + DK)),
            by_head((rows, DK)),
            by_columns(rows, DV),
            by_head((rows, DV)),
            whole(gain.shape),
        ],
        [by_head((stretches, DK, DV)), by_columns(rows, DV), by_columns(rows, DV)],
        [
            shaped((heads, stretches, DK, DV), bf16),
            shaped((rows, heads * DV), f32),
            shaped((rows, heads * DV), bf16),
        ],
        [pltpu.VMEM((heads, DK, DV), f32)],
        3_000_000_000,
        20_000_000,
    )(ends, local, reach, inner, gate_pre, gain)


def run_local_backward(d_branch, core, gate_pre, gain, reach, turn):
    heads, stretches = turn.shape[:2]
    rows = core.shape[0]
    return kernel_call(
        local_backward,
        heads,
        [
            by_columns(rows, DV),
            by_columns(rows, DV),
            by_head((rows, DV)),
            whole(gain.shape),
            by_head((rows, DK)),
            whole(turn.shape),
        ],
        [
            by_columns(rows, DV),
            by_columns(rows, DV),
            whole((1, DV)),
            whole((heads, stretches, DK, DV + DK)),
            whole((heads, DK, DV)),
        ],
        [
            shaped((rows, heads * DV), bf16),
            shaped((rows, heads * DV), bf16),
            shaped((1, DV), f32),
            shaped((heads, stretches, DK, DV + DK), bf16),
            shaped((heads, DK, DV), bf16),
        ],
        [pltpu.VMEM((heads, stretches, DK, DV), f32)],
        4_000_000_000,
        20_000_000,
    )(d_branch, core, gate_pre, gain, reach, turn)


def run_finish_backward(
    ends, grad_ends, mixed, tail, taps, columns, run_rows, solve, score, fresh, states, d_core, local
):
    heads, stretches = local.shape[:2]
    rows = mixed.shape[1]
    groups = rows // GROUP
    count = taps.shape[0]
    return kernel_call(
        finish_backward,
        heads,
        [
            whole(ends.shape),
            whole(grad_ends.shape),
            by_head((rows, INNER)),
            by_head((8, INNER)),
            by_columns(count, INNER),
            whole(columns.shape),
            whole(run_rows.shape),
            by_head((groups, GROUP, GROUP)),
            by_head((groups, GROUP, GROUP)),
            by_head((rows, DV + DK)),
            by_head((stretches, DK, DV)),
            by_columns(rows, DV),
            by_head((stretches, DK, DV + DK)),
        ],
        [
            by_columns(rows, INNER),
            by_columns(8, INNER),
            by_columns(8, INNER),
            by_columns(count, INNER),
        ],
        [
            shaped((rows, heads * INNER), bf16),
            shaped((8, heads * INNER), f32),
            shaped((8, heads * INNER), f32),
            shaped((count, heads * INNER), f32),
        ],
        [
            pltpu.VMEM((rows + 8, INNER), f32),
            pltpu.VMEM((rows + 16, INNER), f32),
            pltpu.VMEM((heads, DK, DV), f32),
        ],
        12_000_000_000,
        20_000_000,
    )(ends, grad_ends, mixed, tail, taps, columns, run_rows, solve, score, fresh, states, d_core, local)


MESH = pl.DeviceIdType.MESH
SIDE = 2


def remote(source, target, send, arrive, device):
    return pltpu.make_async_remote_copy(
        src_ref=source,
        dst_ref=target,
        send_sem=send,
        recv_sem=arrive,
        device_id=device,
        device_id_type=MESH,
    )


def greet(partners):
    barrier = pltpu.get_barrier_semaphore()
    expected = 0
    for device, there in partners:
        if there is None:
            pl.semaphore_signal(barrier, inc=1, device_id=device, device_id_type=MESH)
            expected = expected + 1
        else:

            @pl.when(there)
            def _(device=device):
                pl.semaphore_signal(barrier, inc=1, device_id=device, device_id_type=MESH)

            expected = expected + there.astype(jnp.int32)
    pl.semaphore_wait(barrier, expected)


def head_places():
    head, seq = lax.axis_index("head"), lax.axis_index("seq")
    core = lax.rem(head, 2)
    sibling = head + 1 - 2 * core
    across = lax.rem(head + 2, 4)
    return head, seq, sibling, across


def head_partners():
    head, seq, sibling, across = head_places()
    return [((sibling, seq), None), ((across, seq), None)]


def seq_places():
    head, seq = lax.axis_index("head"), lax.axis_index("seq")
    return head, seq // SIDE, lax.rem(seq, SIDE)


def seq_partners(count):
    head, line, side = seq_places()
    return [
        ((head, line * SIDE + 1 - side), None),
        ((head, (line + 1) * SIDE + side), line < count - 1),
        ((head, (line - 1) * SIDE + side), line > 0),
    ]


def run_together(steps):
    steps = list(steps)
    while steps:
        alive = []
        for step in steps:
            try:
                next(step)
                alive.append(step)
            except StopIteration:
                pass
        steps = alive


def gather_head(own_ref, out_ref, local, send, arrive, pieces):
    head, seq, sibling, across = head_places()
    far = lax.rem(sibling + 2, 4)
    rows = own_ref.shape[0] // pieces
    keep = pltpu.make_async_copy(own_ref, out_ref.at[head], local.at[0])
    keep.start()

    def part(ref, piece):
        return ref.at[pl.ds(piece * rows, rows)]

    outgoing = []
    for piece in range(pieces):
        outgoing.append(
            remote(
                part(own_ref, piece),
                part(out_ref.at[head], piece),
                send.at[0, piece],
                arrive.at[0, piece],
                (across, seq),
            )
        )
    for piece in range(pieces):
        outgoing.append(
            remote(
                part(own_ref, piece),
                part(out_ref.at[head], piece),
                send.at[1, piece],
                arrive.at[1, piece],
                (sibling, seq),
            )
        )
    for copy in outgoing:
        copy.start()
    yield
    forwards = []
    for piece in range(pieces):
        outgoing[piece].wait_recv()
        forward = remote(
            part(out_ref.at[across], piece),
            part(out_ref.at[across], piece),
            send.at[2, piece],
            arrive.at[2, piece],
            (sibling, seq),
        )
        forward.start()
        forwards.append(forward)
        yield
    for copy in outgoing[pieces:] + forwards:
        copy.wait_recv()
    for copy in outgoing + forwards:
        copy.wait_send()
    keep.wait()


def scatter_head(source_at, out_ref, own, crossed, passed, local, send, arrive, hold=0, pause=0):
    head, seq, sibling, across = head_places()
    far = lax.rem(sibling + 2, 4)
    loads = [
        pltpu.make_async_copy(source_at(target), own.at[slot], local.at[slot])
        for slot, target in enumerate((across, head))
    ]
    copies = [
        remote(source_at(target), crossed.at[slot], send.at[slot], arrive.at[slot], (sibling, seq))
        for slot, target in enumerate((far, sibling))
    ]
    for slot in range(2):
        copies[slot].start()
        loads[slot].start()
    for _ in range(1 + hold):
        yield
    loads[0].wait()
    copies[0].wait_recv()
    own[0] = (own[0].astype(f32) + crossed[0].astype(f32)).astype(own.dtype)
    onward = remote(own.at[0], passed, send.at[2], arrive.at[2], (across, seq))
    onward.start()
    for _ in range(1 + pause):
        yield
    loads[1].wait()
    copies[1].wait_recv()
    onward.wait_recv()
    total = own[1].astype(f32) + crossed[1].astype(f32) + passed[...].astype(f32)
    out_ref[...] = total.astype(out_ref.dtype)
    onward.wait_send()
    for copy in copies:
        copy.wait_send()


def gather_seq(own_ref, out_ref, local, side_send, side_arrive, line_send, line_arrive, count):
    head, line, side = seq_places()
    me = line * SIDE + side
    beside = (head, line * SIDE + 1 - side)
    ways = ((1, line < count - 1), (-1, line > 0))
    keep = pltpu.make_async_copy(own_ref, out_ref.at[me], local.at[0])
    keep.start()

    def along(source, block, way, step):
        slot = step if way > 0 else count + step
        return remote(
            source,
            out_ref.at[block],
            line_send.at[slot],
            line_arrive.at[slot],
            (head, (line + way) * SIDE + side),
        )

    def over(source, block, slot):
        return remote(source, out_ref.at[block], side_send.at[slot], side_arrive.at[slot], beside)

    for way, onward in ways:

        @pl.when(onward)
        def _(way=way):
            along(own_ref, me, way, 0).start()

    over(own_ref, me, 0).start()
    yield
    for step in range(1, count):
        for way, onward in ways:
            block = me - way * step * SIDE
            arrives = line >= step if way > 0 else line + step < count

            @pl.when(arrives)
            def _(way=way, onward=onward, block=block, step=step):
                landed = out_ref.at[block]
                slot = step if way > 0 else count + step
                remote(
                    landed, landed, line_send.at[slot - 1], line_arrive.at[slot - 1], beside
                ).wait_recv()

                @pl.when(onward)
                def _():
                    along(landed, block, way, step).start()

                over(landed, block, slot).start()

        yield
    over(own_ref, me, 0).wait()
    for way, onward in ways:

        @pl.when(onward)
        def _(way=way):
            along(own_ref, me, way, 0).wait_send()

    for step in range(1, count):
        for way, onward in ways:
            block = me - way * step * SIDE
            arrives = line >= step if way > 0 else line + step < count

            @pl.when(arrives)
            def _(way=way, onward=onward, block=block, step=step):
                landed = out_ref.at[block]
                slot = step if way > 0 else count + step
                over(landed, block, slot).wait()

                @pl.when(onward)
                def _():
                    along(landed, block, way, step).wait_send()

    keep.wait()


def scatter_seq(source_at, out_at, own, crossed, risen, fallen, local, sends, arrivals, count):
    head, line, side = seq_places()
    beside = (head, line * SIDE + 1 - side)
    pieces = own.shape[0]

    def targets(distance):
        if distance == 0:
            return [(line, None, 0)]
        return [
            (line - distance, line >= distance, -1),
            (line + distance, line + distance < count, 1),
        ]

    def load(piece, target):
        return pltpu.make_async_copy(
            source_at(target, side, piece), own.at[piece, target], local.at[piece, target]
        )

    def cross(piece, target):
        return remote(
            source_at(target, 1 - side, piece),
            crossed.at[piece, target],
            sends.at[0, piece, target],
            arrivals.at[0, piece, target],
            beside,
        )

    def onward(piece, target, way, arriving=False):
        landing = risen if way > 0 else fallen
        return remote(
            own.at[piece, target],
            landing.at[piece, target],
            sends.at[1, piece, target],
            arrivals.at[1 if way > 0 else 2, piece, target],
            beside if arriving else (head, (line + way) * SIDE + side),
        )

    def guarded(there, body):
        if there is None:
            body()
        else:
            pl.when(there)(body)

    def here(piece, target):
        load(piece, target).wait()
        total = own[piece, target].astype(f32)
        if crossed is not None:
            cross(piece, target).wait_recv()
            total += crossed[piece, target].astype(f32)
        return total

    def arrived(piece, target, way):
        landing = risen if way > 0 else fallen
        onward(piece, target, way, True).wait_recv()
        return landing[piece, target].astype(f32)

    for piece in range(pieces):
        for distance in range(count - 1, -1, -1):
            for target, there, _ in targets(distance):

                def begin(piece=piece, target=target):
                    if crossed is not None:
                        cross(piece, target).start()
                    load(piece, target).start()

                guarded(there, begin)
    yield
    for piece in range(pieces):
        for distance in range(count - 1, 0, -1):
            for target, there, way in targets(distance):
                first = line == count - 1 if way < 0 else line == 0

                @pl.when(jnp.logical_and(there, first))
                def _(piece=piece, target=target, way=way):
                    own[piece, target] = here(piece, target).astype(own.dtype)
                    onward(piece, target, way).start()

                @pl.when(jnp.logical_and(there, jnp.logical_not(first)))
                def _(piece=piece, target=target, way=way):
                    total = here(piece, target) + arrived(piece, target, way)
                    own[piece, target] = total.astype(own.dtype)
                    onward(piece, target, way).start()

            yield
        out = out_at(piece)

        @pl.when(line == 0)
        def _(piece=piece, out=out):
            out[...] = (here(piece, line) + arrived(piece, line, -1)).astype(out.dtype)

        @pl.when(line == count - 1)
        def _(piece=piece, out=out):
            out[...] = (here(piece, line) + arrived(piece, line, 1)).astype(out.dtype)

        @pl.when(jnp.logical_and(line > 0, line < count - 1))
        def _(piece=piece, out=out):
            total = here(piece, line) + arrived(piece, line, -1) + arrived(piece, line, 1)
            out[...] = total.astype(out.dtype)

        yield
    for piece in range(pieces):
        for distance in range(count - 1, -1, -1):
            for target, there, way in targets(distance):

                def finish(piece=piece, target=target, way=way):
                    if crossed is not None:
                        cross(piece, target).wait_send()
                    if way:
                        onward(piece, target, way).wait_send()

                guarded(there, finish)


ANY = pl.BlockSpec(memory_space=pl.ANY)
IN_VMEM = pl.BlockSpec(memory_space=pltpu.VMEM)
DMA = pltpu.SemaphoreType.DMA


def link_call(body, number, ins, outs, shapes, scratch, moved):
    return pl.pallas_call(
        body,
        in_specs=ins,
        out_specs=outs,
        out_shape=shapes,
        scratch_shapes=scratch,
        compiler_params=pltpu.CompilerParams(
            collective_id=number, has_side_effects=True, vmem_limit_bytes=VMEM_BYTES
        ),
        cost_estimate=pl.CostEstimate(flops=0, bytes_accessed=moved // 8, transcendentals=0),
    )


def gathered_head(value, number, pieces=4):
    count = lax.axis_size("head")
    if count != 4:
        return lax.all_gather(value, "head", axis=0, tiled=True)
    rows, width = value.shape

    def body(own_ref, out_ref, local, send, arrive):
        greet(head_partners())
        run_together([gather_head(own_ref, out_ref, local, send, arrive, pieces)])

    out = link_call(
        body,
        number,
        [ANY],
        ANY,
        shaped((count, rows, width), value.dtype),
        [DMA((1,)), DMA((3, pieces)), DMA((3, pieces))],
        60_000_000,
    )(value)
    return out.reshape(count * rows, width)


def gathered_crossed(value, half, number, pieces=4):
    count = lax.axis_size("head")
    rows, width = value.shape

    def body(own_ref, half_ref, out_ref, landed_ref, local, send, arrive, crossing):
        head, line, side = seq_places()
        beside = (head, line * SIDE + 1 - side)
        greet(head_partners() + [(beside, None)])
        cross = remote(half_ref, landed_ref, crossing.at[0], crossing.at[1], beside)
        cross.start()
        run_together([gather_head(own_ref, out_ref, local, send, arrive, pieces)])
        cross.wait()

    out, landed = link_call(
        body,
        number,
        [ANY, ANY],
        [ANY, ANY],
        [shaped((count, rows, width), value.dtype), shaped(half.shape, half.dtype)],
        [DMA((1,)), DMA((3, pieces)), DMA((3, pieces)), DMA((2,))],
        60_000_000,
    )(value, half)
    return out.reshape(count * rows, width), landed


def gathered_seq(value, number):
    total = lax.axis_size("seq")
    count = total // SIDE
    rows, width = value.shape
    if total % SIDE or count < 2:
        return lax.all_gather(value, "seq")

    def body(own_ref, out_ref, *sems):
        greet(seq_partners(count))
        run_together([gather_seq(own_ref, out_ref, *sems, count)])

    return link_call(
        body,
        number,
        [ANY],
        ANY,
        shaped((total, rows, width), value.dtype),
        [DMA((1,))] + [DMA((2 * count,)) for _ in range(4)],
        120_000_000,
    )(value)


def head_scratch(rows, width):
    return [
        pltpu.VMEM((2, rows, width), bf16),
        pltpu.VMEM((2, rows, width), bf16),
        pltpu.VMEM((rows, width), bf16),
        DMA((2,)),
        DMA((3,)),
        DMA((3,)),
    ]


def seq_scratch(pieces, count, rows, width):
    return [pltpu.VMEM((pieces, count, rows, width), bf16) for _ in range(4)] + [
        DMA((pieces, count)),
        DMA((2, pieces, count)),
        DMA((3, pieces, count)),
    ]


def scattered_head(value, number, pieces=2):
    count = lax.axis_size("head")
    if count != 4:
        return scattered(value, "head")
    rows, width = value.shape[0] // count, value.shape[1] // pieces

    def body(source, out, *rest):
        greet(head_partners())
        steps = []
        for piece in range(pieces):
            span = pl.ds(piece * width, width)

            def source_at(target, span=span):
                return source.at[pl.ds(pl.multiple_of(target * rows, rows), rows), span]

            steps.append(
                scatter_head(source_at, out.at[:, span], *rest[6 * piece : 6 * piece + 6])
            )
        run_together(steps)

    return link_call(
        body,
        number,
        [ANY],
        IN_VMEM,
        shaped((rows, value.shape[1]), f32),
        head_scratch(rows, width) * pieces,
        60_000_000,
    )(value)


def scattered_seq(value, number, pieces=2):
    total = lax.axis_size("seq")
    count = total // SIDE
    if total % SIDE or count < 2:
        return scattered(value, "seq")
    rows, width = value.shape[0] // total, value.shape[1] // pieces

    def body(source, out, *rest):
        greet(seq_partners(count))

        def source_at(target, side, piece):
            begin = pl.multiple_of((target * SIDE + side) * rows, rows)
            return source.at[pl.ds(begin, rows), pl.ds(piece * width, width)]

        def out_at(piece):
            return out.at[:, pl.ds(piece * width, width)]

        run_together([scatter_seq(source_at, out_at, *rest, count)])

    return link_call(
        body,
        number,
        [ANY],
        IN_VMEM,
        shaped((rows, value.shape[1]), f32),
        seq_scratch(pieces, count, rows, width),
        120_000_000,
    )(value)


def product_steps(left_hbm, right_hbm, out_refs, picks, lefts, rights, tiles, load, store, per_round):
    loads = [
        pltpu.make_async_copy(ref, held, load.at[index])
        for index, (ref, held) in enumerate(zip(left_hbm + right_hbm, lefts + rights))
    ]
    for copy in loads:
        copy.start()
    yield
    for copy in loads:
        copy.wait()
    units, width = tiles.shape[1:]
    block = units // 4 if units % 64 == 0 else units
    span = 512
    stores = []
    done = 0
    for index, pick in enumerate(picks):
        for begin in range(0, width, span):
            columns = pl.ds(begin, span)

            def one(part, carry, index=index, pick=pick, columns=columns):
                rows = pl.ds(pl.multiple_of(part * block, block), block)
                tiles[index, rows, columns] = mm(
                    lefts[index][rows, :], rights[pick][:, columns]
                ).astype(tiles.dtype)
                return carry

            lax.fori_loop(0, units // block, one, 0)
            done += 1
            if done % per_round == 0:
                yield
        copy = pltpu.make_async_copy(tiles.at[index], out_refs[index], store.at[index])
        copy.start()
        stores.append(copy)
    for copy in stores:
        copy.wait()


def scattered_seq_products(value, lefts, rights, picks, number, pieces=2):
    total = lax.axis_size("seq")
    count = total // SIDE
    rows, width = value.shape[0] // total, value.shape[1] // pieces
    units, depth = lefts[0].shape
    breadth = rights[0].shape[1]
    n_left, n_right = len(lefts), len(rights)
    held = 4 * value.size // SIDE + n_left * units * (depth + breadth) + n_right * rights[0].size
    if 2 * held > VMEM_BYTES:
        products = [mm(left, rights[pick]).astype(bf16) for left, pick in zip(lefts, picks)]
        return scattered_seq(value, number, pieces), products

    def body(source, *rest):
        left_hbm, rest = rest[:n_left], rest[n_left:]
        right_hbm, rest = rest[:n_right], rest[n_right:]
        out, out_refs, rest = rest[0], rest[1 : 1 + n_left], rest[1 + n_left :]
        link, rest = rest[:7], rest[7:]
        left_held, rest = rest[:n_left], rest[n_left:]
        right_held, rest = rest[:n_right], rest[n_right:]
        greet(seq_partners(count))

        def source_at(target, side, piece):
            begin = pl.multiple_of((target * SIDE + side) * rows, rows)
            return source.at[pl.ds(begin, rows), pl.ds(piece * width, width)]

        def out_at(piece):
            return out.at[:, pl.ds(piece * width, width)]

        run_together(
            [
                scatter_seq(source_at, out_at, *link, count),
                product_steps(
                    left_hbm, right_hbm, out_refs, picks, left_held, right_held, *rest, 2
                ),
            ]
        )

    outs = link_call(
        body,
        number,
        [ANY] * (1 + n_left + n_right),
        [IN_VMEM] + [ANY] * n_left,
        [shaped((rows, value.shape[1]), f32)]
        + [shaped((units, breadth), bf16) for _ in lefts],
        seq_scratch(pieces, count, rows, width)
        + [pltpu.VMEM((units, depth), bf16) for _ in lefts]
        + [pltpu.VMEM((depth, breadth), bf16) for _ in rights]
        + [
            pltpu.VMEM((n_left, units, breadth), bf16),
            DMA((n_left + n_right,)),
            DMA((n_left,)),
        ],
        120_000_000,
    )(value, *lefts, *rights)
    return outs[0], list(outs[1:])


def gathered_more(ends, half, number, swap=None):
    total, heads = lax.axis_size("seq"), lax.axis_size("head")
    count = total // SIDE
    swaps = [] if swap is None else [swap]

    def body(ends_ref, half_ref, *rest):
        head, line, side = seq_places()
        beside = (head, line * SIDE + 1 - side)
        swap_refs, rest = rest[: len(swaps)], rest[len(swaps) :]
        ends_out, half_out, rest = rest[0], rest[1], rest[2:]
        swap_outs, rest = rest[: len(swaps)], rest[len(swaps) :]
        greet(head_partners() + seq_partners(count))

        def swap_steps(source, target):
            yield
            yield
            copy = remote(source, target, rest[8].at[0], rest[8].at[1], beside)
            copy.start()
            for _ in range(count):
                yield
            copy.wait()

        run_together(
            [
                gather_seq(ends_ref, ends_out, *rest[:5], count),
                gather_head(half_ref, half_out, *rest[5:8], 1),
            ]
            + [swap_steps(*refs) for refs in zip(swap_refs, swap_outs)]
        )

    outs = link_call(
        body,
        number,
        [ANY] * (2 + len(swaps)),
        [ANY] * (2 + len(swaps)),
        [
            shaped((total,) + ends.shape, ends.dtype),
            shaped((heads,) + half.shape, half.dtype),
        ]
        + [shaped(value.shape, value.dtype) for value in swaps],
        [DMA((1,))]
        + [DMA((2 * count,)) for _ in range(4)]
        + [DMA((1,)), DMA((3, 1)), DMA((3, 1)), DMA((2,))],
        150_000_000,
    )(ends, half, *swaps)
    return [outs[0], outs[1].reshape(-1, half.shape[1])] + list(outs[2:])


def scattered_last(qkv, gate, normed, hat, mlp, small, gain_rows, number, pieces=4, gate_pieces=2):
    total, heads = lax.axis_size("seq"), lax.axis_size("head")
    count = total // SIDE
    rows, width = qkv.shape[0] // total, qkv.shape[1] // pieces
    gate_width = gate.shape[1] // gate_pieces
    own_rows = normed.shape[0] // heads
    units, slices = mlp[0].shape[0], mlp[0].shape[1] // heads
    small_rows = small.shape[0]

    def body(qkv_ref, gate_ref, normed_ref, hat_ref, small_ref, *rest):
        mlp_refs, rest = rest[: len(mlp)], rest[len(mlp) :]
        qkv_out, gate_out, normed_out, small_out, rest = rest[0], rest[1], rest[2], rest[3], rest[4:]
        mlp_outs, rest = rest[: len(mlp)], rest[len(mlp) :]
        greet(head_partners() + seq_partners(count))

        def qkv_at(target, side, piece):
            begin = pl.multiple_of((target * SIDE + side) * rows, rows)
            return qkv_ref.at[pl.ds(begin, rows), pl.ds(piece * width, width)]

        def gate_at(target, side, piece):
            begin = pl.multiple_of(target * rows, rows)
            return gate_ref.at[pl.ds(begin, rows), pl.ds(piece * gate_width, gate_width)]

        def normed_at(target):
            return normed_ref.at[pl.ds(pl.multiple_of(target * own_rows, own_rows), own_rows)]

        def normed_steps(four, own, local, *sems):
            yield from scatter_head(normed_at, normed_out, *rest[13:19], 0, 1)
            own[...] = small_ref[...]
            product = jnp.sum(normed_out[...] * hat_ref[...], axis=0, keepdims=True)
            for row in range(product.shape[1] // 128):
                own[row : row + 1] = product[:, row * 128 : (row + 1) * 128]
            yield
            yield from gather_head(own, four, sems[0], sems[1], sems[2], 1)
            own[:gain_rows] = jnp.sum(four[:, :gain_rows], axis=0)
            for step in gather_seq(own, small_out, local, *sems[3:7], count):
                for _ in range(3):
                    yield

        steps = [
            normed_steps(*rest[19:29]),
            scatter_seq(
                gate_at,
                lambda piece: gate_out.at[:, pl.ds(piece * gate_width, gate_width)],
                rest[7],
                None,
                *rest[8:13],
                count,
            ),
            scatter_seq(
                qkv_at,
                lambda piece: qkv_out.at[:, pl.ds(piece * width, width)],
                *rest[:7],
                count,
            ),
        ]
        for index, (ref, out) in enumerate(zip(mlp_refs, mlp_outs)):

            def mlp_at(target, ref=ref):
                return ref.at[:, pl.ds(pl.multiple_of(target * slices, slices), slices)]

            begin = 29 + 6 * index
            steps.append(
                scatter_head(mlp_at, out, *rest[begin : begin + 6], HOLD, 2 + 3 * index)
            )
        run_together(steps)

    line_scratch = seq_scratch(gate_pieces, count, rows, gate_width)
    outs = link_call(
        body,
        number,
        [ANY] * 3 + [IN_VMEM] * 2 + [ANY] * len(mlp),
        [IN_VMEM] * (4 + len(mlp)),
        [
            shaped((rows, qkv.shape[1]), bf16),
            shaped((rows, gate.shape[1]), bf16),
            shaped((own_rows, normed.shape[1]), f32),
            shaped((total, small_rows, small.shape[1]), f32),
        ]
        + [shaped((units, slices), bf16) for _ in mlp],
        seq_scratch(pieces, count, rows, width)
        + line_scratch[1:]
        + head_scratch(own_rows, normed.shape[1])
        + [
            pltpu.VMEM((heads, small_rows, small.shape[1]), f32),
            pltpu.VMEM((small_rows, small.shape[1]), f32),
            DMA((1,)),
            DMA((1,)),
            DMA((3, 1)),
            DMA((3, 1)),
        ]
        + [DMA((2 * count,)) for _ in range(4)]
        + head_scratch(units, slices) * len(mlp),
        250_000_000,
    )(qkv, gate, normed, hat, small, *mlp)
    return outs[0], outs[1], outs[2], outs[3], list(outs[4:])


def side_columns(value, side, rows):
    count = value.shape[1] // (rows * SIDE)
    return jnp.concatenate(
        [
            lax.dynamic_slice_in_dim(value, (place * SIDE + side) * rows, rows, 1)
            for place in range(count)
        ],
        axis=1,
    )


def swapped(value):
    count = lax.axis_size("seq")
    return lax.ppermute(value, "seq", [(place, place ^ 1) for place in range(count)])


def silu_slope(tensor):
    sigmoid_part = jax.nn.sigmoid(tensor)
    return sigmoid_part * (1.0 + tensor * (1.0 - sigmoid_part))


def gathered(value, axis):
    return lax.all_gather(value, axis, axis=0, tiled=True)


def scattered(value, axis, dimension=0):
    return lax.psum_scatter(
        value.astype(bf16), axis, scatter_dimension=dimension, tiled=True
    ).astype(f32)


def on_device(
    block_in,
    out_cot,
    gain_one,
    qkv_weight,
    conv_weight,
    gate_weight,
    gain_out,
    out_weight,
    gain_two,
    mlp_gate,
    mlp_up,
    mlp_down,
    decay_code,
    beta_code,
):
    span_rows = decay_code.shape[0]
    width, heads, inner = qkv_weight.shape
    total_len = span_rows * lax.axis_size("seq")
    lead_rows = conv_weight.shape[0] - 1
    input_f = block_in.astype(f32)
    gain_first = gain_one.astype(f32)
    gain_second = gain_two.astype(f32)
    gain_head = gain_out.reshape(1, -1)
    taps = conv_weight.reshape(conv_weight.shape[0], heads * inner)
    out_flat = out_weight.reshape(heads * DV, width)
    columns, run_rows = token_columns(decay_code, beta_code, total_len)

    cot_all = gathered(out_cot, "seq")
    seq_count, head_count = lax.axis_size("seq"), lax.axis_size("head")
    seq_at, head_at = lax.axis_index("seq"), lax.axis_index("head")
    side = lax.rem(seq_at, SIDE)
    slice_rows = width // seq_count
    scale_own = rms_scale(input_f)
    hat_own = input_f * scale_own
    normed_own = (hat_own * gain_first).astype(bf16)
    normed_first, normed_half = gathered_crossed(
        normed_own, side_columns(normed_own, 1 - side, slice_rows), 1
    )
    mixed_in = jnp.einsum(
        "td,dhc->htc", normed_first, qkv_weight, preferred_element_type=f32
    ).astype(bf16)
    tail_in = passed_along(mixed_in[:, span_rows - 8 :], "seq", 1)
    tail_in = jnp.where(jnp.arange(8)[:, None] >= 8 - lead_rows, tail_in.astype(f32), 0.0)
    solve, score, fresh, reach, inner_part, turn, local_states, piece_end = run_local_forward(
        mixed_in, tail_in, taps, columns, run_rows, heads
    )
    ends, normed_side = gathered_more(piece_end.reshape(-1, DV + DK), normed_half, 2)
    ends = ends.reshape(-1, heads, DK, DV + DK)
    gate_pre = jnp.einsum("td,dhv->htv", normed_first, gate_weight, preferred_element_type=f32)
    states, core, branch = run_finish_forward(
        ends, local_states, reach, inner_part, gate_pre, gain_head
    )
    branch, cot_all = lax.optimization_barrier((branch, cot_all))
    branch_side = swapped(branch)
    middle = input_f + scattered_head(mm(branch, out_flat).astype(bf16), 3)
    scale_two = rms_scale(middle)
    hat_two = middle * scale_two
    normed_two = (hat_two * gain_second).astype(bf16)

    normed_two, branch_side = lax.optimization_barrier((normed_two, branch_side))
    rows_out = gathered_seq(normed_two, 4).reshape(-1, width)
    cot_f = out_cot.astype(f32)
    gate_units, up_units = mlp_gate.T, mlp_up.T
    gate_part = mm_nt(gate_units, rows_out)
    up_part = mm_nt(up_units, rows_out)
    d_hidden = mm_nt(mlp_down, cot_all)
    hidden = (jax.nn.silu(gate_part) * up_part).astype(bf16)
    d_gate_mlp = (d_hidden * up_part * silu_slope(gate_part)).astype(bf16)
    d_up_mlp = (d_hidden * jax.nn.silu(gate_part)).astype(bf16)
    d_rows = (mm_tn(d_gate_mlp, gate_units) + mm_tn(d_up_mlp, up_units)).astype(bf16)
    d_normed_two, (grad_mgate, grad_mup, grad_down) = scattered_seq_products(
        d_rows, [d_gate_mlp, d_up_mlp, hidden], [rows_out, cot_all], [0, 0, 1], 5
    )
    gain_two_part = jnp.sum(d_normed_two * hat_two, 0)
    e_two = d_normed_two * gain_second
    d_middle = cot_f + scale_two * (
        e_two - hat_two * jnp.mean(e_two * hat_two, axis=-1, keepdims=True)
    )
    hidden, d_middle = lax.optimization_barrier((hidden, d_middle))
    mlp_part, d_middle = lax.optimization_barrier(
        (mm_tn(hidden, mlp_down).astype(bf16), d_middle)
    )
    mlp_out = scattered(mlp_part, "seq")
    d_mix = d_middle.astype(bf16)
    d_mix_all, d_mix_half = gathered_crossed(d_mix, side_columns(d_mix, 1 - side, slice_rows), 6)
    d_branch = mm_nt(d_mix_all, out_flat)
    d_core, d_gate_low, gain_out_part, local_grads, grad_end = run_local_backward(
        d_branch, core, gate_pre, gain_head, reach, turn
    )
    grad_ends, d_mix_side, d_gate_side = gathered_more(
        grad_end.reshape(-1, DV), d_mix_half, 7, d_gate_low
    )
    out_half = (
        mm_tn(side_columns(d_mix_all, side, slice_rows), branch) + mm_tn(d_mix_side, branch_side)
    ).astype(bf16)
    out_half, grad_ends, mlp_out = lax.optimization_barrier((out_half, grad_ends, mlp_out))
    output = (middle + mlp_out).astype(bf16)
    grad_out_s = lax.psum_scatter(
        out_half,
        "seq",
        scatter_dimension=0,
        axis_index_groups=[
            [place * SIDE + across for place in range(seq_count // SIDE)] for across in range(SIDE)
        ],
        tiled=True,
    )
    grad_ends = grad_ends.reshape(-1, heads, DK, DV)
    d_mixed, d_tail, d_lead, grad_conv = run_finish_backward(
        ends,
        grad_ends,
        mixed_in,
        tail_in,
        taps,
        columns,
        run_rows,
        solve,
        score,
        fresh,
        states,
        d_core,
        local_grads,
    )
    d_lead, grad_out_s = lax.optimization_barrier((d_lead, grad_out_s))
    from_next = passed_along(d_lead[:lead_rows], "seq", -1)
    d_tail = d_tail.at[8 - lead_rows :].add(from_next).astype(bf16)
    d_mixed = lax.dynamic_update_slice(d_mixed, d_tail, (span_rows - 8, 0))
    d_normed_part = jnp.einsum(
        "thc,dhc->td",
        d_mixed.reshape(span_rows, heads, inner),
        qkv_weight,
        preferred_element_type=f32,
    ) + jnp.einsum(
        "thv,dhv->td",
        d_gate_low.reshape(span_rows, heads, DV),
        gate_weight,
        preferred_element_type=f32,
    )
    grad_qkv = mm_tn(normed_first, d_mixed).astype(bf16)
    grad_gate = (
        mm_tn(side_columns(normed_first, side, slice_rows), d_gate_low)
        + mm_tn(normed_side, d_gate_side)
    ).astype(bf16)

    gains = jnp.concatenate([jnp.zeros_like(gain_two_part), gain_two_part, gain_out_part.reshape(-1)])
    gain_rows = -(-gains.shape[0] // 1024) * 8
    gains = jnp.pad(gains, (0, gain_rows * 128 - gains.shape[0])).reshape(gain_rows, 128)
    small = jnp.concatenate([gains, grad_conv.reshape(-1, 128)])
    grad_qkv_s, grad_gate_s, d_normed_one, small_all, (grad_mgate_t, grad_mup_t, grad_down_h) = (
        scattered_last(
            grad_qkv,
            grad_gate,
            d_normed_part.astype(bf16),
            hat_own,
            [grad_mgate, grad_mup, grad_down],
            small,
            gain_rows,
            8,
        )
    )
    e_one = d_normed_one * gain_first
    d_input = (
        d_middle + scale_own * (e_one - hat_own * jnp.mean(e_one * hat_own, axis=-1, keepdims=True))
    ).astype(bf16)

    small_sum = jnp.sum(small_all, axis=0)
    gains = small_sum[:gain_rows].reshape(-1)

    def own_slice(begin, length):
        length = length // (seq_count * head_count)
        return lax.dynamic_slice(
            gains, (begin + (head_at * seq_count + seq_at) * length,), (length,)
        )

    grad_conv_s = lax.dynamic_slice_in_dim(
        small_sum[gain_rows:].reshape(-1, heads, inner),
        seq_at * (inner // seq_count),
        inner // seq_count,
        2,
    )
    return (
        output,
        d_input,
        own_slice(0, width),
        grad_qkv_s.astype(f32).reshape(-1, heads, inner),
        grad_conv_s,
        grad_gate_s.astype(f32).reshape(-1, heads, DV),
        own_slice(2 * width, DV),
        grad_out_s.astype(f32).T.reshape(heads, DV, -1),
        own_slice(width, width),
        grad_mgate_t.astype(f32).T,
        grad_mup_t.astype(f32).T,
        grad_down_h.astype(f32),
    )


def solution(mesh):
    in_specs = (
        P(("seq", "head"), None),
        P(("seq", "head"), None),
        P(),
        P(None, "head", None),
        P(None, "head", None),
        P(None, "head", None),
        P(),
        P("head", None, None),
        P(),
        P(None, "seq"),
        P(None, "seq"),
        P("seq", None),
        P("seq", "head"),
        P("seq", "head"),
    )
    out_specs = (
        P(("seq", "head"), None),
        P(("seq", "head"), None),
        P(("head", "seq")),
        P("seq", "head", None),
        P(None, "head", "seq"),
        P("seq", "head", None),
        P(("head", "seq")),
        P("head", None, "seq"),
        P(("head", "seq")),
        P("head", "seq"),
        P("head", "seq"),
        P("seq", "head"),
    )
    return jax.shard_map(
        on_device, mesh=mesh, in_specs=in_specs, out_specs=out_specs, check_vma=False
    )
```

```python
import functools
import math

import jax
import jax.numpy as jnp
from jax import lax
from jax.experimental import pallas as pl
from jax.experimental.pallas import tpu as pltpu
from jax.sharding import PartitionSpec as P

DK = 128
DV = 256
STRETCH = 64
GROUP = 4 * STRETCH
INNER = 2 * DK + DV
BETA, GAMMA, BETA_GAMMA, TAIL, LAST, RUN = range(6)

epsilon = 1e-06
bf16 = jnp.bfloat16
f32 = jnp.float32
VMEM_BYTES = 56 * 2**20
HOLD = 4


def passed_along(value, axis, steps):
    count = lax.axis_size(axis)
    first, last = (max(0, -steps), min(count, count - steps))
    return lax.ppermute(value, axis, [(source, source + steps) for source in range(first, last)])


def rms_scale(tensor):
    return lax.rsqrt(jnp.mean(tensor * tensor, axis=-1, keepdims=True) + epsilon)


def log_rates(decay_code, total_len):
    code_level = decay_code.astype(f32) / 1023.0
    smooth = -jnp.exp(-code_level * math.log(total_len / 32.0)) / 32.0
    return jnp.where(decay_code == 1024, -0.25, smooth)


def token_columns(decay_code, beta_code, total_len):
    rows, heads = decay_code.shape
    rates = log_rates(decay_code, total_len)
    run = jnp.einsum(
        "ij,bjh->bih",
        jnp.tril(jnp.ones((STRETCH, STRETCH), f32)),
        rates.reshape(rows // STRETCH, STRETCH, heads),
        precision=lax.Precision.HIGHEST,
    )
    last = jnp.broadcast_to(run[:, -1:], run.shape).reshape(rows, heads)
    run = run.reshape(rows, heads)
    beta = 0.5 + beta_code.astype(f32) / 512.0
    gamma = jnp.exp(run)
    columns = jnp.concatenate(
        [beta, gamma, beta * gamma, jnp.exp(last - run), jnp.exp(last), run], axis=1
    )
    columns = jnp.pad(columns, ((0, 0), (0, 128 - columns.shape[1])))
    run_rows = jnp.pad(run.T, ((0, 8 - heads % 8), (0, 0)))
    return columns, run_rows


def mm(left, right):
    return jnp.dot(left, right, preferred_element_type=f32)


def mm_nt(left, right):
    return lax.dot_general(left, right, (((1,), (1,)), ((), ())), preferred_element_type=f32)


def mm_tn(left, right):
    return lax.dot_general(left, right, (((0,), (0,)), ((), ())), preferred_element_type=f32)


def column(columns_ref, kind, head, heads):
    block = columns_ref[...]
    lanes = lax.broadcasted_iota(jnp.int32, block.shape, 1)
    return jnp.sum(jnp.where(lanes == kind * heads + head, block, 0.0), axis=1, keepdims=True)


def square_ids():
    return (
        lax.broadcasted_iota(jnp.int32, (GROUP, GROUP), 0),
        lax.broadcasted_iota(jnp.int32, (GROUP, GROUP), 1),
    )


def convolved(padded_ref, tail_ref, mixed_ref, taps_ref):
    rows = mixed_ref.shape[0]
    count = taps_ref.shape[0]
    padded_ref[0:8, :] = tail_ref[...]
    padded_ref[8 : 8 + rows, :] = mixed_ref[...].astype(f32)
    taps = taps_ref[...].astype(f32)
    start = 9 - count
    total = taps[0:1] * padded_ref[start : start + rows, :]
    for tap in range(1, count):
        total += taps[tap : tap + 1] * padded_ref[start + tap : start + tap + rows, :]
    return total


def chunk_masks_stack(transposed):
    lanes = lax.broadcasted_iota(jnp.int32, transposed.shape, 1) // STRETCH
    parts = [jnp.where(lanes == part, transposed, 0.0) for part in range(GROUP // STRETCH)]
    return jnp.concatenate(parts, axis=0).astype(bf16)


def local_forward(
    mixed_ref,
    tail_ref,
    taps_ref,
    columns_ref,
    run_rows_ref,
    solve_ref,
    score_ref,
    fresh_ref,
    reach_ref,
    inner_ref,
    turn_ref,
    local_ref,
    end_ref,
    padded,
    turn_t,
    offsets,
):
    head = pl.program_id(0)
    heads = pl.num_programs(0)
    rows = mixed_ref.shape[0]
    per_group = GROUP // STRETCH
    stretches = rows // STRETCH
    total = convolved(padded, tail_ref, mixed_ref, taps_ref)
    activated = total * jax.nn.sigmoid(total)
    raw_q, raw_k = activated[:, :DK], activated[:, DK : 2 * DK]
    queries = raw_q * (
        lax.rsqrt(jnp.sum(raw_q * raw_q, axis=1, keepdims=True) + epsilon) * DK ** (-0.5)
    )
    keys = raw_k * lax.rsqrt(jnp.sum(raw_k * raw_k, axis=1, keepdims=True) + epsilon)
    values = activated[:, 2 * DK :]
    beta = column(columns_ref, BETA, head, heads)
    gamma = column(columns_ref, GAMMA, head, heads)
    beta_gamma = column(columns_ref, BETA_GAMMA, head, heads)
    tail_decay = column(columns_ref, TAIL, head, heads)
    last = column(columns_ref, LAST, head, heads)
    run = column(columns_ref, RUN, head, heads)
    row_id, col_id = square_ids()
    same = row_id // STRETCH == col_id // STRETCH
    causal = same & (row_id >= col_id)
    diagonal = row_id == col_id
    eye = jnp.where(
        lax.broadcasted_iota(jnp.int32, (DK, DK), 0) == lax.broadcasted_iota(jnp.int32, (DK, DK), 1),
        1.0,
        0.0,
    )
    for group in range(rows // GROUP):
        span = slice(group * GROUP, (group + 1) * GROUP)
        key_b = keys[span].astype(bf16)
        query_b = queries[span].astype(bf16)
        gaps = run[span] - run_rows_ref[pl.ds(head, 1), span]
        within = jnp.exp(jnp.where(causal, gaps, -1e30))
        lower = jnp.where(diagonal, 0.0, beta[span] * within * mm_nt(key_b, key_b))
        solve = jnp.where(diagonal, 1.0, jnp.where(row_id // 2 == col_id // 2, -lower, 0.0))
        size = 2
        while size < STRETCH:
            crossing = (row_id // (2 * size) == col_id // (2 * size)) & (
                row_id // size != col_id // size
            )
            solve_b = solve.astype(bf16)
            half = mm(solve_b, jnp.where(crossing, lower, 0.0).astype(bf16))
            solve = solve - mm(half.astype(bf16), solve_b)
            size *= 2
        solve_b = solve.astype(bf16)
        right = jnp.concatenate([beta[span] * values[span], beta_gamma[span] * keys[span]], axis=1)
        fresh_b = mm(solve_b, right.astype(bf16)).astype(bf16)
        score_b = (within * mm_nt(query_b, key_b)).astype(bf16)
        scored = mm(score_b, fresh_b)
        solve_ref[group] = solve_b
        score_ref[group] = score_b
        fresh_ref[span, :] = fresh_b
        inner_ref[span, :] = scored[:, :DV]
        reach_ref[span, :] = (gamma[span] * queries[span] - scored[:, DV:]).astype(bf16)
        tail_keys = (tail_decay[span] * keys[span]).T
        moved = mm(chunk_masks_stack(tail_keys), fresh_b)
        for part in range(per_group):
            at = group * per_group + part
            block = moved[part * DK : (part + 1) * DK]
            stay = last[at * STRETCH : at * STRETCH + 1]
            turned = stay * eye - block[:, DV:]
            turn_t[head, at] = turned.astype(bf16)
            turn_ref[at] = turned.T.astype(bf16)
            offsets[head, at] = block[:, :DV]

    @pl.when(head == heads - 1)
    def _():
        states = [
            jnp.concatenate([jnp.zeros((DK, DV), f32), eye], axis=1)
            for _ in range(local_ref.shape[0])
        ]
        for at in range(stretches):
            for h in range(len(states)):
                state_b = states[h].astype(bf16)
                local_ref[h, at] = state_b
                moved = mm(turn_t[h, at], state_b)
                states[h] = jnp.concatenate(
                    [moved[:, :DV] + offsets[h, at], moved[:, DV:]], axis=1
                )
        for h in range(len(states)):
            end_ref[h] = states[h].astype(bf16)


def finish_forward(
    ends_ref, local_ref, reach_ref, inner_ref, gate_ref, gain_ref, state_ref, core_ref, branch_ref, start
):
    head = pl.program_id(0)
    heads, stretches = start.shape[0], local_ref.shape[0]

    @pl.when(head == 0)
    def _():
        start[...] = jnp.zeros_like(start)

        def one(source, carry):
            for h in range(heads):
                start[h] = (
                    mm(ends_ref[source, h, :, DV:], start[h].astype(bf16))
                    + ends_ref[source, h, :, :DV].astype(f32)
                )
            return carry

        lax.fori_loop(0, lax.axis_index("seq"), one, 0)

    start_b = start[head].astype(bf16)
    cores = []
    for at in range(stretches):
        state_b = (
            local_ref[at, :, :DV].astype(f32) + mm(local_ref[at, :, DV:], start_b)
        ).astype(bf16)
        state_ref[at] = state_b
        span = slice(at * STRETCH, (at + 1) * STRETCH)
        cores.append(inner_ref[span, :] + mm(reach_ref[span, :], state_b))
    core = jnp.concatenate(cores, axis=0)
    core_ref[...] = core
    gate = gate_ref[...]
    branch = core * rms_scale(core) * gain_ref[...].astype(f32) * (gate * jax.nn.sigmoid(gate))
    branch_ref[...] = branch.astype(bf16)


def local_backward(
    d_branch_ref,
    core_ref,
    gate_ref,
    gain_ref,
    reach_ref,
    turn_ref,
    d_core_ref,
    d_gate_ref,
    gain_part_ref,
    local_ref,
    end_ref,
    pulls,
):
    head = pl.program_id(0)
    heads = pl.num_programs(0)
    rows = core_ref.shape[0]
    per_group = GROUP // STRETCH
    stretches = rows // STRETCH
    core = core_ref[...]
    gate = gate_ref[...]
    gain = gain_ref[...].astype(f32)
    d_branch = d_branch_ref[...]
    scale = rms_scale(core)
    nhat = core * scale
    sig = jax.nn.sigmoid(gate)
    gated = d_branch * (gate * sig)

    @pl.when(head == 0)
    def _():
        gain_part_ref[...] = jnp.zeros_like(gain_part_ref)

    gain_part_ref[...] += jnp.sum(gated * nhat, axis=0, keepdims=True)
    f = gated * gain
    d_core = scale * (f - nhat * jnp.mean(f * nhat, axis=1, keepdims=True))
    d_gate_ref[...] = (d_branch * nhat * gain * sig * (1.0 + gate * (1.0 - sig))).astype(bf16)
    d_core_b = d_core.astype(bf16)
    d_core_ref[...] = d_core_b
    for group in range(rows // GROUP):
        span = slice(group * GROUP, (group + 1) * GROUP)
        pulled = mm(chunk_masks_stack(reach_ref[span, :].astype(f32).T), d_core_b[span])
        for part in range(per_group):
            pulls[head, group * per_group + part] = pulled[part * DK : (part + 1) * DK]

    @pl.when(head == heads - 1)
    def _():
        eye = jnp.where(
            lax.broadcasted_iota(jnp.int32, (DK, DK), 0)
            == lax.broadcasted_iota(jnp.int32, (DK, DK), 1),
            1.0,
            0.0,
        )
        grads = [
            jnp.concatenate([jnp.zeros((DK, DV), f32), eye], axis=1)
            for _ in range(local_ref.shape[0])
        ]
        for at in reversed(range(stretches)):
            for h in range(len(grads)):
                grad_b = grads[h].astype(bf16)
                local_ref[h, at] = grad_b
                moved = mm(turn_ref[h, at], grad_b)
                grads[h] = jnp.concatenate([moved[:, :DV] + pulls[h, at], moved[:, DV:]], axis=1)
        for h in range(len(grads)):
            end_ref[h] = grads[h][:, :DV].astype(bf16)


def finish_backward(
    ends_ref,
    grad_ends_ref,
    mixed_ref,
    tail_ref,
    taps_ref,
    columns_ref,
    run_rows_ref,
    solve_ref,
    score_ref,
    fresh_ref,
    state_ref,
    d_core_ref,
    local_ref,
    d_mixed_ref,
    tail_out_ref,
    lead_ref,
    grad_taps_ref,
    padded,
    spread,
    end,
):
    head = pl.program_id(0)
    heads = pl.num_programs(0)
    rows = mixed_ref.shape[0]
    per_group = GROUP // STRETCH

    @pl.when(head == 0)
    def _():
        end[...] = jnp.zeros_like(end)
        count = ends_ref.shape[0]

        def one(turn, carry):
            source = count - 1 - turn
            for h in range(end.shape[0]):
                end[h] = (
                    mm_tn(ends_ref[source, h, :, DV:], end[h].astype(bf16))
                    + grad_ends_ref[source, h].astype(f32)
                )
            return carry

        lax.fori_loop(0, count - 1 - lax.axis_index("seq"), one, 0)

    end_b = end[head].astype(bf16)
    total = convolved(padded, tail_ref, mixed_ref, taps_ref)
    sig = jax.nn.sigmoid(total)
    activated = total * sig
    raw_q, raw_k = activated[:, :DK], activated[:, DK : 2 * DK]
    scale_q = lax.rsqrt(jnp.sum(raw_q * raw_q, axis=1, keepdims=True) + epsilon)
    scale_k = lax.rsqrt(jnp.sum(raw_k * raw_k, axis=1, keepdims=True) + epsilon)
    unit_q = raw_q * scale_q
    keys = raw_k * scale_k
    beta = column(columns_ref, BETA, head, heads)
    gamma = column(columns_ref, GAMMA, head, heads)
    beta_gamma = column(columns_ref, BETA_GAMMA, head, heads)
    tail_decay = column(columns_ref, TAIL, head, heads)
    run = column(columns_ref, RUN, head, heads)
    row_id, col_id = square_ids()
    causal = (row_id // STRETCH == col_id // STRETCH) & (row_id >= col_id)
    diagonal = row_id == col_id
    d_queries, d_keys, d_values = [], [], []
    for group in range(rows // GROUP):
        span = slice(group * GROUP, (group + 1) * GROUP)
        key_b = keys[span].astype(bf16)
        query_b = (unit_q[span] * DK ** (-0.5)).astype(bf16)
        tail_keys = (tail_decay[span] * keys[span]).astype(bf16)
        d_core_b = d_core_ref[span, :]
        grad_bs, from_grad, fresh_parts, from_state = [], [], [], []
        for part in range(per_group):
            at = group * per_group + part
            own = slice(part * STRETCH, (part + 1) * STRETCH)
            rows_at = slice(at * STRETCH, (at + 1) * STRETCH)
            grad_b = (
                local_ref[at, :, :DV].astype(f32) + mm(local_ref[at, :, DV:], end_b)
            ).astype(bf16)
            grad_bs.append(grad_b)
            from_grad.append(mm(tail_keys[own], grad_b))
            fresh_parts.append(mm(fresh_ref[rows_at, DV:], state_ref[at]))
            from_state.append(mm_nt(d_core_b[own], state_ref[at]))
        d_fresh = mm_tn(score_ref[group], d_core_b) + jnp.concatenate(from_grad, axis=0)
        d_right = mm_tn(solve_ref[group], d_fresh.astype(bf16))
        d_right_b = d_right.astype(bf16)
        fresh = fresh_ref[span, :DV].astype(f32) - jnp.concatenate(fresh_parts, axis=0)
        fresh_b = fresh.astype(bf16)
        gaps = run[span] - run_rows_ref[pl.ds(head, 1), span]
        within = jnp.exp(jnp.where(causal, gaps, -1e30))
        d_score = (within * mm_nt(d_core_b, fresh_b)).astype(bf16)
        d_lower = jnp.where(
            diagonal, 0.0, -beta[span] * within * mm_nt(d_right_b, fresh_b)
        ).astype(bf16)
        state_keys, grad_keys = [], []
        for part in range(per_group):
            at = group * per_group + part
            own = slice(part * STRETCH, (part + 1) * STRETCH)
            state_keys.append(mm_nt(d_right_b[own], state_ref[at]))
            grad_keys.append(mm_nt(fresh_b[own], grad_bs[part]))
        d_queries.append(gamma[span] * jnp.concatenate(from_state, axis=0) + mm(d_score, key_b))
        d_keys.append(
            mm_tn(d_score, query_b)
            + mm_tn(d_lower, key_b)
            + mm(d_lower, key_b)
            + tail_decay[span] * jnp.concatenate(grad_keys, axis=0)
            - beta_gamma[span] * jnp.concatenate(state_keys, axis=0)
        )
        d_values.append(beta[span] * d_right)
    g_q = jnp.concatenate(d_queries, axis=0) * DK ** (-0.5)
    g_k = jnp.concatenate(d_keys, axis=0)
    d_act = jnp.concatenate(
        [
            scale_q * (g_q - unit_q * jnp.sum(unit_q * g_q, axis=1, keepdims=True)),
            scale_k * (g_k - keys * jnp.sum(keys * g_k, axis=1, keepdims=True)),
            jnp.concatenate(d_values, axis=0),
        ],
        axis=1,
    )
    d_conv = d_act * (sig * (1.0 + total * (1.0 - sig)))
    taps = taps_ref[...].astype(f32)
    count = taps_ref.shape[0]
    start = 9 - count
    grad_taps_ref[...] = jnp.concatenate(
        [
            jnp.sum(padded[start + tap : start + tap + rows, :] * d_conv, axis=0, keepdims=True)
            for tap in range(count)
        ],
        axis=0,
    )
    spread[0:8, :] = jnp.zeros((8, d_conv.shape[1]), f32)
    spread[8 : 8 + rows, :] = d_conv
    spread[8 + rows : 16 + rows, :] = jnp.zeros((8, d_conv.shape[1]), f32)
    lead = taps[0:1] * spread[8:16, :]
    d_mixed = taps[0:1] * spread[7 + count : 7 + count + rows, :]
    for tap in range(1, count):
        lead += taps[tap : tap + 1] * spread[8 - tap : 16 - tap, :]
        begin = 7 + count - tap
        d_mixed += taps[tap : tap + 1] * spread[begin : begin + rows, :]
    lead_ref[...] = lead
    d_mixed_ref[...] = d_mixed.astype(bf16)
    tail_out_ref[...] = d_mixed[rows - 8 :]


def whole(shape):
    return pl.BlockSpec(shape, lambda h: (0,) * len(shape))


def by_head(shape):
    return pl.BlockSpec((None,) + shape, lambda h: (h,) + (0,) * len(shape))


def by_columns(rows, width):
    return pl.BlockSpec((rows, width), lambda h: (0, h))


def kernel_call(body, heads, ins, outs, out_shapes, scratch, flops, moved):
    return pl.pallas_call(
        body,
        grid=(heads,),
        in_specs=ins,
        out_specs=outs,
        out_shape=out_shapes,
        scratch_shapes=scratch,
        compiler_params=pltpu.CompilerParams(
            dimension_semantics=("arbitrary",), vmem_limit_bytes=VMEM_BYTES
        ),
        cost_estimate=pl.CostEstimate(flops=flops, bytes_accessed=moved, transcendentals=0),
    )


def shaped(shape, kind):
    return jax.ShapeDtypeStruct(shape, kind)


def run_local_forward(mixed, tail, taps, columns, run_rows, heads):
    rows = mixed.shape[1]
    count = taps.shape[0]
    groups, stretches = rows // GROUP, rows // STRETCH
    return kernel_call(
        local_forward,
        heads,
        [
            by_head((rows, INNER)),
            by_head((8, INNER)),
            by_columns(count, INNER),
            whole(columns.shape),
            whole(run_rows.shape),
        ],
        [
            by_head((groups, GROUP, GROUP)),
            by_head((groups, GROUP, GROUP)),
            by_head((rows, DV + DK)),
            by_head((rows, DK)),
            by_columns(rows, DV),
            by_head((stretches, DK, DK)),
            whole((heads, stretches, DK, DV + DK)),
            whole((heads, DK, DV + DK)),
        ],
        [
            shaped((heads, groups, GROUP, GROUP), bf16),
            shaped((heads, groups, GROUP, GROUP), bf16),
            shaped((heads, rows, DV + DK), bf16),
            shaped((heads, rows, DK), bf16),
            shaped((rows, heads * DV), f32),
            shaped((heads, stretches, DK, DK), bf16),
            shaped((heads, stretches, DK, DV + DK), bf16),
            shaped((heads, DK, DV + DK), bf16),
        ],
        [
            pltpu.VMEM((rows + 8, INNER), f32),
            pltpu.VMEM((heads, stretches, DK, DK), bf16),
            pltpu.VMEM((heads, stretches, DK, DV), f32),
        ],
        12_000_000_000,
        20_000_000,
    )(mixed, tail, taps, columns, run_rows)


def run_finish_forward(ends, local, reach, inner, gate_pre, gain):
    heads, stretches = local.shape[:2]
    rows = inner.shape[0]
    return kernel_call(
        finish_forward,
        heads,
        [
            whole(ends.shape),
            by_head((stretches, DK, DV + DK)),
            by_head((rows, DK)),
            by_columns(rows, DV),
            by_head((rows, DV)),
            whole(gain.shape),
        ],
        [by_head((stretches, DK, DV)), by_columns(rows, DV), by_columns(rows, DV)],
        [
            shaped((heads, stretches, DK, DV), bf16),
            shaped((rows, heads * DV), f32),
            shaped((rows, heads * DV), bf16),
        ],
        [pltpu.VMEM((heads, DK, DV), f32)],
        3_000_000_000,
        20_000_000,
    )(ends, local, reach, inner, gate_pre, gain)


def run_local_backward(d_branch, core, gate_pre, gain, reach, turn):
    heads, stretches = turn.shape[:2]
    rows = core.shape[0]
    return kernel_call(
        local_backward,
        heads,
        [
            by_columns(rows, DV),
            by_columns(rows, DV),
            by_head((rows, DV)),
            whole(gain.shape),
            by_head((rows, DK)),
            whole(turn.shape),
        ],
        [
            by_columns(rows, DV),
            by_columns(rows, DV),
            whole((1, DV)),
            whole((heads, stretches, DK, DV + DK)),
            whole((heads, DK, DV)),
        ],
        [
            shaped((rows, heads * DV), bf16),
            shaped((rows, heads * DV), bf16),
            shaped((1, DV), f32),
            shaped((heads, stretches, DK, DV + DK), bf16),
            shaped((heads, DK, DV), bf16),
        ],
        [pltpu.VMEM((heads, stretches, DK, DV), f32)],
        4_000_000_000,
        20_000_000,
    )(d_branch, core, gate_pre, gain, reach, turn)


def run_finish_backward(
    ends, grad_ends, mixed, tail, taps, columns, run_rows, solve, score, fresh, states, d_core, local
):
    heads, stretches = local.shape[:2]
    rows = mixed.shape[1]
    groups = rows // GROUP
    count = taps.shape[0]
    return kernel_call(
        finish_backward,
        heads,
        [
            whole(ends.shape),
            whole(grad_ends.shape),
            by_head((rows, INNER)),
            by_head((8, INNER)),
            by_columns(count, INNER),
            whole(columns.shape),
            whole(run_rows.shape),
            by_head((groups, GROUP, GROUP)),
            by_head((groups, GROUP, GROUP)),
            by_head((rows, DV + DK)),
            by_head((stretches, DK, DV)),
            by_columns(rows, DV),
            by_head((stretches, DK, DV + DK)),
        ],
        [
            by_columns(rows, INNER),
            by_columns(8, INNER),
            by_columns(8, INNER),
            by_columns(count, INNER),
        ],
        [
            shaped((rows, heads * INNER), bf16),
            shaped((8, heads * INNER), f32),
            shaped((8, heads * INNER), f32),
            shaped((count, heads * INNER), f32),
        ],
        [
            pltpu.VMEM((rows + 8, INNER), f32),
            pltpu.VMEM((rows + 16, INNER), f32),
            pltpu.VMEM((heads, DK, DV), f32),
        ],
        12_000_000_000,
        20_000_000,
    )(ends, grad_ends, mixed, tail, taps, columns, run_rows, solve, score, fresh, states, d_core, local)


MESH = pl.DeviceIdType.MESH
SIDE = 2


def remote(source, target, send, arrive, device):
    return pltpu.make_async_remote_copy(
        src_ref=source,
        dst_ref=target,
        send_sem=send,
        recv_sem=arrive,
        device_id=device,
        device_id_type=MESH,
    )


def greet(partners):
    barrier = pltpu.get_barrier_semaphore()
    expected = 0
    for device, there in partners:
        if there is None:
            pl.semaphore_signal(barrier, inc=1, device_id=device, device_id_type=MESH)
            expected = expected + 1
        else:

            @pl.when(there)
            def _(device=device):
                pl.semaphore_signal(barrier, inc=1, device_id=device, device_id_type=MESH)

            expected = expected + there.astype(jnp.int32)
    pl.semaphore_wait(barrier, expected)


def head_places():
    head, seq = lax.axis_index("head"), lax.axis_index("seq")
    core = lax.rem(head, 2)
    sibling = head + 1 - 2 * core
    across = lax.rem(head + 2, 4)
    return head, seq, sibling, across


def head_partners():
    head, seq, sibling, across = head_places()
    return [((sibling, seq), None), ((across, seq), None)]


def seq_places():
    head, seq = lax.axis_index("head"), lax.axis_index("seq")
    return head, seq // SIDE, lax.rem(seq, SIDE)


def seq_partners(count):
    head, line, side = seq_places()
    return [
        ((head, line * SIDE + 1 - side), None),
        ((head, (line + 1) * SIDE + side), line < count - 1),
        ((head, (line - 1) * SIDE + side), line > 0),
    ]


def run_together(steps):
    steps = list(steps)
    while steps:
        alive = []
        for step in steps:
            try:
                next(step)
                alive.append(step)
            except StopIteration:
                pass
        steps = alive


def gather_head(own_ref, out_ref, local, send, arrive, pieces):
    head, seq, sibling, across = head_places()
    far = lax.rem(sibling + 2, 4)
    rows = own_ref.shape[0] // pieces
    keep = pltpu.make_async_copy(own_ref, out_ref.at[head], local.at[0])
    keep.start()

    def part(ref, piece):
        return ref.at[pl.ds(piece * rows, rows)]

    outgoing = []
    for piece in range(pieces):
        outgoing.append(
            remote(
                part(own_ref, piece),
                part(out_ref.at[head], piece),
                send.at[0, piece],
                arrive.at[0, piece],
                (across, seq),
            )
        )
    for piece in range(pieces):
        outgoing.append(
            remote(
                part(own_ref, piece),
                part(out_ref.at[head], piece),
                send.at[1, piece],
                arrive.at[1, piece],
                (sibling, seq),
            )
        )
    for copy in outgoing:
        copy.start()
    yield
    forwards = []
    for piece in range(pieces):
        outgoing[piece].wait_recv()
        forward = remote(
            part(out_ref.at[across], piece),
            part(out_ref.at[across], piece),
            send.at[2, piece],
            arrive.at[2, piece],
            (sibling, seq),
        )
        forward.start()
        forwards.append(forward)
        yield
    for copy in outgoing[pieces:] + forwards:
        copy.wait_recv()
    for copy in outgoing + forwards:
        copy.wait_send()
    keep.wait()


def scatter_head(source_at, out_ref, own, crossed, passed, local, send, arrive, hold=0, pause=0):
    head, seq, sibling, across = head_places()
    far = lax.rem(sibling + 2, 4)
    loads = [
        pltpu.make_async_copy(source_at(target), own.at[slot], local.at[slot])
        for slot, target in enumerate((across, head))
    ]
    copies = [
        remote(source_at(target), crossed.at[slot], send.at[slot], arrive.at[slot], (sibling, seq))
        for slot, target in enumerate((far, sibling))
    ]
    for slot in range(2):
        copies[slot].start()
        loads[slot].start()
    for _ in range(1 + hold):
        yield
    loads[0].wait()
    copies[0].wait_recv()
    own[0] = (own[0].astype(f32) + crossed[0].astype(f32)).astype(own.dtype)
    onward = remote(own.at[0], passed, send.at[2], arrive.at[2], (across, seq))
    onward.start()
    for _ in range(1 + pause):
        yield
    loads[1].wait()
    copies[1].wait_recv()
    onward.wait_recv()
    total = own[1].astype(f32) + crossed[1].astype(f32) + passed[...].astype(f32)
    out_ref[...] = total.astype(out_ref.dtype)
    onward.wait_send()
    for copy in copies:
        copy.wait_send()


def gather_seq(own_ref, out_ref, local, side_send, side_arrive, line_send, line_arrive, count):
    head, line, side = seq_places()
    me = line * SIDE + side
    beside = (head, line * SIDE + 1 - side)
    ways = ((1, line < count - 1), (-1, line > 0))
    keep = pltpu.make_async_copy(own_ref, out_ref.at[me], local.at[0])
    keep.start()

    def along(source, block, way, step):
        slot = step if way > 0 else count + step
        return remote(
            source,
            out_ref.at[block],
            line_send.at[slot],
            line_arrive.at[slot],
            (head, (line + way) * SIDE + side),
        )

    def over(source, block, slot):
        return remote(source, out_ref.at[block], side_send.at[slot], side_arrive.at[slot], beside)

    for way, onward in ways:

        @pl.when(onward)
        def _(way=way):
            along(own_ref, me, way, 0).start()

    over(own_ref, me, 0).start()
    yield
    for step in range(1, count):
        for way, onward in ways:
            block = me - way * step * SIDE
            arrives = line >= step if way > 0 else line + step < count

            @pl.when(arrives)
            def _(way=way, onward=onward, block=block, step=step):
                landed = out_ref.at[block]
                slot = step if way > 0 else count + step
                remote(
                    landed, landed, line_send.at[slot - 1], line_arrive.at[slot - 1], beside
                ).wait_recv()

                @pl.when(onward)
                def _():
                    along(landed, block, way, step).start()

                over(landed, block, slot).start()

        yield
    over(own_ref, me, 0).wait()
    for way, onward in ways:

        @pl.when(onward)
        def _(way=way):
            along(own_ref, me, way, 0).wait_send()

    for step in range(1, count):
        for way, onward in ways:
            block = me - way * step * SIDE
            arrives = line >= step if way > 0 else line + step < count

            @pl.when(arrives)
            def _(way=way, onward=onward, block=block, step=step):
                landed = out_ref.at[block]
                slot = step if way > 0 else count + step
                over(landed, block, slot).wait()

                @pl.when(onward)
                def _():
                    along(landed, block, way, step).wait_send()

    keep.wait()


def scatter_seq(source_at, out_at, own, crossed, risen, fallen, local, sends, arrivals, count):
    head, line, side = seq_places()
    beside = (head, line * SIDE + 1 - side)
    pieces = own.shape[0]

    def targets(distance):
        if distance == 0:
            return [(line, None, 0)]
        return [
            (line - distance, line >= distance, -1),
            (line + distance, line + distance < count, 1),
        ]

    def load(piece, target):
        return pltpu.make_async_copy(
            source_at(target, side, piece), own.at[piece, target], local.at[piece, target]
        )

    def cross(piece, target):
        return remote(
            source_at(target, 1 - side, piece),
            crossed.at[piece, target],
            sends.at[0, piece, target],
            arrivals.at[0, piece, target],
            beside,
        )

    def onward(piece, target, way, arriving=False):
        landing = risen if way > 0 else fallen
        return remote(
            own.at[piece, target],
            landing.at[piece, target],
            sends.at[1, piece, target],
            arrivals.at[1 if way > 0 else 2, piece, target],
            beside if arriving else (head, (line + way) * SIDE + side),
        )

    def guarded(there, body):
        if there is None:
            body()
        else:
            pl.when(there)(body)

    def here(piece, target):
        load(piece, target).wait()
        total = own[piece, target].astype(f32)
        if crossed is not None:
            cross(piece, target).wait_recv()
            total += crossed[piece, target].astype(f32)
        return total

    def arrived(piece, target, way):
        landing = risen if way > 0 else fallen
        onward(piece, target, way, True).wait_recv()
        return landing[piece, target].astype(f32)

    for piece in range(pieces):
        for distance in range(count - 1, -1, -1):
            for target, there, _ in targets(distance):

                def begin(piece=piece, target=target):
                    if crossed is not None:
                        cross(piece, target).start()
                    load(piece, target).start()

                guarded(there, begin)
    yield
    for piece in range(pieces):
        for distance in range(count - 1, 0, -1):
            for target, there, way in targets(distance):
                first = line == count - 1 if way < 0 else line == 0

                @pl.when(jnp.logical_and(there, first))
                def _(piece=piece, target=target, way=way):
                    own[piece, target] = here(piece, target).astype(own.dtype)
                    onward(piece, target, way).start()

                @pl.when(jnp.logical_and(there, jnp.logical_not(first)))
                def _(piece=piece, target=target, way=way):
                    total = here(piece, target) + arrived(piece, target, way)
                    own[piece, target] = total.astype(own.dtype)
                    onward(piece, target, way).start()

            yield
        out = out_at(piece)

        @pl.when(line == 0)
        def _(piece=piece, out=out):
            out[...] = (here(piece, line) + arrived(piece, line, -1)).astype(out.dtype)

        @pl.when(line == count - 1)
        def _(piece=piece, out=out):
            out[...] = (here(piece, line) + arrived(piece, line, 1)).astype(out.dtype)

        @pl.when(jnp.logical_and(line > 0, line < count - 1))
        def _(piece=piece, out=out):
            total = here(piece, line) + arrived(piece, line, -1) + arrived(piece, line, 1)
            out[...] = total.astype(out.dtype)

        yield
    for piece in range(pieces):
        for distance in range(count - 1, -1, -1):
            for target, there, way in targets(distance):

                def finish(piece=piece, target=target, way=way):
                    if crossed is not None:
                        cross(piece, target).wait_send()
                    if way:
                        onward(piece, target, way).wait_send()

                guarded(there, finish)


ANY = pl.BlockSpec(memory_space=pl.ANY)
IN_VMEM = pl.BlockSpec(memory_space=pltpu.VMEM)
DMA = pltpu.SemaphoreType.DMA


def link_call(body, number, ins, outs, shapes, scratch, moved):
    return pl.pallas_call(
        body,
        in_specs=ins,
        out_specs=outs,
        out_shape=shapes,
        scratch_shapes=scratch,
        compiler_params=pltpu.CompilerParams(
            collective_id=number, has_side_effects=True, vmem_limit_bytes=VMEM_BYTES
        ),
        cost_estimate=pl.CostEstimate(flops=0, bytes_accessed=moved // 8, transcendentals=0),
    )


def gathered_head(value, number, pieces=4):
    count = lax.axis_size("head")
    if count != 4:
        return lax.all_gather(value, "head", axis=0, tiled=True)
    rows, width = value.shape

    def body(own_ref, out_ref, local, send, arrive):
        greet(head_partners())
        run_together([gather_head(own_ref, out_ref, local, send, arrive, pieces)])

    out = link_call(
        body,
        number,
        [ANY],
        ANY,
        shaped((count, rows, width), value.dtype),
        [DMA((1,)), DMA((3, pieces)), DMA((3, pieces))],
        60_000_000,
    )(value)
    return out.reshape(count * rows, width)


def gathered_crossed(value, half, number, pieces=4):
    count = lax.axis_size("head")
    rows, width = value.shape

    def body(own_ref, half_ref, out_ref, landed_ref, local, send, arrive, crossing):
        head, line, side = seq_places()
        beside = (head, line * SIDE + 1 - side)
        greet(head_partners() + [(beside, None)])
        cross = remote(half_ref, landed_ref, crossing.at[0], crossing.at[1], beside)
        cross.start()
        run_together([gather_head(own_ref, out_ref, local, send, arrive, pieces)])
        cross.wait()

    out, landed = link_call(
        body,
        number,
        [ANY, ANY],
        [ANY, ANY],
        [shaped((count, rows, width), value.dtype), shaped(half.shape, half.dtype)],
        [DMA((1,)), DMA((3, pieces)), DMA((3, pieces)), DMA((2,))],
        60_000_000,
    )(value, half)
    return out.reshape(count * rows, width), landed


def gathered_seq(value, number):
    total = lax.axis_size("seq")
    count = total // SIDE
    rows, width = value.shape
    if total % SIDE or count < 2:
        return lax.all_gather(value, "seq")

    def body(own_ref, out_ref, *sems):
        greet(seq_partners(count))
        run_together([gather_seq(own_ref, out_ref, *sems, count)])

    return link_call(
        body,
        number,
        [ANY],
        ANY,
        shaped((total, rows, width), value.dtype),
        [DMA((1,))] + [DMA((2 * count,)) for _ in range(4)],
        120_000_000,
    )(value)


def head_scratch(rows, width):
    return [
        pltpu.VMEM((2, rows, width), bf16),
        pltpu.VMEM((2, rows, width), bf16),
        pltpu.VMEM((rows, width), bf16),
        DMA((2,)),
        DMA((3,)),
        DMA((3,)),
    ]


def seq_scratch(pieces, count, rows, width):
    return [pltpu.VMEM((pieces, count, rows, width), bf16) for _ in range(4)] + [
        DMA((pieces, count)),
        DMA((2, pieces, count)),
        DMA((3, pieces, count)),
    ]


def scattered_head(value, number, pieces=2):
    count = lax.axis_size("head")
    if count != 4:
        return scattered(value, "head")
    rows, width = value.shape[0] // count, value.shape[1] // pieces

    def body(source, out, *rest):
        greet(head_partners())
        steps = []
        for piece in range(pieces):
            span = pl.ds(piece * width, width)

            def source_at(target, span=span):
                return source.at[pl.ds(pl.multiple_of(target * rows, rows), rows), span]

            steps.append(
                scatter_head(source_at, out.at[:, span], *rest[6 * piece : 6 * piece + 6])
            )
        run_together(steps)

    return link_call(
        body,
        number,
        [ANY],
        IN_VMEM,
        shaped((rows, value.shape[1]), f32),
        head_scratch(rows, width) * pieces,
        60_000_000,
    )(value)


def scattered_seq(value, number, pieces=2):
    total = lax.axis_size("seq")
    count = total // SIDE
    if total % SIDE or count < 2:
        return scattered(value, "seq")
    rows, width = value.shape[0] // total, value.shape[1] // pieces

    def body(source, out, *rest):
        greet(seq_partners(count))

        def source_at(target, side, piece):
            begin = pl.multiple_of((target * SIDE + side) * rows, rows)
            return source.at[pl.ds(begin, rows), pl.ds(piece * width, width)]

        def out_at(piece):
            return out.at[:, pl.ds(piece * width, width)]

        run_together([scatter_seq(source_at, out_at, *rest, count)])

    return link_call(
        body,
        number,
        [ANY],
        IN_VMEM,
        shaped((rows, value.shape[1]), f32),
        seq_scratch(pieces, count, rows, width),
        120_000_000,
    )(value)


def product_steps(left_hbm, right_hbm, out_refs, picks, lefts, rights, tiles, load, store, per_round):
    loads = [
        pltpu.make_async_copy(ref, held, load.at[index])
        for index, (ref, held) in enumerate(zip(left_hbm + right_hbm, lefts + rights))
    ]
    for copy in loads:
        copy.start()
    yield
    for copy in loads:
        copy.wait()
    units, width = tiles.shape[1:]
    block = units // 4 if units % 64 == 0 else units
    span = 512
    stores = []
    done = 0
    for index, pick in enumerate(picks):
        for begin in range(0, width, span):
            columns = pl.ds(begin, span)

            def one(part, carry, index=index, pick=pick, columns=columns):
                rows = pl.ds(pl.multiple_of(part * block, block), block)
                tiles[index, rows, columns] = mm(
                    lefts[index][rows, :], rights[pick][:, columns]
                ).astype(tiles.dtype)
                return carry

            lax.fori_loop(0, units // block, one, 0)
            done += 1
            if done % per_round == 0:
                yield
        copy = pltpu.make_async_copy(tiles.at[index], out_refs[index], store.at[index])
        copy.start()
        stores.append(copy)
    for copy in stores:
        copy.wait()


def scattered_seq_products(value, lefts, rights, picks, number, pieces=2):
    total = lax.axis_size("seq")
    count = total // SIDE
    rows, width = value.shape[0] // total, value.shape[1] // pieces
    units, depth = lefts[0].shape
    breadth = rights[0].shape[1]
    n_left, n_right = len(lefts), len(rights)
    held = 4 * value.size // SIDE + n_left * units * (depth + breadth) + n_right * rights[0].size
    if 2 * held > VMEM_BYTES:
        products = [mm(left, rights[pick]).astype(bf16) for left, pick in zip(lefts, picks)]
        return scattered_seq(value, number, pieces), products

    def body(source, *rest):
        left_hbm, rest = rest[:n_left], rest[n_left:]
        right_hbm, rest = rest[:n_right], rest[n_right:]
        out, out_refs, rest = rest[0], rest[1 : 1 + n_left], rest[1 + n_left :]
        link, rest = rest[:7], rest[7:]
        left_held, rest = rest[:n_left], rest[n_left:]
        right_held, rest = rest[:n_right], rest[n_right:]
        greet(seq_partners(count))

        def source_at(target, side, piece):
            begin = pl.multiple_of((target * SIDE + side) * rows, rows)
            return source.at[pl.ds(begin, rows), pl.ds(piece * width, width)]

        def out_at(piece):
            return out.at[:, pl.ds(piece * width, width)]

        run_together(
            [
                scatter_seq(source_at, out_at, *link, count),
                product_steps(
                    left_hbm, right_hbm, out_refs, picks, left_held, right_held, *rest, 2
                ),
            ]
        )

    outs = link_call(
        body,
        number,
        [ANY] * (1 + n_left + n_right),
        [IN_VMEM] + [ANY] * n_left,
        [shaped((rows, value.shape[1]), f32)]
        + [shaped((units, breadth), bf16) for _ in lefts],
        seq_scratch(pieces, count, rows, width)
        + [pltpu.VMEM((units, depth), bf16) for _ in lefts]
        + [pltpu.VMEM((depth, breadth), bf16) for _ in rights]
        + [
            pltpu.VMEM((n_left, units, breadth), bf16),
            DMA((n_left + n_right,)),
            DMA((n_left,)),
        ],
        120_000_000,
    )(value, *lefts, *rights)
    return outs[0], list(outs[1:])


def gathered_more(ends, half, number, swap=None):
    total, heads = lax.axis_size("seq"), lax.axis_size("head")
    count = total // SIDE
    swaps = [] if swap is None else [swap]

    def body(ends_ref, half_ref, *rest):
        head, line, side = seq_places()
        beside = (head, line * SIDE + 1 - side)
        swap_refs, rest = rest[: len(swaps)], rest[len(swaps) :]
        ends_out, half_out, rest = rest[0], rest[1], rest[2:]
        swap_outs, rest = rest[: len(swaps)], rest[len(swaps) :]
        greet(head_partners() + seq_partners(count))

        def swap_steps(source, target):
            yield
            yield
            copy = remote(source, target, rest[8].at[0], rest[8].at[1], beside)
            copy.start()
            for _ in range(count):
                yield
            copy.wait()

        run_together(
            [
                gather_seq(ends_ref, ends_out, *rest[:5], count),
                gather_head(half_ref, half_out, *rest[5:8], 1),
            ]
            + [swap_steps(*refs) for refs in zip(swap_refs, swap_outs)]
        )

    outs = link_call(
        body,
        number,
        [ANY] * (2 + len(swaps)),
        [ANY] * (2 + len(swaps)),
        [
            shaped((total,) + ends.shape, ends.dtype),
            shaped((heads,) + half.shape, half.dtype),
        ]
        + [shaped(value.shape, value.dtype) for value in swaps],
        [DMA((1,))]
        + [DMA((2 * count,)) for _ in range(4)]
        + [DMA((1,)), DMA((3, 1)), DMA((3, 1)), DMA((2,))],
        150_000_000,
    )(ends, half, *swaps)
    return [outs[0], outs[1].reshape(-1, half.shape[1])] + list(outs[2:])


def scattered_last(qkv, gate, normed, hat, mlp, small, gain_rows, number, pieces=4, gate_pieces=2):
    total, heads = lax.axis_size("seq"), lax.axis_size("head")
    count = total // SIDE
    rows, width = qkv.shape[0] // total, qkv.shape[1] // pieces
    gate_width = gate.shape[1] // gate_pieces
    own_rows = normed.shape[0] // heads
    units, slices = mlp[0].shape[0], mlp[0].shape[1] // heads
    small_rows = small.shape[0]

    def body(qkv_ref, gate_ref, normed_ref, hat_ref, small_ref, *rest):
        mlp_refs, rest = rest[: len(mlp)], rest[len(mlp) :]
        qkv_out, gate_out, normed_out, small_out, rest = rest[0], rest[1], rest[2], rest[3], rest[4:]
        mlp_outs, rest = rest[: len(mlp)], rest[len(mlp) :]
        greet(head_partners() + seq_partners(count))

        def qkv_at(target, side, piece):
            begin = pl.multiple_of((target * SIDE + side) * rows, rows)
            return qkv_ref.at[pl.ds(begin, rows), pl.ds(piece * width, width)]

        def gate_at(target, side, piece):
            begin = pl.multiple_of(target * rows, rows)
            return gate_ref.at[pl.ds(begin, rows), pl.ds(piece * gate_width, gate_width)]

        def normed_at(target):
            return normed_ref.at[pl.ds(pl.multiple_of(target * own_rows, own_rows), own_rows)]

        def normed_steps(four, own, local, *sems):
            yield from scatter_head(normed_at, normed_out, *rest[13:19], 0, 1)
            own[...] = small_ref[...]
            product = jnp.sum(normed_out[...] * hat_ref[...], axis=0, keepdims=True)
            for row in range(product.shape[1] // 128):
                own[row : row + 1] = product[:, row * 128 : (row + 1) * 128]
            yield
            yield from gather_head(own, four, sems[0], sems[1], sems[2], 1)
            own[:gain_rows] = jnp.sum(four[:, :gain_rows], axis=0)
            for step in gather_seq(own, small_out, local, *sems[3:7], count):
                for _ in range(3):
                    yield

        steps = [
            normed_steps(*rest[19:29]),
            scatter_seq(
                gate_at,
                lambda piece: gate_out.at[:, pl.ds(piece * gate_width, gate_width)],
                rest[7],
                None,
                *rest[8:13],
                count,
            ),
            scatter_seq(
                qkv_at,
                lambda piece: qkv_out.at[:, pl.ds(piece * width, width)],
                *rest[:7],
                count,
            ),
        ]
        for index, (ref, out) in enumerate(zip(mlp_refs, mlp_outs)):

            def mlp_at(target, ref=ref):
                return ref.at[:, pl.ds(pl.multiple_of(target * slices, slices), slices)]

            begin = 29 + 6 * index
            steps.append(
                scatter_head(mlp_at, out, *rest[begin : begin + 6], HOLD, 2 + 3 * index)
            )
        run_together(steps)

    line_scratch = seq_scratch(gate_pieces, count, rows, gate_width)
    outs = link_call(
        body,
        number,
        [ANY] * 3 + [IN_VMEM] * 2 + [ANY] * len(mlp),
        [IN_VMEM] * (4 + len(mlp)),
        [
            shaped((rows, qkv.shape[1]), bf16),
            shaped((rows, gate.shape[1]), bf16),
            shaped((own_rows, normed.shape[1]), f32),
            shaped((total, small_rows, small.shape[1]), f32),
        ]
        + [shaped((units, slices), bf16) for _ in mlp],
        seq_scratch(pieces, count, rows, width)
        + line_scratch[1:]
        + head_scratch(own_rows, normed.shape[1])
        + [
            pltpu.VMEM((heads, small_rows, small.shape[1]), f32),
            pltpu.VMEM((small_rows, small.shape[1]), f32),
            DMA((1,)),
            DMA((1,)),
            DMA((3, 1)),
            DMA((3, 1)),
        ]
        + [DMA((2 * count,)) for _ in range(4)]
        + head_scratch(units, slices) * len(mlp),
        250_000_000,
    )(qkv, gate, normed, hat, small, *mlp)
    return outs[0], outs[1], outs[2], outs[3], list(outs[4:])


def side_columns(value, side, rows):
    count = value.shape[1] // (rows * SIDE)
    return jnp.concatenate(
        [
            lax.dynamic_slice_in_dim(value, (place * SIDE + side) * rows, rows, 1)
            for place in range(count)
        ],
        axis=1,
    )


def swapped(value):
    count = lax.axis_size("seq")
    return lax.ppermute(value, "seq", [(place, place ^ 1) for place in range(count)])


def silu_slope(tensor):
    sigmoid_part = jax.nn.sigmoid(tensor)
    return sigmoid_part * (1.0 + tensor * (1.0 - sigmoid_part))


def gathered(value, axis):
    return lax.all_gather(value, axis, axis=0, tiled=True)


def scattered(value, axis, dimension=0):
    return lax.psum_scatter(
        value.astype(bf16), axis, scatter_dimension=dimension, tiled=True
    ).astype(f32)


def on_device(
    block_in,
    out_cot,
    gain_one,
    qkv_weight,
    conv_weight,
    gate_weight,
    gain_out,
    out_weight,
    gain_two,
    mlp_gate,
    mlp_up,
    mlp_down,
    decay_code,
    beta_code,
):
    span_rows = decay_code.shape[0]
    width, heads, inner = qkv_weight.shape
    total_len = span_rows * lax.axis_size("seq")
    lead_rows = conv_weight.shape[0] - 1
    input_f = block_in.astype(f32)
    gain_first = gain_one.astype(f32)
    gain_second = gain_two.astype(f32)
    gain_head = gain_out.reshape(1, -1)
    taps = conv_weight.reshape(conv_weight.shape[0], heads * inner)
    out_flat = out_weight.reshape(heads * DV, width)
    columns, run_rows = token_columns(decay_code, beta_code, total_len)

    cot_all = gathered(out_cot, "seq")
    seq_count, head_count = lax.axis_size("seq"), lax.axis_size("head")
    seq_at, head_at = lax.axis_index("seq"), lax.axis_index("head")
    side = lax.rem(seq_at, SIDE)
    slice_rows = width // seq_count
    scale_own = rms_scale(input_f)
    hat_own = input_f * scale_own
    normed_own = (hat_own * gain_first).astype(bf16)
    normed_first, normed_half = gathered_crossed(
        normed_own, side_columns(normed_own, 1 - side, slice_rows), 1
    )
    mixed_in = jnp.einsum(
        "td,dhc->htc", normed_first, qkv_weight, preferred_element_type=f32
    ).astype(bf16)
    tail_in = passed_along(mixed_in[:, span_rows - 8 :], "seq", 1)
    tail_in = jnp.where(jnp.arange(8)[:, None] >= 8 - lead_rows, tail_in.astype(f32), 0.0)
    solve, score, fresh, reach, inner_part, turn, local_states, piece_end = run_local_forward(
        mixed_in, tail_in, taps, columns, run_rows, heads
    )
    ends, normed_side = gathered_more(piece_end.reshape(-1, DV + DK), normed_half, 2)
    ends = ends.reshape(-1, heads, DK, DV + DK)
    gate_pre = jnp.einsum("td,dhv->htv", normed_first, gate_weight, preferred_element_type=f32)
    states, core, branch = run_finish_forward(
        ends, local_states, reach, inner_part, gate_pre, gain_head
    )
    branch, cot_all = lax.optimization_barrier((branch, cot_all))
    branch_side = swapped(branch)
    middle = input_f + scattered_head(mm(branch, out_flat).astype(bf16), 3)
    scale_two = rms_scale(middle)
    hat_two = middle * scale_two
    normed_two = (hat_two * gain_second).astype(bf16)

    normed_two, branch_side = lax.optimization_barrier((normed_two, branch_side))
    rows_out = gathered_seq(normed_two, 4).reshape(-1, width)
    cot_f = out_cot.astype(f32)
    gate_units, up_units = mlp_gate.T, mlp_up.T
    gate_part = mm_nt(gate_units, rows_out)
    up_part = mm_nt(up_units, rows_out)
    d_hidden = mm_nt(mlp_down, cot_all)
    hidden = (jax.nn.silu(gate_part) * up_part).astype(bf16)
    d_gate_mlp = (d_hidden * up_part * silu_slope(gate_part)).astype(bf16)
    d_up_mlp = (d_hidden * jax.nn.silu(gate_part)).astype(bf16)
    d_rows = (mm_tn(d_gate_mlp, gate_units) + mm_tn(d_up_mlp, up_units)).astype(bf16)
    d_normed_two, (grad_mgate, grad_mup, grad_down) = scattered_seq_products(
        d_rows, [d_gate_mlp, d_up_mlp, hidden], [rows_out, cot_all], [0, 0, 1], 5
    )
    gain_two_part = jnp.sum(d_normed_two * hat_two, 0)
    e_two = d_normed_two * gain_second
    d_middle = cot_f + scale_two * (
        e_two - hat_two * jnp.mean(e_two * hat_two, axis=-1, keepdims=True)
    )
    hidden, d_middle = lax.optimization_barrier((hidden, d_middle))
    mlp_part, d_middle = lax.optimization_barrier(
        (mm_tn(hidden, mlp_down).astype(bf16), d_middle)
    )
    mlp_out = scattered(mlp_part, "seq")
    d_mix = d_middle.astype(bf16)
    d_mix_all, d_mix_half = gathered_crossed(d_mix, side_columns(d_mix, 1 - side, slice_rows), 6)
    d_branch = mm_nt(d_mix_all, out_flat)
    d_core, d_gate_low, gain_out_part, local_grads, grad_end = run_local_backward(
        d_branch, core, gate_pre, gain_head, reach, turn
    )
    grad_ends, d_mix_side = gathered_more(grad_end.reshape(-1, DV), d_mix_half, 7)
    d_gate_low, grad_ends = lax.optimization_barrier((d_gate_low, grad_ends))
    d_gate_side = swapped(d_gate_low)
    out_half = (
        mm_tn(side_columns(d_mix_all, side, slice_rows), branch) + mm_tn(d_mix_side, branch_side)
    ).astype(bf16)
    out_half, grad_ends, mlp_out = lax.optimization_barrier((out_half, grad_ends, mlp_out))
    output = (middle + mlp_out).astype(bf16)
    grad_out_s = lax.psum_scatter(
        out_half,
        "seq",
        scatter_dimension=0,
        axis_index_groups=[
            [place * SIDE + across for place in range(seq_count // SIDE)] for across in range(SIDE)
        ],
        tiled=True,
    )
    grad_ends = grad_ends.reshape(-1, heads, DK, DV)
    d_mixed, d_tail, d_lead, grad_conv = run_finish_backward(
        ends,
        grad_ends,
        mixed_in,
        tail_in,
        taps,
        columns,
        run_rows,
        solve,
        score,
        fresh,
        states,
        d_core,
        local_grads,
    )
    d_lead, grad_out_s = lax.optimization_barrier((d_lead, grad_out_s))
    from_next = passed_along(d_lead[:lead_rows], "seq", -1)
    d_tail = d_tail.at[8 - lead_rows :].add(from_next).astype(bf16)
    d_mixed = lax.dynamic_update_slice(d_mixed, d_tail, (span_rows - 8, 0))
    d_normed_part = jnp.einsum(
        "thc,dhc->td",
        d_mixed.reshape(span_rows, heads, inner),
        qkv_weight,
        preferred_element_type=f32,
    ) + jnp.einsum(
        "thv,dhv->td",
        d_gate_low.reshape(span_rows, heads, DV),
        gate_weight,
        preferred_element_type=f32,
    )
    grad_qkv = mm_tn(normed_first, d_mixed).astype(bf16)
    grad_gate = (
        mm_tn(side_columns(normed_first, side, slice_rows), d_gate_low)
        + mm_tn(normed_side, d_gate_side)
    ).astype(bf16)

    gains = jnp.concatenate([jnp.zeros_like(gain_two_part), gain_two_part, gain_out_part.reshape(-1)])
    gain_rows = -(-gains.shape[0] // 1024) * 8
    gains = jnp.pad(gains, (0, gain_rows * 128 - gains.shape[0])).reshape(gain_rows, 128)
    small = jnp.concatenate([gains, grad_conv.reshape(-1, 128)])
    grad_qkv_s, grad_gate_s, d_normed_one, small_all, (grad_mgate_t, grad_mup_t, grad_down_h) = (
        scattered_last(
            grad_qkv,
            grad_gate,
            d_normed_part.astype(bf16),
            hat_own,
            [grad_mgate, grad_mup, grad_down],
            small,
            gain_rows,
            8,
        )
    )
    e_one = d_normed_one * gain_first
    d_input = (
        d_middle + scale_own * (e_one - hat_own * jnp.mean(e_one * hat_own, axis=-1, keepdims=True))
    ).astype(bf16)

    small_sum = jnp.sum(small_all, axis=0)
    gains = small_sum[:gain_rows].reshape(-1)

    def own_slice(begin, length):
        length = length // (seq_count * head_count)
        return lax.dynamic_slice(
            gains, (begin + (head_at * seq_count + seq_at) * length,), (length,)
        )

    grad_conv_s = lax.dynamic_slice_in_dim(
        small_sum[gain_rows:].reshape(-1, heads, inner),
        seq_at * (inner // seq_count),
        inner // seq_count,
        2,
    )
    return (
        output,
        d_input,
        own_slice(0, width),
        grad_qkv_s.astype(f32).reshape(-1, heads, inner),
        grad_conv_s,
        grad_gate_s.astype(f32).reshape(-1, heads, DV),
        own_slice(2 * width, DV),
        grad_out_s.astype(f32).T.reshape(heads, DV, -1),
        own_slice(width, width),
        grad_mgate_t.astype(f32).T,
        grad_mup_t.astype(f32).T,
        grad_down_h.astype(f32),
    )


def solution(mesh):
    in_specs = (
        P(("seq", "head"), None),
        P(("seq", "head"), None),
        P(),
        P(None, "head", None),
        P(None, "head", None),
        P(None, "head", None),
        P(),
        P("head", None, None),
        P(),
        P(None, "seq"),
        P(None, "seq"),
        P("seq", None),
        P("seq", "head"),
        P("seq", "head"),
    )
    out_specs = (
        P(("seq", "head"), None),
        P(("seq", "head"), None),
        P(("head", "seq")),
        P("seq", "head", None),
        P(None, "head", "seq"),
        P("seq", "head", None),
        P(("head", "seq")),
        P("head", None, "seq"),
        P(("head", "seq")),
        P("head", "seq"),
        P("head", "seq"),
        P("seq", "head"),
    )
    return jax.shard_map(
        on_device, mesh=mesh, in_specs=in_specs, out_specs=out_specs, check_vma=False
    )
```

```python
import functools
import math

import jax
import jax.numpy as jnp
from jax import lax
from jax.experimental import pallas as pl
from jax.experimental.pallas import tpu as pltpu
from jax.sharding import PartitionSpec as P

DK = 128
DV = 256
STRETCH = 64
GROUP = 4 * STRETCH
INNER = 2 * DK + DV
BETA, GAMMA, BETA_GAMMA, TAIL, LAST, RUN = range(6)

epsilon = 1e-06
bf16 = jnp.bfloat16
f32 = jnp.float32
VMEM_BYTES = 56 * 2**20
HOLD = 4


def passed_along(value, axis, steps):
    count = lax.axis_size(axis)
    first, last = (max(0, -steps), min(count, count - steps))
    return lax.ppermute(value, axis, [(source, source + steps) for source in range(first, last)])


def rms_scale(tensor):
    return lax.rsqrt(jnp.mean(tensor * tensor, axis=-1, keepdims=True) + epsilon)


def log_rates(decay_code, total_len):
    code_level = decay_code.astype(f32) / 1023.0
    smooth = -jnp.exp(-code_level * math.log(total_len / 32.0)) / 32.0
    return jnp.where(decay_code == 1024, -0.25, smooth)


def token_columns(decay_code, beta_code, total_len):
    rows, heads = decay_code.shape
    rates = log_rates(decay_code, total_len)
    run = jnp.einsum(
        "ij,bjh->bih",
        jnp.tril(jnp.ones((STRETCH, STRETCH), f32)),
        rates.reshape(rows // STRETCH, STRETCH, heads),
        precision=lax.Precision.HIGHEST,
    )
    last = jnp.broadcast_to(run[:, -1:], run.shape).reshape(rows, heads)
    run = run.reshape(rows, heads)
    beta = 0.5 + beta_code.astype(f32) / 512.0
    gamma = jnp.exp(run)
    columns = jnp.concatenate(
        [beta, gamma, beta * gamma, jnp.exp(last - run), jnp.exp(last), run], axis=1
    )
    columns = jnp.pad(columns, ((0, 0), (0, 128 - columns.shape[1])))
    run_rows = jnp.pad(run.T, ((0, 8 - heads % 8), (0, 0)))
    return columns, run_rows


def mm(left, right):
    return jnp.dot(left, right, preferred_element_type=f32)


def mm_nt(left, right):
    return lax.dot_general(left, right, (((1,), (1,)), ((), ())), preferred_element_type=f32)


def mm_tn(left, right):
    return lax.dot_general(left, right, (((0,), (0,)), ((), ())), preferred_element_type=f32)


def column(columns_ref, kind, head, heads):
    block = columns_ref[...]
    lanes = lax.broadcasted_iota(jnp.int32, block.shape, 1)
    return jnp.sum(jnp.where(lanes == kind * heads + head, block, 0.0), axis=1, keepdims=True)


def square_ids():
    return (
        lax.broadcasted_iota(jnp.int32, (GROUP, GROUP), 0),
        lax.broadcasted_iota(jnp.int32, (GROUP, GROUP), 1),
    )


def convolved(padded_ref, tail_ref, mixed_ref, taps_ref):
    rows = mixed_ref.shape[0]
    count = taps_ref.shape[0]
    padded_ref[0:8, :] = tail_ref[...]
    padded_ref[8 : 8 + rows, :] = mixed_ref[...].astype(f32)
    taps = taps_ref[...].astype(f32)
    start = 9 - count
    total = taps[0:1] * padded_ref[start : start + rows, :]
    for tap in range(1, count):
        total += taps[tap : tap + 1] * padded_ref[start + tap : start + tap + rows, :]
    return total


def chunk_masks_stack(transposed):
    lanes = lax.broadcasted_iota(jnp.int32, transposed.shape, 1) // STRETCH
    parts = [jnp.where(lanes == part, transposed, 0.0) for part in range(GROUP // STRETCH)]
    return jnp.concatenate(parts, axis=0).astype(bf16)


def local_forward(
    mixed_ref,
    tail_ref,
    taps_ref,
    columns_ref,
    run_rows_ref,
    solve_ref,
    score_ref,
    fresh_ref,
    reach_ref,
    inner_ref,
    turn_ref,
    local_ref,
    end_ref,
    padded,
    turn_t,
    offsets,
):
    head = pl.program_id(0)
    heads = pl.num_programs(0)
    rows = mixed_ref.shape[0]
    per_group = GROUP // STRETCH
    stretches = rows // STRETCH
    total = convolved(padded, tail_ref, mixed_ref, taps_ref)
    activated = total * jax.nn.sigmoid(total)
    raw_q, raw_k = activated[:, :DK], activated[:, DK : 2 * DK]
    queries = raw_q * (
        lax.rsqrt(jnp.sum(raw_q * raw_q, axis=1, keepdims=True) + epsilon) * DK ** (-0.5)
    )
    keys = raw_k * lax.rsqrt(jnp.sum(raw_k * raw_k, axis=1, keepdims=True) + epsilon)
    values = activated[:, 2 * DK :]
    beta = column(columns_ref, BETA, head, heads)
    gamma = column(columns_ref, GAMMA, head, heads)
    beta_gamma = column(columns_ref, BETA_GAMMA, head, heads)
    tail_decay = column(columns_ref, TAIL, head, heads)
    last = column(columns_ref, LAST, head, heads)
    run = column(columns_ref, RUN, head, heads)
    row_id, col_id = square_ids()
    same = row_id // STRETCH == col_id // STRETCH
    causal = same & (row_id >= col_id)
    diagonal = row_id == col_id
    eye = jnp.where(
        lax.broadcasted_iota(jnp.int32, (DK, DK), 0) == lax.broadcasted_iota(jnp.int32, (DK, DK), 1),
        1.0,
        0.0,
    )
    for group in range(rows // GROUP):
        span = slice(group * GROUP, (group + 1) * GROUP)
        key_b = keys[span].astype(bf16)
        query_b = queries[span].astype(bf16)
        gaps = run[span] - run_rows_ref[pl.ds(head, 1), span]
        within = jnp.exp(jnp.where(causal, gaps, -1e30))
        lower = jnp.where(diagonal, 0.0, beta[span] * within * mm_nt(key_b, key_b))
        solve = jnp.where(diagonal, 1.0, jnp.where(row_id // 2 == col_id // 2, -lower, 0.0))
        size = 2
        while size < STRETCH:
            crossing = (row_id // (2 * size) == col_id // (2 * size)) & (
                row_id // size != col_id // size
            )
            solve_b = solve.astype(bf16)
            half = mm(solve_b, jnp.where(crossing, lower, 0.0).astype(bf16))
            solve = solve - mm(half.astype(bf16), solve_b)
            size *= 2
        solve_b = solve.astype(bf16)
        right = jnp.concatenate([beta[span] * values[span], beta_gamma[span] * keys[span]], axis=1)
        fresh_b = mm(solve_b, right.astype(bf16)).astype(bf16)
        score_b = (within * mm_nt(query_b, key_b)).astype(bf16)
        scored = mm(score_b, fresh_b)
        solve_ref[group] = solve_b
        score_ref[group] = score_b
        fresh_ref[span, :] = fresh_b
        inner_ref[span, :] = scored[:, :DV]
        reach_ref[span, :] = (gamma[span] * queries[span] - scored[:, DV:]).astype(bf16)
        tail_keys = (tail_decay[span] * keys[span]).T
        moved = mm(chunk_masks_stack(tail_keys), fresh_b)
        for part in range(per_group):
            at = group * per_group + part
            block = moved[part * DK : (part + 1) * DK]
            stay = last[at * STRETCH : at * STRETCH + 1]
            turned = stay * eye - block[:, DV:]
            turn_t[head, at] = turned.astype(bf16)
            turn_ref[at] = turned.T.astype(bf16)
            offsets[head, at] = block[:, :DV]

    @pl.when(head == heads - 1)
    def _():
        states = [
            jnp.concatenate([jnp.zeros((DK, DV), f32), eye], axis=1)
            for _ in range(local_ref.shape[0])
        ]
        for at in range(stretches):
            for h in range(len(states)):
                state_b = states[h].astype(bf16)
                local_ref[h, at] = state_b
                moved = mm(turn_t[h, at], state_b)
                states[h] = jnp.concatenate(
                    [moved[:, :DV] + offsets[h, at], moved[:, DV:]], axis=1
                )
        for h in range(len(states)):
            end_ref[h] = states[h].astype(bf16)


def finish_forward(
    ends_ref, local_ref, reach_ref, inner_ref, gate_ref, gain_ref, state_ref, core_ref, branch_ref, start
):
    head = pl.program_id(0)
    heads, stretches = start.shape[0], local_ref.shape[0]

    @pl.when(head == 0)
    def _():
        start[...] = jnp.zeros_like(start)

        def one(source, carry):
            for h in range(heads):
                start[h] = (
                    mm(ends_ref[source, h, :, DV:], start[h].astype(bf16))
                    + ends_ref[source, h, :, :DV].astype(f32)
                )
            return carry

        lax.fori_loop(0, lax.axis_index("seq"), one, 0)

    start_b = start[head].astype(bf16)
    cores = []
    for at in range(stretches):
        state_b = (
            local_ref[at, :, :DV].astype(f32) + mm(local_ref[at, :, DV:], start_b)
        ).astype(bf16)
        state_ref[at] = state_b
        span = slice(at * STRETCH, (at + 1) * STRETCH)
        cores.append(inner_ref[span, :] + mm(reach_ref[span, :], state_b))
    core = jnp.concatenate(cores, axis=0)
    core_ref[...] = core
    gate = gate_ref[...]
    branch = core * rms_scale(core) * gain_ref[...].astype(f32) * (gate * jax.nn.sigmoid(gate))
    branch_ref[...] = branch.astype(bf16)


def local_backward(
    d_branch_ref,
    core_ref,
    gate_ref,
    gain_ref,
    reach_ref,
    turn_ref,
    d_core_ref,
    d_gate_ref,
    gain_part_ref,
    local_ref,
    end_ref,
    pulls,
):
    head = pl.program_id(0)
    heads = pl.num_programs(0)
    rows = core_ref.shape[0]
    per_group = GROUP // STRETCH
    stretches = rows // STRETCH
    core = core_ref[...]
    gate = gate_ref[...]
    gain = gain_ref[...].astype(f32)
    d_branch = d_branch_ref[...]
    scale = rms_scale(core)
    nhat = core * scale
    sig = jax.nn.sigmoid(gate)
    gated = d_branch * (gate * sig)

    @pl.when(head == 0)
    def _():
        gain_part_ref[...] = jnp.zeros_like(gain_part_ref)

    gain_part_ref[...] += jnp.sum(gated * nhat, axis=0, keepdims=True)
    f = gated * gain
    d_core = scale * (f - nhat * jnp.mean(f * nhat, axis=1, keepdims=True))
    d_gate_ref[...] = (d_branch * nhat * gain * sig * (1.0 + gate * (1.0 - sig))).astype(bf16)
    d_core_b = d_core.astype(bf16)
    d_core_ref[...] = d_core_b
    for group in range(rows // GROUP):
        span = slice(group * GROUP, (group + 1) * GROUP)
        pulled = mm(chunk_masks_stack(reach_ref[span, :].astype(f32).T), d_core_b[span])
        for part in range(per_group):
            pulls[head, group * per_group + part] = pulled[part * DK : (part + 1) * DK]

    @pl.when(head == heads - 1)
    def _():
        eye = jnp.where(
            lax.broadcasted_iota(jnp.int32, (DK, DK), 0)
            == lax.broadcasted_iota(jnp.int32, (DK, DK), 1),
            1.0,
            0.0,
        )
        grads = [
            jnp.concatenate([jnp.zeros((DK, DV), f32), eye], axis=1)
            for _ in range(local_ref.shape[0])
        ]
        for at in reversed(range(stretches)):
            for h in range(len(grads)):
                grad_b = grads[h].astype(bf16)
                local_ref[h, at] = grad_b
                moved = mm(turn_ref[h, at], grad_b)
                grads[h] = jnp.concatenate([moved[:, :DV] + pulls[h, at], moved[:, DV:]], axis=1)
        for h in range(len(grads)):
            end_ref[h] = grads[h][:, :DV].astype(bf16)


def finish_backward(
    ends_ref,
    grad_ends_ref,
    mixed_ref,
    tail_ref,
    taps_ref,
    columns_ref,
    run_rows_ref,
    solve_ref,
    score_ref,
    fresh_ref,
    state_ref,
    d_core_ref,
    local_ref,
    d_mixed_ref,
    tail_out_ref,
    lead_ref,
    grad_taps_ref,
    padded,
    spread,
    end,
):
    head = pl.program_id(0)
    heads = pl.num_programs(0)
    rows = mixed_ref.shape[0]
    per_group = GROUP // STRETCH

    @pl.when(head == 0)
    def _():
        end[...] = jnp.zeros_like(end)
        count = ends_ref.shape[0]

        def one(turn, carry):
            source = count - 1 - turn
            for h in range(end.shape[0]):
                end[h] = (
                    mm_tn(ends_ref[source, h, :, DV:], end[h].astype(bf16))
                    + grad_ends_ref[source, h].astype(f32)
                )
            return carry

        lax.fori_loop(0, count - 1 - lax.axis_index("seq"), one, 0)

    end_b = end[head].astype(bf16)
    total = convolved(padded, tail_ref, mixed_ref, taps_ref)
    sig = jax.nn.sigmoid(total)
    activated = total * sig
    raw_q, raw_k = activated[:, :DK], activated[:, DK : 2 * DK]
    scale_q = lax.rsqrt(jnp.sum(raw_q * raw_q, axis=1, keepdims=True) + epsilon)
    scale_k = lax.rsqrt(jnp.sum(raw_k * raw_k, axis=1, keepdims=True) + epsilon)
    unit_q = raw_q * scale_q
    keys = raw_k * scale_k
    beta = column(columns_ref, BETA, head, heads)
    gamma = column(columns_ref, GAMMA, head, heads)
    beta_gamma = column(columns_ref, BETA_GAMMA, head, heads)
    tail_decay = column(columns_ref, TAIL, head, heads)
    run = column(columns_ref, RUN, head, heads)
    row_id, col_id = square_ids()
    causal = (row_id // STRETCH == col_id // STRETCH) & (row_id >= col_id)
    diagonal = row_id == col_id
    d_queries, d_keys, d_values = [], [], []
    for group in range(rows // GROUP):
        span = slice(group * GROUP, (group + 1) * GROUP)
        key_b = keys[span].astype(bf16)
        query_b = (unit_q[span] * DK ** (-0.5)).astype(bf16)
        tail_keys = (tail_decay[span] * keys[span]).astype(bf16)
        d_core_b = d_core_ref[span, :]
        grad_bs, from_grad, fresh_parts, from_state = [], [], [], []
        for part in range(per_group):
            at = group * per_group + part
            own = slice(part * STRETCH, (part + 1) * STRETCH)
            rows_at = slice(at * STRETCH, (at + 1) * STRETCH)
            grad_b = (
                local_ref[at, :, :DV].astype(f32) + mm(local_ref[at, :, DV:], end_b)
            ).astype(bf16)
            grad_bs.append(grad_b)
            from_grad.append(mm(tail_keys[own], grad_b))
            fresh_parts.append(mm(fresh_ref[rows_at, DV:], state_ref[at]))
            from_state.append(mm_nt(d_core_b[own], state_ref[at]))
        d_fresh = mm_tn(score_ref[group], d_core_b) + jnp.concatenate(from_grad, axis=0)
        d_right = mm_tn(solve_ref[group], d_fresh.astype(bf16))
        d_right_b = d_right.astype(bf16)
        fresh = fresh_ref[span, :DV].astype(f32) - jnp.concatenate(fresh_parts, axis=0)
        fresh_b = fresh.astype(bf16)
        gaps = run[span] - run_rows_ref[pl.ds(head, 1), span]
        within = jnp.exp(jnp.where(causal, gaps, -1e30))
        d_score = (within * mm_nt(d_core_b, fresh_b)).astype(bf16)
        d_lower = jnp.where(
            diagonal, 0.0, -beta[span] * within * mm_nt(d_right_b, fresh_b)
        ).astype(bf16)
        state_keys, grad_keys = [], []
        for part in range(per_group):
            at = group * per_group + part
            own = slice(part * STRETCH, (part + 1) * STRETCH)
            state_keys.append(mm_nt(d_right_b[own], state_ref[at]))
            grad_keys.append(mm_nt(fresh_b[own], grad_bs[part]))
        d_queries.append(gamma[span] * jnp.concatenate(from_state, axis=0) + mm(d_score, key_b))
        d_keys.append(
            mm_tn(d_score, query_b)
            + mm_tn(d_lower, key_b)
            + mm(d_lower, key_b)
            + tail_decay[span] * jnp.concatenate(grad_keys, axis=0)
            - beta_gamma[span] * jnp.concatenate(state_keys, axis=0)
        )
        d_values.append(beta[span] * d_right)
    g_q = jnp.concatenate(d_queries, axis=0) * DK ** (-0.5)
    g_k = jnp.concatenate(d_keys, axis=0)
    d_act = jnp.concatenate(
        [
            scale_q * (g_q - unit_q * jnp.sum(unit_q * g_q, axis=1, keepdims=True)),
            scale_k * (g_k - keys * jnp.sum(keys * g_k, axis=1, keepdims=True)),
            jnp.concatenate(d_values, axis=0),
        ],
        axis=1,
    )
    d_conv = d_act * (sig * (1.0 + total * (1.0 - sig)))
    taps = taps_ref[...].astype(f32)
    count = taps_ref.shape[0]
    start = 9 - count
    grad_taps_ref[...] = jnp.concatenate(
        [
            jnp.sum(padded[start + tap : start + tap + rows, :] * d_conv, axis=0, keepdims=True)
            for tap in range(count)
        ],
        axis=0,
    )
    spread[0:8, :] = jnp.zeros((8, d_conv.shape[1]), f32)
    spread[8 : 8 + rows, :] = d_conv
    spread[8 + rows : 16 + rows, :] = jnp.zeros((8, d_conv.shape[1]), f32)
    lead = taps[0:1] * spread[8:16, :]
    d_mixed = taps[0:1] * spread[7 + count : 7 + count + rows, :]
    for tap in range(1, count):
        lead += taps[tap : tap + 1] * spread[8 - tap : 16 - tap, :]
        begin = 7 + count - tap
        d_mixed += taps[tap : tap + 1] * spread[begin : begin + rows, :]
    lead_ref[...] = lead
    d_mixed_ref[...] = d_mixed.astype(bf16)
    tail_out_ref[...] = d_mixed[rows - 8 :]


def whole(shape):
    return pl.BlockSpec(shape, lambda h: (0,) * len(shape))


def by_head(shape):
    return pl.BlockSpec((None,) + shape, lambda h: (h,) + (0,) * len(shape))


def by_columns(rows, width):
    return pl.BlockSpec((rows, width), lambda h: (0, h))


def kernel_call(body, heads, ins, outs, out_shapes, scratch, flops, moved):
    return pl.pallas_call(
        body,
        grid=(heads,),
        in_specs=ins,
        out_specs=outs,
        out_shape=out_shapes,
        scratch_shapes=scratch,
        compiler_params=pltpu.CompilerParams(
            dimension_semantics=("arbitrary",), vmem_limit_bytes=VMEM_BYTES
        ),
        cost_estimate=pl.CostEstimate(flops=flops, bytes_accessed=moved, transcendentals=0),
    )


def shaped(shape, kind):
    return jax.ShapeDtypeStruct(shape, kind)


def run_local_forward(mixed, tail, taps, columns, run_rows, heads):
    rows = mixed.shape[1]
    count = taps.shape[0]
    groups, stretches = rows // GROUP, rows // STRETCH
    return kernel_call(
        local_forward,
        heads,
        [
            by_head((rows, INNER)),
            by_head((8, INNER)),
            by_columns(count, INNER),
            whole(columns.shape),
            whole(run_rows.shape),
        ],
        [
            by_head((groups, GROUP, GROUP)),
            by_head((groups, GROUP, GROUP)),
            by_head((rows, DV + DK)),
            by_head((rows, DK)),
            by_columns(rows, DV),
            by_head((stretches, DK, DK)),
            whole((heads, stretches, DK, DV + DK)),
            whole((heads, DK, DV + DK)),
        ],
        [
            shaped((heads, groups, GROUP, GROUP), bf16),
            shaped((heads, groups, GROUP, GROUP), bf16),
            shaped((heads, rows, DV + DK), bf16),
            shaped((heads, rows, DK), bf16),
            shaped((rows, heads * DV), f32),
            shaped((heads, stretches, DK, DK), bf16),
            shaped((heads, stretches, DK, DV + DK), bf16),
            shaped((heads, DK, DV + DK), bf16),
        ],
        [
            pltpu.VMEM((rows + 8, INNER), f32),
            pltpu.VMEM((heads, stretches, DK, DK), bf16),
            pltpu.VMEM((heads, stretches, DK, DV), f32),
        ],
        12_000_000_000,
        20_000_000,
    )(mixed, tail, taps, columns, run_rows)


def run_finish_forward(ends, local, reach, inner, gate_pre, gain):
    heads, stretches = local.shape[:2]
    rows = inner.shape[0]
    return kernel_call(
        finish_forward,
        heads,
        [
            whole(ends.shape),
            by_head((stretches, DK, DV + DK)),
            by_head((rows, DK)),
            by_columns(rows, DV),
            by_head((rows, DV)),
            whole(gain.shape),
        ],
        [by_head((stretches, DK, DV)), by_columns(rows, DV), by_columns(rows, DV)],
        [
            shaped((heads, stretches, DK, DV), bf16),
            shaped((rows, heads * DV), f32),
            shaped((rows, heads * DV), bf16),
        ],
        [pltpu.VMEM((heads, DK, DV), f32)],
        3_000_000_000,
        20_000_000,
    )(ends, local, reach, inner, gate_pre, gain)


def run_local_backward(d_branch, core, gate_pre, gain, reach, turn):
    heads, stretches = turn.shape[:2]
    rows = core.shape[0]
    return kernel_call(
        local_backward,
        heads,
        [
            by_columns(rows, DV),
            by_columns(rows, DV),
            by_head((rows, DV)),
            whole(gain.shape),
            by_head((rows, DK)),
            whole(turn.shape),
        ],
        [
            by_columns(rows, DV),
            by_columns(rows, DV),
            whole((1, DV)),
            whole((heads, stretches, DK, DV + DK)),
            whole((heads, DK, DV)),
        ],
        [
            shaped((rows, heads * DV), bf16),
            shaped((rows, heads * DV), bf16),
            shaped((1, DV), f32),
            shaped((heads, stretches, DK, DV + DK), bf16),
            shaped((heads, DK, DV), bf16),
        ],
        [pltpu.VMEM((heads, stretches, DK, DV), f32)],
        4_000_000_000,
        20_000_000,
    )(d_branch, core, gate_pre, gain, reach, turn)


def run_finish_backward(
    ends, grad_ends, mixed, tail, taps, columns, run_rows, solve, score, fresh, states, d_core, local
):
    heads, stretches = local.shape[:2]
    rows = mixed.shape[1]
    groups = rows // GROUP
    count = taps.shape[0]
    return kernel_call(
        finish_backward,
        heads,
        [
            whole(ends.shape),
            whole(grad_ends.shape),
            by_head((rows, INNER)),
            by_head((8, INNER)),
            by_columns(count, INNER),
            whole(columns.shape),
            whole(run_rows.shape),
            by_head((groups, GROUP, GROUP)),
            by_head((groups, GROUP, GROUP)),
            by_head((rows, DV + DK)),
            by_head((stretches, DK, DV)),
            by_columns(rows, DV),
            by_head((stretches, DK, DV + DK)),
        ],
        [
            by_columns(rows, INNER),
            by_columns(8, INNER),
            by_columns(8, INNER),
            by_columns(count, INNER),
        ],
        [
            shaped((rows, heads * INNER), bf16),
            shaped((8, heads * INNER), f32),
            shaped((8, heads * INNER), f32),
            shaped((count, heads * INNER), f32),
        ],
        [
            pltpu.VMEM((rows + 8, INNER), f32),
            pltpu.VMEM((rows + 16, INNER), f32),
            pltpu.VMEM((heads, DK, DV), f32),
        ],
        12_000_000_000,
        20_000_000,
    )(ends, grad_ends, mixed, tail, taps, columns, run_rows, solve, score, fresh, states, d_core, local)


MESH = pl.DeviceIdType.MESH
SIDE = 2


def remote(source, target, send, arrive, device):
    return pltpu.make_async_remote_copy(
        src_ref=source,
        dst_ref=target,
        send_sem=send,
        recv_sem=arrive,
        device_id=device,
        device_id_type=MESH,
    )


def greet(partners):
    barrier = pltpu.get_barrier_semaphore()
    expected = 0
    for device, there in partners:
        if there is None:
            pl.semaphore_signal(barrier, inc=1, device_id=device, device_id_type=MESH)
            expected = expected + 1
        else:

            @pl.when(there)
            def _(device=device):
                pl.semaphore_signal(barrier, inc=1, device_id=device, device_id_type=MESH)

            expected = expected + there.astype(jnp.int32)
    pl.semaphore_wait(barrier, expected)


def head_places():
    head, seq = lax.axis_index("head"), lax.axis_index("seq")
    core = lax.rem(head, 2)
    sibling = head + 1 - 2 * core
    across = lax.rem(head + 2, 4)
    return head, seq, sibling, across


def head_partners():
    head, seq, sibling, across = head_places()
    return [((sibling, seq), None), ((across, seq), None)]


def seq_places():
    head, seq = lax.axis_index("head"), lax.axis_index("seq")
    return head, seq // SIDE, lax.rem(seq, SIDE)


def seq_partners(count):
    head, line, side = seq_places()
    return [
        ((head, line * SIDE + 1 - side), None),
        ((head, (line + 1) * SIDE + side), line < count - 1),
        ((head, (line - 1) * SIDE + side), line > 0),
    ]


def run_together(steps):
    steps = list(steps)
    while steps:
        alive = []
        for step in steps:
            try:
                next(step)
                alive.append(step)
            except StopIteration:
                pass
        steps = alive


def gather_head(own_ref, out_ref, local, send, arrive, pieces):
    head, seq, sibling, across = head_places()
    far = lax.rem(sibling + 2, 4)
    rows = own_ref.shape[0] // pieces
    keep = pltpu.make_async_copy(own_ref, out_ref.at[head], local.at[0])
    keep.start()

    def part(ref, piece):
        return ref.at[pl.ds(piece * rows, rows)]

    outgoing = []
    for piece in range(pieces):
        outgoing.append(
            remote(
                part(own_ref, piece),
                part(out_ref.at[head], piece),
                send.at[0, piece],
                arrive.at[0, piece],
                (across, seq),
            )
        )
    for piece in range(pieces):
        outgoing.append(
            remote(
                part(own_ref, piece),
                part(out_ref.at[head], piece),
                send.at[1, piece],
                arrive.at[1, piece],
                (sibling, seq),
            )
        )
    for copy in outgoing:
        copy.start()
    yield
    forwards = []
    for piece in range(pieces):
        outgoing[piece].wait_recv()
        forward = remote(
            part(out_ref.at[across], piece),
            part(out_ref.at[across], piece),
            send.at[2, piece],
            arrive.at[2, piece],
            (sibling, seq),
        )
        forward.start()
        forwards.append(forward)
        yield
    for copy in outgoing[pieces:] + forwards:
        copy.wait_recv()
    for copy in outgoing + forwards:
        copy.wait_send()
    keep.wait()


def scatter_head(source_at, out_ref, own, crossed, passed, local, send, arrive, hold=0, pause=0):
    head, seq, sibling, across = head_places()
    far = lax.rem(sibling + 2, 4)
    loads = [
        pltpu.make_async_copy(source_at(target), own.at[slot], local.at[slot])
        for slot, target in enumerate((across, head))
    ]
    copies = [
        remote(source_at(target), crossed.at[slot], send.at[slot], arrive.at[slot], (sibling, seq))
        for slot, target in enumerate((far, sibling))
    ]
    for slot in range(2):
        copies[slot].start()
        loads[slot].start()
    for _ in range(1 + hold):
        yield
    loads[0].wait()
    copies[0].wait_recv()
    own[0] = (own[0].astype(f32) + crossed[0].astype(f32)).astype(own.dtype)
    onward = remote(own.at[0], passed, send.at[2], arrive.at[2], (across, seq))
    onward.start()
    for _ in range(1 + pause):
        yield
    loads[1].wait()
    copies[1].wait_recv()
    onward.wait_recv()
    total = own[1].astype(f32) + crossed[1].astype(f32) + passed[...].astype(f32)
    out_ref[...] = total.astype(out_ref.dtype)
    onward.wait_send()
    for copy in copies:
        copy.wait_send()


def gather_seq(own_ref, out_ref, local, side_send, side_arrive, line_send, line_arrive, count):
    head, line, side = seq_places()
    me = line * SIDE + side
    beside = (head, line * SIDE + 1 - side)
    ways = ((1, line < count - 1), (-1, line > 0))
    keep = pltpu.make_async_copy(own_ref, out_ref.at[me], local.at[0])
    keep.start()

    def along(source, block, way, step):
        slot = step if way > 0 else count + step
        return remote(
            source,
            out_ref.at[block],
            line_send.at[slot],
            line_arrive.at[slot],
            (head, (line + way) * SIDE + side),
        )

    def over(source, block, slot):
        return remote(source, out_ref.at[block], side_send.at[slot], side_arrive.at[slot], beside)

    for way, onward in ways:

        @pl.when(onward)
        def _(way=way):
            along(own_ref, me, way, 0).start()

    over(own_ref, me, 0).start()
    yield
    for step in range(1, count):
        for way, onward in ways:
            block = me - way * step * SIDE
            arrives = line >= step if way > 0 else line + step < count

            @pl.when(arrives)
            def _(way=way, onward=onward, block=block, step=step):
                landed = out_ref.at[block]
                slot = step if way > 0 else count + step
                remote(
                    landed, landed, line_send.at[slot - 1], line_arrive.at[slot - 1], beside
                ).wait_recv()

                @pl.when(onward)
                def _():
                    along(landed, block, way, step).start()

                over(landed, block, slot).start()

        yield
    over(own_ref, me, 0).wait()
    for way, onward in ways:

        @pl.when(onward)
        def _(way=way):
            along(own_ref, me, way, 0).wait_send()

    for step in range(1, count):
        for way, onward in ways:
            block = me - way * step * SIDE
            arrives = line >= step if way > 0 else line + step < count

            @pl.when(arrives)
            def _(way=way, onward=onward, block=block, step=step):
                landed = out_ref.at[block]
                slot = step if way > 0 else count + step
                over(landed, block, slot).wait()

                @pl.when(onward)
                def _():
                    along(landed, block, way, step).wait_send()

    keep.wait()


def scatter_seq(source_at, out_at, own, crossed, risen, fallen, local, sends, arrivals, count):
    head, line, side = seq_places()
    beside = (head, line * SIDE + 1 - side)
    pieces = own.shape[0]

    def targets(distance):
        if distance == 0:
            return [(line, None, 0)]
        return [
            (line - distance, line >= distance, -1),
            (line + distance, line + distance < count, 1),
        ]

    def load(piece, target):
        return pltpu.make_async_copy(
            source_at(target, side, piece), own.at[piece, target], local.at[piece, target]
        )

    def cross(piece, target):
        return remote(
            source_at(target, 1 - side, piece),
            crossed.at[piece, target],
            sends.at[0, piece, target],
            arrivals.at[0, piece, target],
            beside,
        )

    def onward(piece, target, way, arriving=False):
        landing = risen if way > 0 else fallen
        return remote(
            own.at[piece, target],
            landing.at[piece, target],
            sends.at[1, piece, target],
            arrivals.at[1 if way > 0 else 2, piece, target],
            beside if arriving else (head, (line + way) * SIDE + side),
        )

    def guarded(there, body):
        if there is None:
            body()
        else:
            pl.when(there)(body)

    def here(piece, target):
        load(piece, target).wait()
        total = own[piece, target].astype(f32)
        if crossed is not None:
            cross(piece, target).wait_recv()
            total += crossed[piece, target].astype(f32)
        return total

    def arrived(piece, target, way):
        landing = risen if way > 0 else fallen
        onward(piece, target, way, True).wait_recv()
        return landing[piece, target].astype(f32)

    for piece in range(pieces):
        for distance in range(count - 1, -1, -1):
            for target, there, _ in targets(distance):

                def begin(piece=piece, target=target):
                    if crossed is not None:
                        cross(piece, target).start()
                    load(piece, target).start()

                guarded(there, begin)
    yield
    for piece in range(pieces):
        for distance in range(count - 1, 0, -1):
            for target, there, way in targets(distance):
                first = line == count - 1 if way < 0 else line == 0

                @pl.when(jnp.logical_and(there, first))
                def _(piece=piece, target=target, way=way):
                    own[piece, target] = here(piece, target).astype(own.dtype)
                    onward(piece, target, way).start()

                @pl.when(jnp.logical_and(there, jnp.logical_not(first)))
                def _(piece=piece, target=target, way=way):
                    total = here(piece, target) + arrived(piece, target, way)
                    own[piece, target] = total.astype(own.dtype)
                    onward(piece, target, way).start()

            yield
        out = out_at(piece)

        @pl.when(line == 0)
        def _(piece=piece, out=out):
            out[...] = (here(piece, line) + arrived(piece, line, -1)).astype(out.dtype)

        @pl.when(line == count - 1)
        def _(piece=piece, out=out):
            out[...] = (here(piece, line) + arrived(piece, line, 1)).astype(out.dtype)

        @pl.when(jnp.logical_and(line > 0, line < count - 1))
        def _(piece=piece, out=out):
            total = here(piece, line) + arrived(piece, line, -1) + arrived(piece, line, 1)
            out[...] = total.astype(out.dtype)

        yield
    for piece in range(pieces):
        for distance in range(count - 1, -1, -1):
            for target, there, way in targets(distance):

                def finish(piece=piece, target=target, way=way):
                    if crossed is not None:
                        cross(piece, target).wait_send()
                    if way:
                        onward(piece, target, way).wait_send()

                guarded(there, finish)


ANY = pl.BlockSpec(memory_space=pl.ANY)
IN_VMEM = pl.BlockSpec(memory_space=pltpu.VMEM)
DMA = pltpu.SemaphoreType.DMA


def link_call(body, number, ins, outs, shapes, scratch, moved):
    return pl.pallas_call(
        body,
        in_specs=ins,
        out_specs=outs,
        out_shape=shapes,
        scratch_shapes=scratch,
        compiler_params=pltpu.CompilerParams(
            collective_id=number, has_side_effects=True, vmem_limit_bytes=VMEM_BYTES
        ),
        cost_estimate=pl.CostEstimate(flops=0, bytes_accessed=moved // 8, transcendentals=0),
    )


def gathered_head(value, number, pieces=4):
    count = lax.axis_size("head")
    if count != 4:
        return lax.all_gather(value, "head", axis=0, tiled=True)
    rows, width = value.shape

    def body(own_ref, out_ref, local, send, arrive):
        greet(head_partners())
        run_together([gather_head(own_ref, out_ref, local, send, arrive, pieces)])

    out = link_call(
        body,
        number,
        [ANY],
        ANY,
        shaped((count, rows, width), value.dtype),
        [DMA((1,)), DMA((3, pieces)), DMA((3, pieces))],
        60_000_000,
    )(value)
    return out.reshape(count * rows, width)


def gathered_crossed(value, half, number, pieces=4):
    count = lax.axis_size("head")
    rows, width = value.shape

    def body(own_ref, half_ref, out_ref, landed_ref, local, send, arrive, crossing):
        head, line, side = seq_places()
        beside = (head, line * SIDE + 1 - side)
        greet(head_partners() + [(beside, None)])
        cross = remote(half_ref, landed_ref, crossing.at[0], crossing.at[1], beside)
        cross.start()
        run_together([gather_head(own_ref, out_ref, local, send, arrive, pieces)])
        cross.wait()

    out, landed = link_call(
        body,
        number,
        [ANY, ANY],
        [ANY, ANY],
        [shaped((count, rows, width), value.dtype), shaped(half.shape, half.dtype)],
        [DMA((1,)), DMA((3, pieces)), DMA((3, pieces)), DMA((2,))],
        60_000_000,
    )(value, half)
    return out.reshape(count * rows, width), landed


def gathered_seq(value, number):
    total = lax.axis_size("seq")
    count = total // SIDE
    rows, width = value.shape
    if total % SIDE or count < 2:
        return lax.all_gather(value, "seq")

    def body(own_ref, out_ref, *sems):
        greet(seq_partners(count))
        run_together([gather_seq(own_ref, out_ref, *sems, count)])

    return link_call(
        body,
        number,
        [ANY],
        ANY,
        shaped((total, rows, width), value.dtype),
        [DMA((1,))] + [DMA((2 * count,)) for _ in range(4)],
        120_000_000,
    )(value)


def head_scratch(rows, width):
    return [
        pltpu.VMEM((2, rows, width), bf16),
        pltpu.VMEM((2, rows, width), bf16),
        pltpu.VMEM((rows, width), bf16),
        DMA((2,)),
        DMA((3,)),
        DMA((3,)),
    ]


def seq_scratch(pieces, count, rows, width):
    return [pltpu.VMEM((pieces, count, rows, width), bf16) for _ in range(4)] + [
        DMA((pieces, count)),
        DMA((2, pieces, count)),
        DMA((3, pieces, count)),
    ]


def scattered_head(value, number, pieces=2):
    count = lax.axis_size("head")
    if count != 4:
        return scattered(value, "head")
    rows, width = value.shape[0] // count, value.shape[1] // pieces

    def body(source, out, *rest):
        greet(head_partners())
        steps = []
        for piece in range(pieces):
            span = pl.ds(piece * width, width)

            def source_at(target, span=span):
                return source.at[pl.ds(pl.multiple_of(target * rows, rows), rows), span]

            steps.append(
                scatter_head(source_at, out.at[:, span], *rest[6 * piece : 6 * piece + 6])
            )
        run_together(steps)

    return link_call(
        body,
        number,
        [ANY],
        IN_VMEM,
        shaped((rows, value.shape[1]), f32),
        head_scratch(rows, width) * pieces,
        60_000_000,
    )(value)


def scattered_seq(value, number, pieces=2):
    total = lax.axis_size("seq")
    count = total // SIDE
    if total % SIDE or count < 2:
        return scattered(value, "seq")
    rows, width = value.shape[0] // total, value.shape[1] // pieces

    def body(source, out, *rest):
        greet(seq_partners(count))

        def source_at(target, side, piece):
            begin = pl.multiple_of((target * SIDE + side) * rows, rows)
            return source.at[pl.ds(begin, rows), pl.ds(piece * width, width)]

        def out_at(piece):
            return out.at[:, pl.ds(piece * width, width)]

        run_together([scatter_seq(source_at, out_at, *rest, count)])

    return link_call(
        body,
        number,
        [ANY],
        IN_VMEM,
        shaped((rows, value.shape[1]), f32),
        seq_scratch(pieces, count, rows, width),
        120_000_000,
    )(value)


def product_steps(left_hbm, right_hbm, out_refs, picks, lefts, rights, tiles, load, store, per_round):
    loads = [
        pltpu.make_async_copy(ref, held, load.at[index])
        for index, (ref, held) in enumerate(zip(left_hbm + right_hbm, lefts + rights))
    ]
    for copy in loads:
        copy.start()
    yield
    for copy in loads:
        copy.wait()
    units, width = tiles.shape[1:]
    block = units // 4 if units % 64 == 0 else units
    span = 512
    stores = []
    done = 0
    for index, pick in enumerate(picks):
        for begin in range(0, width, span):
            columns = pl.ds(begin, span)

            def one(part, carry, index=index, pick=pick, columns=columns):
                rows = pl.ds(pl.multiple_of(part * block, block), block)
                tiles[index, rows, columns] = mm(
                    lefts[index][rows, :], rights[pick][:, columns]
                ).astype(tiles.dtype)
                return carry

            lax.fori_loop(0, units // block, one, 0)
            done += 1
            if done % per_round == 0:
                yield
        copy = pltpu.make_async_copy(tiles.at[index], out_refs[index], store.at[index])
        copy.start()
        stores.append(copy)
    for copy in stores:
        copy.wait()


def scattered_seq_products(value, lefts, rights, picks, number, pieces=2):
    total = lax.axis_size("seq")
    count = total // SIDE
    rows, width = value.shape[0] // total, value.shape[1] // pieces
    units, depth = lefts[0].shape
    breadth = rights[0].shape[1]
    n_left, n_right = len(lefts), len(rights)
    held = 4 * value.size // SIDE + n_left * units * (depth + breadth) + n_right * rights[0].size
    if 2 * held > VMEM_BYTES:
        products = [mm(left, rights[pick]).astype(bf16) for left, pick in zip(lefts, picks)]
        return scattered_seq(value, number, pieces), products

    def body(source, *rest):
        left_hbm, rest = rest[:n_left], rest[n_left:]
        right_hbm, rest = rest[:n_right], rest[n_right:]
        out, out_refs, rest = rest[0], rest[1 : 1 + n_left], rest[1 + n_left :]
        link, rest = rest[:7], rest[7:]
        left_held, rest = rest[:n_left], rest[n_left:]
        right_held, rest = rest[:n_right], rest[n_right:]
        greet(seq_partners(count))

        def source_at(target, side, piece):
            begin = pl.multiple_of((target * SIDE + side) * rows, rows)
            return source.at[pl.ds(begin, rows), pl.ds(piece * width, width)]

        def out_at(piece):
            return out.at[:, pl.ds(piece * width, width)]

        run_together(
            [
                scatter_seq(source_at, out_at, *link, count),
                product_steps(
                    left_hbm, right_hbm, out_refs, picks, left_held, right_held, *rest, 2
                ),
            ]
        )

    outs = link_call(
        body,
        number,
        [ANY] * (1 + n_left + n_right),
        [IN_VMEM] + [ANY] * n_left,
        [shaped((rows, value.shape[1]), f32)]
        + [shaped((units, breadth), bf16) for _ in lefts],
        seq_scratch(pieces, count, rows, width)
        + [pltpu.VMEM((units, depth), bf16) for _ in lefts]
        + [pltpu.VMEM((depth, breadth), bf16) for _ in rights]
        + [
            pltpu.VMEM((n_left, units, breadth), bf16),
            DMA((n_left + n_right,)),
            DMA((n_left,)),
        ],
        120_000_000,
    )(value, *lefts, *rights)
    return outs[0], list(outs[1:])


def gathered_more(ends, half, number, swap=None):
    total, heads = lax.axis_size("seq"), lax.axis_size("head")
    count = total // SIDE
    swaps = [] if swap is None else [swap]

    def body(ends_ref, half_ref, *rest):
        head, line, side = seq_places()
        beside = (head, line * SIDE + 1 - side)
        swap_refs, rest = rest[: len(swaps)], rest[len(swaps) :]
        ends_out, half_out, rest = rest[0], rest[1], rest[2:]
        swap_outs, rest = rest[: len(swaps)], rest[len(swaps) :]
        greet(head_partners() + seq_partners(count))

        def swap_steps(source, target):
            yield
            yield
            copy = remote(source, target, rest[8].at[0], rest[8].at[1], beside)
            copy.start()
            for _ in range(count):
                yield
            copy.wait()

        run_together(
            [
                gather_seq(ends_ref, ends_out, *rest[:5], count),
                gather_head(half_ref, half_out, *rest[5:8], 1),
            ]
            + [swap_steps(*refs) for refs in zip(swap_refs, swap_outs)]
        )

    outs = link_call(
        body,
        number,
        [ANY] * (2 + len(swaps)),
        [ANY] * (2 + len(swaps)),
        [
            shaped((total,) + ends.shape, ends.dtype),
            shaped((heads,) + half.shape, half.dtype),
        ]
        + [shaped(value.shape, value.dtype) for value in swaps],
        [DMA((1,))]
        + [DMA((2 * count,)) for _ in range(4)]
        + [DMA((1,)), DMA((3, 1)), DMA((3, 1)), DMA((2,))],
        150_000_000,
    )(ends, half, *swaps)
    return [outs[0], outs[1].reshape(-1, half.shape[1])] + list(outs[2:])


def scattered_last(qkv, gate, normed, hat, mlp, small, gain_rows, number, pieces=4, gate_pieces=2):
    total, heads = lax.axis_size("seq"), lax.axis_size("head")
    count = total // SIDE
    rows, width = qkv.shape[0] // total, qkv.shape[1] // pieces
    gate_width = gate.shape[1] // gate_pieces
    own_rows = normed.shape[0] // heads
    units, slices = mlp[0].shape[0], mlp[0].shape[1] // heads
    small_rows = small.shape[0]

    def body(qkv_ref, gate_ref, normed_ref, hat_ref, small_ref, *rest):
        mlp_refs, rest = rest[: len(mlp)], rest[len(mlp) :]
        qkv_out, gate_out, normed_out, small_out, rest = rest[0], rest[1], rest[2], rest[3], rest[4:]
        mlp_outs, rest = rest[: len(mlp)], rest[len(mlp) :]
        greet(head_partners() + seq_partners(count))

        def qkv_at(target, side, piece):
            begin = pl.multiple_of((target * SIDE + side) * rows, rows)
            return qkv_ref.at[pl.ds(begin, rows), pl.ds(piece * width, width)]

        def gate_at(target, side, piece):
            begin = pl.multiple_of(target * rows, rows)
            return gate_ref.at[pl.ds(begin, rows), pl.ds(piece * gate_width, gate_width)]

        def normed_at(target):
            return normed_ref.at[pl.ds(pl.multiple_of(target * own_rows, own_rows), own_rows)]

        def normed_steps(four, own, local, *sems):
            yield from scatter_head(normed_at, normed_out, *rest[13:19], 0, 1)
            own[...] = small_ref[...]
            product = jnp.sum(normed_out[...] * hat_ref[...], axis=0, keepdims=True)
            for row in range(product.shape[1] // 128):
                own[row : row + 1] = product[:, row * 128 : (row + 1) * 128]
            yield
            yield from gather_head(own, four, sems[0], sems[1], sems[2], 1)
            own[:gain_rows] = jnp.sum(four[:, :gain_rows], axis=0)
            for step in gather_seq(own, small_out, local, *sems[3:7], count):
                for _ in range(3):
                    yield

        steps = [
            normed_steps(*rest[19:29]),
            scatter_seq(
                gate_at,
                lambda piece: gate_out.at[:, pl.ds(piece * gate_width, gate_width)],
                rest[7],
                None,
                *rest[8:13],
                count,
            ),
            scatter_seq(
                qkv_at,
                lambda piece: qkv_out.at[:, pl.ds(piece * width, width)],
                *rest[:7],
                count,
            ),
        ]
        for index, (ref, out) in enumerate(zip(mlp_refs, mlp_outs)):

            def mlp_at(target, ref=ref):
                return ref.at[:, pl.ds(pl.multiple_of(target * slices, slices), slices)]

            begin = 29 + 6 * index
            steps.append(
                scatter_head(mlp_at, out, *rest[begin : begin + 6], HOLD, 2 + 3 * index)
            )
        run_together(steps)

    line_scratch = seq_scratch(gate_pieces, count, rows, gate_width)
    outs = link_call(
        body,
        number,
        [ANY] * 3 + [IN_VMEM] * 2 + [ANY] * len(mlp),
        [IN_VMEM] * (4 + len(mlp)),
        [
            shaped((rows, qkv.shape[1]), bf16),
            shaped((rows, gate.shape[1]), bf16),
            shaped((own_rows, normed.shape[1]), f32),
            shaped((total, small_rows, small.shape[1]), f32),
        ]
        + [shaped((units, slices), bf16) for _ in mlp],
        seq_scratch(pieces, count, rows, width)
        + line_scratch[1:]
        + head_scratch(own_rows, normed.shape[1])
        + [
            pltpu.VMEM((heads, small_rows, small.shape[1]), f32),
            pltpu.VMEM((small_rows, small.shape[1]), f32),
            DMA((1,)),
            DMA((1,)),
            DMA((3, 1)),
            DMA((3, 1)),
        ]
        + [DMA((2 * count,)) for _ in range(4)]
        + head_scratch(units, slices) * len(mlp),
        250_000_000,
    )(qkv, gate, normed, hat, small, *mlp)
    return outs[0], outs[1], outs[2], outs[3], list(outs[4:])


def side_columns(value, side, rows):
    count = value.shape[1] // (rows * SIDE)
    return jnp.concatenate(
        [
            lax.dynamic_slice_in_dim(value, (place * SIDE + side) * rows, rows, 1)
            for place in range(count)
        ],
        axis=1,
    )


def swapped(value):
    count = lax.axis_size("seq")
    return lax.ppermute(value, "seq", [(place, place ^ 1) for place in range(count)])


def silu_slope(tensor):
    sigmoid_part = jax.nn.sigmoid(tensor)
    return sigmoid_part * (1.0 + tensor * (1.0 - sigmoid_part))


def gathered(value, axis):
    return lax.all_gather(value, axis, axis=0, tiled=True)


def scattered(value, axis, dimension=0):
    return lax.psum_scatter(
        value.astype(bf16), axis, scatter_dimension=dimension, tiled=True
    ).astype(f32)


def on_device(
    block_in,
    out_cot,
    gain_one,
    qkv_weight,
    conv_weight,
    gate_weight,
    gain_out,
    out_weight,
    gain_two,
    mlp_gate,
    mlp_up,
    mlp_down,
    decay_code,
    beta_code,
):
    span_rows = decay_code.shape[0]
    width, heads, inner = qkv_weight.shape
    total_len = span_rows * lax.axis_size("seq")
    lead_rows = conv_weight.shape[0] - 1
    input_f = block_in.astype(f32)
    gain_first = gain_one.astype(f32)
    gain_second = gain_two.astype(f32)
    gain_head = gain_out.reshape(1, -1)
    taps = conv_weight.reshape(conv_weight.shape[0], heads * inner)
    out_flat = out_weight.reshape(heads * DV, width)
    columns, run_rows = token_columns(decay_code, beta_code, total_len)

    cot_all = gathered(out_cot, "seq")
    seq_count, head_count = lax.axis_size("seq"), lax.axis_size("head")
    seq_at, head_at = lax.axis_index("seq"), lax.axis_index("head")
    side = lax.rem(seq_at, SIDE)
    slice_rows = width // seq_count
    scale_own = rms_scale(input_f)
    hat_own = input_f * scale_own
    normed_own = (hat_own * gain_first).astype(bf16)
    normed_first, normed_half = gathered_crossed(
        normed_own, side_columns(normed_own, 1 - side, slice_rows), 1
    )
    mixed_in = jnp.einsum(
        "td,dhc->htc", normed_first, qkv_weight, preferred_element_type=f32
    ).astype(bf16)
    tail_in = passed_along(mixed_in[:, span_rows - 8 :], "seq", 1)
    tail_in = jnp.where(jnp.arange(8)[:, None] >= 8 - lead_rows, tail_in.astype(f32), 0.0)
    solve, score, fresh, reach, inner_part, turn, local_states, piece_end = run_local_forward(
        mixed_in, tail_in, taps, columns, run_rows, heads
    )
    ends, normed_side = gathered_more(piece_end.reshape(-1, DV + DK), normed_half, 2)
    ends = ends.reshape(-1, heads, DK, DV + DK)
    gate_pre = jnp.einsum("td,dhv->htv", normed_first, gate_weight, preferred_element_type=f32)
    states, core, branch = run_finish_forward(
        ends, local_states, reach, inner_part, gate_pre, gain_head
    )
    branch, cot_all = lax.optimization_barrier((branch, cot_all))
    branch_side = swapped(branch)
    middle = input_f + scattered_head(mm(branch, out_flat).astype(bf16), 3)
    scale_two = rms_scale(middle)
    hat_two = middle * scale_two
    normed_two = (hat_two * gain_second).astype(bf16)

    normed_two, branch_side = lax.optimization_barrier((normed_two, branch_side))
    rows_out = gathered_seq(normed_two, 4).reshape(-1, width)
    cot_f = out_cot.astype(f32)
    gate_units, up_units = mlp_gate.T, mlp_up.T
    gate_part = mm_nt(gate_units, rows_out)
    up_part = mm_nt(up_units, rows_out)
    d_hidden = mm_nt(mlp_down, cot_all)
    hidden = (jax.nn.silu(gate_part) * up_part).astype(bf16)
    d_gate_mlp = (d_hidden * up_part * silu_slope(gate_part)).astype(bf16)
    d_up_mlp = (d_hidden * jax.nn.silu(gate_part)).astype(bf16)
    d_rows = (mm_tn(d_gate_mlp, gate_units) + mm_tn(d_up_mlp, up_units)).astype(bf16)
    d_normed_two, (grad_mgate, grad_mup, grad_down) = scattered_seq_products(
        d_rows, [d_gate_mlp, d_up_mlp, hidden], [rows_out, cot_all], [0, 0, 1], 5
    )
    gain_two_part = jnp.sum(d_normed_two * hat_two, 0)
    e_two = d_normed_two * gain_second
    d_middle = cot_f + scale_two * (
        e_two - hat_two * jnp.mean(e_two * hat_two, axis=-1, keepdims=True)
    )
    hidden, d_middle = lax.optimization_barrier((hidden, d_middle))
    mlp_part, d_middle = lax.optimization_barrier(
        (mm_tn(hidden, mlp_down).astype(bf16), d_middle)
    )
    mlp_out = scattered(mlp_part, "seq")
    d_mix = d_middle.astype(bf16)
    d_mix_all, d_mix_half = gathered_crossed(d_mix, side_columns(d_mix, 1 - side, slice_rows), 6)
    d_branch = mm_nt(d_mix_all, out_flat)
    d_core, d_gate_low, gain_out_part, local_grads, grad_end = run_local_backward(
        d_branch, core, gate_pre, gain_head, reach, turn
    )
    grad_ends, d_mix_side = gathered_more(grad_end.reshape(-1, DV), d_mix_half, 7)
    d_gate_low, grad_ends = lax.optimization_barrier((d_gate_low, grad_ends))
    d_gate_side = swapped(d_gate_low)
    out_half = (
        mm_tn(side_columns(d_mix_all, side, slice_rows), branch) + mm_tn(d_mix_side, branch_side)
    ).astype(bf16)
    grad_ends = grad_ends.reshape(-1, heads, DK, DV)
    d_mixed, d_tail, d_lead, grad_conv = run_finish_backward(
        ends,
        grad_ends,
        mixed_in,
        tail_in,
        taps,
        columns,
        run_rows,
        solve,
        score,
        fresh,
        states,
        d_core,
        local_grads,
    )
    out_half, mlp_out, d_lead, d_gate_side = lax.optimization_barrier(
        (out_half, mlp_out, d_lead, d_gate_side)
    )
    output = (middle + mlp_out).astype(bf16)
    grad_out_s = lax.psum_scatter(
        out_half,
        "seq",
        scatter_dimension=0,
        axis_index_groups=[
            [place * SIDE + across for place in range(seq_count // SIDE)] for across in range(SIDE)
        ],
        tiled=True,
    )
    from_next = passed_along(d_lead[:lead_rows], "seq", -1)
    d_tail = d_tail.at[8 - lead_rows :].add(from_next).astype(bf16)
    d_mixed = lax.dynamic_update_slice(d_mixed, d_tail, (span_rows - 8, 0))
    d_normed_part = jnp.einsum(
        "thc,dhc->td",
        d_mixed.reshape(span_rows, heads, inner),
        qkv_weight,
        preferred_element_type=f32,
    ) + jnp.einsum(
        "thv,dhv->td",
        d_gate_low.reshape(span_rows, heads, DV),
        gate_weight,
        preferred_element_type=f32,
    )
    grad_qkv = mm_tn(normed_first, d_mixed).astype(bf16)
    grad_gate = (
        mm_tn(side_columns(normed_first, side, slice_rows), d_gate_low)
        + mm_tn(normed_side, d_gate_side)
    ).astype(bf16)

    grad_qkv, grad_out_s = lax.optimization_barrier((grad_qkv, grad_out_s))
    gains = jnp.concatenate([jnp.zeros_like(gain_two_part), gain_two_part, gain_out_part.reshape(-1)])
    gain_rows = -(-gains.shape[0] // 1024) * 8
    gains = jnp.pad(gains, (0, gain_rows * 128 - gains.shape[0])).reshape(gain_rows, 128)
    small = jnp.concatenate([gains, grad_conv.reshape(-1, 128)])
    grad_qkv_s, grad_gate_s, d_normed_one, small_all, (grad_mgate_t, grad_mup_t, grad_down_h) = (
        scattered_last(
            grad_qkv,
            grad_gate,
            d_normed_part.astype(bf16),
            hat_own,
            [grad_mgate, grad_mup, grad_down],
            small,
            gain_rows,
            8,
        )
    )
    e_one = d_normed_one * gain_first
    d_input = (
        d_middle + scale_own * (e_one - hat_own * jnp.mean(e_one * hat_own, axis=-1, keepdims=True))
    ).astype(bf16)

    small_sum = jnp.sum(small_all, axis=0)
    gains = small_sum[:gain_rows].reshape(-1)

    def own_slice(begin, length):
        length = length // (seq_count * head_count)
        return lax.dynamic_slice(
            gains, (begin + (head_at * seq_count + seq_at) * length,), (length,)
        )

    grad_conv_s = lax.dynamic_slice_in_dim(
        small_sum[gain_rows:].reshape(-1, heads, inner),
        seq_at * (inner // seq_count),
        inner // seq_count,
        2,
    )
    return (
        output,
        d_input,
        own_slice(0, width),
        grad_qkv_s.astype(f32).reshape(-1, heads, inner),
        grad_conv_s,
        grad_gate_s.astype(f32).reshape(-1, heads, DV),
        own_slice(2 * width, DV),
        grad_out_s.astype(f32).T.reshape(heads, DV, -1),
        own_slice(width, width),
        grad_mgate_t.astype(f32).T,
        grad_mup_t.astype(f32).T,
        grad_down_h.astype(f32),
    )


def solution(mesh):
    in_specs = (
        P(("seq", "head"), None),
        P(("seq", "head"), None),
        P(),
        P(None, "head", None),
        P(None, "head", None),
        P(None, "head", None),
        P(),
        P("head", None, None),
        P(),
        P(None, "seq"),
        P(None, "seq"),
        P("seq", None),
        P("seq", "head"),
        P("seq", "head"),
    )
    out_specs = (
        P(("seq", "head"), None),
        P(("seq", "head"), None),
        P(("head", "seq")),
        P("seq", "head", None),
        P(None, "head", "seq"),
        P("seq", "head", None),
        P(("head", "seq")),
        P("head", None, "seq"),
        P(("head", "seq")),
        P("head", "seq"),
        P("head", "seq"),
        P("seq", "head"),
    )
    return jax.shard_map(
        on_device, mesh=mesh, in_specs=in_specs, out_specs=out_specs, check_vma=False
    )
```
